32 devices in a mesh: grp: 8 (over z, x), sp: 4 (over y, core).
Axes of the slice: x: 2, y: 2, z: 4, core: 2. Of those that a mesh axis runs over, the one named last changes fastest.
Arguments:
- queries: bfloat16 [5120, 4096], P(('grp', 'sp')), may hold values from -128 to 128
- fresh_key_values: bfloat16 [5120, 1024], P(('grp', 'sp')), may hold values from -4 to 4
- cache: bfloat16 [8, 4, 512, 256], P('grp', 'sp'), may hold values from -4 to 4
- lengths: int32 [8, 4], P('grp', 'sp'), may hold values from 1 to 160, 512 in all within a row
- out_weight: bfloat16 [4096, 2048], P('sp'), may hold values from -1 to 1
- residual: bfloat16 [5120, 2048], P(('grp', 'sp')), may hold values from -36 to 36
- norm_gain: float32 [2048], replicated, may hold values from 0.1 to 1.9
- expert_ids: int32 [5120, 8], P(('grp', 'sp')), may hold values from 0 to 31, all different within a row; in each aligned block of 160 rows (0 to 159, 160 to 319, ...) at most 64 rows name the same one
- gate_values: float32 [5120, 8], P(('grp', 'sp')), may hold values from 0.05 to 0.5
- up_gate_weight: bfloat16 [32, 2048, 1536], P(('grp', 'sp')), may hold values from -0.125 to 0.125
- down_weight: bfloat16 [32, 768, 2048], P(('grp', 'sp')), may hold values from -0.21875 to 0.21875
Outputs:
- attended: bfloat16 [5120, 2048], P(('grp', 'sp'))
- moe_out: bfloat16 [5120, 2048], P(('grp', 'sp'))
The draws below stay inside these ranges and needn't reach their ends.
Inputs may be any that keep to these rules, and one draw needn't show every extreme that they name: Each group's 4 lengths sum to 512, and in every group one device has exactly 160. `expert_ids`: each slot names 8 different experts; among the 160 slots of one device no expert is named more than 64 times, and one expert is named exactly 64 times by the slots of some device.
All inputs are finite; a program needn't handle non-finite values.
Results may differ from the reference program's by a relative error of at most 0.02.
Values may be sent and summed in bfloat16 or wider, within the bound.
No kernel may reach another device: no remote copies, remote signals or barrier semaphores. Data moves between devices by JAX's collectives and lax.ppermute only.
A program may use at most 128 MiB of HBM per device.

```python
import math
import jax
import jax.numpy as jnp
import numpy as np
from jax import lax

D = 2048
QUERY_HEADS = 32
KEY_VALUE_HEADS = 4
HEAD_SIZE = 128
FF = 768
TOPK = 8
CACHED_POSITIONS = 512
TOKEN_GROUPS = 8
GROUP_DEVICES = 4
E = 32
ROWS = 160
TOK_GRP = 512
SLOTS_PER_GROUP = 640
TOTAL_SLOTS = 5120
DEVICE_CACHE = 512
CAP = 64
DEVICES = 32


def cache_logical(key):
    starting_rows = jnp.clip(jax.random.normal(jax.random.fold_in(key, 701), (TOKEN_GROUPS, KEY_VALUE_HEADS, CACHED_POSITIONS, 2 * HEAD_SIZE), jnp.float32), -4.0, 4.0)
    return starting_rows


def draw_cache(key, part):
    return cache_logical(key).reshape(TOKEN_GROUPS, GROUP_DEVICES, DEVICE_CACHE, 2 * HEAD_SIZE).astype(jnp.bfloat16)


def draw_queries(key, part):
    query_key = jax.random.fold_in(key, 702)
    noise = jnp.clip(jax.random.normal(query_key, (TOTAL_SLOTS, QUERY_HEADS * HEAD_SIZE), jnp.float32), -4.0, 4.0) * 1.5
    return noise.astype(jnp.bfloat16)


def draw_residual(key, part):
    split_keys = jax.random.split(jax.random.fold_in(key, 703), 3)
    row_scale = jnp.exp(jax.random.uniform(split_keys[0], (TOTAL_SLOTS, 1), jnp.float32, minval=math.log(0.3), maxval=math.log(3.0)))
    col_scale = jnp.exp(jax.random.uniform(split_keys[1], (1, D), jnp.float32, minval=math.log(0.3), maxval=math.log(3.0)))
    core = jnp.clip(jax.random.normal(split_keys[2], (TOTAL_SLOTS, D), jnp.float32), -4.0, 4.0)
    return (core * row_scale * col_scale).astype(jnp.bfloat16)


def shard_levels(stream_key, dims, cuts, smallest, top_value):
    def one(axis_at, blocks):
        heights = jax.random.uniform(jax.random.fold_in(jax.random.fold_in(stream_key, 6), axis_at), (blocks,), jnp.float32, smallest / len(cuts), top_value / len(cuts))
        return jnp.repeat(jnp.exp(heights), dims[axis_at] // blocks).reshape((-1,) + (1,) * (len(dims) - axis_at - 1))

    level = one(*cuts[0])
    for cut in cuts[1:]:
        level = level * one(*cut)
    return level


def length_profile(amount, total, bound, skew):
    loads = [(1 << 20) // math.isqrt(standing ** skew) + 1 for standing in range(2, amount + 1)]
    spare, holding = total - bound - (amount - 1), [1] * (amount - 1)
    while spare > 0:
        candidates = [i for i in range(amount - 1) if holding[i] < bound]
        whole, budget = sum([loads[i] for i in candidates]), spare
        for i in candidates:
            extra = min(bound - holding[i], max(1, budget * loads[i] // whole), spare)
            holding[i] = holding[i] + extra
            spare = spare - extra
    return np.array([bound] + holding)


def ragged(rng, count, total, reach, lean):
    if count == 2:
        one = jax.random.randint(rng, (), max(1, total - reach), min(reach, total - 1) + 1)
        return jnp.stack([one, total - one])
    sizes = jnp.asarray(length_profile(count, total, reach, lean), jnp.int32)
    pairs = (count - 1) // 2
    donor, sink = sizes[1:1 + 2 * pairs:2], sizes[2:2 + 2 * pairs:2]
    slack = jnp.minimum(donor - 1, reach - sink)
    shifted = jax.random.randint(jax.random.fold_in(rng, 1), (pairs,), 0, 1 << 20) % (slack + 1)
    sizes = sizes.at[1:1 + 2 * pairs:2].set(donor - shifted).at[2:2 + 2 * pairs:2].set(sink + shifted)
    return sizes[jax.random.permutation(jax.random.fold_in(rng, 2), count)]


def assign_block(stream_key, own, number, rows, amount, top, most, lean):
    ranking = jax.random.permutation(stream_key, amount)
    packed, usual = shares(amount, rows * top, most, lean, True), shares(amount, rows * top, most, lean, False)
    places = jnp.arange(amount)

    def named(sizes, offset_by):
        used = int((sizes > 0).sum())
        fixed = max(1, used // 4)
        shifted = fixed + (places - fixed + offset_by * (used - fixed)) % max(1, amount - fixed)
        return jnp.zeros((amount,), jnp.int32).at[ranking[jnp.where(places < fixed, places, shifted)]].set(jnp.asarray(sizes, jnp.int32))

    sizes = jnp.where(number % 4 == 0, named(packed, number // 4), named(usual, number - number // 4 - 1))
    mixed = jax.random.permutation(jax.random.fold_in(own, 3), amount)
    giver, taker = mixed[0:amount // 2 * 2:2], mixed[1:amount // 2 * 2:2]
    slack = jnp.minimum(sizes[giver] - 1, most - sizes[taker]) // 2
    slack = jnp.where((giver == ranking[0]) | (taker == ranking[0]) | (sizes[taker] == 0), 0, jnp.maximum(slack, 0))
    shifted = jax.random.randint(jax.random.fold_in(own, 4), (amount // 2,), 0, 1 << 20) % (slack + 1)
    sizes = sizes.at[giver].add(-shifted).at[taker].add(shifted)
    labels = jnp.searchsorted(jnp.cumsum(sizes), jnp.arange(rows * top), side="right").astype(jnp.int32)
    table = labels.reshape(top, rows).T
    table = table[jax.random.permutation(jax.random.fold_in(own, 1), rows)]
    offset_by = jax.random.randint(jax.random.fold_in(own, 2), (rows, 1), 0, top)
    return jnp.take_along_axis(table, (jnp.arange(top)[None, :] + offset_by) % top, axis=1)


def shares(amount, total, reach, slope, full):
    weights = [(1 << 20) // math.isqrt(standing ** slope) + 1 for standing in range(1, amount + 1)]
    largest = reach if full else min(reach, max(-(-total // amount), total * weights[0] // sum(weights)))
    least = 1 if total - largest >= amount - 1 else 0
    counts, spare = [largest] + [least] * (amount - 1), total - largest - least * (amount - 1)
    while spare > 0:
        free = [i for i in range(1, amount) if counts[i] < largest] or [i for i in range(1, amount) if counts[i] < reach]
        pool, budget = sum([weights[i] for i in free]), spare
        for i in free:
            extra = min(reach - counts[i], max(1, budget * weights[i] // pool), spare)
            counts[i] = counts[i] + extra
            spare = spare - extra
    return np.array(counts)


def bell_draw(key, extent, deviation, limit, cuts=(), held_as=jnp.bfloat16):
    loudness = shard_levels(key, extent, cuts, -0.22, 0.18) if cuts else 1.0
    result = jax.random.normal(key, extent, jnp.float32) * deviation * loudness
    return jnp.minimum(jnp.maximum(result, -limit), limit).astype(held_as)


def setup_inputs(seed: int = 0) -> dict:
    key_list = jax.random.split(jax.random.key(seed), 12)
    queries = draw_queries(jax.random.fold_in(key_list[11], 71), 0)
    fresh_key_values = bell_draw(key_list[1], (TOTAL_SLOTS, 2 * KEY_VALUE_HEADS * HEAD_SIZE), 1.0, 4.0, ((0, 32),))
    cache = draw_cache(jax.random.fold_in(key_list[11], 71), 0)
    lengths = jax.vmap(lambda own: ragged(own, GROUP_DEVICES, TOK_GRP, ROWS, 2))(jax.random.split(key_list[3], TOKEN_GROUPS)).reshape((TOKEN_GROUPS, GROUP_DEVICES)).astype(jnp.int32)
    out_weight = bell_draw(key_list[4], (QUERY_HEADS * HEAD_SIZE, D), 0.0625, 1.0, ((0, 4),))
    residual = draw_residual(jax.random.fold_in(key_list[11], 71), 0)
    norm_gain = jnp.clip(1.0 + 0.18 * jax.random.normal(key_list[6], (D,), jnp.float32), 0.1, 1.9)
    expert_ids_keys = jax.random.split(jax.random.fold_in(key_list[7], 1), TOTAL_SLOTS // ROWS)
    expert_ids_turns = jax.random.permutation(jax.random.fold_in(key_list[7], 3), TOTAL_SLOTS // ROWS)
    expert_ids = jax.vmap(lambda own, number: assign_block(jax.random.fold_in(key_list[7], 2), own, number, ROWS, E, TOPK, CAP, 2))(expert_ids_keys, expert_ids_turns).reshape((TOTAL_SLOTS, TOPK))
    gate_values = jnp.clip(jnp.exp(math.log(0.5) - 2.3025851 * jax.random.uniform(key_list[8], (TOTAL_SLOTS, TOPK), jnp.float32) ** shard_levels(key_list[8], (TOTAL_SLOTS, TOPK), ((0, 32),), -0.2, 0.2)), 0.05, 0.5)
    up_gate_weight = bell_draw(key_list[9], (E, D, 2 * FF), D ** -0.5, 0.125, ((0, 32),))
    down_weight = bell_draw(key_list[10], (E, FF, D), FF ** -0.5, 0.21875, ((0, 32),))
    return {"queries": queries, "fresh_key_values": fresh_key_values, "cache": cache, "lengths": lengths, "out_weight": out_weight, "residual": residual, "norm_gain": norm_gain, "expert_ids": expert_ids, "gate_values": gate_values, "up_gate_weight": up_gate_weight, "down_weight": down_weight}


def attend_group(inputs, out_weight):
    rows_of_queries, key_value_rows, cached_rows, stretch_lens = inputs
    rows_of_group = rows_of_queries.shape[0]
    queries_per_key_head = QUERY_HEADS // KEY_VALUE_HEADS
    stretch_lens = stretch_lens.astype(jnp.int32)
    offsets = (jnp.cumsum(stretch_lens) - stretch_lens).astype(jnp.int32)
    slot_ids = jnp.arange(rows_of_group, dtype=jnp.int32)
    source = slot_ids // ROWS
    within = slot_ids % ROWS
    is_live = within < stretch_lens[source]
    position = offsets[source] + within
    allowed = is_live[None, :] & (position[None, :] <= position[:, None])
    visible = jnp.concatenate([jnp.ones((rows_of_group, CACHED_POSITIONS), dtype=bool), allowed], axis=1)
    cached_heads = cached_rows.reshape(KEY_VALUE_HEADS, CACHED_POSITIONS, 2 * HEAD_SIZE)
    queries_by_head = rows_of_queries.reshape(rows_of_group, KEY_VALUE_HEADS, queries_per_key_head, HEAD_SIZE).transpose(1, 2, 0, 3)
    fresh_keys = key_value_rows[:, :KEY_VALUE_HEADS * HEAD_SIZE].reshape(rows_of_group, KEY_VALUE_HEADS, HEAD_SIZE).transpose(1, 0, 2)
    fresh_values = key_value_rows[:, KEY_VALUE_HEADS * HEAD_SIZE:].reshape(rows_of_group, KEY_VALUE_HEADS, HEAD_SIZE).transpose(1, 0, 2)

    def one_head(parts):
        query_part, key_new, value_new, cache_part = parts
        key_all = jnp.concatenate([cache_part[:, :HEAD_SIZE], key_new], axis=0).astype(jnp.float32)
        value_all = jnp.concatenate([cache_part[:, HEAD_SIZE:], value_new], axis=0).astype(jnp.float32)
        scores = jnp.einsum('grd,kd->grk', query_part.astype(jnp.float32), key_all) / math.sqrt(HEAD_SIZE)
        scores = jnp.where(visible[None], scores, -jnp.inf)
        row_max = lax.optimization_barrier(jnp.max(scores, axis=-1, keepdims=True))
        weights = jnp.exp(scores - row_max)
        totals = lax.optimization_barrier(jnp.sum(weights, axis=-1, keepdims=True))
        probs = lax.optimization_barrier(weights.astype(jnp.bfloat16)).astype(jnp.float32)
        return (jnp.einsum('grk,kd->grd', probs, value_all) / totals).astype(jnp.bfloat16)
    results = lax.map(one_head, (queries_by_head, fresh_keys, fresh_values, cached_heads))
    heads = results.reshape(QUERY_HEADS, rows_of_group, HEAD_SIZE).transpose(1, 0, 2).reshape(rows_of_group, QUERY_HEADS * HEAD_SIZE)
    return (jnp.dot(heads, out_weight, preferred_element_type=jnp.float32), is_live)

def reference(queries, fresh_key_values, cache, lengths, out_weight, residual, norm_gain, expert_ids, gate_values, up_gate_weight, down_weight):

    def group_labour(parts):
        return attend_group(parts, out_weight)
    attention_groups, active_groups = lax.map(group_labour, (queries.reshape(TOKEN_GROUPS, SLOTS_PER_GROUP, QUERY_HEADS * HEAD_SIZE), fresh_key_values.reshape(TOKEN_GROUPS, SLOTS_PER_GROUP, 2 * KEY_VALUE_HEADS * HEAD_SIZE), cache.reshape(TOKEN_GROUPS, GROUP_DEVICES * DEVICE_CACHE, 2 * HEAD_SIZE), lengths))
    attn_sum = attention_groups.reshape(TOTAL_SLOTS, D)
    is_live = active_groups.reshape(TOTAL_SLOTS)
    attended = jnp.where(is_live[:, None], attn_sum, 0.0).astype(jnp.bfloat16)
    mixed_rows = residual.astype(jnp.float32) + attn_sum
    normed = (mixed_rows * lax.rsqrt(lax.optimization_barrier(jnp.mean(mixed_rows * mixed_rows, axis=-1, keepdims=True)) + 1e-06) * norm_gain).astype(jnp.bfloat16)
    route_ids = expert_ids.reshape(DEVICES, ROWS, TOPK)
    live_dev = is_live.reshape(DEVICES, ROWS)
    expert_range = jnp.arange(E, dtype=jnp.int32)
    chosen = jnp.any(route_ids[..., None] == expert_range, axis=2) & live_dev[..., None]
    counted = chosen.astype(jnp.int32)
    prefix = (jnp.cumsum(counted, axis=1) - counted).astype(jnp.int32)
    slot_in = jnp.take_along_axis(prefix, route_ids, axis=2).astype(jnp.int32)
    device_ids = jnp.arange(DEVICES, dtype=jnp.int32)[:, None, None]
    table_size = E * DEVICES * CAP
    target = jnp.where(live_dev[..., None], route_ids * (DEVICES * CAP) + device_ids * CAP + slot_in, table_size).reshape(-1).astype(jnp.int32)
    token_ids = jnp.broadcast_to(jnp.arange(TOTAL_SLOTS, dtype=jnp.int32).reshape(DEVICES, ROWS, 1), route_ids.shape).reshape(-1)
    token_table = jnp.full((table_size + 1,), TOTAL_SLOTS, dtype=jnp.int32).at[target].set(token_ids)[:table_size].reshape(E, DEVICES * CAP)
    gate_table = jnp.zeros((table_size + 1,), jnp.float32).at[target].set(gate_values.reshape(-1))[:table_size].reshape(E, DEVICES * CAP)
    padded = jnp.concatenate([normed, jnp.zeros((1, D), jnp.bfloat16)], axis=0)

    def one_expert(accum, parts):
        token_col, gate_col, up_gate, down_part = parts
        rows_in = padded[token_col]
        projected = jnp.dot(rows_in, up_gate, preferred_element_type=jnp.float32)
        hidden = (jax.nn.silu(projected[:, :FF]) * projected[:, FF:]).astype(jnp.bfloat16)
        expert_out = jnp.dot(hidden, down_part, preferred_element_type=jnp.float32).astype(jnp.bfloat16)
        return (accum.at[token_col].add(gate_col[:, None] * expert_out.astype(jnp.float32)), None)
    accum = lax.scan(one_expert, jnp.zeros((TOTAL_SLOTS + 1, D), jnp.float32), (token_table, gate_table, up_gate_weight, down_weight))[0]
    moe_out = jnp.where(is_live[:, None], accum[:TOTAL_SLOTS], 0.0).astype(jnp.bfloat16)
    return (attended, moe_out)
```

```python
import math

import jax
import jax.numpy as jnp
from jax import lax
from jax.sharding import PartitionSpec as P


def partner_2(value, axis, bit):
    mask = 2**bit
    pairs = [(source, source ^ mask) for source in range(lax.axis_size(axis))]
    return lax.ppermute(value, axis, pairs)


def experts_by_exchange(
    normed, own_live, expert_ids, gate_values, up_gate_weight, down_weight, capacity
):
    slot_rows, model_width = normed.shape
    top_count = expert_ids.shape[1]
    hidden_width = down_weight.shape[1]
    experts = up_gate_weight.shape[0] * lax.axis_size(("grp", "sp"))
    choose = expert_ids[:, :, None] == jnp.arange(experts, dtype=jnp.int32)[None, None, :]
    routed = (jnp.any(choose, axis=1) & own_live[:, None]).astype(jnp.float32)
    earlier = (jnp.arange(slot_rows)[:, None] > jnp.arange(slot_rows)[None, :]).astype(jnp.float32)
    prefix = jnp.dot(earlier, routed, precision=lax.Precision.HIGHEST)
    slot_in = jnp.sum(jnp.where(choose, prefix[:, None, :], 0.0), axis=2).astype(jnp.int32)
    dump_slot = experts * capacity
    target = jnp.where(own_live[:, None], expert_ids * capacity + slot_in, dump_slot)
    source_rows = (
        jnp.full((dump_slot + 1,), slot_rows, jnp.int32)
        .at[target.reshape(-1)]
        .set(jnp.repeat(jnp.arange(slot_rows, dtype=jnp.int32), top_count))[:dump_slot]
    )
    padded = jnp.concatenate([normed, jnp.zeros((1, model_width), jnp.bfloat16)], axis=0)
    outgoing = padded[source_rows].reshape(experts, capacity, model_width)
    received = lax.all_to_all(outgoing, ("grp", "sp"), split_axis=0, concat_axis=0, tiled=True)
    flat_rows = received.reshape(-1, model_width)
    projected = jnp.dot(flat_rows, up_gate_weight[0], preferred_element_type=jnp.float32)
    hidden = (jax.nn.silu(projected[:, :hidden_width]) * projected[:, hidden_width:]).astype(
        jnp.bfloat16
    )
    returned = lax.all_to_all(
        jnp.dot(hidden, down_weight[0], preferred_element_type=jnp.float32)
        .astype(jnp.bfloat16)
        .reshape(received.shape),
        ("grp", "sp"),
        split_axis=0,
        concat_axis=0,
        tiled=True,
    )
    back_rows = jnp.concatenate(
        [returned.reshape(dump_slot, model_width), jnp.zeros((1, model_width), jnp.bfloat16)],
        axis=0,
    )
    picked = back_rows[target]
    combined = jnp.sum(gate_values[:, :, None] * picked.astype(jnp.float32), axis=1)
    moe_out = jnp.where(own_live[:, None], combined, 0.0).astype(jnp.bfloat16)
    return moe_out


def experts_by_gather(
    normed, own_live, expert_ids, gate_values, up_gate_weight, down_weight, capacity
):
    axes = ("grp", "sp")
    slot_rows, model_width = normed.shape
    hidden_width = down_weight.shape[1]
    devices = lax.axis_size(axes)
    mine = lax.axis_index(axes)
    live_ids = jnp.where(own_live[:, None], expert_ids, -1)
    ids_all = lax.all_gather(live_ids, axes, axis=0, tiled=False)
    gates_all = lax.all_gather(gate_values, axes, axis=0, tiled=False)
    chosen = ids_all == mine
    wanted = jnp.any(chosen, axis=2)
    gate = jnp.sum(jnp.where(chosen, gates_all, 0.0), axis=2)
    place = jnp.cumsum(wanted.astype(jnp.int32), axis=1) - 1
    pick = wanted[:, None, :] & (
        place[:, None, :] == jnp.arange(capacity, dtype=jnp.int32)[None, :, None]
    )
    rows_all = lax.all_gather(normed, axes, axis=0, tiled=False)
    picked = jnp.einsum(
        "bsr,brd->bsd", pick.astype(jnp.bfloat16), rows_all, preferred_element_type=jnp.float32
    ).astype(jnp.bfloat16)
    projected = jnp.dot(
        picked.reshape(devices * capacity, model_width),
        up_gate_weight[0],
        preferred_element_type=jnp.float32,
    )
    hidden = (jax.nn.silu(projected[:, :hidden_width]) * projected[:, hidden_width:]).astype(
        jnp.bfloat16
    )
    result = jnp.dot(hidden, down_weight[0], preferred_element_type=jnp.float32).astype(
        jnp.bfloat16
    )
    weight = jnp.where(pick, gate[:, None, :], 0.0).astype(jnp.bfloat16)
    share = jnp.einsum(
        "bsr,bsd->brd",
        weight,
        result.reshape(devices, capacity, model_width),
        preferred_element_type=jnp.float32,
    ).astype(jnp.bfloat16)
    return lax.psum_scatter(
        share.reshape(devices * slot_rows, model_width), axes, scatter_dimension=0, tiled=True
    )


def per_device(
    queries,
    fresh_key_values,
    cache,
    lengths,
    out_weight,
    residual,
    norm_gain,
    expert_ids,
    gate_values,
    up_gate_weight,
    down_weight,
):
    seq_devices = lax.axis_size("sp")
    slot_rows = queries.shape[0]
    head_width = cache.shape[-1] // 2
    model_width = residual.shape[1]
    kv_heads = fresh_key_values.shape[1] // (2 * head_width)
    repeat = seq_devices // kv_heads
    keys_new = fresh_key_values[:, : kv_heads * head_width].reshape(
        slot_rows, kv_heads, 1, head_width
    )
    values_new = fresh_key_values[:, kv_heads * head_width :].reshape(
        slot_rows, kv_heads, 1, head_width
    )
    paired = jnp.concatenate([keys_new, values_new], axis=3)
    spread = jnp.broadcast_to(paired, (slot_rows, kv_heads, repeat, 2 * head_width)).reshape(
        slot_rows, seq_devices * 2 * head_width
    )
    all_lengths = lax.all_gather(lengths, "sp", axis=1, tiled=True)
    queries_by_head, head_kv = (
        lax.all_to_all(queries, "sp", split_axis=1, concat_axis=0, tiled=True),
        lax.all_to_all(spread, "sp", split_axis=1, concat_axis=0, tiled=True),
    )
    cache_block = cache[0, 0]
    my_index = lax.axis_index("sp")
    for bit_pos in range(repeat.bit_length() - 1):
        partner = partner_2(cache_block, "sp", bit_pos)
        is_upper = my_index // 2**bit_pos % 2 == 1
        cache_block = jnp.where(
            is_upper,
            jnp.concatenate([partner, cache_block], axis=0),
            jnp.concatenate([cache_block, partner], axis=0),
        )
    stretch_lens = all_lengths[0]
    offsets = jnp.cumsum(stretch_lens) - stretch_lens
    rows_of_group = queries_by_head.shape[0]
    slot_ids = jnp.arange(rows_of_group, dtype=jnp.int32)
    source = slot_ids // slot_rows
    within = slot_ids % slot_rows
    from_device = source[:, None] == jnp.arange(seq_devices, dtype=jnp.int32)[None, :]
    is_live = within < jnp.sum(jnp.where(from_device, stretch_lens[None, :], 0), axis=1)
    position = within + jnp.sum(jnp.where(from_device, offsets[None, :], 0), axis=1)
    per_dev = queries_by_head.shape[1] // head_width
    cache_len = cache_block.shape[0]
    key_all = jnp.concatenate([cache_block[:, :head_width], head_kv[:, :head_width]], axis=0)
    value_all = jnp.concatenate([cache_block[:, head_width:], head_kv[:, head_width:]], axis=0)
    block_count = 2 if rows_of_group % 2 == 0 and rows_of_group >= 1024 else 1
    block_rows = rows_of_group // block_count

    def attend(parts):
        query_block, place_block = parts
        scores = jnp.einsum(
            "rhd,kd->hrk", query_block, key_all, preferred_element_type=jnp.float32
        ) / math.sqrt(head_width)
        allowed = jnp.concatenate(
            [
                jnp.ones((block_rows, cache_len), dtype=bool),
                is_live[None, :] & (position[None, :] <= place_block[:, None]),
            ],
            axis=1,
        )
        scores = jnp.where(allowed[None], scores, -jnp.inf)
        row_max = jnp.max(scores, axis=-1, keepdims=True)
        weights = jnp.exp(scores - row_max)
        totals = jnp.sum(weights, axis=-1, keepdims=True)
        result = (
            jnp.einsum(
                "hrk,kd->hrd",
                weights.astype(jnp.bfloat16),
                value_all,
                preferred_element_type=jnp.float32,
            )
            / totals
        )
        return (
            result.astype(jnp.bfloat16).transpose(1, 0, 2).reshape(block_rows, per_dev * head_width)
        )

    attn_heads = lax.map(
        attend,
        (
            queries_by_head.reshape(block_count, block_rows, per_dev, head_width),
            position.reshape(block_count, block_rows),
        ),
    ).reshape(rows_of_group, per_dev * head_width)
    attn_sum = lax.psum_scatter(
        jnp.dot(attn_heads, out_weight, preferred_element_type=jnp.float32).astype(jnp.bfloat16),
        "sp",
        scatter_dimension=0,
        tiled=True,
    ).astype(jnp.float32)
    own_live = jnp.arange(slot_rows, dtype=jnp.int32) < lengths[0, 0]
    attended = jnp.where(own_live[:, None], attn_sum, 0.0).astype(jnp.bfloat16)
    mixed_rows = residual.astype(jnp.float32) + attn_sum
    normed = (
        mixed_rows
        * lax.rsqrt(jnp.mean(mixed_rows * mixed_rows, axis=-1, keepdims=True) + 1e-06)
        * norm_gain
    ).astype(jnp.bfloat16)
    group_count = lax.axis_size("grp")
    experts = up_gate_weight.shape[0] * group_count * seq_devices
    top_count = expert_ids.shape[1]
    capacity = max(2, 8 * slot_rows * top_count // (5 * experts))
    if experts <= 4 * top_count:
        moe_out = experts_by_gather(
            normed, own_live, expert_ids, gate_values, up_gate_weight, down_weight, capacity
        )
    else:
        moe_out = experts_by_exchange(
            normed, own_live, expert_ids, gate_values, up_gate_weight, down_weight, capacity
        )
    return (attended, moe_out)


def solution(mesh):
    in_specs = (
        P(("grp", "sp"), None),
        P(("grp", "sp"), None),
        P("grp", "sp", None, None),
        P("grp", "sp"),
        P("sp", None),
        P(("grp", "sp"), None),
        P(),
        P(("grp", "sp"), None),
        P(("grp", "sp"), None),
        P(("grp", "sp"), None, None),
        P(("grp", "sp"), None, None),
    )
    out_specs = (P(("grp", "sp"), None), P(("grp", "sp"), None))
    return jax.shard_map(
        per_device, mesh=mesh, in_specs=in_specs, out_specs=out_specs, check_vma=False
    )
```

```python
import math

import jax
import jax.numpy as jnp
from jax import lax
from jax.experimental import pallas as pl
from jax.experimental.pallas import tpu as pltpu
from jax.sharding import PartitionSpec as P


def partner_2(value, axis, bit):
    mask = 2**bit
    pairs = [(source, source ^ mask) for source in range(lax.axis_size(axis))]
    return lax.ppermute(value, axis, pairs)


def experts_by_exchange(
    normed, own_live, expert_ids, gate_values, up_gate_weight, down_weight, capacity
):
    slot_rows, model_width = normed.shape
    top_count = expert_ids.shape[1]
    hidden_width = down_weight.shape[1]
    experts = up_gate_weight.shape[0] * lax.axis_size(("grp", "sp"))
    choose = expert_ids[:, :, None] == jnp.arange(experts, dtype=jnp.int32)[None, None, :]
    routed = (jnp.any(choose, axis=1) & own_live[:, None]).astype(jnp.float32)
    earlier = (jnp.arange(slot_rows)[:, None] > jnp.arange(slot_rows)[None, :]).astype(jnp.float32)
    prefix = jnp.dot(earlier, routed, precision=lax.Precision.HIGHEST)
    slot_in = jnp.sum(jnp.where(choose, prefix[:, None, :], 0.0), axis=2).astype(jnp.int32)
    dump_slot = experts * capacity
    target = jnp.where(own_live[:, None], expert_ids * capacity + slot_in, dump_slot)
    source_rows = (
        jnp.full((dump_slot + 1,), slot_rows, jnp.int32)
        .at[target.reshape(-1)]
        .set(jnp.repeat(jnp.arange(slot_rows, dtype=jnp.int32), top_count))[:dump_slot]
    )
    padded = jnp.concatenate([normed, jnp.zeros((1, model_width), jnp.bfloat16)], axis=0)
    outgoing = padded[source_rows].reshape(experts, capacity, model_width)
    received = lax.all_to_all(outgoing, ("grp", "sp"), split_axis=0, concat_axis=0, tiled=True)
    flat_rows = received.reshape(-1, model_width)
    projected = jnp.dot(flat_rows, up_gate_weight[0], preferred_element_type=jnp.float32)
    hidden = (jax.nn.silu(projected[:, :hidden_width]) * projected[:, hidden_width:]).astype(
        jnp.bfloat16
    )
    returned = lax.all_to_all(
        jnp.dot(hidden, down_weight[0], preferred_element_type=jnp.float32)
        .astype(jnp.bfloat16)
        .reshape(received.shape),
        ("grp", "sp"),
        split_axis=0,
        concat_axis=0,
        tiled=True,
    )
    back_rows = jnp.concatenate(
        [returned.reshape(dump_slot, model_width), jnp.zeros((1, model_width), jnp.bfloat16)],
        axis=0,
    )
    picked = back_rows[target]
    combined = jnp.sum(gate_values[:, :, None] * picked.astype(jnp.float32), axis=1)
    moe_out = jnp.where(own_live[:, None], combined, 0.0).astype(jnp.bfloat16)
    return moe_out


def shift_z(value, back=False):
    groups = lax.axis_size("grp")
    hop = -2 if back else 2
    return lax.ppermute(value, "grp", [(g, (g + hop) % groups) for g in range(groups)])


def swap_x(value):
    return partner_2(value, "grp", 0)


def swap_y(value):
    return partner_2(value, "sp", 1)


def swap_core(value):
    return partner_2(value, "sp", 0)


def pick_kernel(pick_ref, *refs):
    blocks = pick_ref.shape[0]
    halves, (own_ref, sibling_ref) = refs[: 2 * blocks], refs[2 * blocks :]
    capacity = pick_ref.shape[1] // 2
    half = own_ref.shape[1] // 2
    for block in range(blocks):
        for side in range(2):
            chosen = jnp.dot(
                pick_ref[block], halves[2 * block + side][...], preferred_element_type=jnp.float32
            ).astype(jnp.bfloat16)
            rows, columns = pl.ds(block * capacity, capacity), pl.ds(side * half, half)
            own_ref[rows, columns] = chosen[:capacity]
            sibling_ref[rows, columns] = chosen[capacity:]


def pick_rows(pick, halves):
    blocks, slots, rows = pick.shape
    half = halves[0].shape[1]
    shape = jax.ShapeDtypeStruct((blocks * slots // 2, 2 * half), jnp.bfloat16)
    return pl.pallas_call(
        pick_kernel,
        out_shape=(shape, shape),
        compiler_params=pltpu.CompilerParams(vmem_limit_bytes=48 * 2**20),
        cost_estimate=pl.CostEstimate(
            flops=4 * blocks * slots * rows * half,
            bytes_accessed=4 * blocks * (rows + slots) * half,
            transcendentals=0,
        ),
    )(pick, *halves)


def combine_kernel(weight_ref, own_ref, other_ref, *out_refs):
    blocks = weight_ref.shape[0]
    capacity = weight_ref.shape[2] // 2
    half = own_ref.shape[1] // 2
    for block in range(blocks):
        weight = weight_ref[block]
        for side in range(2):
            rows, columns = pl.ds(block * capacity, capacity), pl.ds(side * half, half)
            both = jnp.concatenate([own_ref[rows, columns], other_ref[rows, columns]], axis=0)
            out_refs[2 * block + side][...] = jnp.dot(
                weight, both, preferred_element_type=jnp.float32
            ).astype(jnp.bfloat16)


def combine_rows(weight, own, other):
    blocks, rows, slots = weight.shape
    half = own.shape[1] // 2
    return pl.pallas_call(
        combine_kernel,
        out_shape=[jax.ShapeDtypeStruct((rows, half), jnp.bfloat16)] * (2 * blocks),
        compiler_params=pltpu.CompilerParams(vmem_limit_bytes=48 * 2**20),
        cost_estimate=pl.CostEstimate(
            flops=4 * blocks * slots * rows * half,
            bytes_accessed=4 * blocks * (rows + slots) * half,
            transcendentals=0,
        ),
    )(weight, own, other)


def gather_routing(own_live, expert_ids, gate_values):
    live_ids = jnp.where(own_live[:, None], expert_ids, -1).astype(jnp.float32)
    routing = jnp.concatenate([live_ids, gate_values], axis=1).T
    depth = lax.axis_size("grp") // 2
    lines = [routing]
    for _ in range(depth - 1):
        lines.append(shift_z(lines[-1]))
    lines = jnp.stack(lines)
    lines = jnp.stack([lines, swap_x(lines)], axis=1)
    return jnp.stack([lines, swap_y(lines)], axis=2)


def selections(routing, top_count, capacity):
    mine = lax.axis_index(("grp", "sp"))
    ids, gates = routing[..., :top_count, :].astype(jnp.int32), routing[..., top_count:, :]
    rows = ids.shape[-1]
    picks, weights = [], []
    for expert in (mine, mine ^ 1):
        chosen = ids == expert
        wanted = jnp.any(chosen, axis=-2)
        gate = jnp.sum(jnp.where(chosen, gates, 0.0), axis=-2)
        place = jnp.cumsum(wanted.astype(jnp.int32), axis=-1) - 1
        place = jnp.where(wanted, place, -1)
        slots = jnp.arange(capacity, dtype=jnp.int32)
        picks.append((place[..., None, :] == slots[:, None]).astype(jnp.bfloat16))
        weights.append(
            jnp.where(place[..., :, None] == slots, gate[..., :, None], 0.0).astype(jnp.bfloat16)
        )
    depth = ids.shape[0]
    pick = jnp.concatenate(picks, axis=-2).reshape(depth, -1, 2 * capacity, rows)
    weight = jnp.concatenate(weights, axis=-1).reshape(depth, -1, rows, 2 * capacity)
    return pick, weight


def experts_by_gather(normed, pick, weight, up_gate_weight, down_weight):
    half = normed.shape[1] // 2
    hidden_width = down_weight.shape[1]
    depth = lax.axis_size("grp") // 2
    first, second = normed[:, :half], normed[:, half:]
    lines = [(first, second)]
    for _ in range(depth - 1):
        lines.append((shift_z(lines[-1][0]), shift_z(lines[-1][1])))
    shares = []
    for level, (first, second) in enumerate(lines):
        first_x, second_y = swap_x(first), swap_y(second)
        first_y, second_x = swap_y(first), swap_x(second)
        first_xy, second_xy = swap_y(first_x), swap_x(second_y)
        own, sibling = pick_rows(
            pick[level],
            [first, second, first_y, second_y, first_x, second_x, first_xy, second_xy],
        )
        rows = jnp.concatenate([own, swap_core(sibling)], axis=0)
        projected = jnp.dot(rows, up_gate_weight[0], preferred_element_type=jnp.float32)
        hidden = (jax.nn.silu(projected[:, :hidden_width]) * projected[:, hidden_width:]).astype(
            jnp.bfloat16
        )
        result = jnp.dot(hidden, down_weight[0], preferred_element_type=jnp.float32).astype(
            jnp.bfloat16
        )
        count = own.shape[0]
        parts = combine_rows(weight[level], result[:count], swap_core(result[count:]))
        first, second, first_y, second_y, first_x, second_x, first_xy, second_xy = parts
        first, first_x = first + swap_y(first_y), first_x + swap_y(first_xy)
        second, second_y = second + swap_x(second_x), second_y + swap_x(second_xy)
        shares.append((first + swap_x(first_x), second + swap_y(second_y)))
    first, second = shares[-1]
    for level in reversed(range(depth - 1)):
        first = shares[level][0] + shift_z(first, back=True)
        second = shares[level][1] + shift_z(second, back=True)
    return jnp.concatenate([first, second], axis=1)


def per_device(
    queries,
    fresh_key_values,
    cache,
    lengths,
    out_weight,
    residual,
    norm_gain,
    expert_ids,
    gate_values,
    up_gate_weight,
    down_weight,
):
    seq_devices = lax.axis_size("sp")
    slot_rows = queries.shape[0]
    head_width = cache.shape[-1] // 2
    model_width = residual.shape[1]
    kv_heads = fresh_key_values.shape[1] // (2 * head_width)
    repeat = seq_devices // kv_heads
    keys_new = fresh_key_values[:, : kv_heads * head_width].reshape(
        slot_rows, kv_heads, 1, head_width
    )
    values_new = fresh_key_values[:, kv_heads * head_width :].reshape(
        slot_rows, kv_heads, 1, head_width
    )
    paired = jnp.concatenate([keys_new, values_new], axis=3)
    spread = jnp.broadcast_to(paired, (slot_rows, kv_heads, repeat, 2 * head_width)).reshape(
        slot_rows, seq_devices * 2 * head_width
    )
    all_lengths = lax.all_gather(lengths, "sp", axis=1, tiled=True)
    queries_by_head, head_kv = (
        lax.all_to_all(queries, "sp", split_axis=1, concat_axis=0, tiled=True),
        lax.all_to_all(spread, "sp", split_axis=1, concat_axis=0, tiled=True),
    )
    cache_block = cache[0, 0]
    my_index = lax.axis_index("sp")
    for bit_pos in range(repeat.bit_length() - 1):
        partner = partner_2(cache_block, "sp", bit_pos)
        is_upper = my_index // 2**bit_pos % 2 == 1
        cache_block = jnp.where(
            is_upper,
            jnp.concatenate([partner, cache_block], axis=0),
            jnp.concatenate([cache_block, partner], axis=0),
        )
    stretch_lens = all_lengths[0]
    offsets = jnp.cumsum(stretch_lens) - stretch_lens
    rows_of_group = queries_by_head.shape[0]
    slot_ids = jnp.arange(rows_of_group, dtype=jnp.int32)
    source = slot_ids // slot_rows
    within = slot_ids % slot_rows
    from_device = source[:, None] == jnp.arange(seq_devices, dtype=jnp.int32)[None, :]
    is_live = within < jnp.sum(jnp.where(from_device, stretch_lens[None, :], 0), axis=1)
    position = within + jnp.sum(jnp.where(from_device, offsets[None, :], 0), axis=1)
    per_dev = queries_by_head.shape[1] // head_width
    cache_len = cache_block.shape[0]
    key_all = jnp.concatenate([cache_block[:, :head_width], head_kv[:, :head_width]], axis=0)
    value_all = jnp.concatenate([cache_block[:, head_width:], head_kv[:, head_width:]], axis=0)
    block_count = 2 if rows_of_group % 2 == 0 and rows_of_group >= 1024 else 1
    block_rows = rows_of_group // block_count

    def attend(parts):
        query_block, place_block = parts
        scores = jnp.einsum(
            "rhd,kd->hrk", query_block, key_all, preferred_element_type=jnp.float32
        ) / math.sqrt(head_width)
        allowed = jnp.concatenate(
            [
                jnp.ones((block_rows, cache_len), dtype=bool),
                is_live[None, :] & (position[None, :] <= place_block[:, None]),
            ],
            axis=1,
        )
        scores = jnp.where(allowed[None], scores, -jnp.inf)
        row_max = jnp.max(scores, axis=-1, keepdims=True)
        weights = jnp.exp(scores - row_max)
        totals = jnp.sum(weights, axis=-1, keepdims=True)
        result = (
            jnp.einsum(
                "hrk,kd->hrd",
                weights.astype(jnp.bfloat16),
                value_all,
                preferred_element_type=jnp.float32,
            )
            / totals
        )
        return (
            result.astype(jnp.bfloat16).transpose(1, 0, 2).reshape(block_rows, per_dev * head_width)
        )

    attn_heads = lax.map(
        attend,
        (
            queries_by_head.reshape(block_count, block_rows, per_dev, head_width),
            position.reshape(block_count, block_rows),
        ),
    ).reshape(rows_of_group, per_dev * head_width)
    attn_sum = lax.psum_scatter(
        jnp.dot(attn_heads, out_weight, preferred_element_type=jnp.float32).astype(jnp.bfloat16),
        "sp",
        scatter_dimension=0,
        tiled=True,
    ).astype(jnp.float32)
    own_live = jnp.arange(slot_rows, dtype=jnp.int32) < lengths[0, 0]
    attended = jnp.where(own_live[:, None], attn_sum, 0.0).astype(jnp.bfloat16)
    mixed_rows = residual.astype(jnp.float32) + attn_sum
    normed = (
        mixed_rows
        * lax.rsqrt(jnp.mean(mixed_rows * mixed_rows, axis=-1, keepdims=True) + 1e-06)
        * norm_gain
    ).astype(jnp.bfloat16)
    group_count = lax.axis_size("grp")
    experts = up_gate_weight.shape[0] * group_count * seq_devices
    top_count = expert_ids.shape[1]
    capacity = max(2, 8 * slot_rows * top_count // (5 * experts))
    if experts <= 4 * top_count and group_count % 2 == 0 and seq_devices == 4:
        routing = gather_routing(own_live, expert_ids, gate_values)
        pick, weight = selections(routing, top_count, capacity)
        moe_out = experts_by_gather(normed, pick, weight, up_gate_weight, down_weight)
    else:
        moe_out = experts_by_exchange(
            normed, own_live, expert_ids, gate_values, up_gate_weight, down_weight, capacity
        )
    return (attended, moe_out)


def solution(mesh):
    in_specs = (
        P(("grp", "sp"), None),
        P(("grp", "sp"), None),
        P("grp", "sp", None, None),
        P("grp", "sp"),
        P("sp", None),
        P(("grp", "sp"), None),
        P(),
        P(("grp", "sp"), None),
        P(("grp", "sp"), None),
        P(("grp", "sp"), None, None),
        P(("grp", "sp"), None, None),
    )
    out_specs = (P(("grp", "sp"), None), P(("grp", "sp"), None))
    return jax.shard_map(
        per_device, mesh=mesh, in_specs=in_specs, out_specs=out_specs, check_vma=False
    )
```

```python
import math

import jax
import jax.numpy as jnp
from jax import lax
from jax.experimental import pallas as pl
from jax.experimental.pallas import tpu as pltpu
from jax.sharding import PartitionSpec as P


def partner_2(value, axis, bit):
    mask = 2**bit
    pairs = [(source, source ^ mask) for source in range(lax.axis_size(axis))]
    return lax.ppermute(value, axis, pairs)


def shift_z(value, back=False):
    groups = lax.axis_size("grp")
    hop = -2 if back else 2
    return lax.ppermute(value, "grp", [(g, (g + hop) % groups) for g in range(groups)])


def swap_x(value):
    return partner_2(value, "grp", 0)


def swap_y(value):
    return partner_2(value, "sp", 1)


def swap_core(value):
    return partner_2(value, "sp", 0)


def pick_kernel(pick_ref, *refs):
    blocks = pick_ref.shape[0]
    halves, (own_ref, sibling_ref) = refs[: 2 * blocks], refs[2 * blocks :]
    capacity = pick_ref.shape[1] // 2
    half = own_ref.shape[1] // 2
    for block in range(blocks):
        for side in range(2):
            chosen = jnp.dot(
                pick_ref[block], halves[2 * block + side][...], preferred_element_type=jnp.float32
            ).astype(jnp.bfloat16)
            rows, columns = pl.ds(block * capacity, capacity), pl.ds(side * half, half)
            own_ref[rows, columns] = chosen[:capacity]
            sibling_ref[rows, columns] = chosen[capacity:]


def pick_rows(pick, halves):
    blocks, slots, rows = pick.shape
    half = halves[0].shape[1]
    shape = jax.ShapeDtypeStruct((blocks * slots // 2, 2 * half), jnp.bfloat16)
    return pl.pallas_call(
        pick_kernel,
        out_shape=(shape, shape),
        compiler_params=pltpu.CompilerParams(vmem_limit_bytes=48 * 2**20),
        cost_estimate=pl.CostEstimate(
            flops=4 * blocks * slots * rows * half,
            bytes_accessed=4 * blocks * (rows + slots) * half,
            transcendentals=0,
        ),
    )(pick, *halves)


def combine_kernel(weight_ref, own_ref, other_ref, *out_refs):
    blocks = weight_ref.shape[0]
    capacity = weight_ref.shape[2] // 2
    half = own_ref.shape[1] // 2
    for block in range(blocks):
        weight = weight_ref[block]
        for side in range(2):
            rows, columns = pl.ds(block * capacity, capacity), pl.ds(side * half, half)
            both = jnp.concatenate([own_ref[rows, columns], other_ref[rows, columns]], axis=0)
            out_refs[2 * block + side][...] = jnp.dot(
                weight, both, preferred_element_type=jnp.float32
            ).astype(jnp.bfloat16)


def combine_rows(weight, own, other):
    blocks, rows, slots = weight.shape
    half = own.shape[1] // 2
    return pl.pallas_call(
        combine_kernel,
        out_shape=[jax.ShapeDtypeStruct((rows, half), jnp.bfloat16)] * (2 * blocks),
        compiler_params=pltpu.CompilerParams(vmem_limit_bytes=48 * 2**20),
        cost_estimate=pl.CostEstimate(
            flops=4 * blocks * slots * rows * half,
            bytes_accessed=4 * blocks * (rows + slots) * half,
            transcendentals=0,
        ),
    )(weight, own, other)


def after(value, *earlier):
    return lax.optimization_barrier((value, *earlier))[0]


def xor_group(value, mask):
    return lax.ppermute(value, "sp", [(s, s ^ mask) for s in range(lax.axis_size("sp"))])


def attend_kernel(query_ref, row_place_ref, key_place_ref, cache_ref, *refs):
    fresh_refs, (out_ref, keys, values, bias) = refs[:-4], refs[-4:]
    rows = query_ref.shape[0]
    cached, width = cache_ref.shape[0], cache_ref.shape[1] // 2
    keys[:cached, :] = cache_ref[:, :width]
    values[:cached, :] = cache_ref[:, width:]
    for block, fresh_ref in enumerate(fresh_refs):
        places = pl.ds(cached + block * rows, rows)
        keys[places, :] = fresh_ref[:rows, :width]
        values[places, :] = fresh_ref[:rows, width:]
    bias[...] = jnp.where(key_place_ref[...] <= row_place_ref[...], 0.0, -1e30)
    scale = math.log2(math.e) / math.sqrt(width)
    for head in range(query_ref.shape[1] // width):
        columns = pl.ds(head * width, width)
        scores = lax.dot_general(
            query_ref[:, columns],
            keys[...],
            (((1,), (1,)), ((), ())),
            preferred_element_type=jnp.float32,
        )
        old, new = scores[:, :cached] * scale, scores[:, cached:] * scale + bias[...]
        row_max = jnp.maximum(
            jnp.max(old, axis=1, keepdims=True), jnp.max(new, axis=1, keepdims=True)
        )
        old, new = jnp.exp2(old - row_max), jnp.exp2(new - row_max)
        totals = jnp.sum(old, axis=1, keepdims=True) + jnp.sum(new, axis=1, keepdims=True)
        result = jnp.dot(
            old.astype(jnp.bfloat16), values[:cached, :], preferred_element_type=jnp.float32
        ) + jnp.dot(
            new.astype(jnp.bfloat16), values[cached:, :], preferred_element_type=jnp.float32
        )
        out_ref[:, columns] = (result / totals).astype(jnp.bfloat16)


def attend_block(query, row_place, key_place, cache_block, fresh):
    rows, columns = query.shape
    cached, width = cache_block.shape[0], cache_block.shape[1] // 2
    new = rows * len(fresh)
    return pl.pallas_call(
        attend_kernel,
        out_shape=jax.ShapeDtypeStruct((rows, columns), jnp.bfloat16),
        scratch_shapes=[
            pltpu.VMEM((cached + new, width), jnp.bfloat16),
            pltpu.VMEM((cached + new, width), jnp.bfloat16),
            pltpu.VMEM((rows, new), jnp.float32),
        ],
        compiler_params=pltpu.CompilerParams(vmem_limit_bytes=40 * 2**20),
        cost_estimate=pl.CostEstimate(
            flops=4 * rows * columns * (cached + new),
            bytes_accessed=4 * (rows * columns + (cached + new) * width),
            transcendentals=rows * columns // width * (cached + new),
        ),
    )(query, row_place, key_place, cache_block, *fresh)


def norm_kernel(
    own_ref, core_ref, far_ref, residual_ref, gain_ref, live_ref, attended_ref, first_ref, second_ref
):
    attn_sum = (
        own_ref[...].astype(jnp.float32)
        + core_ref[...].astype(jnp.float32)
        + far_ref[...].astype(jnp.float32)
    )
    attended_ref[...] = jnp.where(live_ref[...] > 0, attn_sum, 0.0).astype(jnp.bfloat16)
    mixed = residual_ref[...].astype(jnp.float32) + attn_sum
    scale = lax.rsqrt(jnp.mean(mixed * mixed, axis=1, keepdims=True) + 1e-06)
    normed = (mixed * scale * gain_ref[...]).astype(jnp.bfloat16)
    half = first_ref.shape[1]
    first_ref[...] = normed[:, :half]
    second_ref[...] = normed[:, half:]


def normalize(own, core, far, residual, gain, live):
    rows, width = own.shape
    part = jax.ShapeDtypeStruct((rows, width // 2), jnp.bfloat16)
    return pl.pallas_call(
        norm_kernel,
        out_shape=(jax.ShapeDtypeStruct((rows, width), jnp.bfloat16), part, part),
        compiler_params=pltpu.CompilerParams(vmem_limit_bytes=40 * 2**20),
        cost_estimate=pl.CostEstimate(
            flops=10 * rows * width, bytes_accessed=12 * rows * width, transcendentals=rows
        ),
    )(own, core, far, residual, gain, live)


def gather_routing(own_live, expert_ids, gate_values):
    live_ids = jnp.where(own_live[:, None], expert_ids, -1).astype(jnp.float32)
    routing = jnp.concatenate([live_ids, gate_values], axis=1).T
    lines = [routing]
    for _ in range(lax.axis_size("grp") // 2 - 1):
        lines.append(shift_z(lines[-1]))
    lines = jnp.stack(lines)
    lines = jnp.stack([lines, swap_x(lines)], axis=1)
    return jnp.stack([lines, swap_y(lines)], axis=2)


def selections(routing, top_count, capacity):
    mine = lax.axis_index(("grp", "sp"))
    depth, rows = routing.shape[0], routing.shape[-1]
    routing = routing.reshape(-1, 2 * top_count, rows)
    ids, gates = routing[:, :top_count].astype(jnp.int32), routing[:, top_count:]
    experts = jnp.stack([mine, mine ^ 1])
    chosen = ids[:, None] == experts[None, :, None, None]
    wanted = jnp.any(chosen, axis=2)
    gate = jnp.sum(jnp.where(chosen, gates[:, None], 0.0), axis=2)
    order = jnp.arange(rows)
    earlier = (order[:, None] < order[None, :]).astype(jnp.bfloat16)
    place = jnp.einsum(
        "bcr,rt->bct", wanted.astype(jnp.bfloat16), earlier, preferred_element_type=jnp.float32
    ).astype(jnp.int32)
    place = jnp.where(wanted, place, -1)
    slots = jnp.arange(capacity, dtype=jnp.int32)
    pick = (place[:, :, None, :] == slots[:, None]).astype(jnp.bfloat16)
    weight = jnp.where(place[:, :, :, None] == slots, gate[:, :, :, None], 0.0)
    weight = weight.astype(jnp.bfloat16).transpose(0, 2, 1, 3)
    return (
        pick.reshape(depth, -1, 2 * capacity, rows),
        weight.reshape(depth, -1, rows, 2 * capacity),
    )


def run_expert(rows, up_gate_weight, down_weight):
    hidden_width = down_weight.shape[1]
    projected = jnp.dot(rows, up_gate_weight[0], preferred_element_type=jnp.float32)
    hidden = (jax.nn.silu(projected[:, :hidden_width]) * projected[:, hidden_width:]).astype(
        jnp.bfloat16
    )
    return jnp.dot(hidden, down_weight[0], preferred_element_type=jnp.float32).astype(jnp.bfloat16)


def experts_by_gather(first, second, pick, weight, up_gate_weight, down_weight):
    depth = lax.axis_size("grp") // 2
    results = []
    shares = []
    for level in range(depth):
        if level >= 2:
            first, second = after(first, results[level - 2]), after(second, results[level - 2])
        if level + 1 < depth:
            next_first, next_second = shift_z(first), shift_z(second)
        first_x, second_y = swap_x(first), swap_y(second)
        first_y, second_x = swap_y(first), swap_x(second)
        first_xy, second_xy = swap_y(first_x), swap_x(second_y)
        own, sibling = pick_rows(
            pick[level],
            [first, second, first_y, second_y, first_x, second_x, first_xy, second_xy],
        )
        rows = jnp.concatenate([own, swap_core(sibling)], axis=0)
        result = run_expert(rows, up_gate_weight, down_weight)
        results.append(result)
        count = own.shape[0]
        parts = combine_rows(weight[level], result[:count], swap_core(result[count:]))
        first, second, first_y, second_y, first_x, second_x, first_xy, second_xy = parts
        first, first_x = first + swap_y(first_y), first_x + swap_y(first_xy)
        second, second_y = second + swap_x(second_x), second_y + swap_x(second_xy)
        shares.append((first + swap_x(first_x), second + swap_y(second_y)))
        first, second = next_first, next_second
    if depth > 1:
        first, second = shares[1]
        for level in range(2, depth):
            first = shares[level][0] + shift_z(first)
            second = shares[level][1] + shift_z(second)
        first, second = shares[0][0] + shift_z(first), shares[0][1] + shift_z(second)
    else:
        first, second = shares[0]
    return jnp.concatenate([first, second], axis=1)


def per_device_pairs(
    queries,
    fresh_key_values,
    cache,
    lengths,
    out_weight,
    residual,
    norm_gain,
    expert_ids,
    gate_values,
    up_gate_weight,
    down_weight,
):
    seq_devices = lax.axis_size("sp")
    mine = lax.axis_index("sp")
    slot_rows = queries.shape[0]
    width = cache.shape[-1] // 2
    head_columns = queries.shape[1] // seq_devices
    top_count = expert_ids.shape[1]
    experts = up_gate_weight.shape[0] * lax.axis_size("grp") * seq_devices
    capacity = max(2, 8 * slot_rows * top_count // (5 * experts))
    own_length = lengths[0, 0]
    own_live = jnp.arange(slot_rows, dtype=jnp.int32) < own_length

    def key_values_for(target):
        keys = lax.dynamic_slice(fresh_key_values, (0, target * width), (slot_rows, width))
        values = lax.dynamic_slice(
            fresh_key_values, (0, (seq_devices + target) * width), (slot_rows, width)
        )
        lane = jnp.arange(2 * width, dtype=jnp.int32)[None, :]
        note = jnp.where(lane == 0, own_length // 256, jnp.where(lane == 1, own_length % 256, 0))
        note = jnp.broadcast_to(note, (16, 2 * width)).astype(jnp.bfloat16)
        return jnp.concatenate([jnp.concatenate([keys, values], axis=1), note], axis=0)

    def queries_for(target):
        return lax.dynamic_slice(
            queries, (0, target * head_columns), (slot_rows, head_columns)
        )

    fresh = [key_values_for(mine)]
    fresh += [xor_group(key_values_for(mine ^ mask), mask) for mask in range(1, seq_devices)]
    query_blocks = [queries_for(mine)]
    query_blocks += [xor_group(queries_for(mine ^ mask), mask) for mask in range(1, seq_devices)]
    notes = jnp.stack([block[slot_rows, :2] for block in fresh]).astype(jnp.int32)
    block_lengths = notes[:, 0] * 256 + notes[:, 1]
    block_ids = jnp.arange(seq_devices, dtype=jnp.int32) ^ mine
    offsets = jnp.sum(
        jnp.where(block_ids[None, :] < block_ids[:, None], block_lengths[None, :], 0), axis=1
    )
    within = jnp.arange(slot_rows, dtype=jnp.int32)
    places = offsets[:, None] + within[None, :]
    live = within[None, :] < block_lengths[:, None]
    key_place = jnp.where(live, places, jnp.iinfo(jnp.int32).max).reshape(1, -1)
    cache_block = cache[0, 0]
    routing = gather_routing(own_live, expert_ids, gate_values)
    pick, weight = selections(routing, top_count, capacity)

    def share_of(block):
        heads = attend_block(
            query_blocks[block], places[block][:, None], key_place, cache_block, fresh
        )
        return jnp.dot(heads, out_weight, preferred_element_type=jnp.float32).astype(jnp.bfloat16)

    shares = {block: share_of(block) for block in (0, 3, 2, 1)}
    far = shares[2] + swap_core(shares[3])
    attended, first, second = normalize(
        shares[0],
        swap_core(shares[1]),
        swap_y(far),
        residual,
        norm_gain[None, :],
        own_live[:, None].astype(jnp.float32),
    )
    moe_out = experts_by_gather(first, second, pick, weight, up_gate_weight, down_weight)
    return (attended, moe_out)


def per_device(
    queries,
    fresh_key_values,
    cache,
    lengths,
    out_weight,
    residual,
    norm_gain,
    expert_ids,
    gate_values,
    up_gate_weight,
    down_weight,
):
    seq_devices = lax.axis_size("sp")
    slot_rows = queries.shape[0]
    head_width = cache.shape[-1] // 2
    model_width = residual.shape[1]
    kv_heads = fresh_key_values.shape[1] // (2 * head_width)
    repeat = seq_devices // kv_heads
    keys_new = fresh_key_values[:, : kv_heads * head_width].reshape(
        slot_rows, kv_heads, 1, head_width
    )
    values_new = fresh_key_values[:, kv_heads * head_width :].reshape(
        slot_rows, kv_heads, 1, head_width
    )
    paired = jnp.concatenate([keys_new, values_new], axis=3)
    spread = jnp.broadcast_to(paired, (slot_rows, kv_heads, repeat, 2 * head_width)).reshape(
        slot_rows, seq_devices * 2 * head_width
    )
    all_lengths = lax.all_gather(lengths, "sp", axis=1, tiled=True)
    queries_by_head, head_kv = (
        lax.all_to_all(queries, "sp", split_axis=1, concat_axis=0, tiled=True),
        lax.all_to_all(spread, "sp", split_axis=1, concat_axis=0, tiled=True),
    )
    cache_block = cache[0, 0]
    my_index = lax.axis_index("sp")
    for bit_pos in range(repeat.bit_length() - 1):
        partner = partner_2(cache_block, "sp", bit_pos)
        is_upper = my_index // 2**bit_pos % 2 == 1
        cache_block = jnp.where(
            is_upper,
            jnp.concatenate([partner, cache_block], axis=0),
            jnp.concatenate([cache_block, partner], axis=0),
        )
    stretch_lens = all_lengths[0]
    offsets = jnp.cumsum(stretch_lens) - stretch_lens
    rows_of_group = queries_by_head.shape[0]
    slot_ids = jnp.arange(rows_of_group, dtype=jnp.int32)
    source = slot_ids // slot_rows
    within = slot_ids % slot_rows
    from_device = source[:, None] == jnp.arange(seq_devices, dtype=jnp.int32)[None, :]
    is_live = within < jnp.sum(jnp.where(from_device, stretch_lens[None, :], 0), axis=1)
    position = within + jnp.sum(jnp.where(from_device, offsets[None, :], 0), axis=1)
    per_dev = queries_by_head.shape[1] // head_width
    cache_len = cache_block.shape[0]
    key_all = jnp.concatenate([cache_block[:, :head_width], head_kv[:, :head_width]], axis=0)
    value_all = jnp.concatenate([cache_block[:, head_width:], head_kv[:, head_width:]], axis=0)
    block_count = 2 if rows_of_group % 2 == 0 and rows_of_group >= 1024 else 1
    block_rows = rows_of_group // block_count

    def attend(parts):
        query_block, place_block = parts
        scores = jnp.einsum(
            "rhd,kd->hrk", query_block, key_all, preferred_element_type=jnp.float32
        ) / math.sqrt(head_width)
        allowed = jnp.concatenate(
            [
                jnp.ones((block_rows, cache_len), dtype=bool),
                is_live[None, :] & (position[None, :] <= place_block[:, None]),
            ],
            axis=1,
        )
        scores = jnp.where(allowed[None], scores, -jnp.inf)
        row_max = jnp.max(scores, axis=-1, keepdims=True)
        weights = jnp.exp(scores - row_max)
        totals = jnp.sum(weights, axis=-1, keepdims=True)
        result = (
            jnp.einsum(
                "hrk,kd->hrd",
                weights.astype(jnp.bfloat16),
                value_all,
                preferred_element_type=jnp.float32,
            )
            / totals
        )
        return (
            result.astype(jnp.bfloat16).transpose(1, 0, 2).reshape(block_rows, per_dev * head_width)
        )

    attn_heads = lax.map(
        attend,
        (
            queries_by_head.reshape(block_count, block_rows, per_dev, head_width),
            position.reshape(block_count, block_rows),
        ),
    ).reshape(rows_of_group, per_dev * head_width)
    attn_sum = lax.psum_scatter(
        jnp.dot(attn_heads, out_weight, preferred_element_type=jnp.float32).astype(jnp.bfloat16),
        "sp",
        scatter_dimension=0,
        tiled=True,
    ).astype(jnp.float32)
    own_live = jnp.arange(slot_rows, dtype=jnp.int32) < lengths[0, 0]
    attended = jnp.where(own_live[:, None], attn_sum, 0.0).astype(jnp.bfloat16)
    mixed_rows = residual.astype(jnp.float32) + attn_sum
    normed = (
        mixed_rows
        * lax.rsqrt(jnp.mean(mixed_rows * mixed_rows, axis=-1, keepdims=True) + 1e-06)
        * norm_gain
    ).astype(jnp.bfloat16)
    group_count = lax.axis_size("grp")
    experts = up_gate_weight.shape[0] * group_count * seq_devices
    top_count = expert_ids.shape[1]
    capacity = max(2, 8 * slot_rows * top_count // (5 * experts))
    hidden_width = down_weight.shape[1]
    choose = expert_ids[:, :, None] == jnp.arange(experts, dtype=jnp.int32)[None, None, :]
    routed = (jnp.any(choose, axis=1) & own_live[:, None]).astype(jnp.float32)
    earlier = (jnp.arange(slot_rows)[:, None] > jnp.arange(slot_rows)[None, :]).astype(jnp.float32)
    prefix = jnp.dot(earlier, routed, precision=lax.Precision.HIGHEST)
    slot_in = jnp.sum(jnp.where(choose, prefix[:, None, :], 0.0), axis=2).astype(jnp.int32)
    dump_slot = experts * capacity
    target = jnp.where(own_live[:, None], expert_ids * capacity + slot_in, dump_slot)
    source_rows = (
        jnp.full((dump_slot + 1,), slot_rows, jnp.int32)
        .at[target.reshape(-1)]
        .set(jnp.repeat(jnp.arange(slot_rows, dtype=jnp.int32), top_count))[:dump_slot]
    )
    padded = jnp.concatenate([normed, jnp.zeros((1, model_width), jnp.bfloat16)], axis=0)
    outgoing = padded[source_rows].reshape(experts, capacity, model_width)
    received = lax.all_to_all(outgoing, ("grp", "sp"), split_axis=0, concat_axis=0, tiled=True)
    flat_rows = received.reshape(-1, model_width)
    projected = jnp.dot(flat_rows, up_gate_weight[0], preferred_element_type=jnp.float32)
    hidden = (jax.nn.silu(projected[:, :hidden_width]) * projected[:, hidden_width:]).astype(
        jnp.bfloat16
    )
    returned = lax.all_to_all(
        jnp.dot(hidden, down_weight[0], preferred_element_type=jnp.float32)
        .astype(jnp.bfloat16)
        .reshape(received.shape),
        ("grp", "sp"),
        split_axis=0,
        concat_axis=0,
        tiled=True,
    )
    back_rows = jnp.concatenate(
        [returned.reshape(dump_slot, model_width), jnp.zeros((1, model_width), jnp.bfloat16)],
        axis=0,
    )
    picked = back_rows[target]
    combined = jnp.sum(gate_values[:, :, None] * picked.astype(jnp.float32), axis=1)
    moe_out = jnp.where(own_live[:, None], combined, 0.0).astype(jnp.bfloat16)
    return (attended, moe_out)


def solution(mesh):
    in_specs = (
        P(("grp", "sp"), None),
        P(("grp", "sp"), None),
        P("grp", "sp", None, None),
        P("grp", "sp"),
        P("sp", None),
        P(("grp", "sp"), None),
        P(),
        P(("grp", "sp"), None),
        P(("grp", "sp"), None),
        P(("grp", "sp"), None, None),
        P(("grp", "sp"), None, None),
    )
    out_specs = (P(("grp", "sp"), None), P(("grp", "sp"), None))
    groups, seq_devices = mesh.shape["grp"], mesh.shape["sp"]

    def run(*args):
        kv_heads = args[1].shape[1] // args[2].shape[-1]
        experts, top_count = args[9].shape[0], args[7].shape[1]
        pairs = seq_devices == kv_heads == 4 and groups % 2 == 0 and experts <= 4 * top_count
        return mapped(per_device_pairs if pairs else per_device)(*args)

    def mapped(body):
        return jax.shard_map(
            body, mesh=mesh, in_specs=in_specs, out_specs=out_specs, check_vma=False
        )

    return run
```

```python
import functools
import math

import jax
import jax.numpy as jnp
from jax import lax
from jax.experimental import pallas as pl
from jax.experimental.pallas import tpu as pltpu
from jax.sharding import PartitionSpec as P


def partner_2(value, axis, bit):
    mask = 2**bit
    pairs = [(source, source ^ mask) for source in range(lax.axis_size(axis))]
    return lax.ppermute(value, axis, pairs)


def shift_z(value, back=False):
    groups = lax.axis_size("grp")
    hop = -2 if back else 2
    return lax.ppermute(value, "grp", [(g, (g + hop) % groups) for g in range(groups)])


def swap_x(value):
    return partner_2(value, "grp", 0)


def swap_y(value):
    return partner_2(value, "sp", 1)


def swap_core(value):
    return partner_2(value, "sp", 0)


def after(value, *earlier):
    return lax.optimization_barrier((value, *earlier))[0]


def xor_group(value, mask):
    return lax.ppermute(value, "sp", [(s, s ^ mask) for s in range(lax.axis_size("sp"))])


def attend_kernel(index, mine_ref, query_ref, cache_ref, *refs):
    fresh_refs, (out_ref, keys, values, bias) = refs[:-4], refs[-4:]
    rows = query_ref.shape[0]
    cached, width = cache_ref.shape[0], cache_ref.shape[1] // 2
    keys[:cached, :] = cache_ref[:, :width]
    values[:cached, :] = cache_ref[:, width:]
    lengths = []
    for block, fresh_ref in enumerate(fresh_refs):
        places = pl.ds(cached + block * rows, rows)
        keys[places, :] = fresh_ref[:rows, :width]
        values[places, :] = fresh_ref[:rows, width:]
        note = fresh_ref[rows : rows + 16, :].astype(jnp.float32)
        lengths.append(note[:1, :1] * 256.0 + note[:1, width : width + 1])
    mine = mine_ref[0]
    offsets = []
    for block in range(len(fresh_refs)):
        offset = jnp.zeros((1, 1), jnp.float32)
        for other in range(len(fresh_refs)):
            before = (mine ^ other) < (mine ^ block)
            offset = offset + lengths[other] * before.astype(jnp.float32)
        offsets.append(offset)
    column = lax.broadcasted_iota(jnp.int32, (1, bias.shape[1]), 1)
    key_place = jnp.zeros((1, bias.shape[1]), jnp.float32)
    for block in range(len(fresh_refs)):
        within = (column - block * rows).astype(jnp.float32)
        place = jnp.where(within < lengths[block], within + offsets[block], 1e9)
        key_place = jnp.where(column >= block * rows, place, key_place)
    row_place = lax.broadcasted_iota(jnp.int32, bias.shape, 0).astype(jnp.float32) + offsets[index]
    bias[...] = jnp.where(key_place <= row_place, 0.0, -1e30)
    scale = math.log2(math.e) / math.sqrt(width)
    for head in range(query_ref.shape[1] // width):
        columns = pl.ds(head * width, width)
        scores = lax.dot_general(
            query_ref[:, columns],
            keys[...],
            (((1,), (1,)), ((), ())),
            preferred_element_type=jnp.float32,
        )
        old, new = scores[:, :cached] * scale, scores[:, cached:] * scale + bias[...]
        row_max = jnp.maximum(
            jnp.max(old, axis=1, keepdims=True), jnp.max(new, axis=1, keepdims=True)
        )
        old, new = jnp.exp2(old - row_max), jnp.exp2(new - row_max)
        totals = jnp.sum(old, axis=1, keepdims=True) + jnp.sum(new, axis=1, keepdims=True)
        result = jnp.dot(
            old.astype(jnp.bfloat16), values[:cached, :], preferred_element_type=jnp.float32
        ) + jnp.dot(
            new.astype(jnp.bfloat16), values[cached:, :], preferred_element_type=jnp.float32
        )
        out_ref[:, columns] = (result / totals).astype(jnp.bfloat16)


def attend_block(index, mine, query, cache_block, fresh):
    rows, columns = query.shape
    cached, width = cache_block.shape[0], cache_block.shape[1] // 2
    new = rows * len(fresh)
    inside = pl.BlockSpec(memory_space=pltpu.VMEM)
    return pl.pallas_call(
        functools.partial(attend_kernel, index),
        out_shape=jax.ShapeDtypeStruct((rows, columns), jnp.bfloat16),
        in_specs=[pl.BlockSpec(memory_space=pltpu.SMEM)] + [inside] * (2 + len(fresh)),
        out_specs=inside,
        scratch_shapes=[
            pltpu.VMEM((cached + new, width), jnp.bfloat16),
            pltpu.VMEM((cached + new, width), jnp.bfloat16),
            pltpu.VMEM((rows, new), jnp.float32),
        ],
        compiler_params=pltpu.CompilerParams(vmem_limit_bytes=40 * 2**20),
        cost_estimate=pl.CostEstimate(
            flops=4 * rows * columns * (cached + new),
            bytes_accessed=4 * (rows * columns + (cached + new) * width),
            transcendentals=rows * columns // width * (cached + new),
        ),
    )(mine, query, cache_block, *fresh)


def norm_kernel(
    length_ref,
    own_ref,
    core_ref,
    far_ref,
    residual_ref,
    gain_ref,
    attended_ref,
    first_ref,
    second_ref,
):
    attn_sum = (
        own_ref[...].astype(jnp.float32)
        + core_ref[...].astype(jnp.float32)
        + far_ref[...].astype(jnp.float32)
    )
    live = lax.broadcasted_iota(jnp.int32, attn_sum.shape, 0) < length_ref[0]
    attended_ref[...] = jnp.where(live, attn_sum, 0.0).astype(jnp.bfloat16)
    mixed = residual_ref[...].astype(jnp.float32) + attn_sum
    scale = lax.rsqrt(jnp.mean(mixed * mixed, axis=1, keepdims=True) + 1e-06)
    normed = (mixed * scale * gain_ref[...]).astype(jnp.bfloat16)
    half = first_ref.shape[1]
    first_ref[...] = normed[:, :half]
    second_ref[...] = normed[:, half:]


def normalize(length, own, core, far, residual, gain):
    rows, width = own.shape
    part = jax.ShapeDtypeStruct((rows, width // 2), jnp.bfloat16)
    inside = pl.BlockSpec(memory_space=pltpu.VMEM)
    return pl.pallas_call(
        norm_kernel,
        out_shape=(jax.ShapeDtypeStruct((rows, width), jnp.bfloat16), part, part),
        in_specs=[pl.BlockSpec(memory_space=pltpu.SMEM)] + [inside] * 5,
        out_specs=(inside, inside, inside),
        compiler_params=pltpu.CompilerParams(vmem_limit_bytes=40 * 2**20),
        cost_estimate=pl.CostEstimate(
            flops=10 * rows * width, bytes_accessed=12 * rows * width, transcendentals=rows
        ),
    )(length, own, core, far, residual, gain)


def pick_kernel(capacity, place_ref, *refs):
    blocks = place_ref.shape[0]
    halves, (own_ref, sibling_ref) = refs[: 2 * blocks], refs[2 * blocks :]
    half = own_ref.shape[1] // 2
    slot = lax.broadcasted_iota(jnp.int32, (capacity, place_ref.shape[2]), 0)
    for block in range(blocks):
        pick = jnp.concatenate(
            [(place_ref[block, pl.ds(core, 1), :] == slot) for core in range(2)], axis=0
        )
        pick = jnp.where(pick, 1.0, 0.0).astype(jnp.bfloat16)
        for side in range(2):
            chosen = jnp.dot(
                pick, halves[2 * block + side][...], preferred_element_type=jnp.float32
            ).astype(jnp.bfloat16)
            rows, columns = pl.ds(block * capacity, capacity), pl.ds(side * half, half)
            own_ref[rows, columns] = chosen[:capacity]
            sibling_ref[rows, columns] = chosen[capacity:]


def pick_rows(capacity, place, halves):
    blocks, _, rows = place.shape
    half = halves[0].shape[1]
    shape = jax.ShapeDtypeStruct((blocks * capacity, 2 * half), jnp.bfloat16)
    return pl.pallas_call(
        functools.partial(pick_kernel, capacity),
        out_shape=(shape, shape),
        compiler_params=pltpu.CompilerParams(vmem_limit_bytes=48 * 2**20),
        cost_estimate=pl.CostEstimate(
            flops=8 * blocks * capacity * rows * half,
            bytes_accessed=4 * blocks * (rows + 2 * capacity) * half,
            transcendentals=0,
        ),
    )(place, *halves)


def combine_kernel(place_ref, gate_ref, own_ref, other_ref, *out_refs):
    blocks, _, rows = place_ref.shape
    capacity = own_ref.shape[0] // blocks
    half = own_ref.shape[1] // 2
    slot = lax.broadcasted_iota(jnp.int32, (capacity, rows), 0)
    for block in range(blocks):
        weight = jnp.concatenate(
            [
                jnp.where(
                    place_ref[block, pl.ds(core, 1), :] == slot,
                    gate_ref[block, pl.ds(core, 1), :],
                    0.0,
                )
                for core in range(2)
            ],
            axis=0,
        )
        weight = weight.T.astype(jnp.bfloat16)
        level, (far_x, far_y) = block // 4, (block // 2 % 2, block % 2)
        for side in range(2):
            inner = pl.ds(block * capacity, capacity), pl.ds(side * half, half)
            both = jnp.concatenate([own_ref[inner], other_ref[inner]], axis=0)
            share = jnp.dot(weight, both, preferred_element_type=jnp.float32).astype(jnp.bfloat16)
            sent, place = (far_x, far_y) if side else (far_y, far_x)
            if sent:
                out_refs[6 * level + 3 * side + 2][pl.ds(place * rows, rows), :] = share
            else:
                out_refs[6 * level + 3 * side + place][...] = share


def combine_rows(place, gate, own, other):
    blocks, _, rows = place.shape
    half = own.shape[1] // 2
    kept = jax.ShapeDtypeStruct((rows, half), jnp.bfloat16)
    sent = jax.ShapeDtypeStruct((2 * rows, half), jnp.bfloat16)
    return pl.pallas_call(
        combine_kernel,
        out_shape=[kept, kept, sent] * (blocks // 2),
        compiler_params=pltpu.CompilerParams(vmem_limit_bytes=48 * 2**20),
        cost_estimate=pl.CostEstimate(
            flops=8 * own.shape[0] * rows * half,
            bytes_accessed=4 * (blocks * rows + 2 * own.shape[0]) * half,
            transcendentals=0,
        ),
    )(place, gate, own, other)


def gather_routing(own_live, expert_ids, gate_values, earlier):
    live_ids = jnp.where(own_live[:, None], expert_ids, -1).astype(jnp.float32)
    routing = after(jnp.concatenate([live_ids, gate_values], axis=1).T, earlier)
    groups = lax.axis_size("grp")
    lines = [routing]
    for hop in range(2, groups, 2):
        lines.append(
            lax.ppermute(routing, "grp", [(g, (g + hop) % groups) for g in range(groups)])
        )
    lines = jnp.stack(lines)
    lines = jnp.stack([lines, swap_x(lines)], axis=1)
    return jnp.stack([lines, swap_y(lines)], axis=2)


def selections(routing, top_count):
    mine = lax.axis_index(("grp", "sp"))
    depth, rows = routing.shape[0], routing.shape[-1]
    routing = routing.reshape(-1, 2 * top_count, rows)
    ids, gates = routing[:, :top_count].astype(jnp.int32), routing[:, top_count:]
    experts = jnp.stack([mine, mine ^ 1])
    chosen = ids[:, None] == experts[None, :, None, None]
    wanted = jnp.any(chosen, axis=2)
    gate = jnp.sum(jnp.where(chosen, gates[:, None], 0.0), axis=2)
    order = jnp.arange(rows)
    earlier = (order[:, None] < order[None, :]).astype(jnp.bfloat16)
    place = jnp.einsum(
        "bcr,rt->bct", wanted.astype(jnp.bfloat16), earlier, preferred_element_type=jnp.float32
    ).astype(jnp.int32)
    return jnp.where(wanted, place, -1), gate


def run_expert(rows, up_gate_weight, down_weight):
    hidden_width = down_weight.shape[1]
    projected = jnp.dot(rows, up_gate_weight[0], preferred_element_type=jnp.float32)
    hidden = (jax.nn.silu(projected[:, :hidden_width]) * projected[:, hidden_width:]).astype(
        jnp.bfloat16
    )
    return jnp.dot(hidden, down_weight[0], preferred_element_type=jnp.float32).astype(jnp.bfloat16)


def experts_by_gather(first, second, place, gate, capacity, up_gate_weight, down_weight):
    depth = lax.axis_size("grp") // 2
    per_level = place.shape[0] // depth
    lines, beside, across = [(first, second)], [], []
    for level in range(depth):
        first, second = lines[level]
        beside.append((swap_x(first), swap_y(second)))
        across.append((swap_y(first), swap_x(second)))
        if level + 1 < depth:
            if level:
                earlier = beside[level - 1] + across[level - 1]
                first, second = after(first, *earlier), after(second, *earlier)
            lines.append((shift_z(first), shift_z(second)))
    diagonal = []
    for level, (first_x, second_y) in enumerate(beside):
        if level < 2 < depth:
            first_x, second_y = after(first_x, *lines[2]), after(second_y, *lines[2])
        diagonal.append((swap_y(first_x), swap_x(second_y)))
    shares, returned, parts = [], [], []
    for start in range(0, depth, 2):
        levels = range(start, min(start + 2, depth))
        gathered = []
        for level in levels:
            (first_y, second_x), (first_x, second_y) = across[level], beside[level]
            gathered += [*lines[level], first_y, second_y, first_x, second_x, *diagonal[level]]
        ahead, last = levels[-1] + 1, levels[-1] + 2
        if last < depth:
            gathered[0] = after(gathered[0], *lines[last])
        if parts:
            gathered[0] = after(gathered[0], parts[0])
        blocks = slice(start * per_level, (start + len(levels)) * per_level)
        own, sibling = pick_rows(capacity, place[blocks], gathered)
        if last < depth:
            sibling = after(sibling, *beside[ahead], *across[ahead])
        other = swap_core(sibling)
        other_result = run_expert(other, up_gate_weight, down_weight)
        if last < depth:
            own = after(own, *beside[last], *diagonal[ahead])
        if returned:
            own = after(own, *returned)
        own_result = run_expert(own, up_gate_weight, down_weight)
        other_result = swap_core(other_result)
        if last < depth:
            own_result = after(own_result, *across[last])
        parts = combine_rows(place[blocks], gate[blocks], own_result, other_result)
        for index in range(len(levels)):
            first, first_x, first_sent, second, second_y, second_sent = parts[
                6 * index : 6 * index + 6
            ]
            rows = first.shape[0]
            returned = first_back, second_back = swap_y(first_sent), swap_x(second_sent)
            first, first_x = first + first_back[:rows], first_x + first_back[rows:]
            second, second_y = second + second_back[:rows], second_y + second_back[rows:]
            shares.append((first + swap_x(first_x), second + swap_y(second_y)))
    if depth > 1:
        first, second = shares[1]
        for level in range(2, depth):
            first = shares[level][0] + shift_z(first)
            second = shares[level][1] + shift_z(second)
        first, second = shares[0][0] + shift_z(first), shares[0][1] + shift_z(second)
    else:
        first, second = shares[0]
    return jnp.concatenate([first, second], axis=1)


def per_device_pairs(
    queries,
    fresh_key_values,
    cache,
    lengths,
    out_weight,
    residual,
    norm_gain,
    expert_ids,
    gate_values,
    up_gate_weight,
    down_weight,
):
    seq_devices = lax.axis_size("sp")
    mine = lax.axis_index("sp")
    slot_rows = queries.shape[0]
    width = cache.shape[-1] // 2
    head_columns = queries.shape[1] // seq_devices
    top_count = expert_ids.shape[1]
    experts = up_gate_weight.shape[0] * lax.axis_size("grp") * seq_devices
    capacity = max(2, 8 * slot_rows * top_count // (5 * experts))
    own_length = lengths[0, 0]
    own_live = jnp.arange(slot_rows, dtype=jnp.int32) < own_length

    def key_values_for(target):
        keys = lax.dynamic_slice(fresh_key_values, (0, target * width), (slot_rows, width))
        values = lax.dynamic_slice(
            fresh_key_values, (0, (seq_devices + target) * width), (slot_rows, width)
        )
        lane = jnp.arange(2 * width, dtype=jnp.int32)[None, :]
        note = jnp.where(lane < width, own_length // 256, own_length % 256)
        note = jnp.broadcast_to(note, (16, 2 * width)).astype(jnp.bfloat16)
        return jnp.concatenate([jnp.concatenate([keys, values], axis=1), note], axis=0)

    def queries_for(target):
        return lax.dynamic_slice(queries, (0, target * head_columns), (slot_rows, head_columns))

    masks = range(1, seq_devices)
    fresh = [key_values_for(mine)] + [xor_group(key_values_for(mine ^ m), m) for m in masks]
    query_blocks = [queries_for(mine)] + [xor_group(queries_for(mine ^ m), m) for m in masks]
    cache_block = cache[0, 0]

    def share_of(block, query):
        heads = attend_block(block, mine[None], query, cache_block, fresh)
        return jnp.dot(heads, out_weight, preferred_element_type=jnp.float32).astype(jnp.bfloat16)

    own = share_of(0, query_blocks[0])
    far_core = share_of(3, after(query_blocks[3], query_blocks[2], own))
    far = share_of(2, query_blocks[2]) + swap_core(far_core)
    near = share_of(1, after(query_blocks[1], far))
    routing = gather_routing(own_live, expert_ids, gate_values, own)
    place, gate = selections(routing, top_count)
    attended, first, second = normalize(
        lengths[0], after(own, place, gate), swap_core(near), swap_y(far), residual, norm_gain[None, :]
    )
    moe_out = experts_by_gather(
        first, second, place, gate, capacity, up_gate_weight, down_weight
    )
    return (attended, moe_out)


def per_device(
    queries,
    fresh_key_values,
    cache,
    lengths,
    out_weight,
    residual,
    norm_gain,
    expert_ids,
    gate_values,
    up_gate_weight,
    down_weight,
):
    seq_devices = lax.axis_size("sp")
    slot_rows = queries.shape[0]
    head_width = cache.shape[-1] // 2
    model_width = residual.shape[1]
    kv_heads = fresh_key_values.shape[1] // (2 * head_width)
    repeat = seq_devices // kv_heads
    keys_new = fresh_key_values[:, : kv_heads * head_width].reshape(
        slot_rows, kv_heads, 1, head_width
    )
    values_new = fresh_key_values[:, kv_heads * head_width :].reshape(
        slot_rows, kv_heads, 1, head_width
    )
    paired = jnp.concatenate([keys_new, values_new], axis=3)
    spread = jnp.broadcast_to(paired, (slot_rows, kv_heads, repeat, 2 * head_width)).reshape(
        slot_rows, seq_devices * 2 * head_width
    )
    all_lengths = lax.all_gather(lengths, "sp", axis=1, tiled=True)
    queries_by_head, head_kv = (
        lax.all_to_all(queries, "sp", split_axis=1, concat_axis=0, tiled=True),
        lax.all_to_all(spread, "sp", split_axis=1, concat_axis=0, tiled=True),
    )
    cache_block = cache[0, 0]
    my_index = lax.axis_index("sp")
    for bit_pos in range(repeat.bit_length() - 1):
        partner = partner_2(cache_block, "sp", bit_pos)
        is_upper = my_index // 2**bit_pos % 2 == 1
        cache_block = jnp.where(
            is_upper,
            jnp.concatenate([partner, cache_block], axis=0),
            jnp.concatenate([cache_block, partner], axis=0),
        )
    stretch_lens = all_lengths[0]
    offsets = jnp.cumsum(stretch_lens) - stretch_lens
    rows_of_group = queries_by_head.shape[0]
    slot_ids = jnp.arange(rows_of_group, dtype=jnp.int32)
    source = slot_ids // slot_rows
    within = slot_ids % slot_rows
    from_device = source[:, None] == jnp.arange(seq_devices, dtype=jnp.int32)[None, :]
    is_live = within < jnp.sum(jnp.where(from_device, stretch_lens[None, :], 0), axis=1)
    position = within + jnp.sum(jnp.where(from_device, offsets[None, :], 0), axis=1)
    per_dev = queries_by_head.shape[1] // head_width
    cache_len = cache_block.shape[0]
    key_all = jnp.concatenate([cache_block[:, :head_width], head_kv[:, :head_width]], axis=0)
    value_all = jnp.concatenate([cache_block[:, head_width:], head_kv[:, head_width:]], axis=0)
    block_count = 2 if rows_of_group % 2 == 0 and rows_of_group >= 1024 else 1
    block_rows = rows_of_group // block_count

    def attend(parts):
        query_block, place_block = parts
        scores = jnp.einsum(
            "rhd,kd->hrk", query_block, key_all, preferred_element_type=jnp.float32
        ) / math.sqrt(head_width)
        allowed = jnp.concatenate(
            [
                jnp.ones((block_rows, cache_len), dtype=bool),
                is_live[None, :] & (position[None, :] <= place_block[:, None]),
            ],
            axis=1,
        )
        scores = jnp.where(allowed[None], scores, -jnp.inf)
        row_max = jnp.max(scores, axis=-1, keepdims=True)
        weights = jnp.exp(scores - row_max)
        totals = jnp.sum(weights, axis=-1, keepdims=True)
        result = (
            jnp.einsum(
                "hrk,kd->hrd",
                weights.astype(jnp.bfloat16),
                value_all,
                preferred_element_type=jnp.float32,
            )
            / totals
        )
        return (
            result.astype(jnp.bfloat16).transpose(1, 0, 2).reshape(block_rows, per_dev * head_width)
        )

    attn_heads = lax.map(
        attend,
        (
            queries_by_head.reshape(block_count, block_rows, per_dev, head_width),
            position.reshape(block_count, block_rows),
        ),
    ).reshape(rows_of_group, per_dev * head_width)
    attn_sum = lax.psum_scatter(
        jnp.dot(attn_heads, out_weight, preferred_element_type=jnp.float32).astype(jnp.bfloat16),
        "sp",
        scatter_dimension=0,
        tiled=True,
    ).astype(jnp.float32)
    own_live = jnp.arange(slot_rows, dtype=jnp.int32) < lengths[0, 0]
    attended = jnp.where(own_live[:, None], attn_sum, 0.0).astype(jnp.bfloat16)
    mixed_rows = residual.astype(jnp.float32) + attn_sum
    normed = (
        mixed_rows
        * lax.rsqrt(jnp.mean(mixed_rows * mixed_rows, axis=-1, keepdims=True) + 1e-06)
        * norm_gain
    ).astype(jnp.bfloat16)
    group_count = lax.axis_size("grp")
    experts = up_gate_weight.shape[0] * group_count * seq_devices
    top_count = expert_ids.shape[1]
    capacity = max(2, 8 * slot_rows * top_count // (5 * experts))
    hidden_width = down_weight.shape[1]
    choose = expert_ids[:, :, None] == jnp.arange(experts, dtype=jnp.int32)[None, None, :]
    routed = (jnp.any(choose, axis=1) & own_live[:, None]).astype(jnp.float32)
    earlier = (jnp.arange(slot_rows)[:, None] > jnp.arange(slot_rows)[None, :]).astype(jnp.float32)
    prefix = jnp.dot(earlier, routed, precision=lax.Precision.HIGHEST)
    slot_in = jnp.sum(jnp.where(choose, prefix[:, None, :], 0.0), axis=2).astype(jnp.int32)
    dump_slot = experts * capacity
    target = jnp.where(own_live[:, None], expert_ids * capacity + slot_in, dump_slot)
    source_rows = (
        jnp.full((dump_slot + 1,), slot_rows, jnp.int32)
        .at[target.reshape(-1)]
        .set(jnp.repeat(jnp.arange(slot_rows, dtype=jnp.int32), top_count))[:dump_slot]
    )
    padded = jnp.concatenate([normed, jnp.zeros((1, model_width), jnp.bfloat16)], axis=0)
    outgoing = padded[source_rows].reshape(experts, capacity, model_width)
    received = lax.all_to_all(outgoing, ("grp", "sp"), split_axis=0, concat_axis=0, tiled=True)
    flat_rows = received.reshape(-1, model_width)
    projected = jnp.dot(flat_rows, up_gate_weight[0], preferred_element_type=jnp.float32)
    hidden = (jax.nn.silu(projected[:, :hidden_width]) * projected[:, hidden_width:]).astype(
        jnp.bfloat16
    )
    returned = lax.all_to_all(
        jnp.dot(hidden, down_weight[0], preferred_element_type=jnp.float32)
        .astype(jnp.bfloat16)
        .reshape(received.shape),
        ("grp", "sp"),
        split_axis=0,
        concat_axis=0,
        tiled=True,
    )
    back_rows = jnp.concatenate(
        [returned.reshape(dump_slot, model_width), jnp.zeros((1, model_width), jnp.bfloat16)],
        axis=0,
    )
    picked = back_rows[target]
    combined = jnp.sum(gate_values[:, :, None] * picked.astype(jnp.float32), axis=1)
    moe_out = jnp.where(own_live[:, None], combined, 0.0).astype(jnp.bfloat16)
    return (attended, moe_out)


def solution(mesh):
    in_specs = (
        P(("grp", "sp"), None),
        P(("grp", "sp"), None),
        P("grp", "sp", None, None),
        P("grp", "sp"),
        P("sp", None),
        P(("grp", "sp"), None),
        P(),
        P(("grp", "sp"), None),
        P(("grp", "sp"), None),
        P(("grp", "sp"), None, None),
        P(("grp", "sp"), None, None),
    )
    out_specs = (P(("grp", "sp"), None), P(("grp", "sp"), None))
    groups, seq_devices = mesh.shape["grp"], mesh.shape["sp"]

    def run(*args):
        kv_heads = args[1].shape[1] // args[2].shape[-1]
        experts, top_count = args[9].shape[0], args[7].shape[1]
        pairs = seq_devices == kv_heads == 4 and groups % 2 == 0 and experts <= 4 * top_count
        return mapped(per_device_pairs if pairs else per_device)(*args)

    def mapped(body):
        return jax.shard_map(
            body, mesh=mesh, in_specs=in_specs, out_specs=out_specs, check_vma=False
        )

    return run
```

```python
import functools
import math

import jax
import jax.numpy as jnp
from jax import lax
from jax.experimental import pallas as pl
from jax.experimental.pallas import tpu as pltpu
from jax.sharding import PartitionSpec as P


def partner_2(value, axis, bit):
    mask = 2**bit
    pairs = [(source, source ^ mask) for source in range(lax.axis_size(axis))]
    return lax.ppermute(value, axis, pairs)


def shift_z(value, back=False):
    groups = lax.axis_size("grp")
    hop = -2 if back else 2
    return lax.ppermute(value, "grp", [(g, (g + hop) % groups) for g in range(groups)])


def swap_x(value):
    return partner_2(value, "grp", 0)


def swap_y(value):
    return partner_2(value, "sp", 1)


def swap_core(value):
    return partner_2(value, "sp", 0)


def after(value, *earlier):
    return lax.optimization_barrier((value, *earlier))[0]


def xor_group(value, mask):
    return lax.ppermute(value, "sp", [(s, s ^ mask) for s in range(lax.axis_size("sp"))])


def attend_kernel(index, mine_ref, query_ref, cache_ref, *refs):
    fresh_refs, (out_ref, keys, values, bias) = refs[:-4], refs[-4:]
    rows = query_ref.shape[0]
    cached, width = cache_ref.shape[0], cache_ref.shape[1] // 2
    keys[:cached, :] = cache_ref[:, :width]
    values[:cached, :] = cache_ref[:, width:]
    lengths = []
    for block, fresh_ref in enumerate(fresh_refs):
        places = pl.ds(cached + block * rows, rows)
        keys[places, :] = fresh_ref[:rows, :width]
        values[places, :] = fresh_ref[:rows, width:]
        note = fresh_ref[rows : rows + 16, :].astype(jnp.float32)
        lengths.append(note[:1, :1] * 256.0 + note[:1, width : width + 1])
    mine = mine_ref[0]
    offsets = []
    for block in range(len(fresh_refs)):
        offset = jnp.zeros((1, 1), jnp.float32)
        for other in range(len(fresh_refs)):
            before = (mine ^ other) < (mine ^ block)
            offset = offset + lengths[other] * before.astype(jnp.float32)
        offsets.append(offset)
    column = lax.broadcasted_iota(jnp.int32, (1, bias.shape[1]), 1)
    key_place = jnp.zeros((1, bias.shape[1]), jnp.float32)
    for block in range(len(fresh_refs)):
        within = (column - block * rows).astype(jnp.float32)
        place = jnp.where(within < lengths[block], within + offsets[block], 1e9)
        key_place = jnp.where(column >= block * rows, place, key_place)
    row_place = lax.broadcasted_iota(jnp.int32, bias.shape, 0).astype(jnp.float32) + offsets[index]
    bias[...] = jnp.where(key_place <= row_place, 0.0, -1e30)
    scale = math.log2(math.e) / math.sqrt(width)
    for head in range(query_ref.shape[1] // width):
        columns = pl.ds(head * width, width)
        scores = lax.dot_general(
            query_ref[:, columns],
            keys[...],
            (((1,), (1,)), ((), ())),
            preferred_element_type=jnp.float32,
        )
        old, new = scores[:, :cached] * scale, scores[:, cached:] * scale + bias[...]
        row_max = jnp.maximum(
            jnp.max(old, axis=1, keepdims=True), jnp.max(new, axis=1, keepdims=True)
        )
        old, new = jnp.exp2(old - row_max), jnp.exp2(new - row_max)
        totals = jnp.sum(old, axis=1, keepdims=True) + jnp.sum(new, axis=1, keepdims=True)
        result = jnp.dot(
            old.astype(jnp.bfloat16), values[:cached, :], preferred_element_type=jnp.float32
        ) + jnp.dot(
            new.astype(jnp.bfloat16), values[cached:, :], preferred_element_type=jnp.float32
        )
        out_ref[:, columns] = (result / totals).astype(jnp.bfloat16)


def attend_block(index, mine, query, cache_block, fresh):
    rows, columns = query.shape
    cached, width = cache_block.shape[0], cache_block.shape[1] // 2
    new = rows * len(fresh)
    inside = pl.BlockSpec(memory_space=pltpu.VMEM)
    return pl.pallas_call(
        functools.partial(attend_kernel, index),
        out_shape=jax.ShapeDtypeStruct((rows, columns), jnp.bfloat16),
        in_specs=[pl.BlockSpec(memory_space=pltpu.SMEM)] + [inside] * (2 + len(fresh)),
        out_specs=inside,
        scratch_shapes=[
            pltpu.VMEM((cached + new, width), jnp.bfloat16),
            pltpu.VMEM((cached + new, width), jnp.bfloat16),
            pltpu.VMEM((rows, new), jnp.float32),
        ],
        compiler_params=pltpu.CompilerParams(vmem_limit_bytes=40 * 2**20),
        cost_estimate=pl.CostEstimate(
            flops=4 * rows * columns * (cached + new),
            bytes_accessed=4 * (rows * columns + (cached + new) * width),
            transcendentals=rows * columns // width * (cached + new),
        ),
    )(mine, query, cache_block, *fresh)


def norm_kernel(
    length_ref,
    own_ref,
    core_ref,
    far_ref,
    residual_ref,
    gain_ref,
    attended_ref,
    packed_ref,
):
    attn_sum = (
        own_ref[...].astype(jnp.float32)
        + core_ref[...].astype(jnp.float32)
        + far_ref[...].astype(jnp.float32)
    )
    live = lax.broadcasted_iota(jnp.int32, attn_sum.shape, 0) < length_ref[0]
    attended_ref[...] = jnp.where(live, attn_sum, 0.0).astype(jnp.bfloat16)
    mixed = residual_ref[...].astype(jnp.float32) + attn_sum
    scale = lax.rsqrt(jnp.mean(mixed * mixed, axis=1, keepdims=True) + 1e-06)
    normed = (mixed * scale * gain_ref[...]).astype(jnp.bfloat16)
    rows, half = packed_ref.shape[0] // 2, packed_ref.shape[1]
    packed_ref[:rows, :] = normed[:, :half]
    packed_ref[rows:, :] = normed[:, half:]


def normalize(length, own, core, far, residual, gain):
    rows, width = own.shape
    packed = jax.ShapeDtypeStruct((2 * rows, width // 2), jnp.bfloat16)
    inside = pl.BlockSpec(memory_space=pltpu.VMEM)
    return pl.pallas_call(
        norm_kernel,
        out_shape=(jax.ShapeDtypeStruct((rows, width), jnp.bfloat16), packed),
        in_specs=[pl.BlockSpec(memory_space=pltpu.SMEM)] + [inside] * 5,
        out_specs=(inside, inside),
        compiler_params=pltpu.CompilerParams(vmem_limit_bytes=40 * 2**20),
        cost_estimate=pl.CostEstimate(
            flops=10 * rows * width, bytes_accessed=12 * rows * width, transcendentals=rows
        ),
    )(length, own, core, far, residual, gain)


def pick_kernel(capacity, place_ref, *refs):
    blocks, _, rows = place_ref.shape
    own_ref, sibling_ref = refs[-2:]
    half = own_ref.shape[1] // 2
    slot = lax.broadcasted_iota(jnp.int32, (capacity, rows), 0)
    for block in range(blocks):
        pick = jnp.concatenate(
            [(place_ref[block, pl.ds(core, 1), :] == slot) for core in range(2)], axis=0
        )
        pick = jnp.where(pick, 1.0, 0.0).astype(jnp.bfloat16)
        level, spot = block // 4, block % 4
        for side in range(2):
            if spot < 3:
                source = refs[5 * level + spot][pl.ds(side * rows, rows), :]
            else:
                source = refs[5 * level + 3 + side][...]
            chosen = jnp.dot(pick, source, preferred_element_type=jnp.float32)
            chosen = chosen.astype(jnp.bfloat16)
            inner = pl.ds(block * capacity, capacity), pl.ds(side * half, half)
            own_ref[inner] = chosen[:capacity]
            sibling_ref[inner] = chosen[capacity:]


def pick_rows(capacity, place, gathered):
    blocks, _, rows = place.shape
    half = gathered[0].shape[1]
    shape = jax.ShapeDtypeStruct((blocks * capacity, 2 * half), jnp.bfloat16)
    return pl.pallas_call(
        functools.partial(pick_kernel, capacity),
        out_shape=(shape, shape),
        compiler_params=pltpu.CompilerParams(vmem_limit_bytes=48 * 2**20),
        cost_estimate=pl.CostEstimate(
            flops=8 * blocks * capacity * rows * half,
            bytes_accessed=4 * blocks * (rows + 2 * capacity) * half,
            transcendentals=0,
        ),
    )(place, *gathered)


def combine_kernel(place_ref, gate_ref, own_ref, other_ref, *out_refs):
    blocks, _, rows = place_ref.shape
    capacity = own_ref.shape[0] // blocks
    half = own_ref.shape[1] // 2
    slot = lax.broadcasted_iota(jnp.int32, (capacity, rows), 0)
    for block in range(blocks):
        weight = jnp.concatenate(
            [
                jnp.where(
                    place_ref[block, pl.ds(core, 1), :] == slot,
                    gate_ref[block, pl.ds(core, 1), :],
                    0.0,
                )
                for core in range(2)
            ],
            axis=0,
        )
        weight = weight.T.astype(jnp.bfloat16)
        level, (far_x, far_y) = block // 4, (block // 2 % 2, block % 2)
        for side in range(2):
            inner = pl.ds(block * capacity, capacity), pl.ds(side * half, half)
            both = jnp.concatenate([own_ref[inner], other_ref[inner]], axis=0)
            share = jnp.dot(weight, both, preferred_element_type=jnp.float32).astype(jnp.bfloat16)
            sent, place = (far_x, far_y) if side else (far_y, far_x)
            if sent:
                out_refs[6 * level + 3 * side + 2][pl.ds(place * rows, rows), :] = share
            else:
                out_refs[6 * level + 3 * side + place][...] = share


def combine_rows(place, gate, own, other):
    blocks, _, rows = place.shape
    half = own.shape[1] // 2
    kept = jax.ShapeDtypeStruct((rows, half), jnp.bfloat16)
    sent = jax.ShapeDtypeStruct((2 * rows, half), jnp.bfloat16)
    return pl.pallas_call(
        combine_kernel,
        out_shape=[kept, kept, sent] * (blocks // 2),
        compiler_params=pltpu.CompilerParams(vmem_limit_bytes=48 * 2**20),
        cost_estimate=pl.CostEstimate(
            flops=8 * own.shape[0] * rows * half,
            bytes_accessed=4 * (blocks * rows + 2 * own.shape[0]) * half,
            transcendentals=0,
        ),
    )(place, gate, own, other)


def routing_lines(own_live, expert_ids, gate_values):
    live_ids = jnp.where(own_live[:, None], expert_ids, -1).astype(jnp.float32)
    routing = jnp.concatenate([live_ids, gate_values], axis=1).T
    groups = lax.axis_size("grp")
    lines = [routing]
    for hop in range(2, groups, 2):
        lines.append(
            lax.ppermute(routing, "grp", [(g, (g + hop) % groups) for g in range(groups)])
        )
    return lines


def routing_planes(lines):
    lines = jnp.stack(lines)
    lines = jnp.stack([lines, swap_x(lines)], axis=1)
    return jnp.stack([lines, swap_y(lines)], axis=2)


def selections(routing, top_count):
    mine = lax.axis_index(("grp", "sp"))
    depth, rows = routing.shape[0], routing.shape[-1]
    routing = routing.reshape(-1, 2 * top_count, rows)
    ids, gates = routing[:, :top_count].astype(jnp.int32), routing[:, top_count:]
    experts = jnp.stack([mine, mine ^ 1])
    chosen = ids[:, None] == experts[None, :, None, None]
    wanted = jnp.any(chosen, axis=2)
    gate = jnp.sum(jnp.where(chosen, gates[:, None], 0.0), axis=2)
    order = jnp.arange(rows)
    earlier = (order[:, None] < order[None, :]).astype(jnp.bfloat16)
    place = jnp.einsum(
        "bcr,rt->bct", wanted.astype(jnp.bfloat16), earlier, preferred_element_type=jnp.float32
    ).astype(jnp.int32)
    return jnp.where(wanted, place, -1), gate


def run_expert(rows, up_gate_weight, down_weight):
    hidden_width = down_weight.shape[1]
    projected = jnp.dot(rows, up_gate_weight[0], preferred_element_type=jnp.float32)
    hidden = (jax.nn.silu(projected[:, :hidden_width]) * projected[:, hidden_width:]).astype(
        jnp.bfloat16
    )
    return jnp.dot(hidden, down_weight[0], preferred_element_type=jnp.float32).astype(jnp.bfloat16)


def experts_by_gather(packed, place, gate, capacity, up_gate_weight, down_weight):
    depth = lax.axis_size("grp") // 2
    per_level = place.shape[0] // depth
    rows = packed.shape[0] // 2
    lines, beside_x, beside_y = [packed], [], []
    for level in range(depth):
        line = lines[level]
        beside_x.append(swap_x(line))
        beside_y.append(swap_y(line))
        if level + 1 < depth:
            if level:
                line = after(line, beside_x[level - 1], beside_y[level - 1])
            lines.append(shift_z(line))
    diagonal = []
    for level in range(depth):
        first_x, second_y = beside_x[level], beside_y[level]
        if level < 2 < depth:
            first_x, second_y = after(first_x, lines[2]), after(second_y, lines[2])
        diagonal.append((swap_y(first_x[:rows]), swap_x(second_y[rows:])))
    kept, sent, back, joined = {}, {}, {}, {}

    def send_back(level, *earlier):
        first_sent, second_sent = sent[level]
        if earlier:
            first_sent, second_sent = after(first_sent, *earlier), after(second_sent, *earlier)
        back[level] = swap_y(first_sent), swap_x(second_sent)

    def join(level):
        first, first_x, second, second_y = kept[level]
        first_back, second_back = back[level]
        first, first_x = first + first_back[:rows], first_x + first_back[rows:]
        second, second_y = second + second_back[:rows], second_y + second_back[rows:]
        joined[level] = first, second, swap_x(first_x), swap_y(second_y)

    for start in range(0, depth, 2):
        levels = range(start, min(start + 2, depth))
        gathered = []
        for level in levels:
            gathered += [lines[level], beside_y[level], beside_x[level], *diagonal[level]]
        ahead, last = levels[-1] + 1, levels[-1] + 2
        if last < depth:
            gathered[0] = after(gathered[0], lines[last])
        if start:
            gathered[0] = after(gathered[0], kept[start - 1][0])
        blocks = slice(start * per_level, (start + len(levels)) * per_level)
        own, sibling = pick_rows(capacity, place[blocks], gathered)
        if last < depth:
            sibling = after(sibling, beside_x[ahead], beside_y[ahead])
        other = swap_core(sibling)
        other_result = run_expert(other, up_gate_weight, down_weight)
        if last < depth:
            own = after(own, beside_x[last], beside_y[last])
        if start:
            own = after(own, *back[start - 1])
        own_result = run_expert(own, up_gate_weight, down_weight)
        other_result = swap_core(other_result)
        if last < depth:
            own_result = after(own_result, *diagonal[ahead])
        if start:
            own_result = after(own_result, *joined[start - 1], *back[start - 2])
        parts = combine_rows(place[blocks], gate[blocks], own_result, other_result)
        for index, level in enumerate(levels):
            first, first_x, first_sent, second, second_y, second_sent = parts[
                6 * index : 6 * index + 6
            ]
            kept[level] = first, first_x, second, second_y
            sent[level] = first_sent, second_sent
        if start or len(levels) == 1:
            send_back(start)
            if len(levels) == 2:
                send_back(start + 1, *back[start])
        else:
            send_back(start + 1)
            send_back(start)
        for level in levels:
            join(level)
    shares = {}
    for level in range(depth):
        first, second, first_far, second_far = joined[level]
        shares[level] = first + first_far, second + second_far
    first, second = shares[0]
    if depth > 1:
        total = jnp.concatenate(shares[1], axis=0)
        for level in range(2, depth):
            total = jnp.concatenate(shares[level], axis=0) + shift_z(total)
        total = shift_z(total)
        first, second = first + total[:rows], second + total[rows:]
    return jnp.concatenate([first, second], axis=1)


def per_device_pairs(
    queries,
    fresh_key_values,
    cache,
    lengths,
    out_weight,
    residual,
    norm_gain,
    expert_ids,
    gate_values,
    up_gate_weight,
    down_weight,
):
    seq_devices = lax.axis_size("sp")
    mine = lax.axis_index("sp")
    slot_rows = queries.shape[0]
    width = cache.shape[-1] // 2
    head_columns = queries.shape[1] // seq_devices
    top_count = expert_ids.shape[1]
    experts = up_gate_weight.shape[0] * lax.axis_size("grp") * seq_devices
    capacity = max(2, 8 * slot_rows * top_count // (5 * experts))
    own_length = lengths[0, 0]
    own_live = jnp.arange(slot_rows, dtype=jnp.int32) < own_length

    def key_values_for(target):
        keys = lax.dynamic_slice(fresh_key_values, (0, target * width), (slot_rows, width))
        values = lax.dynamic_slice(
            fresh_key_values, (0, (seq_devices + target) * width), (slot_rows, width)
        )
        lane = jnp.arange(2 * width, dtype=jnp.int32)[None, :]
        note = jnp.where(lane < width, own_length // 256, own_length % 256)
        note = jnp.broadcast_to(note, (16, 2 * width)).astype(jnp.bfloat16)
        return jnp.concatenate([jnp.concatenate([keys, values], axis=1), note], axis=0)

    def queries_for(target):
        return lax.dynamic_slice(queries, (0, target * head_columns), (slot_rows, head_columns))

    masks = range(1, seq_devices)
    fresh = [key_values_for(mine)] + [xor_group(key_values_for(mine ^ m), m) for m in masks]
    query_blocks = [queries_for(mine)] + [xor_group(queries_for(mine ^ m), m) for m in masks]
    cache_block = cache[0, 0]

    def share_of(block, query):
        heads = attend_block(block, mine[None], query, cache_block, fresh)
        return jnp.dot(heads, out_weight, preferred_element_type=jnp.float32).astype(jnp.bfloat16)

    lines = routing_lines(own_live, expert_ids, gate_values)
    own = share_of(0, after(query_blocks[0], *lines[1:]))
    routing = routing_planes(lines)
    far_core = share_of(3, after(query_blocks[3], query_blocks[2], own, routing))
    far = share_of(2, query_blocks[2]) + swap_core(far_core)
    near = share_of(1, after(query_blocks[1], far))
    place, gate = selections(routing, top_count)
    attended, packed = normalize(
        lengths[0], after(own, place, gate), swap_core(near), swap_y(far), residual, norm_gain[None, :]
    )
    moe_out = experts_by_gather(packed, place, gate, capacity, up_gate_weight, down_weight)
    return (attended, moe_out)


def per_device(
    queries,
    fresh_key_values,
    cache,
    lengths,
    out_weight,
    residual,
    norm_gain,
    expert_ids,
    gate_values,
    up_gate_weight,
    down_weight,
):
    seq_devices = lax.axis_size("sp")
    slot_rows = queries.shape[0]
    head_width = cache.shape[-1] // 2
    model_width = residual.shape[1]
    kv_heads = fresh_key_values.shape[1] // (2 * head_width)
    repeat = seq_devices // kv_heads
    keys_new = fresh_key_values[:, : kv_heads * head_width].reshape(
        slot_rows, kv_heads, 1, head_width
    )
    values_new = fresh_key_values[:, kv_heads * head_width :].reshape(
        slot_rows, kv_heads, 1, head_width
    )
    paired = jnp.concatenate([keys_new, values_new], axis=3)
    spread = jnp.broadcast_to(paired, (slot_rows, kv_heads, repeat, 2 * head_width)).reshape(
        slot_rows, seq_devices * 2 * head_width
    )
    all_lengths = lax.all_gather(lengths, "sp", axis=1, tiled=True)
    queries_by_head, head_kv = (
        lax.all_to_all(queries, "sp", split_axis=1, concat_axis=0, tiled=True),
        lax.all_to_all(spread, "sp", split_axis=1, concat_axis=0, tiled=True),
    )
    cache_block = cache[0, 0]
    my_index = lax.axis_index("sp")
    for bit_pos in range(repeat.bit_length() - 1):
        partner = partner_2(cache_block, "sp", bit_pos)
        is_upper = my_index // 2**bit_pos % 2 == 1
        cache_block = jnp.where(
            is_upper,
            jnp.concatenate([partner, cache_block], axis=0),
            jnp.concatenate([cache_block, partner], axis=0),
        )
    stretch_lens = all_lengths[0]
    offsets = jnp.cumsum(stretch_lens) - stretch_lens
    rows_of_group = queries_by_head.shape[0]
    slot_ids = jnp.arange(rows_of_group, dtype=jnp.int32)
    source = slot_ids // slot_rows
    within = slot_ids % slot_rows
    from_device = source[:, None] == jnp.arange(seq_devices, dtype=jnp.int32)[None, :]
    is_live = within < jnp.sum(jnp.where(from_device, stretch_lens[None, :], 0), axis=1)
    position = within + jnp.sum(jnp.where(from_device, offsets[None, :], 0), axis=1)
    per_dev = queries_by_head.shape[1] // head_width
    cache_len = cache_block.shape[0]
    key_all = jnp.concatenate([cache_block[:, :head_width], head_kv[:, :head_width]], axis=0)
    value_all = jnp.concatenate([cache_block[:, head_width:], head_kv[:, head_width:]], axis=0)
    block_count = 2 if rows_of_group % 2 == 0 and rows_of_group >= 1024 else 1
    block_rows = rows_of_group // block_count

    def attend(parts):
        query_block, place_block = parts
        scores = jnp.einsum(
            "rhd,kd->hrk", query_block, key_all, preferred_element_type=jnp.float32
        ) / math.sqrt(head_width)
        allowed = jnp.concatenate(
            [
                jnp.ones((block_rows, cache_len), dtype=bool),
                is_live[None, :] & (position[None, :] <= place_block[:, None]),
            ],
            axis=1,
        )
        scores = jnp.where(allowed[None], scores, -jnp.inf)
        row_max = jnp.max(scores, axis=-1, keepdims=True)
        weights = jnp.exp(scores - row_max)
        totals = jnp.sum(weights, axis=-1, keepdims=True)
        result = (
            jnp.einsum(
                "hrk,kd->hrd",
                weights.astype(jnp.bfloat16),
                value_all,
                preferred_element_type=jnp.float32,
            )
            / totals
        )
        return (
            result.astype(jnp.bfloat16).transpose(1, 0, 2).reshape(block_rows, per_dev * head_width)
        )

    attn_heads = lax.map(
        attend,
        (
            queries_by_head.reshape(block_count, block_rows, per_dev, head_width),
            position.reshape(block_count, block_rows),
        ),
    ).reshape(rows_of_group, per_dev * head_width)
    attn_sum = lax.psum_scatter(
        jnp.dot(attn_heads, out_weight, preferred_element_type=jnp.float32).astype(jnp.bfloat16),
        "sp",
        scatter_dimension=0,
        tiled=True,
    ).astype(jnp.float32)
    own_live = jnp.arange(slot_rows, dtype=jnp.int32) < lengths[0, 0]
    attended = jnp.where(own_live[:, None], attn_sum, 0.0).astype(jnp.bfloat16)
    mixed_rows = residual.astype(jnp.float32) + attn_sum
    normed = (
        mixed_rows
        * lax.rsqrt(jnp.mean(mixed_rows * mixed_rows, axis=-1, keepdims=True) + 1e-06)
        * norm_gain
    ).astype(jnp.bfloat16)
    group_count = lax.axis_size("grp")
    experts = up_gate_weight.shape[0] * group_count * seq_devices
    top_count = expert_ids.shape[1]
    capacity = max(2, 8 * slot_rows * top_count // (5 * experts))
    hidden_width = down_weight.shape[1]
    choose = expert_ids[:, :, None] == jnp.arange(experts, dtype=jnp.int32)[None, None, :]
    routed = (jnp.any(choose, axis=1) & own_live[:, None]).astype(jnp.float32)
    earlier = (jnp.arange(slot_rows)[:, None] > jnp.arange(slot_rows)[None, :]).astype(jnp.float32)
    prefix = jnp.dot(earlier, routed, precision=lax.Precision.HIGHEST)
    slot_in = jnp.sum(jnp.where(choose, prefix[:, None, :], 0.0), axis=2).astype(jnp.int32)
    dump_slot = experts * capacity
    target = jnp.where(own_live[:, None], expert_ids * capacity + slot_in, dump_slot)
    source_rows = (
        jnp.full((dump_slot + 1,), slot_rows, jnp.int32)
        .at[target.reshape(-1)]
        .set(jnp.repeat(jnp.arange(slot_rows, dtype=jnp.int32), top_count))[:dump_slot]
    )
    padded = jnp.concatenate([normed, jnp.zeros((1, model_width), jnp.bfloat16)], axis=0)
    outgoing = padded[source_rows].reshape(experts, capacity, model_width)
    received = lax.all_to_all(outgoing, ("grp", "sp"), split_axis=0, concat_axis=0, tiled=True)
    flat_rows = received.reshape(-1, model_width)
    projected = jnp.dot(flat_rows, up_gate_weight[0], preferred_element_type=jnp.float32)
    hidden = (jax.nn.silu(projected[:, :hidden_width]) * projected[:, hidden_width:]).astype(
        jnp.bfloat16
    )
    returned = lax.all_to_all(
        jnp.dot(hidden, down_weight[0], preferred_element_type=jnp.float32)
        .astype(jnp.bfloat16)
        .reshape(received.shape),
        ("grp", "sp"),
        split_axis=0,
        concat_axis=0,
        tiled=True,
    )
    back_rows = jnp.concatenate(
        [returned.reshape(dump_slot, model_width), jnp.zeros((1, model_width), jnp.bfloat16)],
        axis=0,
    )
    picked = back_rows[target]
    combined = jnp.sum(gate_values[:, :, None] * picked.astype(jnp.float32), axis=1)
    moe_out = jnp.where(own_live[:, None], combined, 0.0).astype(jnp.bfloat16)
    return (attended, moe_out)


def solution(mesh):
    in_specs = (
        P(("grp", "sp"), None),
        P(("grp", "sp"), None),
        P("grp", "sp", None, None),
        P("grp", "sp"),
        P("sp", None),
        P(("grp", "sp"), None),
        P(),
        P(("grp", "sp"), None),
        P(("grp", "sp"), None),
        P(("grp", "sp"), None, None),
        P(("grp", "sp"), None, None),
    )
    out_specs = (P(("grp", "sp"), None), P(("grp", "sp"), None))
    groups, seq_devices = mesh.shape["grp"], mesh.shape["sp"]

    def run(*args):
        kv_heads = args[1].shape[1] // args[2].shape[-1]
        experts, top_count = args[9].shape[0], args[7].shape[1]
        pairs = seq_devices == kv_heads == 4 and groups % 2 == 0 and experts <= 4 * top_count
        return mapped(per_device_pairs if pairs else per_device)(*args)

    def mapped(body):
        return jax.shard_map(
            body, mesh=mesh, in_specs=in_specs, out_specs=out_specs, check_vma=False
        )

    return run
```

```python
import functools
import math

import jax
import jax.numpy as jnp
from jax import lax
from jax.experimental import pallas as pl
from jax.experimental.pallas import tpu as pltpu
from jax.sharding import PartitionSpec as P


def partner_2(value, axis, bit):
    mask = 2**bit
    pairs = [(source, source ^ mask) for source in range(lax.axis_size(axis))]
    return lax.ppermute(value, axis, pairs)


def shift_z(value):
    groups = lax.axis_size("grp")
    return lax.ppermute(value, "grp", [(g, (g + 2) % groups) for g in range(groups)])


def shift_back(value, level):
    groups = lax.axis_size("grp")
    return lax.ppermute(value, "grp", [(g, (g - 2 * level) % groups) for g in range(groups)])


def swap_x(value):
    return partner_2(value, "grp", 0)


def swap_y(value):
    return partner_2(value, "sp", 1)


def swap_core(value):
    return partner_2(value, "sp", 0)


def after(value, *earlier):
    return lax.optimization_barrier((value, *earlier))[0]


def xor_group(value, mask):
    return lax.ppermute(value, "sp", [(s, s ^ mask) for s in range(lax.axis_size("sp"))])


def attend_kernel(index, mine_ref, query_ref, cache_ref, *refs):
    fresh_refs, (out_ref, keys, values, bias) = refs[:-4], refs[-4:]
    rows = query_ref.shape[0]
    cached, width = cache_ref.shape[0], cache_ref.shape[1] // 2
    keys[:cached, :] = cache_ref[:, :width]
    values[:cached, :] = cache_ref[:, width:]
    lengths = []
    for block, fresh_ref in enumerate(fresh_refs):
        places = pl.ds(cached + block * rows, rows)
        keys[places, :] = fresh_ref[:rows, :width]
        values[places, :] = fresh_ref[:rows, width:]
        note = fresh_ref[rows : rows + 16, :].astype(jnp.float32)
        lengths.append(note[:1, :1] * 256.0 + note[:1, width : width + 1])
    mine = mine_ref[0]
    offsets = []
    for block in range(len(fresh_refs)):
        offset = jnp.zeros((1, 1), jnp.float32)
        for other in range(len(fresh_refs)):
            before = (mine ^ other) < (mine ^ block)
            offset = offset + lengths[other] * before.astype(jnp.float32)
        offsets.append(offset)
    column = lax.broadcasted_iota(jnp.int32, (1, bias.shape[1]), 1)
    key_place = jnp.zeros((1, bias.shape[1]), jnp.float32)
    for block in range(len(fresh_refs)):
        within = (column - block * rows).astype(jnp.float32)
        place = jnp.where(within < lengths[block], within + offsets[block], 1e9)
        key_place = jnp.where(column >= block * rows, place, key_place)
    row_place = lax.broadcasted_iota(jnp.int32, bias.shape, 0).astype(jnp.float32) + offsets[index]
    bias[...] = jnp.where(key_place <= row_place, 0.0, -1e30)
    scale = math.log2(math.e) / math.sqrt(width)
    for head in range(query_ref.shape[1] // width):
        columns = pl.ds(head * width, width)
        scores = lax.dot_general(
            query_ref[:, columns],
            keys[...],
            (((1,), (1,)), ((), ())),
            preferred_element_type=jnp.float32,
        )
        old, new = scores[:, :cached] * scale, scores[:, cached:] * scale + bias[...]
        row_max = jnp.maximum(
            jnp.max(old, axis=1, keepdims=True), jnp.max(new, axis=1, keepdims=True)
        )
        old, new = jnp.exp2(old - row_max), jnp.exp2(new - row_max)
        totals = jnp.sum(old, axis=1, keepdims=True) + jnp.sum(new, axis=1, keepdims=True)
        result = jnp.dot(
            old.astype(jnp.bfloat16), values[:cached, :], preferred_element_type=jnp.float32
        ) + jnp.dot(
            new.astype(jnp.bfloat16), values[cached:, :], preferred_element_type=jnp.float32
        )
        out_ref[:, columns] = (result / totals).astype(jnp.bfloat16)


def attend_block(index, mine, query, cache_block, fresh):
    rows, columns = query.shape
    cached, width = cache_block.shape[0], cache_block.shape[1] // 2
    new = rows * len(fresh)
    inside = pl.BlockSpec(memory_space=pltpu.VMEM)
    return pl.pallas_call(
        functools.partial(attend_kernel, index),
        out_shape=jax.ShapeDtypeStruct((rows, columns), jnp.bfloat16),
        in_specs=[pl.BlockSpec(memory_space=pltpu.SMEM)] + [inside] * (2 + len(fresh)),
        out_specs=inside,
        scratch_shapes=[
            pltpu.VMEM((cached + new, width), jnp.bfloat16),
            pltpu.VMEM((cached + new, width), jnp.bfloat16),
            pltpu.VMEM((rows, new), jnp.float32),
        ],
        compiler_params=pltpu.CompilerParams(vmem_limit_bytes=40 * 2**20),
        cost_estimate=pl.CostEstimate(
            flops=4 * rows * columns * (cached + new),
            bytes_accessed=4 * (rows * columns + (cached + new) * width),
            transcendentals=rows * columns // width * (cached + new),
        ),
    )(mine, query, cache_block, *fresh)


def norm_kernel(
    length_ref,
    own_ref,
    core_ref,
    far_ref,
    residual_ref,
    gain_ref,
    attended_ref,
    packed_ref,
):
    attn_sum = (
        own_ref[...].astype(jnp.float32)
        + core_ref[...].astype(jnp.float32)
        + far_ref[...].astype(jnp.float32)
    )
    live = lax.broadcasted_iota(jnp.int32, attn_sum.shape, 0) < length_ref[0]
    attended_ref[...] = jnp.where(live, attn_sum, 0.0).astype(jnp.bfloat16)
    mixed = residual_ref[...].astype(jnp.float32) + attn_sum
    scale = lax.rsqrt(jnp.mean(mixed * mixed, axis=1, keepdims=True) + 1e-06)
    normed = (mixed * scale * gain_ref[...]).astype(jnp.bfloat16)
    rows, half = packed_ref.shape[0] // 2, packed_ref.shape[1]
    packed_ref[:rows, :] = normed[:, :half]
    packed_ref[rows:, :] = normed[:, half:]


def normalize(length, own, core, far, residual, gain):
    rows, width = own.shape
    packed = jax.ShapeDtypeStruct((2 * rows, width // 2), jnp.bfloat16)
    inside = pl.BlockSpec(memory_space=pltpu.VMEM)
    return pl.pallas_call(
        norm_kernel,
        out_shape=(jax.ShapeDtypeStruct((rows, width), jnp.bfloat16), packed),
        in_specs=[pl.BlockSpec(memory_space=pltpu.SMEM)] + [inside] * 5,
        out_specs=(inside, inside),
        compiler_params=pltpu.CompilerParams(vmem_limit_bytes=40 * 2**20),
        cost_estimate=pl.CostEstimate(
            flops=10 * rows * width, bytes_accessed=12 * rows * width, transcendentals=rows
        ),
    )(length, own, core, far, residual, gain)


def pick_kernel(capacity, place_ref, *refs):
    blocks, _, rows = place_ref.shape
    own_ref, sibling_ref = refs[-2:]
    half = own_ref.shape[1] // 2
    slot = lax.broadcasted_iota(jnp.int32, (capacity, rows), 0)
    for block in range(blocks):
        pick = jnp.concatenate(
            [(place_ref[block, pl.ds(core, 1), :] == slot) for core in range(2)], axis=0
        )
        pick = jnp.where(pick, 1.0, 0.0).astype(jnp.bfloat16)
        level, spot = block // 4, block % 4
        for side in range(2):
            if spot < 3:
                source = refs[5 * level + spot][pl.ds(side * rows, rows), :]
            else:
                source = refs[5 * level + 3 + side][...]
            chosen = jnp.dot(pick, source, preferred_element_type=jnp.float32)
            chosen = chosen.astype(jnp.bfloat16)
            inner = pl.ds(block * capacity, capacity), pl.ds(side * half, half)
            own_ref[inner] = chosen[:capacity]
            sibling_ref[inner] = chosen[capacity:]


def pick_rows(capacity, place, gathered):
    blocks, _, rows = place.shape
    half = gathered[0].shape[1]
    shape = jax.ShapeDtypeStruct((blocks * capacity, 2 * half), jnp.bfloat16)
    return pl.pallas_call(
        functools.partial(pick_kernel, capacity),
        out_shape=(shape, shape),
        compiler_params=pltpu.CompilerParams(vmem_limit_bytes=48 * 2**20),
        cost_estimate=pl.CostEstimate(
            flops=8 * blocks * capacity * rows * half,
            bytes_accessed=4 * blocks * (rows + 2 * capacity) * half,
            transcendentals=0,
        ),
    )(place, *gathered)


def combine_kernel(place_ref, gate_ref, own_ref, other_ref, *out_refs):
    blocks, _, rows = place_ref.shape
    capacity = own_ref.shape[0] // blocks
    half = own_ref.shape[1] // 2
    slot = lax.broadcasted_iota(jnp.int32, (capacity, rows), 0)
    for block in range(blocks):
        weight = jnp.concatenate(
            [
                jnp.where(
                    place_ref[block, pl.ds(core, 1), :] == slot,
                    gate_ref[block, pl.ds(core, 1), :],
                    0.0,
                )
                for core in range(2)
            ],
            axis=0,
        )
        weight = weight.T.astype(jnp.bfloat16)
        level, (far_x, far_y) = block // 4, (block // 2 % 2, block % 2)
        for side in range(2):
            inner = pl.ds(block * capacity, capacity), pl.ds(side * half, half)
            both = jnp.concatenate([own_ref[inner], other_ref[inner]], axis=0)
            share = jnp.dot(weight, both, preferred_element_type=jnp.float32).astype(jnp.bfloat16)
            sent, place = (far_x, far_y) if side else (far_y, far_x)
            if sent:
                out_refs[6 * level + 3 * side + 2][pl.ds(place * rows, rows), :] = share
            else:
                out_refs[6 * level + 3 * side + place][...] = share


def combine_rows(place, gate, own, other):
    blocks, _, rows = place.shape
    half = own.shape[1] // 2
    kept = jax.ShapeDtypeStruct((rows, half), jnp.bfloat16)
    sent = jax.ShapeDtypeStruct((2 * rows, half), jnp.bfloat16)
    return pl.pallas_call(
        combine_kernel,
        out_shape=[kept, kept, sent] * (blocks // 2),
        compiler_params=pltpu.CompilerParams(vmem_limit_bytes=48 * 2**20),
        cost_estimate=pl.CostEstimate(
            flops=8 * own.shape[0] * rows * half,
            bytes_accessed=4 * (blocks * rows + 2 * own.shape[0]) * half,
            transcendentals=0,
        ),
    )(place, gate, own, other)


def routing_start(own_live, expert_ids, gate_values, earlier):
    live_ids = jnp.where(own_live[:, None], expert_ids, -1).astype(jnp.float32)
    routing = after(jnp.concatenate([live_ids, gate_values], axis=1).T, earlier)
    groups = lax.axis_size("grp")
    lines = [routing]
    for hop in range(2, groups, 2):
        lines.append(
            lax.ppermute(routing, "grp", [(g, (g + hop) % groups) for g in range(groups)])
        )
    return jnp.stack(lines)


def routing_pair(routing, swap):
    return jnp.stack([routing, swap(routing)], axis=routing.ndim - 2)


def selections(routing, top_count):
    mine = lax.axis_index(("grp", "sp"))
    depth, rows = routing.shape[0], routing.shape[-1]
    routing = routing.reshape(-1, 2 * top_count, rows)
    ids, gates = routing[:, :top_count].astype(jnp.int32), routing[:, top_count:]
    experts = jnp.stack([mine, mine ^ 1])
    chosen = ids[:, None] == experts[None, :, None, None]
    wanted = jnp.any(chosen, axis=2)
    gate = jnp.sum(jnp.where(chosen, gates[:, None], 0.0), axis=2)
    order = jnp.arange(rows)
    earlier = (order[:, None] < order[None, :]).astype(jnp.bfloat16)
    place = jnp.einsum(
        "bcr,rt->bct", wanted.astype(jnp.bfloat16), earlier, preferred_element_type=jnp.float32
    ).astype(jnp.int32)
    return jnp.where(wanted, place, -1), gate


def run_expert(rows, up_gate_weight, down_weight):
    hidden_width = down_weight.shape[1]
    projected = jnp.dot(rows, up_gate_weight[0], preferred_element_type=jnp.float32)
    hidden = (jax.nn.silu(projected[:, :hidden_width]) * projected[:, hidden_width:]).astype(
        jnp.bfloat16
    )
    return jnp.dot(hidden, down_weight[0], preferred_element_type=jnp.float32).astype(jnp.bfloat16)


def experts_by_gather(packed, place, gate, capacity, up_gate_weight, down_weight):
    depth = lax.axis_size("grp") // 2
    per_level = place.shape[0] // depth
    rows = packed.shape[0] // 2
    lines, beside_x, beside_y, diagonal = [packed], [], [], []

    def cross(level, earlier):
        first_x, second_y = beside_x[level][:rows], beside_y[level][rows:]
        if earlier is not None:
            first_x, second_y = after(first_x, earlier), after(second_y, earlier)
        diagonal.append((swap_y(first_x), swap_x(second_y)))

    for level in range(depth):
        line = lines[level]
        if level == 2:
            cross(0, line)
            cross(1, line)
            line = after(line, *diagonal[0], *diagonal[1])
        elif level > 2:
            line = after(line, beside_x[level - 1], beside_y[level - 1])
        beside_x.append(swap_x(line))
        beside_y.append(swap_y(line))
        if level + 1 < depth:
            line = lines[level]
            if level:
                line = after(line, beside_x[level - 1], beside_y[level - 1])
            lines.append(shift_z(line))
    for level in range(len(diagonal), depth):
        cross(level, None)
    kept, sent, back, joined = {}, {}, {}, {}

    def send_back(level, *earlier):
        first_sent, second_sent = sent[level]
        if earlier:
            first_sent, second_sent = after(first_sent, *earlier), after(second_sent, *earlier)
        back[level] = swap_y(first_sent), swap_x(second_sent)

    def join(level):
        first, first_x, second, second_y = kept[level]
        first_back, second_back = back[level]
        first, first_x = first + first_back[:rows], first_x + first_back[rows:]
        second, second_y = second + second_back[:rows], second_y + second_back[rows:]
        joined[level] = first, second, swap_x(first_x), swap_y(second_y)

    for start in range(0, depth, 2):
        levels = range(start, min(start + 2, depth))
        gathered = []
        for level in levels:
            gathered += [lines[level], beside_y[level], beside_x[level], *diagonal[level]]
        ahead, last = levels[-1] + 1, levels[-1] + 2
        if last < depth:
            gathered[0] = after(gathered[0], lines[last])
        if start:
            gathered[0] = after(gathered[0], kept[start - 1][0])
        blocks = slice(start * per_level, (start + len(levels)) * per_level)
        own, sibling = pick_rows(capacity, place[blocks], gathered)
        other = swap_core(sibling)
        other_result = run_expert(other, up_gate_weight, down_weight)
        if last < depth:
            own = after(own, beside_x[ahead], beside_y[ahead])
        if start:
            back[start - 1] = tuple(after(part, other_result) for part in back[start - 1])
            join(start - 1)
            own = after(own, *back[start - 1])
        own_result = run_expert(own, up_gate_weight, down_weight)
        other_result = swap_core(other_result)
        if last < depth:
            own_result = after(own_result, beside_x[last], beside_y[last], *diagonal[ahead])
        if start:
            own_result = after(own_result, *joined[start - 1], *back[start - 2])
        parts = combine_rows(place[blocks], gate[blocks], own_result, other_result)
        for index, level in enumerate(levels):
            first, first_x, first_sent, second, second_y, second_sent = parts[
                6 * index : 6 * index + 6
            ]
            kept[level] = first, first_x, second, second_y
            sent[level] = first_sent, second_sent
        if start or len(levels) == 1:
            send_back(start)
            if len(levels) == 2:
                send_back(start + 1, *back[start])
        else:
            send_back(start + 1)
            send_back(start)
        if ahead < depth:
            levels = levels[:-1]
        for level in levels:
            join(level)
    shares = {}
    for level in range(depth):
        first, second, first_far, second_far = joined[level]
        shares[level] = first + first_far, second + second_far
    first, second = (part.astype(jnp.float32) for part in shares[0])
    for level in range(1, depth):
        arrived = shift_back(jnp.concatenate(shares[level], axis=0), level).astype(jnp.float32)
        first, second = first + arrived[:rows], second + arrived[rows:]
    return jnp.concatenate([first, second], axis=1).astype(jnp.bfloat16)


def per_device_pairs(
    queries,
    fresh_key_values,
    cache,
    lengths,
    out_weight,
    residual,
    norm_gain,
    expert_ids,
    gate_values,
    up_gate_weight,
    down_weight,
):
    seq_devices = lax.axis_size("sp")
    mine = lax.axis_index("sp")
    slot_rows = queries.shape[0]
    width = cache.shape[-1] // 2
    head_columns = queries.shape[1] // seq_devices
    top_count = expert_ids.shape[1]
    experts = up_gate_weight.shape[0] * lax.axis_size("grp") * seq_devices
    capacity = max(2, 8 * slot_rows * top_count // (5 * experts))
    own_length = lengths[0, 0]
    own_live = jnp.arange(slot_rows, dtype=jnp.int32) < own_length

    def key_values_for(target):
        keys = lax.dynamic_slice(fresh_key_values, (0, target * width), (slot_rows, width))
        values = lax.dynamic_slice(
            fresh_key_values, (0, (seq_devices + target) * width), (slot_rows, width)
        )
        lane = jnp.arange(2 * width, dtype=jnp.int32)[None, :]
        note = jnp.where(lane < width, own_length // 256, own_length % 256)
        note = jnp.broadcast_to(note, (16, 2 * width)).astype(jnp.bfloat16)
        return jnp.concatenate([jnp.concatenate([keys, values], axis=1), note], axis=0)

    def queries_for(target):
        return lax.dynamic_slice(queries, (0, target * head_columns), (slot_rows, head_columns))

    masks = range(1, seq_devices)
    fresh = [key_values_for(mine)] + [xor_group(key_values_for(mine ^ m), m) for m in masks]
    query_blocks = [queries_for(mine)] + [xor_group(queries_for(mine ^ m), m) for m in masks]
    cache_block = cache[0, 0]

    def share_of(block, query):
        heads = attend_block(block, mine[None], query, cache_block, fresh)
        return jnp.dot(heads, out_weight, preferred_element_type=jnp.float32).astype(jnp.bfloat16)

    own = share_of(0, query_blocks[0])
    routing = routing_start(own_live, expert_ids, gate_values, own)
    far_core = share_of(3, after(query_blocks[3], query_blocks[2], own, routing))
    routing = routing_pair(routing, swap_x)
    far = share_of(2, after(query_blocks[2], routing)) + swap_core(far_core)
    routing = routing_pair(after(routing, far), swap_y)
    near = share_of(1, after(query_blocks[1], far))
    place, gate = selections(routing, top_count)
    attended, packed = normalize(
        lengths[0], after(own, routing), swap_core(near), swap_y(far), residual, norm_gain[None, :]
    )
    moe_out = experts_by_gather(packed, place, gate, capacity, up_gate_weight, down_weight)
    return (attended, moe_out)


def per_device(
    queries,
    fresh_key_values,
    cache,
    lengths,
    out_weight,
    residual,
    norm_gain,
    expert_ids,
    gate_values,
    up_gate_weight,
    down_weight,
):
    seq_devices = lax.axis_size("sp")
    slot_rows = queries.shape[0]
    head_width = cache.shape[-1] // 2
    model_width = residual.shape[1]
    kv_heads = fresh_key_values.shape[1] // (2 * head_width)
    repeat = seq_devices // kv_heads
    keys_new = fresh_key_values[:, : kv_heads * head_width].reshape(
        slot_rows, kv_heads, 1, head_width
    )
    values_new = fresh_key_values[:, kv_heads * head_width :].reshape(
        slot_rows, kv_heads, 1, head_width
    )
    paired = jnp.concatenate([keys_new, values_new], axis=3)
    spread = jnp.broadcast_to(paired, (slot_rows, kv_heads, repeat, 2 * head_width)).reshape(
        slot_rows, seq_devices * 2 * head_width
    )
    all_lengths = lax.all_gather(lengths, "sp", axis=1, tiled=True)
    queries_by_head, head_kv = (
        lax.all_to_all(queries, "sp", split_axis=1, concat_axis=0, tiled=True),
        lax.all_to_all(spread, "sp", split_axis=1, concat_axis=0, tiled=True),
    )
    cache_block = cache[0, 0]
    my_index = lax.axis_index("sp")
    for bit_pos in range(repeat.bit_length() - 1):
        partner = partner_2(cache_block, "sp", bit_pos)
        is_upper = my_index // 2**bit_pos % 2 == 1
        cache_block = jnp.where(
            is_upper,
            jnp.concatenate([partner, cache_block], axis=0),
            jnp.concatenate([cache_block, partner], axis=0),
        )
    stretch_lens = all_lengths[0]
    offsets = jnp.cumsum(stretch_lens) - stretch_lens
    rows_of_group = queries_by_head.shape[0]
    slot_ids = jnp.arange(rows_of_group, dtype=jnp.int32)
    source = slot_ids // slot_rows
    within = slot_ids % slot_rows
    from_device = source[:, None] == jnp.arange(seq_devices, dtype=jnp.int32)[None, :]
    is_live = within < jnp.sum(jnp.where(from_device, stretch_lens[None, :], 0), axis=1)
    position = within + jnp.sum(jnp.where(from_device, offsets[None, :], 0), axis=1)
    per_dev = queries_by_head.shape[1] // head_width
    cache_len = cache_block.shape[0]
    key_all = jnp.concatenate([cache_block[:, :head_width], head_kv[:, :head_width]], axis=0)
    value_all = jnp.concatenate([cache_block[:, head_width:], head_kv[:, head_width:]], axis=0)
    block_count = 2 if rows_of_group % 2 == 0 and rows_of_group >= 1024 else 1
    block_rows = rows_of_group // block_count

    def attend(parts):
        query_block, place_block = parts
        scores = jnp.einsum(
            "rhd,kd->hrk", query_block, key_all, preferred_element_type=jnp.float32
        ) / math.sqrt(head_width)
        allowed = jnp.concatenate(
            [
                jnp.ones((block_rows, cache_len), dtype=bool),
                is_live[None, :] & (position[None, :] <= place_block[:, None]),
            ],
            axis=1,
        )
        scores = jnp.where(allowed[None], scores, -jnp.inf)
        row_max = jnp.max(scores, axis=-1, keepdims=True)
        weights = jnp.exp(scores - row_max)
        totals = jnp.sum(weights, axis=-1, keepdims=True)
        result = (
            jnp.einsum(
                "hrk,kd->hrd",
                weights.astype(jnp.bfloat16),
                value_all,
                preferred_element_type=jnp.float32,
            )
            / totals
        )
        return (
            result.astype(jnp.bfloat16).transpose(1, 0, 2).reshape(block_rows, per_dev * head_width)
        )

    attn_heads = lax.map(
        attend,
        (
            queries_by_head.reshape(block_count, block_rows, per_dev, head_width),
            position.reshape(block_count, block_rows),
        ),
    ).reshape(rows_of_group, per_dev * head_width)
    attn_sum = lax.psum_scatter(
        jnp.dot(attn_heads, out_weight, preferred_element_type=jnp.float32).astype(jnp.bfloat16),
        "sp",
        scatter_dimension=0,
        tiled=True,
    ).astype(jnp.float32)
    own_live = jnp.arange(slot_rows, dtype=jnp.int32) < lengths[0, 0]
    attended = jnp.where(own_live[:, None], attn_sum, 0.0).astype(jnp.bfloat16)
    mixed_rows = residual.astype(jnp.float32) + attn_sum
    normed = (
        mixed_rows
        * lax.rsqrt(jnp.mean(mixed_rows * mixed_rows, axis=-1, keepdims=True) + 1e-06)
        * norm_gain
    ).astype(jnp.bfloat16)
    group_count = lax.axis_size("grp")
    experts = up_gate_weight.shape[0] * group_count * seq_devices
    top_count = expert_ids.shape[1]
    capacity = max(2, 8 * slot_rows * top_count // (5 * experts))
    hidden_width = down_weight.shape[1]
    choose = expert_ids[:, :, None] == jnp.arange(experts, dtype=jnp.int32)[None, None, :]
    routed = (jnp.any(choose, axis=1) & own_live[:, None]).astype(jnp.float32)
    earlier = (jnp.arange(slot_rows)[:, None] > jnp.arange(slot_rows)[None, :]).astype(jnp.float32)
    prefix = jnp.dot(earlier, routed, precision=lax.Precision.HIGHEST)
    slot_in = jnp.sum(jnp.where(choose, prefix[:, None, :], 0.0), axis=2).astype(jnp.int32)
    dump_slot = experts * capacity
    target = jnp.where(own_live[:, None], expert_ids * capacity + slot_in, dump_slot)
    source_rows = (
        jnp.full((dump_slot + 1,), slot_rows, jnp.int32)
        .at[target.reshape(-1)]
        .set(jnp.repeat(jnp.arange(slot_rows, dtype=jnp.int32), top_count))[:dump_slot]
    )
    padded = jnp.concatenate([normed, jnp.zeros((1, model_width), jnp.bfloat16)], axis=0)
    outgoing = padded[source_rows].reshape(experts, capacity, model_width)
    received = lax.all_to_all(outgoing, ("grp", "sp"), split_axis=0, concat_axis=0, tiled=True)
    flat_rows = received.reshape(-1, model_width)
    projected = jnp.dot(flat_rows, up_gate_weight[0], preferred_element_type=jnp.float32)
    hidden = (jax.nn.silu(projected[:, :hidden_width]) * projected[:, hidden_width:]).astype(
        jnp.bfloat16
    )
    returned = lax.all_to_all(
        jnp.dot(hidden, down_weight[0], preferred_element_type=jnp.float32)
        .astype(jnp.bfloat16)
        .reshape(received.shape),
        ("grp", "sp"),
        split_axis=0,
        concat_axis=0,
        tiled=True,
    )
    back_rows = jnp.concatenate(
        [returned.reshape(dump_slot, model_width), jnp.zeros((1, model_width), jnp.bfloat16)],
        axis=0,
    )
    picked = back_rows[target]
    combined = jnp.sum(gate_values[:, :, None] * picked.astype(jnp.float32), axis=1)
    moe_out = jnp.where(own_live[:, None], combined, 0.0).astype(jnp.bfloat16)
    return (attended, moe_out)


def solution(mesh):
    in_specs = (
        P(("grp", "sp"), None),
        P(("grp", "sp"), None),
        P("grp", "sp", None, None),
        P("grp", "sp"),
        P("sp", None),
        P(("grp", "sp"), None),
        P(),
        P(("grp", "sp"), None),
        P(("grp", "sp"), None),
        P(("grp", "sp"), None, None),
        P(("grp", "sp"), None, None),
    )
    out_specs = (P(("grp", "sp"), None), P(("grp", "sp"), None))
    groups, seq_devices = mesh.shape["grp"], mesh.shape["sp"]

    def run(*args):
        kv_heads = args[1].shape[1] // args[2].shape[-1]
        experts, top_count = args[9].shape[0], args[7].shape[1]
        pairs = seq_devices == kv_heads == 4 and groups % 2 == 0 and experts <= 4 * top_count
        return mapped(per_device_pairs if pairs else per_device)(*args)

    def mapped(body):
        return jax.shard_map(
            body, mesh=mesh, in_specs=in_specs, out_specs=out_specs, check_vma=False
        )

    return run
```

```python
import functools
import math

import jax
import jax.numpy as jnp
from jax import lax
from jax.experimental import pallas as pl
from jax.experimental.pallas import tpu as pltpu
from jax.sharding import PartitionSpec as P


def partner_2(value, axis, bit):
    mask = 2**bit
    pairs = [(source, source ^ mask) for source in range(lax.axis_size(axis))]
    return lax.ppermute(value, axis, pairs)


def shift_z(value):
    groups = lax.axis_size("grp")
    return lax.ppermute(value, "grp", [(g, (g + 2) % groups) for g in range(groups)])


def swap_x(value):
    return partner_2(value, "grp", 0)


def swap_y(value):
    return partner_2(value, "sp", 1)


def swap_core(value):
    return partner_2(value, "sp", 0)


def after(value, *earlier):
    return lax.optimization_barrier((value, *earlier))[0]


def xor_group(value, mask):
    return lax.ppermute(value, "sp", [(s, s ^ mask) for s in range(lax.axis_size("sp"))])


def attend_kernel(index, mine_ref, query_ref, cache_ref, *refs):
    fresh_refs, (out_ref, keys, values, bias) = refs[:-4], refs[-4:]
    rows = query_ref.shape[0]
    cached, width = cache_ref.shape[0], cache_ref.shape[1] // 2
    keys[:cached, :] = cache_ref[:, :width]
    values[:cached, :] = cache_ref[:, width:]
    lengths = []
    for block, fresh_ref in enumerate(fresh_refs):
        places = pl.ds(cached + block * rows, rows)
        keys[places, :] = fresh_ref[:rows, :width]
        values[places, :] = fresh_ref[:rows, width:]
        note = fresh_ref[rows : rows + 16, :].astype(jnp.float32)
        lengths.append(note[:1, :1] * 256.0 + note[:1, width : width + 1])
    mine = mine_ref[0]
    offsets = []
    for block in range(len(fresh_refs)):
        offset = jnp.zeros((1, 1), jnp.float32)
        for other in range(len(fresh_refs)):
            before = (mine ^ other) < (mine ^ block)
            offset = offset + lengths[other] * before.astype(jnp.float32)
        offsets.append(offset)
    column = lax.broadcasted_iota(jnp.int32, (1, bias.shape[1]), 1)
    key_place = jnp.zeros((1, bias.shape[1]), jnp.float32)
    for block in range(len(fresh_refs)):
        within = (column - block * rows).astype(jnp.float32)
        place = jnp.where(within < lengths[block], within + offsets[block], 1e9)
        key_place = jnp.where(column >= block * rows, place, key_place)
    row_place = lax.broadcasted_iota(jnp.int32, bias.shape, 0).astype(jnp.float32) + offsets[index]
    bias[...] = jnp.where(key_place <= row_place, 0.0, -1e30)
    scale = math.log2(math.e) / math.sqrt(width)
    for head in range(query_ref.shape[1] // width):
        columns = pl.ds(head * width, width)
        scores = lax.dot_general(
            query_ref[:, columns],
            keys[...],
            (((1,), (1,)), ((), ())),
            preferred_element_type=jnp.float32,
        )
        old, new = scores[:, :cached] * scale, scores[:, cached:] * scale + bias[...]
        row_max = jnp.maximum(
            jnp.max(old, axis=1, keepdims=True), jnp.max(new, axis=1, keepdims=True)
        )
        old, new = jnp.exp2(old - row_max), jnp.exp2(new - row_max)
        totals = jnp.sum(old, axis=1, keepdims=True) + jnp.sum(new, axis=1, keepdims=True)
        result = jnp.dot(
            old.astype(jnp.bfloat16), values[:cached, :], preferred_element_type=jnp.float32
        ) + jnp.dot(
            new.astype(jnp.bfloat16), values[cached:, :], preferred_element_type=jnp.float32
        )
        out_ref[:, columns] = (result / totals).astype(jnp.bfloat16)


def attend_block(index, mine, query, cache_block, fresh):
    rows, columns = query.shape
    cached, width = cache_block.shape[0], cache_block.shape[1] // 2
    new = rows * len(fresh)
    inside = pl.BlockSpec(memory_space=pltpu.VMEM)
    return pl.pallas_call(
        functools.partial(attend_kernel, index),
        out_shape=jax.ShapeDtypeStruct((rows, columns), jnp.bfloat16),
        in_specs=[pl.BlockSpec(memory_space=pltpu.SMEM)] + [inside] * (2 + len(fresh)),
        out_specs=inside,
        scratch_shapes=[
            pltpu.VMEM((cached + new, width), jnp.bfloat16),
            pltpu.VMEM((cached + new, width), jnp.bfloat16),
            pltpu.VMEM((rows, new), jnp.float32),
        ],
        compiler_params=pltpu.CompilerParams(vmem_limit_bytes=40 * 2**20),
        cost_estimate=pl.CostEstimate(
            flops=4 * rows * columns * (cached + new),
            bytes_accessed=4 * (rows * columns + (cached + new) * width),
            transcendentals=rows * columns // width * (cached + new),
        ),
    )(mine, query, cache_block, *fresh)


def norm_kernel(
    length_ref,
    own_ref,
    core_ref,
    far_ref,
    residual_ref,
    gain_ref,
    attended_ref,
    packed_ref,
):
    attn_sum = (
        own_ref[...].astype(jnp.float32)
        + core_ref[...].astype(jnp.float32)
        + far_ref[...].astype(jnp.float32)
    )
    live = lax.broadcasted_iota(jnp.int32, attn_sum.shape, 0) < length_ref[0]
    attended_ref[...] = jnp.where(live, attn_sum, 0.0).astype(jnp.bfloat16)
    mixed = residual_ref[...].astype(jnp.float32) + attn_sum
    scale = lax.rsqrt(jnp.mean(mixed * mixed, axis=1, keepdims=True) + 1e-06)
    normed = (mixed * scale * gain_ref[...]).astype(jnp.bfloat16)
    rows, half = packed_ref.shape[0] // 2, packed_ref.shape[1]
    packed_ref[:rows, :] = normed[:, :half]
    packed_ref[rows:, :] = normed[:, half:]


def normalize(length, own, core, far, residual, gain):
    rows, width = own.shape
    packed = jax.ShapeDtypeStruct((2 * rows, width // 2), jnp.bfloat16)
    inside = pl.BlockSpec(memory_space=pltpu.VMEM)
    return pl.pallas_call(
        norm_kernel,
        out_shape=(jax.ShapeDtypeStruct((rows, width), jnp.bfloat16), packed),
        in_specs=[pl.BlockSpec(memory_space=pltpu.SMEM)] + [inside] * 5,
        out_specs=(inside, inside),
        compiler_params=pltpu.CompilerParams(vmem_limit_bytes=40 * 2**20),
        cost_estimate=pl.CostEstimate(
            flops=10 * rows * width, bytes_accessed=12 * rows * width, transcendentals=rows
        ),
    )(length, own, core, far, residual, gain)


def pick_kernel(capacity, place_ref, *refs):
    blocks, _, rows = place_ref.shape
    own_ref, sibling_ref = refs[-2:]
    half = own_ref.shape[1] // 2
    slot = lax.broadcasted_iota(jnp.int32, (capacity, rows), 0)
    for block in range(blocks):
        pick = jnp.concatenate(
            [(place_ref[block, pl.ds(core, 1), :] == slot) for core in range(2)], axis=0
        )
        pick = jnp.where(pick, 1.0, 0.0).astype(jnp.bfloat16)
        level, spot = block // 4, block % 4
        for side in range(2):
            if spot < 3:
                source = refs[5 * level + spot][pl.ds(side * rows, rows), :]
            else:
                source = refs[5 * level + 3 + side][...]
            chosen = jnp.dot(pick, source, preferred_element_type=jnp.float32)
            chosen = chosen.astype(jnp.bfloat16)
            inner = pl.ds(block * capacity, capacity), pl.ds(side * half, half)
            own_ref[inner] = chosen[:capacity]
            sibling_ref[inner] = chosen[capacity:]


def pick_rows(capacity, place, gathered):
    blocks, _, rows = place.shape
    half = gathered[0].shape[1]
    shape = jax.ShapeDtypeStruct((blocks * capacity, 2 * half), jnp.bfloat16)
    return pl.pallas_call(
        functools.partial(pick_kernel, capacity),
        out_shape=(shape, shape),
        compiler_params=pltpu.CompilerParams(vmem_limit_bytes=48 * 2**20),
        cost_estimate=pl.CostEstimate(
            flops=8 * blocks * capacity * rows * half,
            bytes_accessed=4 * blocks * (rows + 2 * capacity) * half,
            transcendentals=0,
        ),
    )(place, *gathered)


def combine_kernel(place_ref, gate_ref, own_ref, other_ref, *out_refs):
    blocks, _, rows = place_ref.shape
    capacity = own_ref.shape[0] // blocks
    half = own_ref.shape[1] // 2
    slot = lax.broadcasted_iota(jnp.int32, (capacity, rows), 0)
    for block in range(blocks):
        weight = jnp.concatenate(
            [
                jnp.where(
                    place_ref[block, pl.ds(core, 1), :] == slot,
                    gate_ref[block, pl.ds(core, 1), :],
                    0.0,
                )
                for core in range(2)
            ],
            axis=0,
        )
        weight = weight.T.astype(jnp.bfloat16)
        level, (far_x, far_y) = block // 4, (block // 2 % 2, block % 2)
        for side in range(2):
            inner = pl.ds(block * capacity, capacity), pl.ds(side * half, half)
            both = jnp.concatenate([own_ref[inner], other_ref[inner]], axis=0)
            share = jnp.dot(weight, both, preferred_element_type=jnp.float32).astype(jnp.bfloat16)
            sent, place = (far_x, far_y) if side else (far_y, far_x)
            if sent:
                out_refs[6 * level + 3 * side + 2][pl.ds(place * rows, rows), :] = share
            else:
                out_refs[6 * level + 3 * side + place][...] = share


def combine_rows(place, gate, own, other):
    blocks, _, rows = place.shape
    half = own.shape[1] // 2
    kept = jax.ShapeDtypeStruct((rows, half), jnp.bfloat16)
    sent = jax.ShapeDtypeStruct((2 * rows, half), jnp.bfloat16)
    return pl.pallas_call(
        combine_kernel,
        out_shape=[kept, kept, sent] * (blocks // 2),
        compiler_params=pltpu.CompilerParams(vmem_limit_bytes=48 * 2**20),
        cost_estimate=pl.CostEstimate(
            flops=8 * own.shape[0] * rows * half,
            bytes_accessed=4 * (blocks * rows + 2 * own.shape[0]) * half,
            transcendentals=0,
        ),
    )(place, gate, own, other)


def routing_start(own_live, expert_ids, gate_values, earlier):
    live_ids = jnp.where(own_live[:, None], expert_ids, -1).astype(jnp.float32)
    routing = after(jnp.concatenate([live_ids, gate_values], axis=1).T, earlier)
    groups = lax.axis_size("grp")
    lines = [routing]
    for hop in range(2, groups, 2):
        lines.append(
            lax.ppermute(routing, "grp", [(g, (g + hop) % groups) for g in range(groups)])
        )
    return jnp.stack(lines)


def routing_pair(routing, swap):
    return jnp.stack([routing, swap(routing)], axis=routing.ndim - 2)


def selections(routing, top_count):
    mine = lax.axis_index(("grp", "sp"))
    depth, rows = routing.shape[0], routing.shape[-1]
    routing = routing.reshape(-1, 2 * top_count, rows)
    ids, gates = routing[:, :top_count].astype(jnp.int32), routing[:, top_count:]
    experts = jnp.stack([mine, mine ^ 1])
    chosen = ids[:, None] == experts[None, :, None, None]
    wanted = jnp.any(chosen, axis=2)
    gate = jnp.sum(jnp.where(chosen, gates[:, None], 0.0), axis=2)
    order = jnp.arange(rows)
    earlier = (order[:, None] < order[None, :]).astype(jnp.bfloat16)
    place = jnp.einsum(
        "bcr,rt->bct", wanted.astype(jnp.bfloat16), earlier, preferred_element_type=jnp.float32
    ).astype(jnp.int32)
    return jnp.where(wanted, place, -1), gate


def run_expert(rows, up_gate_weight, down_weight):
    hidden_width = down_weight.shape[1]
    projected = jnp.dot(rows, up_gate_weight[0], preferred_element_type=jnp.float32)
    hidden = (jax.nn.silu(projected[:, :hidden_width]) * projected[:, hidden_width:]).astype(
        jnp.bfloat16
    )
    return jnp.dot(hidden, down_weight[0], preferred_element_type=jnp.float32).astype(jnp.bfloat16)


def experts_by_gather(packed, place, gate, capacity, up_gate_weight, down_weight):
    depth = lax.axis_size("grp") // 2
    per_level = place.shape[0] // depth
    rows = packed.shape[0] // 2
    lines, beside_x, beside_y, diagonal = [packed], [], [], []

    def cross(level, earlier):
        first_x, second_y = beside_x[level][:rows], beside_y[level][rows:]
        if earlier is not None:
            first_x, second_y = after(first_x, earlier), after(second_y, earlier)
        diagonal.append((swap_y(first_x), swap_x(second_y)))

    for level in range(depth):
        line = lines[level]
        if level == 2:
            cross(0, line)
            cross(1, line)
            line = after(line, *diagonal[0], *diagonal[1])
        elif level > 2:
            line = after(line, beside_x[level - 1], beside_y[level - 1])
        beside_x.append(swap_x(line))
        beside_y.append(swap_y(line))
        if level + 1 < depth:
            line = lines[level]
            if level:
                line = after(line, beside_x[level - 1], beside_y[level - 1])
            lines.append(shift_z(line))
    for level in range(len(diagonal), depth):
        cross(level, None)
    kept, sent, back, joined = {}, {}, {}, {}

    def send_back(level, *earlier):
        first_sent, second_sent = sent[level]
        if earlier:
            first_sent, second_sent = after(first_sent, *earlier), after(second_sent, *earlier)
        back[level] = swap_y(first_sent), swap_x(second_sent)

    def join(level):
        first, first_x, second, second_y = kept[level]
        first_back, second_back = back[level]
        first, first_x = first + first_back[:rows], first_x + first_back[rows:]
        second, second_y = second + second_back[:rows], second_y + second_back[rows:]
        joined[level] = first, second, swap_x(first_x), swap_y(second_y)

    for start in range(0, depth, 2):
        levels = range(start, min(start + 2, depth))
        gathered = []
        for level in levels:
            gathered += [lines[level], beside_y[level], beside_x[level], *diagonal[level]]
        ahead, last = levels[-1] + 1, levels[-1] + 2
        if last < depth:
            gathered[0] = after(gathered[0], lines[last])
        if start:
            gathered[0] = after(gathered[0], kept[start - 1][0])
        blocks = slice(start * per_level, (start + len(levels)) * per_level)
        own, sibling = pick_rows(capacity, place[blocks], gathered)
        if last < depth:
            sibling = after(sibling, beside_x[ahead], beside_y[ahead])
        other = swap_core(sibling)
        other_result = run_expert(other, up_gate_weight, down_weight)
        if last < depth:
            own = after(own, beside_x[last], beside_y[last])
        if start:
            back[start - 1] = tuple(after(part, other_result) for part in back[start - 1])
            join(start - 1)
            own = after(own, *back[start - 1])
        own_result = run_expert(own, up_gate_weight, down_weight)
        other_result = swap_core(other_result)
        if last < depth:
            own_result = after(own_result, *diagonal[ahead])
        if start:
            own_result = after(own_result, *joined[start - 1])
        parts = combine_rows(place[blocks], gate[blocks], own_result, other_result)
        for index, level in enumerate(levels):
            first, first_x, first_sent, second, second_y, second_sent = parts[
                6 * index : 6 * index + 6
            ]
            kept[level] = first, first_x, second, second_y
            sent[level] = first_sent, second_sent
        levels = [level for level in levels if level]
        for level in levels:
            send_back(level, *back.get(level - 1, ()))
        if ahead < depth:
            levels = levels[:-1]
        for level in levels:
            join(level)
    send_back(0, *back.get(depth - 1, ()))
    join(0)
    shares = {}
    for level in range(depth):
        first, second, first_far, second_far = joined[level]
        shares[level] = first + first_far, second + second_far
    first, second = shares[0]
    if depth > 1:
        total = jnp.concatenate(shares[1], axis=0)
        for level in range(2, depth):
            total = jnp.concatenate(shares[level], axis=0) + shift_z(total)
        total = shift_z(total)
        first, second = first + total[:rows], second + total[rows:]
    return jnp.concatenate([first, second], axis=1)


def per_device_pairs(
    queries,
    fresh_key_values,
    cache,
    lengths,
    out_weight,
    residual,
    norm_gain,
    expert_ids,
    gate_values,
    up_gate_weight,
    down_weight,
):
    seq_devices = lax.axis_size("sp")
    mine = lax.axis_index("sp")
    slot_rows = queries.shape[0]
    width = cache.shape[-1] // 2
    head_columns = queries.shape[1] // seq_devices
    top_count = expert_ids.shape[1]
    experts = up_gate_weight.shape[0] * lax.axis_size("grp") * seq_devices
    capacity = max(2, 8 * slot_rows * top_count // (5 * experts))
    own_length = lengths[0, 0]
    own_live = jnp.arange(slot_rows, dtype=jnp.int32) < own_length

    def key_values_for(target):
        keys = lax.dynamic_slice(fresh_key_values, (0, target * width), (slot_rows, width))
        values = lax.dynamic_slice(
            fresh_key_values, (0, (seq_devices + target) * width), (slot_rows, width)
        )
        lane = jnp.arange(2 * width, dtype=jnp.int32)[None, :]
        note = jnp.where(lane < width, own_length // 256, own_length % 256)
        note = jnp.broadcast_to(note, (16, 2 * width)).astype(jnp.bfloat16)
        return jnp.concatenate([jnp.concatenate([keys, values], axis=1), note], axis=0)

    def queries_for(target):
        return lax.dynamic_slice(queries, (0, target * head_columns), (slot_rows, head_columns))

    masks = range(1, seq_devices)
    fresh = [key_values_for(mine)] + [xor_group(key_values_for(mine ^ m), m) for m in masks]
    query_blocks = [queries_for(mine)] + [xor_group(queries_for(mine ^ m), m) for m in masks]
    cache_block = cache[0, 0]

    def share_of(block, query):
        heads = attend_block(block, mine[None], query, cache_block, fresh)
        return jnp.dot(heads, out_weight, preferred_element_type=jnp.float32).astype(jnp.bfloat16)

    own = share_of(0, query_blocks[0])
    routing = routing_start(own_live, expert_ids, gate_values, own)
    far_core = share_of(3, after(query_blocks[3], query_blocks[2], own, routing))
    routing = routing_pair(routing, swap_x)
    far = share_of(2, after(query_blocks[2], routing)) + swap_core(far_core)
    near = share_of(1, after(query_blocks[1], far))
    far = swap_y(far)
    attended, packed = normalize(
        lengths[0], own, swap_core(after(near, far)), far, residual, norm_gain[None, :]
    )
    routing = routing_pair(after(routing, packed), swap_y)
    place, gate = selections(routing, top_count)
    moe_out = experts_by_gather(packed, place, gate, capacity, up_gate_weight, down_weight)
    return (attended, moe_out)


def per_device(
    queries,
    fresh_key_values,
    cache,
    lengths,
    out_weight,
    residual,
    norm_gain,
    expert_ids,
    gate_values,
    up_gate_weight,
    down_weight,
):
    seq_devices = lax.axis_size("sp")
    slot_rows = queries.shape[0]
    head_width = cache.shape[-1] // 2
    model_width = residual.shape[1]
    kv_heads = fresh_key_values.shape[1] // (2 * head_width)
    repeat = seq_devices // kv_heads
    keys_new = fresh_key_values[:, : kv_heads * head_width].reshape(
        slot_rows, kv_heads, 1, head_width
    )
    values_new = fresh_key_values[:, kv_heads * head_width :].reshape(
        slot_rows, kv_heads, 1, head_width
    )
    paired = jnp.concatenate([keys_new, values_new], axis=3)
    spread = jnp.broadcast_to(paired, (slot_rows, kv_heads, repeat, 2 * head_width)).reshape(
        slot_rows, seq_devices * 2 * head_width
    )
    all_lengths = lax.all_gather(lengths, "sp", axis=1, tiled=True)
    queries_by_head, head_kv = (
        lax.all_to_all(queries, "sp", split_axis=1, concat_axis=0, tiled=True),
        lax.all_to_all(spread, "sp", split_axis=1, concat_axis=0, tiled=True),
    )
    cache_block = cache[0, 0]
    my_index = lax.axis_index("sp")
    for bit_pos in range(repeat.bit_length() - 1):
        partner = partner_2(cache_block, "sp", bit_pos)
        is_upper = my_index // 2**bit_pos % 2 == 1
        cache_block = jnp.where(
            is_upper,
            jnp.concatenate([partner, cache_block], axis=0),
            jnp.concatenate([cache_block, partner], axis=0),
        )
    stretch_lens = all_lengths[0]
    offsets = jnp.cumsum(stretch_lens) - stretch_lens
    rows_of_group = queries_by_head.shape[0]
    slot_ids = jnp.arange(rows_of_group, dtype=jnp.int32)
    source = slot_ids // slot_rows
    within = slot_ids % slot_rows
    from_device = source[:, None] == jnp.arange(seq_devices, dtype=jnp.int32)[None, :]
    is_live = within < jnp.sum(jnp.where(from_device, stretch_lens[None, :], 0), axis=1)
    position = within + jnp.sum(jnp.where(from_device, offsets[None, :], 0), axis=1)
    per_dev = queries_by_head.shape[1] // head_width
    cache_len = cache_block.shape[0]
    key_all = jnp.concatenate([cache_block[:, :head_width], head_kv[:, :head_width]], axis=0)
    value_all = jnp.concatenate([cache_block[:, head_width:], head_kv[:, head_width:]], axis=0)
    block_count = 2 if rows_of_group % 2 == 0 and rows_of_group >= 1024 else 1
    block_rows = rows_of_group // block_count

    def attend(parts):
        query_block, place_block = parts
        scores = jnp.einsum(
            "rhd,kd->hrk", query_block, key_all, preferred_element_type=jnp.float32
        ) / math.sqrt(head_width)
        allowed = jnp.concatenate(
            [
                jnp.ones((block_rows, cache_len), dtype=bool),
                is_live[None, :] & (position[None, :] <= place_block[:, None]),
            ],
            axis=1,
        )
        scores = jnp.where(allowed[None], scores, -jnp.inf)
        row_max = jnp.max(scores, axis=-1, keepdims=True)
        weights = jnp.exp(scores - row_max)
        totals = jnp.sum(weights, axis=-1, keepdims=True)
        result = (
            jnp.einsum(
                "hrk,kd->hrd",
                weights.astype(jnp.bfloat16),
                value_all,
                preferred_element_type=jnp.float32,
            )
            / totals
        )
        return (
            result.astype(jnp.bfloat16).transpose(1, 0, 2).reshape(block_rows, per_dev * head_width)
        )

    attn_heads = lax.map(
        attend,
        (
            queries_by_head.reshape(block_count, block_rows, per_dev, head_width),
            position.reshape(block_count, block_rows),
        ),
    ).reshape(rows_of_group, per_dev * head_width)
    attn_sum = lax.psum_scatter(
        jnp.dot(attn_heads, out_weight, preferred_element_type=jnp.float32).astype(jnp.bfloat16),
        "sp",
        scatter_dimension=0,
        tiled=True,
    ).astype(jnp.float32)
    own_live = jnp.arange(slot_rows, dtype=jnp.int32) < lengths[0, 0]
    attended = jnp.where(own_live[:, None], attn_sum, 0.0).astype(jnp.bfloat16)
    mixed_rows = residual.astype(jnp.float32) + attn_sum
    normed = (
        mixed_rows
        * lax.rsqrt(jnp.mean(mixed_rows * mixed_rows, axis=-1, keepdims=True) + 1e-06)
        * norm_gain
    ).astype(jnp.bfloat16)
    group_count = lax.axis_size("grp")
    experts = up_gate_weight.shape[0] * group_count * seq_devices
    top_count = expert_ids.shape[1]
    capacity = max(2, 8 * slot_rows * top_count // (5 * experts))
    hidden_width = down_weight.shape[1]
    choose = expert_ids[:, :, None] == jnp.arange(experts, dtype=jnp.int32)[None, None, :]
    routed = (jnp.any(choose, axis=1) & own_live[:, None]).astype(jnp.float32)
    earlier = (jnp.arange(slot_rows)[:, None] > jnp.arange(slot_rows)[None, :]).astype(jnp.float32)
    prefix = jnp.dot(earlier, routed, precision=lax.Precision.HIGHEST)
    slot_in = jnp.sum(jnp.where(choose, prefix[:, None, :], 0.0), axis=2).astype(jnp.int32)
    dump_slot = experts * capacity
    target = jnp.where(own_live[:, None], expert_ids * capacity + slot_in, dump_slot)
    source_rows = (
        jnp.full((dump_slot + 1,), slot_rows, jnp.int32)
        .at[target.reshape(-1)]
        .set(jnp.repeat(jnp.arange(slot_rows, dtype=jnp.int32), top_count))[:dump_slot]
    )
    padded = jnp.concatenate([normed, jnp.zeros((1, model_width), jnp.bfloat16)], axis=0)
    outgoing = padded[source_rows].reshape(experts, capacity, model_width)
    received = lax.all_to_all(outgoing, ("grp", "sp"), split_axis=0, concat_axis=0, tiled=True)
    flat_rows = received.reshape(-1, model_width)
    projected = jnp.dot(flat_rows, up_gate_weight[0], preferred_element_type=jnp.float32)
    hidden = (jax.nn.silu(projected[:, :hidden_width]) * projected[:, hidden_width:]).astype(
        jnp.bfloat16
    )
    returned = lax.all_to_all(
        jnp.dot(hidden, down_weight[0], preferred_element_type=jnp.float32)
        .astype(jnp.bfloat16)
        .reshape(received.shape),
        ("grp", "sp"),
        split_axis=0,
        concat_axis=0,
        tiled=True,
    )
    back_rows = jnp.concatenate(
        [returned.reshape(dump_slot, model_width), jnp.zeros((1, model_width), jnp.bfloat16)],
        axis=0,
    )
    picked = back_rows[target]
    combined = jnp.sum(gate_values[:, :, None] * picked.astype(jnp.float32), axis=1)
    moe_out = jnp.where(own_live[:, None], combined, 0.0).astype(jnp.bfloat16)
    return (attended, moe_out)


def solution(mesh):
    in_specs = (
        P(("grp", "sp"), None),
        P(("grp", "sp"), None),
        P("grp", "sp", None, None),
        P("grp", "sp"),
        P("sp", None),
        P(("grp", "sp"), None),
        P(),
        P(("grp", "sp"), None),
        P(("grp", "sp"), None),
        P(("grp", "sp"), None, None),
        P(("grp", "sp"), None, None),
    )
    out_specs = (P(("grp", "sp"), None), P(("grp", "sp"), None))
    groups, seq_devices = mesh.shape["grp"], mesh.shape["sp"]

    def run(*args):
        kv_heads = args[1].shape[1] // args[2].shape[-1]
        experts, top_count = args[9].shape[0], args[7].shape[1]
        pairs = seq_devices == kv_heads == 4 and groups % 2 == 0 and experts <= 4 * top_count
        return mapped(per_device_pairs if pairs else per_device)(*args)

    def mapped(body):
        return jax.shard_map(
            body, mesh=mesh, in_specs=in_specs, out_specs=out_specs, check_vma=False
        )

    return run
```

```python
import functools
import math

import jax
import jax.numpy as jnp
from jax import lax
from jax.experimental import pallas as pl
from jax.experimental.pallas import tpu as pltpu
from jax.sharding import PartitionSpec as P


def partner_2(value, axis, bit):
    mask = 2**bit
    pairs = [(source, source ^ mask) for source in range(lax.axis_size(axis))]
    return lax.ppermute(value, axis, pairs)


def shift_z(value):
    groups = lax.axis_size("grp")
    return lax.ppermute(value, "grp", [(g, (g + 2) % groups) for g in range(groups)])


def swap_x(value):
    return partner_2(value, "grp", 0)


def swap_y(value):
    return partner_2(value, "sp", 1)


def swap_core(value):
    return partner_2(value, "sp", 0)


def after(value, *earlier):
    return lax.optimization_barrier((value, *earlier))[0]


def xor_group(value, mask):
    return lax.ppermute(value, "sp", [(s, s ^ mask) for s in range(lax.axis_size("sp"))])


def attend_kernel(index, mine_ref, query_ref, cache_ref, *refs):
    fresh_refs, (out_ref, keys, values, bias) = refs[:-4], refs[-4:]
    rows = query_ref.shape[0]
    cached, width = cache_ref.shape[0], cache_ref.shape[1] // 2
    keys[:cached, :] = cache_ref[:, :width]
    values[:cached, :] = cache_ref[:, width:]
    lengths = []
    for block, fresh_ref in enumerate(fresh_refs):
        places = pl.ds(cached + block * rows, rows)
        keys[places, :] = fresh_ref[:rows, :width]
        values[places, :] = fresh_ref[:rows, width:]
        note = fresh_ref[rows : rows + 16, :].astype(jnp.float32)
        lengths.append(note[:1, :1] * 256.0 + note[:1, width : width + 1])
    mine = mine_ref[0]
    offsets = []
    for block in range(len(fresh_refs)):
        offset = jnp.zeros((1, 1), jnp.float32)
        for other in range(len(fresh_refs)):
            before = (mine ^ other) < (mine ^ block)
            offset = offset + lengths[other] * before.astype(jnp.float32)
        offsets.append(offset)
    column = lax.broadcasted_iota(jnp.int32, (1, bias.shape[1]), 1)
    key_place = jnp.zeros((1, bias.shape[1]), jnp.float32)
    for block in range(len(fresh_refs)):
        within = (column - block * rows).astype(jnp.float32)
        place = jnp.where(within < lengths[block], within + offsets[block], 1e9)
        key_place = jnp.where(column >= block * rows, place, key_place)
    row_place = lax.broadcasted_iota(jnp.int32, bias.shape, 0).astype(jnp.float32) + offsets[index]
    bias[...] = jnp.where(key_place <= row_place, 0.0, -1e30)
    scale = math.log2(math.e) / math.sqrt(width)
    for head in range(query_ref.shape[1] // width):
        columns = pl.ds(head * width, width)
        scores = lax.dot_general(
            query_ref[:, columns],
            keys[...],
            (((1,), (1,)), ((), ())),
            preferred_element_type=jnp.float32,
        )
        old, new = scores[:, :cached] * scale, scores[:, cached:] * scale + bias[...]
        row_max = jnp.maximum(
            jnp.max(old, axis=1, keepdims=True), jnp.max(new, axis=1, keepdims=True)
        )
        old, new = jnp.exp2(old - row_max), jnp.exp2(new - row_max)
        totals = jnp.sum(old, axis=1, keepdims=True) + jnp.sum(new, axis=1, keepdims=True)
        result = jnp.dot(
            old.astype(jnp.bfloat16), values[:cached, :], preferred_element_type=jnp.float32
        ) + jnp.dot(
            new.astype(jnp.bfloat16), values[cached:, :], preferred_element_type=jnp.float32
        )
        out_ref[:, columns] = (result / totals).astype(jnp.bfloat16)


def attend_block(index, mine, query, cache_block, fresh):
    rows, columns = query.shape
    cached, width = cache_block.shape[0], cache_block.shape[1] // 2
    new = rows * len(fresh)
    inside = pl.BlockSpec(memory_space=pltpu.VMEM)
    return pl.pallas_call(
        functools.partial(attend_kernel, index),
        out_shape=jax.ShapeDtypeStruct((rows, columns), jnp.bfloat16),
        in_specs=[pl.BlockSpec(memory_space=pltpu.SMEM)] + [inside] * (2 + len(fresh)),
        out_specs=inside,
        scratch_shapes=[
            pltpu.VMEM((cached + new, width), jnp.bfloat16),
            pltpu.VMEM((cached + new, width), jnp.bfloat16),
            pltpu.VMEM((rows, new), jnp.float32),
        ],
        compiler_params=pltpu.CompilerParams(vmem_limit_bytes=40 * 2**20),
        cost_estimate=pl.CostEstimate(
            flops=4 * rows * columns * (cached + new),
            bytes_accessed=4 * (rows * columns + (cached + new) * width),
            transcendentals=rows * columns // width * (cached + new),
        ),
    )(mine, query, cache_block, *fresh)


def norm_kernel(
    length_ref,
    own_ref,
    core_ref,
    far_ref,
    residual_ref,
    gain_ref,
    attended_ref,
    packed_ref,
):
    attn_sum = (
        own_ref[...].astype(jnp.float32)
        + core_ref[...].astype(jnp.float32)
        + far_ref[...].astype(jnp.float32)
    )
    live = lax.broadcasted_iota(jnp.int32, attn_sum.shape, 0) < length_ref[0]
    attended_ref[...] = jnp.where(live, attn_sum, 0.0).astype(jnp.bfloat16)
    mixed = residual_ref[...].astype(jnp.float32) + attn_sum
    scale = lax.rsqrt(jnp.mean(mixed * mixed, axis=1, keepdims=True) + 1e-06)
    normed = (mixed * scale * gain_ref[...]).astype(jnp.bfloat16)
    rows, half = packed_ref.shape[0] // 2, packed_ref.shape[1]
    packed_ref[:rows, :] = normed[:, :half]
    packed_ref[rows:, :] = normed[:, half:]


def normalize(length, own, core, far, residual, gain):
    rows, width = own.shape
    packed = jax.ShapeDtypeStruct((2 * rows, width // 2), jnp.bfloat16)
    inside = pl.BlockSpec(memory_space=pltpu.VMEM)
    return pl.pallas_call(
        norm_kernel,
        out_shape=(jax.ShapeDtypeStruct((rows, width), jnp.bfloat16), packed),
        in_specs=[pl.BlockSpec(memory_space=pltpu.SMEM)] + [inside] * 5,
        out_specs=(inside, inside),
        compiler_params=pltpu.CompilerParams(vmem_limit_bytes=40 * 2**20),
        cost_estimate=pl.CostEstimate(
            flops=10 * rows * width, bytes_accessed=12 * rows * width, transcendentals=rows
        ),
    )(length, own, core, far, residual, gain)


def pick_kernel(capacity, place_ref, *refs):
    blocks, _, rows = place_ref.shape
    own_ref, sibling_ref = refs[-2:]
    half = own_ref.shape[1] // 2
    slot = lax.broadcasted_iota(jnp.int32, (capacity, rows), 0)
    for block in range(blocks):
        pick = jnp.concatenate(
            [(place_ref[block, pl.ds(core, 1), :] == slot) for core in range(2)], axis=0
        )
        pick = jnp.where(pick, 1.0, 0.0).astype(jnp.bfloat16)
        level, spot = block // 4, block % 4
        for side in range(2):
            if spot < 3:
                source = refs[5 * level + spot][pl.ds(side * rows, rows), :]
            else:
                source = refs[5 * level + 3 + side][...]
            chosen = jnp.dot(pick, source, preferred_element_type=jnp.float32)
            chosen = chosen.astype(jnp.bfloat16)
            inner = pl.ds(block * capacity, capacity), pl.ds(side * half, half)
            own_ref[inner] = chosen[:capacity]
            sibling_ref[inner] = chosen[capacity:]


def pick_rows(capacity, place, gathered):
    blocks, _, rows = place.shape
    half = gathered[0].shape[1]
    shape = jax.ShapeDtypeStruct((blocks * capacity, 2 * half), jnp.bfloat16)
    return pl.pallas_call(
        functools.partial(pick_kernel, capacity),
        out_shape=(shape, shape),
        compiler_params=pltpu.CompilerParams(vmem_limit_bytes=48 * 2**20),
        cost_estimate=pl.CostEstimate(
            flops=8 * blocks * capacity * rows * half,
            bytes_accessed=4 * blocks * (rows + 2 * capacity) * half,
            transcendentals=0,
        ),
    )(place, *gathered)


def combine_kernel(place_ref, gate_ref, own_ref, other_ref, *out_refs):
    blocks, _, rows = place_ref.shape
    capacity = own_ref.shape[0] // blocks
    half = own_ref.shape[1] // 2
    slot = lax.broadcasted_iota(jnp.int32, (capacity, rows), 0)
    for block in range(blocks):
        weight = jnp.concatenate(
            [
                jnp.where(
                    place_ref[block, pl.ds(core, 1), :] == slot,
                    gate_ref[block, pl.ds(core, 1), :],
                    0.0,
                )
                for core in range(2)
            ],
            axis=0,
        )
        weight = weight.T.astype(jnp.bfloat16)
        far_x, far_y = block // 2, block % 2
        for side in range(2):
            inner = pl.ds(block * capacity, capacity), pl.ds(side * half, half)
            both = jnp.concatenate([own_ref[inner], other_ref[inner]], axis=0)
            share = jnp.dot(weight, both, preferred_element_type=jnp.float32).astype(jnp.bfloat16)
            sent, place = (far_x, far_y) if side else (far_y, far_x)
            if sent:
                out_refs[3 * side + 2][pl.ds(place * rows, rows), :] = share
            else:
                out_refs[3 * side + place][...] = share


def combine_rows(part, parts, place, gate, own, other):
    blocks, _, rows = place.shape
    half = own.shape[1] // 2
    kept = jax.ShapeDtypeStruct((rows, half), jnp.bfloat16)
    sent = jax.ShapeDtypeStruct((2 * rows, half), jnp.bfloat16)
    count = own.shape[0] // parts
    whole = lambda shape: pl.BlockSpec(shape, lambda j: (0,) * len(shape))
    level = pl.BlockSpec((count, 2 * half), lambda j: (part, 0))
    return pl.pallas_call(
        combine_kernel,
        out_shape=[kept, kept, sent] * 2,
        grid=(1,),
        in_specs=[whole(place.shape), whole(gate.shape), level, level],
        out_specs=[whole(kept.shape), whole(kept.shape), whole(sent.shape)] * 2,
        compiler_params=pltpu.CompilerParams(vmem_limit_bytes=44 * 2**20),
        cost_estimate=pl.CostEstimate(
            flops=8 * count * rows * half,
            bytes_accessed=4 * (blocks * rows + 2 * count) * half,
            transcendentals=0,
        ),
    )(place, gate, own, other)


def routing_start(own_live, expert_ids, gate_values, earlier):
    live_ids = jnp.where(own_live[:, None], expert_ids, -1).astype(jnp.float32)
    routing = after(jnp.concatenate([live_ids, gate_values], axis=1).T, earlier)
    groups = lax.axis_size("grp")
    lines = [routing]
    for hop in range(2, groups, 2):
        lines.append(
            lax.ppermute(routing, "grp", [(g, (g + hop) % groups) for g in range(groups)])
        )
    return jnp.stack(lines)


def routing_pair(routing, swap):
    return jnp.stack([routing, swap(routing)], axis=routing.ndim - 2)


def selections(routing, top_count):
    mine = lax.axis_index(("grp", "sp"))
    depth, rows = routing.shape[0], routing.shape[-1]
    routing = routing.reshape(-1, 2 * top_count, rows)
    ids, gates = routing[:, :top_count].astype(jnp.int32), routing[:, top_count:]
    experts = jnp.stack([mine, mine ^ 1])
    chosen = ids[:, None] == experts[None, :, None, None]
    wanted = jnp.any(chosen, axis=2)
    gate = jnp.sum(jnp.where(chosen, gates[:, None], 0.0), axis=2)
    order = jnp.arange(rows)
    earlier = (order[:, None] < order[None, :]).astype(jnp.bfloat16)
    place = jnp.einsum(
        "bcr,rt->bct", wanted.astype(jnp.bfloat16), earlier, preferred_element_type=jnp.float32
    ).astype(jnp.int32)
    return jnp.where(wanted, place, -1), gate


def expert_kernel(rows_ref, gate_ref, up_ref, down_ref, out_ref, total):
    step = pl.program_id(0)
    rows = rows_ref[...]
    gate = jnp.dot(rows, gate_ref[0], preferred_element_type=jnp.float32)
    up = jnp.dot(rows, up_ref[0], preferred_element_type=jnp.float32)
    hidden = (gate / (1.0 + jnp.exp(-gate)) * up).astype(jnp.bfloat16)
    part = jnp.dot(hidden, down_ref[0], preferred_element_type=jnp.float32)
    last = pl.num_programs(0) - 1

    @pl.when(step == 0)
    def _():
        total[...] = part

    @pl.when((step > 0) & (step < last))
    def _():
        total[...] += part

    @pl.when(step == last)
    def _():
        out_ref[...] = (total[...] + part).astype(jnp.bfloat16)


def run_expert(rows, up_gate_weight, down_weight):
    count, width = rows.shape
    hidden_width = down_weight.shape[1]
    tile = 256
    steps = hidden_width // tile
    return pl.pallas_call(
        expert_kernel,
        out_shape=jax.ShapeDtypeStruct((count, width), jnp.bfloat16),
        grid=(steps,),
        in_specs=[
            pl.BlockSpec((count, width), lambda j: (0, 0)),
            pl.BlockSpec((1, width, tile), lambda j: (0, 0, j)),
            pl.BlockSpec((1, width, tile), lambda j: (0, 0, j + steps)),
            pl.BlockSpec((1, tile, width), lambda j: (0, j, 0)),
        ],
        out_specs=pl.BlockSpec((count, width), lambda j: (0, 0)),
        scratch_shapes=[pltpu.VMEM((count, width), jnp.float32)],
        compiler_params=pltpu.CompilerParams(vmem_limit_bytes=44 * 2**20),
        cost_estimate=pl.CostEstimate(
            flops=6 * count * width * hidden_width,
            bytes_accessed=6 * width * hidden_width + 4 * count * width,
            transcendentals=count * hidden_width,
        ),
    )(rows, up_gate_weight, up_gate_weight, down_weight)


def experts_by_gather(packed, routing, top_count, capacity, up_gate_weight, down_weight):
    depth = lax.axis_size("grp") // 2
    rows = packed.shape[0] // 2
    routing = routing_pair(after(routing, packed), swap_x)
    lines, beside_x, beside_y, diagonal = [packed], [], [], []
    halves = []

    def cross(level, earlier):
        first_x, second_y = halves[level]
        if earlier is not None:
            first_x, second_y = after(first_x, *earlier), after(second_y, *earlier)
        diagonal.append((swap_y(first_x), swap_x(second_y)))

    for level in range(depth):
        line = lines[level]
        if level == 1:
            line = after(line, routing)
            routing = routing_pair(after(routing, *halves[0]), swap_y)
        if level == 2:
            cross(0, (line, routing))
            cross(1, (line,))
            line = after(line, *diagonal[0], *diagonal[1])
        elif level > 2:
            line = after(line, beside_x[level - 1], beside_y[level - 1])
        beside_x.append(swap_x(line))
        beside_y.append(swap_y(line))
        halves.append((beside_x[level][:rows], beside_y[level][rows:]))
        if level + 1 < depth:
            line = lines[level]
            if level:
                line = after(line, beside_x[level - 1], beside_y[level - 1])
            lines.append(shift_z(line))
    for level in range(len(diagonal), depth):
        cross(level, None)
    if depth == 1:
        routing = routing_pair(routing, swap_y)
    place, gate = selections(routing, top_count)
    per_level = place.shape[0] // depth
    results, kept, sent, back, joined = {}, {}, {}, {}, {}

    def combine(level, *earlier):
        index, count, own_result, other_result = results[level]
        if earlier:
            own_result = after(own_result, *earlier)
        blocks = slice(level * per_level, (level + 1) * per_level)
        parts = combine_rows(index, count, place[blocks], gate[blocks], own_result, other_result)
        first, first_x, first_sent, second, second_y, second_sent = parts
        kept[level] = first, first_x, second, second_y
        sent[level] = first_sent, second_sent

    def send_back(level, *earlier):
        first_sent, second_sent = sent[level]
        if earlier:
            first_sent, second_sent = after(first_sent, *earlier), after(second_sent, *earlier)
        back[level] = swap_y(first_sent), swap_x(second_sent)

    def join(level):
        first, first_x, second, second_y = kept[level]
        first_back, second_back = back[level]
        first, first_x = first + first_back[:rows], first_x + first_back[rows:]
        second, second_y = second + second_back[:rows], second_y + second_back[rows:]
        joined[level] = first, second, swap_x(first_x), swap_y(second_y)

    for start in range(0, depth, 2):
        levels = range(start, min(start + 2, depth))
        gathered = []
        for level in levels:
            gathered += [lines[level], beside_y[level], beside_x[level], *diagonal[level]]
        ahead, last = levels[-1] + 1, levels[-1] + 2
        if start:
            gathered[0] = after(gathered[0], kept[start - 1][0])
        blocks = slice(start * per_level, (start + len(levels)) * per_level)
        own, sibling = pick_rows(capacity, place[blocks], gathered)
        if last < depth:
            sibling = after(sibling, beside_x[ahead], beside_y[ahead], lines[last])
        other = swap_core(sibling)
        other_result = run_expert(other, up_gate_weight, down_weight)
        if last < depth:
            other_result = after(other_result, beside_x[last], beside_y[last])
            own = after(own, other_result)
        if start:
            back[start - 1] = tuple(after(part, other_result) for part in back[start - 1])
            join(start - 1)
            own = after(own, *back[start - 1])
        own_result = run_expert(own, up_gate_weight, down_weight)
        other_result = swap_core(other_result)
        if last < depth:
            own_result = after(own_result, *diagonal[ahead])
        if start:
            own_result = after(own_result, *joined[start - 1])
        for index, level in enumerate(levels):
            results[level] = index, len(levels), own_result, other_result
            if level:
                combine(level)
                send_back(level, *back.get(level - 1, ()))
        for level in levels:
            if level and (ahead >= depth or level < levels[-1]):
                join(level)
    combine(0, *(kept[depth - 1][:1] if depth > 1 else ()))
    send_back(0, *back.get(depth - 1, ()))
    join(0)
    shares = {}
    for level in range(depth):
        first, second, first_far, second_far = joined[level]
        shares[level] = first + first_far, second + second_far
    first, second = shares[0]
    if depth > 1:
        total = jnp.concatenate(shares[1], axis=0)
        for level in range(2, depth):
            total = jnp.concatenate(shares[level], axis=0) + shift_z(total)
        total = shift_z(total)
        first, second = first + total[:rows], second + total[rows:]
    return jnp.concatenate([first, second], axis=1)


def per_device_pairs(
    queries,
    fresh_key_values,
    cache,
    lengths,
    out_weight,
    residual,
    norm_gain,
    expert_ids,
    gate_values,
    up_gate_weight,
    down_weight,
):
    seq_devices = lax.axis_size("sp")
    mine = lax.axis_index("sp")
    slot_rows = queries.shape[0]
    width = cache.shape[-1] // 2
    head_columns = queries.shape[1] // seq_devices
    top_count = expert_ids.shape[1]
    experts = up_gate_weight.shape[0] * lax.axis_size("grp") * seq_devices
    capacity = max(2, 8 * slot_rows * top_count // (5 * experts))
    own_length = lengths[0, 0]
    own_live = jnp.arange(slot_rows, dtype=jnp.int32) < own_length

    def key_values_for(target):
        keys = lax.dynamic_slice(fresh_key_values, (0, target * width), (slot_rows, width))
        values = lax.dynamic_slice(
            fresh_key_values, (0, (seq_devices + target) * width), (slot_rows, width)
        )
        lane = jnp.arange(2 * width, dtype=jnp.int32)[None, :]
        note = jnp.where(lane < width, own_length // 256, own_length % 256)
        note = jnp.broadcast_to(note, (16, 2 * width)).astype(jnp.bfloat16)
        return jnp.concatenate([jnp.concatenate([keys, values], axis=1), note], axis=0)

    def queries_for(target):
        return lax.dynamic_slice(queries, (0, target * head_columns), (slot_rows, head_columns))

    masks = range(1, seq_devices)
    fresh = [key_values_for(mine)] + [xor_group(key_values_for(mine ^ m), m) for m in masks]
    query_blocks = [queries_for(mine)] + [xor_group(queries_for(mine ^ m), m) for m in masks]
    cache_block = cache[0, 0]

    def share_of(block, query):
        heads = attend_block(block, mine[None], query, cache_block, fresh)
        return jnp.dot(heads, out_weight, preferred_element_type=jnp.float32).astype(jnp.bfloat16)

    own = share_of(0, query_blocks[0])
    routing = routing_start(own_live, expert_ids, gate_values, own)
    far_core = share_of(3, after(query_blocks[3], query_blocks[2], own, routing))
    far = share_of(2, query_blocks[2]) + swap_core(far_core)
    near = share_of(1, after(query_blocks[1], far))
    far = swap_y(far)
    attended, packed = normalize(
        lengths[0], own, swap_core(after(near, far)), far, residual, norm_gain[None, :]
    )
    moe_out = experts_by_gather(
        packed, routing, top_count, capacity, up_gate_weight, down_weight
    )
    return (attended, moe_out)


def per_device(
    queries,
    fresh_key_values,
    cache,
    lengths,
    out_weight,
    residual,
    norm_gain,
    expert_ids,
    gate_values,
    up_gate_weight,
    down_weight,
):
    seq_devices = lax.axis_size("sp")
    slot_rows = queries.shape[0]
    head_width = cache.shape[-1] // 2
    model_width = residual.shape[1]
    kv_heads = fresh_key_values.shape[1] // (2 * head_width)
    repeat = seq_devices // kv_heads
    keys_new = fresh_key_values[:, : kv_heads * head_width].reshape(
        slot_rows, kv_heads, 1, head_width
    )
    values_new = fresh_key_values[:, kv_heads * head_width :].reshape(
        slot_rows, kv_heads, 1, head_width
    )
    paired = jnp.concatenate([keys_new, values_new], axis=3)
    spread = jnp.broadcast_to(paired, (slot_rows, kv_heads, repeat, 2 * head_width)).reshape(
        slot_rows, seq_devices * 2 * head_width
    )
    all_lengths = lax.all_gather(lengths, "sp", axis=1, tiled=True)
    queries_by_head, head_kv = (
        lax.all_to_all(queries, "sp", split_axis=1, concat_axis=0, tiled=True),
        lax.all_to_all(spread, "sp", split_axis=1, concat_axis=0, tiled=True),
    )
    cache_block = cache[0, 0]
    my_index = lax.axis_index("sp")
    for bit_pos in range(repeat.bit_length() - 1):
        partner = partner_2(cache_block, "sp", bit_pos)
        is_upper = my_index // 2**bit_pos % 2 == 1
        cache_block = jnp.where(
            is_upper,
            jnp.concatenate([partner, cache_block], axis=0),
            jnp.concatenate([cache_block, partner], axis=0),
        )
    stretch_lens = all_lengths[0]
    offsets = jnp.cumsum(stretch_lens) - stretch_lens
    rows_of_group = queries_by_head.shape[0]
    slot_ids = jnp.arange(rows_of_group, dtype=jnp.int32)
    source = slot_ids // slot_rows
    within = slot_ids % slot_rows
    from_device = source[:, None] == jnp.arange(seq_devices, dtype=jnp.int32)[None, :]
    is_live = within < jnp.sum(jnp.where(from_device, stretch_lens[None, :], 0), axis=1)
    position = within + jnp.sum(jnp.where(from_device, offsets[None, :], 0), axis=1)
    per_dev = queries_by_head.shape[1] // head_width
    cache_len = cache_block.shape[0]
    key_all = jnp.concatenate([cache_block[:, :head_width], head_kv[:, :head_width]], axis=0)
    value_all = jnp.concatenate([cache_block[:, head_width:], head_kv[:, head_width:]], axis=0)
    block_count = 2 if rows_of_group % 2 == 0 and rows_of_group >= 1024 else 1
    block_rows = rows_of_group // block_count

    def attend(parts):
        query_block, place_block = parts
        scores = jnp.einsum(
            "rhd,kd->hrk", query_block, key_all, preferred_element_type=jnp.float32
        ) / math.sqrt(head_width)
        allowed = jnp.concatenate(
            [
                jnp.ones((block_rows, cache_len), dtype=bool),
                is_live[None, :] & (position[None, :] <= place_block[:, None]),
            ],
            axis=1,
        )
        scores = jnp.where(allowed[None], scores, -jnp.inf)
        row_max = jnp.max(scores, axis=-1, keepdims=True)
        weights = jnp.exp(scores - row_max)
        totals = jnp.sum(weights, axis=-1, keepdims=True)
        result = (
            jnp.einsum(
                "hrk,kd->hrd",
                weights.astype(jnp.bfloat16),
                value_all,
                preferred_element_type=jnp.float32,
            )
            / totals
        )
        return (
            result.astype(jnp.bfloat16).transpose(1, 0, 2).reshape(block_rows, per_dev * head_width)
        )

    attn_heads = lax.map(
        attend,
        (
            queries_by_head.reshape(block_count, block_rows, per_dev, head_width),
            position.reshape(block_count, block_rows),
        ),
    ).reshape(rows_of_group, per_dev * head_width)
    attn_sum = lax.psum_scatter(
        jnp.dot(attn_heads, out_weight, preferred_element_type=jnp.float32).astype(jnp.bfloat16),
        "sp",
        scatter_dimension=0,
        tiled=True,
    ).astype(jnp.float32)
    own_live = jnp.arange(slot_rows, dtype=jnp.int32) < lengths[0, 0]
    attended = jnp.where(own_live[:, None], attn_sum, 0.0).astype(jnp.bfloat16)
    mixed_rows = residual.astype(jnp.float32) + attn_sum
    normed = (
        mixed_rows
        * lax.rsqrt(jnp.mean(mixed_rows * mixed_rows, axis=-1, keepdims=True) + 1e-06)
        * norm_gain
    ).astype(jnp.bfloat16)
    group_count = lax.axis_size("grp")
    experts = up_gate_weight.shape[0] * group_count * seq_devices
    top_count = expert_ids.shape[1]
    capacity = max(2, 8 * slot_rows * top_count // (5 * experts))
    hidden_width = down_weight.shape[1]
    choose = expert_ids[:, :, None] == jnp.arange(experts, dtype=jnp.int32)[None, None, :]
    routed = (jnp.any(choose, axis=1) & own_live[:, None]).astype(jnp.float32)
    earlier = (jnp.arange(slot_rows)[:, None] > jnp.arange(slot_rows)[None, :]).astype(jnp.float32)
    prefix = jnp.dot(earlier, routed, precision=lax.Precision.HIGHEST)
    slot_in = jnp.sum(jnp.where(choose, prefix[:, None, :], 0.0), axis=2).astype(jnp.int32)
    dump_slot = experts * capacity
    target = jnp.where(own_live[:, None], expert_ids * capacity + slot_in, dump_slot)
    source_rows = (
        jnp.full((dump_slot + 1,), slot_rows, jnp.int32)
        .at[target.reshape(-1)]
        .set(jnp.repeat(jnp.arange(slot_rows, dtype=jnp.int32), top_count))[:dump_slot]
    )
    padded = jnp.concatenate([normed, jnp.zeros((1, model_width), jnp.bfloat16)], axis=0)
    outgoing = padded[source_rows].reshape(experts, capacity, model_width)
    received = lax.all_to_all(outgoing, ("grp", "sp"), split_axis=0, concat_axis=0, tiled=True)
    flat_rows = received.reshape(-1, model_width)
    projected = jnp.dot(flat_rows, up_gate_weight[0], preferred_element_type=jnp.float32)
    hidden = (jax.nn.silu(projected[:, :hidden_width]) * projected[:, hidden_width:]).astype(
        jnp.bfloat16
    )
    returned = lax.all_to_all(
        jnp.dot(hidden, down_weight[0], preferred_element_type=jnp.float32)
        .astype(jnp.bfloat16)
        .reshape(received.shape),
        ("grp", "sp"),
        split_axis=0,
        concat_axis=0,
        tiled=True,
    )
    back_rows = jnp.concatenate(
        [returned.reshape(dump_slot, model_width), jnp.zeros((1, model_width), jnp.bfloat16)],
        axis=0,
    )
    picked = back_rows[target]
    combined = jnp.sum(gate_values[:, :, None] * picked.astype(jnp.float32), axis=1)
    moe_out = jnp.where(own_live[:, None], combined, 0.0).astype(jnp.bfloat16)
    return (attended, moe_out)


def solution(mesh):
    in_specs = (
        P(("grp", "sp"), None),
        P(("grp", "sp"), None),
        P("grp", "sp", None, None),
        P("grp", "sp"),
        P("sp", None),
        P(("grp", "sp"), None),
        P(),
        P(("grp", "sp"), None),
        P(("grp", "sp"), None),
        P(("grp", "sp"), None, None),
        P(("grp", "sp"), None, None),
    )
    out_specs = (P(("grp", "sp"), None), P(("grp", "sp"), None))
    groups, seq_devices = mesh.shape["grp"], mesh.shape["sp"]

    def run(*args):
        kv_heads = args[1].shape[1] // args[2].shape[-1]
        experts, top_count = args[9].shape[0], args[7].shape[1]
        pairs = seq_devices == kv_heads == 4 and groups % 2 == 0 and experts <= 4 * top_count
        return mapped(per_device_pairs if pairs else per_device)(*args)

    def mapped(body):
        return jax.shard_map(
            body, mesh=mesh, in_specs=in_specs, out_specs=out_specs, check_vma=False
        )

    return run
```

```python
import functools
import math

import jax
import jax.numpy as jnp
from jax import lax
from jax.experimental import pallas as pl
from jax.experimental.pallas import tpu as pltpu
from jax.sharding import PartitionSpec as P


def partner_2(value, axis, bit):
    mask = 2**bit
    pairs = [(source, source ^ mask) for source in range(lax.axis_size(axis))]
    return lax.ppermute(value, axis, pairs)


def shift_z(value):
    groups = lax.axis_size("grp")
    return lax.ppermute(value, "grp", [(g, (g + 2) % groups) for g in range(groups)])


def swap_x(value):
    return partner_2(value, "grp", 0)


def swap_y(value):
    return partner_2(value, "sp", 1)


def swap_core(value):
    return partner_2(value, "sp", 0)


def after(value, *earlier):
    return lax.optimization_barrier((value, *earlier))[0]


def xor_group(value, mask):
    return lax.ppermute(value, "sp", [(s, s ^ mask) for s in range(lax.axis_size("sp"))])


def attend_kernel(index, mine_ref, query_ref, cache_ref, *refs):
    fresh_refs, (out_ref, keys, values, bias) = refs[:-4], refs[-4:]
    rows = query_ref.shape[0]
    cached, width = cache_ref.shape[0], cache_ref.shape[1] // 2
    keys[:cached, :] = cache_ref[:, :width]
    values[:cached, :] = cache_ref[:, width:]
    lengths = []
    for block, fresh_ref in enumerate(fresh_refs):
        places = pl.ds(cached + block * rows, rows)
        keys[places, :] = fresh_ref[:rows, :width]
        values[places, :] = fresh_ref[:rows, width:]
        note = fresh_ref[rows : rows + 16, :].astype(jnp.float32)
        lengths.append(note[:1, :1] * 256.0 + note[:1, width : width + 1])
    mine = mine_ref[0]
    offsets = []
    for block in range(len(fresh_refs)):
        offset = jnp.zeros((1, 1), jnp.float32)
        for other in range(len(fresh_refs)):
            before = (mine ^ other) < (mine ^ block)
            offset = offset + lengths[other] * before.astype(jnp.float32)
        offsets.append(offset)
    column = lax.broadcasted_iota(jnp.int32, (1, bias.shape[1]), 1)
    key_place = jnp.zeros((1, bias.shape[1]), jnp.float32)
    for block in range(len(fresh_refs)):
        within = (column - block * rows).astype(jnp.float32)
        place = jnp.where(within < lengths[block], within + offsets[block], 1e9)
        key_place = jnp.where(column >= block * rows, place, key_place)
    row_place = lax.broadcasted_iota(jnp.int32, bias.shape, 0).astype(jnp.float32) + offsets[index]
    bias[...] = jnp.where(key_place <= row_place, 0.0, -1e30)
    scale = math.log2(math.e) / math.sqrt(width)
    for head in range(query_ref.shape[1] // width):
        columns = pl.ds(head * width, width)
        scores = lax.dot_general(
            query_ref[:, columns],
            keys[...],
            (((1,), (1,)), ((), ())),
            preferred_element_type=jnp.float32,
        )
        old, new = scores[:, :cached] * scale, scores[:, cached:] * scale + bias[...]
        row_max = jnp.maximum(
            jnp.max(old, axis=1, keepdims=True), jnp.max(new, axis=1, keepdims=True)
        )
        old, new = jnp.exp2(old - row_max), jnp.exp2(new - row_max)
        totals = jnp.sum(old, axis=1, keepdims=True) + jnp.sum(new, axis=1, keepdims=True)
        result = jnp.dot(
            old.astype(jnp.bfloat16), values[:cached, :], preferred_element_type=jnp.float32
        ) + jnp.dot(
            new.astype(jnp.bfloat16), values[cached:, :], preferred_element_type=jnp.float32
        )
        out_ref[:, columns] = (result / totals).astype(jnp.bfloat16)


def attend_block(index, mine, query, cache_block, fresh):
    rows, columns = query.shape
    cached, width = cache_block.shape[0], cache_block.shape[1] // 2
    new = rows * len(fresh)
    inside = pl.BlockSpec(memory_space=pltpu.VMEM)
    return pl.pallas_call(
        functools.partial(attend_kernel, index),
        out_shape=jax.ShapeDtypeStruct((rows, columns), jnp.bfloat16),
        in_specs=[pl.BlockSpec(memory_space=pltpu.SMEM)] + [inside] * (2 + len(fresh)),
        out_specs=inside,
        scratch_shapes=[
            pltpu.VMEM((cached + new, width), jnp.bfloat16),
            pltpu.VMEM((cached + new, width), jnp.bfloat16),
            pltpu.VMEM((rows, new), jnp.float32),
        ],
        compiler_params=pltpu.CompilerParams(vmem_limit_bytes=12 * 2**20),
        cost_estimate=pl.CostEstimate(
            flops=4 * rows * columns * (cached + new),
            bytes_accessed=4 * (rows * columns + (cached + new) * width),
            transcendentals=rows * columns // width * (cached + new),
        ),
    )(mine, query, cache_block, *fresh)


def norm_kernel(
    length_ref,
    own_ref,
    core_ref,
    far_ref,
    residual_ref,
    gain_ref,
    attended_ref,
    packed_ref,
):
    attn_sum = (
        own_ref[...].astype(jnp.float32)
        + core_ref[...].astype(jnp.float32)
        + far_ref[...].astype(jnp.float32)
    )
    live = lax.broadcasted_iota(jnp.int32, attn_sum.shape, 0) < length_ref[0]
    attended_ref[...] = jnp.where(live, attn_sum, 0.0).astype(jnp.bfloat16)
    mixed = residual_ref[...].astype(jnp.float32) + attn_sum
    scale = lax.rsqrt(jnp.mean(mixed * mixed, axis=1, keepdims=True) + 1e-06)
    normed = (mixed * scale * gain_ref[...]).astype(jnp.bfloat16)
    rows, half = packed_ref.shape[0] // 2, packed_ref.shape[1]
    packed_ref[:rows, :] = normed[:, :half]
    packed_ref[rows:, :] = normed[:, half:]


def normalize(length, own, core, far, residual, gain):
    rows, width = own.shape
    packed = jax.ShapeDtypeStruct((2 * rows, width // 2), jnp.bfloat16)
    inside = pl.BlockSpec(memory_space=pltpu.VMEM)
    return pl.pallas_call(
        norm_kernel,
        out_shape=(jax.ShapeDtypeStruct((rows, width), jnp.bfloat16), packed),
        in_specs=[pl.BlockSpec(memory_space=pltpu.SMEM)] + [inside] * 5,
        out_specs=(inside, inside),
        compiler_params=pltpu.CompilerParams(vmem_limit_bytes=12 * 2**20),
        cost_estimate=pl.CostEstimate(
            flops=10 * rows * width, bytes_accessed=12 * rows * width, transcendentals=rows
        ),
    )(length, own, core, far, residual, gain)


def pick_kernel(capacity, place_ref, *refs):
    blocks, _, rows = place_ref.shape
    own_ref, sibling_ref = refs[-2:]
    half = own_ref.shape[1] // 2
    slot = lax.broadcasted_iota(jnp.int32, (capacity, rows), 0)
    for block in range(blocks):
        pick = jnp.concatenate(
            [(place_ref[block, pl.ds(core, 1), :] == slot) for core in range(2)], axis=0
        )
        pick = jnp.where(pick, 1.0, 0.0).astype(jnp.bfloat16)
        level, spot = block // 4, block % 4
        for side in range(2):
            if spot < 3:
                source = refs[5 * level + spot][pl.ds(side * rows, rows), :]
            else:
                source = refs[5 * level + 3 + side][...]
            chosen = jnp.dot(pick, source, preferred_element_type=jnp.float32)
            chosen = chosen.astype(jnp.bfloat16)
            inner = pl.ds(block * capacity, capacity), pl.ds(side * half, half)
            own_ref[inner] = chosen[:capacity]
            sibling_ref[inner] = chosen[capacity:]


def pick_rows(capacity, place, gathered):
    blocks, _, rows = place.shape
    half = gathered[0].shape[1]
    shape = jax.ShapeDtypeStruct((blocks * capacity, 2 * half), jnp.bfloat16)
    return pl.pallas_call(
        functools.partial(pick_kernel, capacity),
        out_shape=(shape, shape),
        compiler_params=pltpu.CompilerParams(vmem_limit_bytes=20 * 2**20),
        cost_estimate=pl.CostEstimate(
            flops=8 * blocks * capacity * rows * half,
            bytes_accessed=4 * blocks * (rows + 2 * capacity) * half,
            transcendentals=0,
        ),
    )(place, *gathered)


def combine_kernel(place_ref, gate_ref, own_ref, other_ref, *out_refs):
    blocks, _, rows = place_ref.shape
    capacity = own_ref.shape[0] // blocks
    half = own_ref.shape[1] // 2
    slot = lax.broadcasted_iota(jnp.int32, (capacity, rows), 0)
    for block in range(blocks):
        weight = jnp.concatenate(
            [
                jnp.where(
                    place_ref[block, pl.ds(core, 1), :] == slot,
                    gate_ref[block, pl.ds(core, 1), :],
                    0.0,
                )
                for core in range(2)
            ],
            axis=0,
        )
        weight = weight.T.astype(jnp.bfloat16)
        far_x, far_y = block // 2, block % 2
        for side in range(2):
            inner = pl.ds(block * capacity, capacity), pl.ds(side * half, half)
            both = jnp.concatenate([own_ref[inner], other_ref[inner]], axis=0)
            share = jnp.dot(weight, both, preferred_element_type=jnp.float32).astype(jnp.bfloat16)
            sent, place = (far_x, far_y) if side else (far_y, far_x)
            if sent:
                out_refs[3 * side + 2][pl.ds(place * rows, rows), :] = share
            else:
                out_refs[3 * side + place][...] = share


def combine_rows(part, parts, place, gate, own, other):
    blocks, _, rows = place.shape
    half = own.shape[1] // 2
    kept = jax.ShapeDtypeStruct((rows, half), jnp.bfloat16)
    sent = jax.ShapeDtypeStruct((2 * rows, half), jnp.bfloat16)
    count = own.shape[0] // parts
    whole = lambda shape: pl.BlockSpec(shape, lambda j: (0,) * len(shape))
    level = pl.BlockSpec((count, 2 * half), lambda j: (part, 0))
    return pl.pallas_call(
        combine_kernel,
        out_shape=[kept, kept, sent] * 2,
        grid=(1,),
        in_specs=[whole(place.shape), whole(gate.shape), level, level],
        out_specs=[whole(kept.shape), whole(kept.shape), whole(sent.shape)] * 2,
        compiler_params=pltpu.CompilerParams(vmem_limit_bytes=16 * 2**20),
        cost_estimate=pl.CostEstimate(
            flops=8 * count * rows * half,
            bytes_accessed=4 * (blocks * rows + 2 * count) * half,
            transcendentals=0,
        ),
    )(place, gate, own, other)


def routing_start(own_live, expert_ids, gate_values, earlier):
    live_ids = jnp.where(own_live[:, None], expert_ids, -1).astype(jnp.float32)
    routing = after(jnp.concatenate([live_ids, gate_values], axis=1).T, earlier)
    groups = lax.axis_size("grp")
    lines = [routing]
    for hop in range(2, groups, 2):
        lines.append(
            lax.ppermute(routing, "grp", [(g, (g + hop) % groups) for g in range(groups)])
        )
    return jnp.stack(lines)


def routing_pair(routing, swap):
    return jnp.stack([routing, swap(routing)], axis=routing.ndim - 2)


def selections(routing, top_count):
    mine = lax.axis_index(("grp", "sp"))
    depth, rows = routing.shape[0], routing.shape[-1]
    routing = routing.reshape(-1, 2 * top_count, rows)
    ids, gates = routing[:, :top_count].astype(jnp.int32), routing[:, top_count:]
    experts = jnp.stack([mine, mine ^ 1])
    chosen = ids[:, None] == experts[None, :, None, None]
    wanted = jnp.any(chosen, axis=2)
    gate = jnp.sum(jnp.where(chosen, gates[:, None], 0.0), axis=2)
    order = jnp.arange(rows)
    earlier = (order[:, None] < order[None, :]).astype(jnp.bfloat16)
    place = jnp.einsum(
        "bcr,rt->bct", wanted.astype(jnp.bfloat16), earlier, preferred_element_type=jnp.float32
    ).astype(jnp.int32)
    return jnp.where(wanted, place, -1), gate


def expert_kernel(rows_ref, up_gate_ref, down_ref, out_ref, hidden):
    hidden_width, width = down_ref.shape[1], down_ref.shape[2]
    tile = 256
    for start in range(0, hidden_width, tile):
        gate = jnp.dot(
            rows_ref[...],
            up_gate_ref[0, :, start : start + tile],
            preferred_element_type=jnp.float32,
        )
        up = jnp.dot(
            rows_ref[...],
            up_gate_ref[0, :, hidden_width + start : hidden_width + start + tile],
            preferred_element_type=jnp.float32,
        )
        hidden[:, start : start + tile] = (gate / (1.0 + jnp.exp(-gate)) * up).astype(
            jnp.bfloat16
        )
    for start in range(0, width, tile):
        out_ref[:, start : start + tile] = jnp.dot(
            hidden[...], down_ref[0, :, start : start + tile], preferred_element_type=jnp.float32
        ).astype(jnp.bfloat16)


def run_expert(rows, up_gate_weight, down_weight):
    count, width = rows.shape
    hidden_width = down_weight.shape[1]
    return pl.pallas_call(
        expert_kernel,
        out_shape=jax.ShapeDtypeStruct((count, width), jnp.bfloat16),
        scratch_shapes=[pltpu.VMEM((count, hidden_width), jnp.bfloat16)],
        compiler_params=pltpu.CompilerParams(vmem_limit_bytes=20 * 2**20),
        cost_estimate=pl.CostEstimate(
            flops=6 * count * width * hidden_width,
            bytes_accessed=6 * width * hidden_width + 4 * count * width,
            transcendentals=count * hidden_width,
        ),
    )(rows, up_gate_weight, down_weight)


def experts_by_gather(packed, routing, top_count, capacity, up_gate_weight, down_weight):
    depth = lax.axis_size("grp") // 2
    rows = packed.shape[0] // 2
    routing = routing_pair(after(routing, packed), swap_x)
    lines, beside_x, beside_y, diagonal = [packed], [], [], []
    halves = []

    def cross(level, earlier):
        first_x, second_y = halves[level]
        if earlier is not None:
            first_x, second_y = after(first_x, *earlier), after(second_y, *earlier)
        diagonal.append((swap_y(first_x), swap_x(second_y)))

    for level in range(depth):
        line = lines[level]
        if level == 1:
            line = after(line, routing)
            routing = routing_pair(after(routing, *halves[0]), swap_y)
        if level == 2:
            cross(0, (line, routing))
            cross(1, (line,))
            line = after(line, *diagonal[0], *diagonal[1])
        elif level > 2:
            line = after(line, beside_x[level - 1], beside_y[level - 1])
        beside_x.append(swap_x(line))
        beside_y.append(swap_y(line))
        halves.append((beside_x[level][:rows], beside_y[level][rows:]))
        if level + 1 < depth:
            line = lines[level]
            if level:
                line = after(line, beside_x[level - 1], beside_y[level - 1])
            lines.append(shift_z(line))
    for level in range(len(diagonal), depth):
        cross(level, None)
    if depth == 1:
        routing = routing_pair(routing, swap_y)
    place, gate = selections(routing, top_count)
    per_level = place.shape[0] // depth
    results, kept, sent, back, joined = {}, {}, {}, {}, {}

    def combine(level, *earlier):
        index, count, own_result, other_result = results[level]
        if earlier:
            own_result = after(own_result, *earlier)
        blocks = slice(level * per_level, (level + 1) * per_level)
        parts = combine_rows(index, count, place[blocks], gate[blocks], own_result, other_result)
        first, first_x, first_sent, second, second_y, second_sent = parts
        kept[level] = first, first_x, second, second_y
        sent[level] = first_sent, second_sent

    def send_back(level, *earlier):
        first_sent, second_sent = sent[level]
        if earlier:
            first_sent, second_sent = after(first_sent, *earlier), after(second_sent, *earlier)
        back[level] = swap_y(first_sent), swap_x(second_sent)

    def join(level):
        first, first_x, second, second_y = kept[level]
        first_back, second_back = back[level]
        first, first_x = first + first_back[:rows], first_x + first_back[rows:]
        second, second_y = second + second_back[:rows], second_y + second_back[rows:]
        joined[level] = first, second, swap_x(first_x), swap_y(second_y)

    for start in range(0, depth, 2):
        levels = range(start, min(start + 2, depth))
        gathered = []
        for level in levels:
            gathered += [lines[level], beside_y[level], beside_x[level], *diagonal[level]]
        ahead, last = levels[-1] + 1, levels[-1] + 2
        if start:
            gathered[0] = after(gathered[0], kept[start - 1][0])
        blocks = slice(start * per_level, (start + len(levels)) * per_level)
        own, sibling = pick_rows(capacity, place[blocks], gathered)
        if last < depth:
            sibling = after(sibling, beside_x[ahead], beside_y[ahead], lines[last])
        other = swap_core(sibling)
        other_result = run_expert(other, up_gate_weight, down_weight)
        if last < depth:
            other_result = after(
                other_result, beside_x[last], beside_y[last], *diagonal[ahead]
            )
            own = after(own, other_result)
        if start:
            back[start - 1] = tuple(after(part, other_result) for part in back[start - 1])
            join(start - 1)
            own = after(own, *back[start - 1])
        own_result = run_expert(own, up_gate_weight, down_weight)
        other_result = swap_core(other_result)
        if start:
            own_result = after(own_result, *joined[start - 1])
        for index, level in enumerate(levels):
            results[level] = index, len(levels), own_result, other_result
            if level:
                combine(level)
                send_back(level, *back.get(level - 1, ()))
        for level in levels:
            if level and (ahead >= depth or level < levels[-1]):
                join(level)
    combine(0, *(kept[depth - 1][:1] if depth > 1 else ()))
    send_back(0, *back.get(depth - 1, ()))
    join(0)
    shares = {}
    for level in range(depth):
        first, second, first_far, second_far = joined[level]
        shares[level] = first + first_far, second + second_far
    first, second = shares[0]
    if depth > 1:
        total = jnp.concatenate(shares[1], axis=0)
        for level in range(2, depth):
            total = jnp.concatenate(shares[level], axis=0) + shift_z(total)
        total = shift_z(total)
        first, second = first + total[:rows], second + total[rows:]
    return jnp.concatenate([first, second], axis=1)


def per_device_pairs(
    queries,
    fresh_key_values,
    cache,
    lengths,
    out_weight,
    residual,
    norm_gain,
    expert_ids,
    gate_values,
    up_gate_weight,
    down_weight,
):
    seq_devices = lax.axis_size("sp")
    mine = lax.axis_index("sp")
    slot_rows = queries.shape[0]
    width = cache.shape[-1] // 2
    head_columns = queries.shape[1] // seq_devices
    top_count = expert_ids.shape[1]
    experts = up_gate_weight.shape[0] * lax.axis_size("grp") * seq_devices
    capacity = max(2, 8 * slot_rows * top_count // (5 * experts))
    own_length = lengths[0, 0]
    own_live = jnp.arange(slot_rows, dtype=jnp.int32) < own_length

    def key_values_for(target):
        keys = lax.dynamic_slice(fresh_key_values, (0, target * width), (slot_rows, width))
        values = lax.dynamic_slice(
            fresh_key_values, (0, (seq_devices + target) * width), (slot_rows, width)
        )
        lane = jnp.arange(2 * width, dtype=jnp.int32)[None, :]
        note = jnp.where(lane < width, own_length // 256, own_length % 256)
        note = jnp.broadcast_to(note, (16, 2 * width)).astype(jnp.bfloat16)
        return jnp.concatenate([jnp.concatenate([keys, values], axis=1), note], axis=0)

    def queries_for(target):
        return lax.dynamic_slice(queries, (0, target * head_columns), (slot_rows, head_columns))

    masks = range(1, seq_devices)
    fresh = [key_values_for(mine)] + [xor_group(key_values_for(mine ^ m), m) for m in masks]
    query_blocks = [queries_for(mine)] + [xor_group(queries_for(mine ^ m), m) for m in masks]
    cache_block = cache[0, 0]

    def share_of(block, query):
        heads = attend_block(block, mine[None], query, cache_block, fresh)
        return jnp.dot(heads, out_weight, preferred_element_type=jnp.float32).astype(jnp.bfloat16)

    own = share_of(0, query_blocks[0])
    far_core = share_of(3, after(query_blocks[3], query_blocks[2], own))
    far = share_of(2, query_blocks[2]) + swap_core(far_core)
    near = share_of(1, after(query_blocks[1], far))
    routing = routing_start(own_live, expert_ids, gate_values, far)
    far = swap_y(far)
    attended, packed = normalize(
        lengths[0], own, swap_core(after(near, far, routing)), far, residual, norm_gain[None, :]
    )
    moe_out = experts_by_gather(
        packed, routing, top_count, capacity, up_gate_weight, down_weight
    )
    return (attended, moe_out)


def per_device(
    queries,
    fresh_key_values,
    cache,
    lengths,
    out_weight,
    residual,
    norm_gain,
    expert_ids,
    gate_values,
    up_gate_weight,
    down_weight,
):
    seq_devices = lax.axis_size("sp")
    slot_rows = queries.shape[0]
    head_width = cache.shape[-1] // 2
    model_width = residual.shape[1]
    kv_heads = fresh_key_values.shape[1] // (2 * head_width)
    repeat = seq_devices // kv_heads
    keys_new = fresh_key_values[:, : kv_heads * head_width].reshape(
        slot_rows, kv_heads, 1, head_width
    )
    values_new = fresh_key_values[:, kv_heads * head_width :].reshape(
        slot_rows, kv_heads, 1, head_width
    )
    paired = jnp.concatenate([keys_new, values_new], axis=3)
    spread = jnp.broadcast_to(paired, (slot_rows, kv_heads, repeat, 2 * head_width)).reshape(
        slot_rows, seq_devices * 2 * head_width
    )
    all_lengths = lax.all_gather(lengths, "sp", axis=1, tiled=True)
    queries_by_head, head_kv = (
        lax.all_to_all(queries, "sp", split_axis=1, concat_axis=0, tiled=True),
        lax.all_to_all(spread, "sp", split_axis=1, concat_axis=0, tiled=True),
    )
    cache_block = cache[0, 0]
    my_index = lax.axis_index("sp")
    for bit_pos in range(repeat.bit_length() - 1):
        partner = partner_2(cache_block, "sp", bit_pos)
        is_upper = my_index // 2**bit_pos % 2 == 1
        cache_block = jnp.where(
            is_upper,
            jnp.concatenate([partner, cache_block], axis=0),
            jnp.concatenate([cache_block, partner], axis=0),
        )
    stretch_lens = all_lengths[0]
    offsets = jnp.cumsum(stretch_lens) - stretch_lens
    rows_of_group = queries_by_head.shape[0]
    slot_ids = jnp.arange(rows_of_group, dtype=jnp.int32)
    source = slot_ids // slot_rows
    within = slot_ids % slot_rows
    from_device = source[:, None] == jnp.arange(seq_devices, dtype=jnp.int32)[None, :]
    is_live = within < jnp.sum(jnp.where(from_device, stretch_lens[None, :], 0), axis=1)
    position = within + jnp.sum(jnp.where(from_device, offsets[None, :], 0), axis=1)
    per_dev = queries_by_head.shape[1] // head_width
    cache_len = cache_block.shape[0]
    key_all = jnp.concatenate([cache_block[:, :head_width], head_kv[:, :head_width]], axis=0)
    value_all = jnp.concatenate([cache_block[:, head_width:], head_kv[:, head_width:]], axis=0)
    block_count = 2 if rows_of_group % 2 == 0 and rows_of_group >= 1024 else 1
    block_rows = rows_of_group // block_count

    def attend(parts):
        query_block, place_block = parts
        scores = jnp.einsum(
            "rhd,kd->hrk", query_block, key_all, preferred_element_type=jnp.float32
        ) / math.sqrt(head_width)
        allowed = jnp.concatenate(
            [
                jnp.ones((block_rows, cache_len), dtype=bool),
                is_live[None, :] & (position[None, :] <= place_block[:, None]),
            ],
            axis=1,
        )
        scores = jnp.where(allowed[None], scores, -jnp.inf)
        row_max = jnp.max(scores, axis=-1, keepdims=True)
        weights = jnp.exp(scores - row_max)
        totals = jnp.sum(weights, axis=-1, keepdims=True)
        result = (
            jnp.einsum(
                "hrk,kd->hrd",
                weights.astype(jnp.bfloat16),
                value_all,
                preferred_element_type=jnp.float32,
            )
            / totals
        )
        return (
            result.astype(jnp.bfloat16).transpose(1, 0, 2).reshape(block_rows, per_dev * head_width)
        )

    attn_heads = lax.map(
        attend,
        (
            queries_by_head.reshape(block_count, block_rows, per_dev, head_width),
            position.reshape(block_count, block_rows),
        ),
    ).reshape(rows_of_group, per_dev * head_width)
    attn_sum = lax.psum_scatter(
        jnp.dot(attn_heads, out_weight, preferred_element_type=jnp.float32).astype(jnp.bfloat16),
        "sp",
        scatter_dimension=0,
        tiled=True,
    ).astype(jnp.float32)
    own_live = jnp.arange(slot_rows, dtype=jnp.int32) < lengths[0, 0]
    attended = jnp.where(own_live[:, None], attn_sum, 0.0).astype(jnp.bfloat16)
    mixed_rows = residual.astype(jnp.float32) + attn_sum
    normed = (
        mixed_rows
        * lax.rsqrt(jnp.mean(mixed_rows * mixed_rows, axis=-1, keepdims=True) + 1e-06)
        * norm_gain
    ).astype(jnp.bfloat16)
    group_count = lax.axis_size("grp")
    experts = up_gate_weight.shape[0] * group_count * seq_devices
    top_count = expert_ids.shape[1]
    capacity = max(2, 8 * slot_rows * top_count // (5 * experts))
    hidden_width = down_weight.shape[1]
    choose = expert_ids[:, :, None] == jnp.arange(experts, dtype=jnp.int32)[None, None, :]
    routed = (jnp.any(choose, axis=1) & own_live[:, None]).astype(jnp.float32)
    earlier = (jnp.arange(slot_rows)[:, None] > jnp.arange(slot_rows)[None, :]).astype(jnp.float32)
    prefix = jnp.dot(earlier, routed, precision=lax.Precision.HIGHEST)
    slot_in = jnp.sum(jnp.where(choose, prefix[:, None, :], 0.0), axis=2).astype(jnp.int32)
    dump_slot = experts * capacity
    target = jnp.where(own_live[:, None], expert_ids * capacity + slot_in, dump_slot)
    source_rows = (
        jnp.full((dump_slot + 1,), slot_rows, jnp.int32)
        .at[target.reshape(-1)]
        .set(jnp.repeat(jnp.arange(slot_rows, dtype=jnp.int32), top_count))[:dump_slot]
    )
    padded = jnp.concatenate([normed, jnp.zeros((1, model_width), jnp.bfloat16)], axis=0)
    outgoing = padded[source_rows].reshape(experts, capacity, model_width)
    received = lax.all_to_all(outgoing, ("grp", "sp"), split_axis=0, concat_axis=0, tiled=True)
    flat_rows = received.reshape(-1, model_width)
    projected = jnp.dot(flat_rows, up_gate_weight[0], preferred_element_type=jnp.float32)
    hidden = (jax.nn.silu(projected[:, :hidden_width]) * projected[:, hidden_width:]).astype(
        jnp.bfloat16
    )
    returned = lax.all_to_all(
        jnp.dot(hidden, down_weight[0], preferred_element_type=jnp.float32)
        .astype(jnp.bfloat16)
        .reshape(received.shape),
        ("grp", "sp"),
        split_axis=0,
        concat_axis=0,
        tiled=True,
    )
    back_rows = jnp.concatenate(
        [returned.reshape(dump_slot, model_width), jnp.zeros((1, model_width), jnp.bfloat16)],
        axis=0,
    )
    picked = back_rows[target]
    combined = jnp.sum(gate_values[:, :, None] * picked.astype(jnp.float32), axis=1)
    moe_out = jnp.where(own_live[:, None], combined, 0.0).astype(jnp.bfloat16)
    return (attended, moe_out)


def solution(mesh):
    in_specs = (
        P(("grp", "sp"), None),
        P(("grp", "sp"), None),
        P("grp", "sp", None, None),
        P("grp", "sp"),
        P("sp", None),
        P(("grp", "sp"), None),
        P(),
        P(("grp", "sp"), None),
        P(("grp", "sp"), None),
        P(("grp", "sp"), None, None),
        P(("grp", "sp"), None, None),
    )
    out_specs = (P(("grp", "sp"), None), P(("grp", "sp"), None))
    groups, seq_devices = mesh.shape["grp"], mesh.shape["sp"]

    def run(*args):
        kv_heads = args[1].shape[1] // args[2].shape[-1]
        experts, top_count = args[9].shape[0], args[7].shape[1]
        pairs = seq_devices == kv_heads == 4 and groups % 2 == 0 and experts <= 4 * top_count
        return mapped(per_device_pairs if pairs else per_device)(*args)

    def mapped(body):
        return jax.shard_map(
            body, mesh=mesh, in_specs=in_specs, out_specs=out_specs, check_vma=False
        )

    return run
```

```python
import functools
import math

import jax
import jax.numpy as jnp
from jax import lax
from jax.experimental import pallas as pl
from jax.experimental.pallas import tpu as pltpu
from jax.sharding import PartitionSpec as P


def partner_2(value, axis, bit):
    mask = 2**bit
    pairs = [(source, source ^ mask) for source in range(lax.axis_size(axis))]
    return lax.ppermute(value, axis, pairs)


def shift_z(value):
    groups = lax.axis_size("grp")
    return lax.ppermute(value, "grp", [(g, (g + 2) % groups) for g in range(groups)])


def swap_x(value):
    return partner_2(value, "grp", 0)


def swap_y(value):
    return partner_2(value, "sp", 1)


def swap_core(value):
    return partner_2(value, "sp", 0)


def after(value, *earlier):
    return lax.optimization_barrier((value, *earlier))[0]


def xor_group(value, mask):
    return lax.ppermute(value, "sp", [(s, s ^ mask) for s in range(lax.axis_size("sp"))])


def attend_kernel(index, mine_ref, query_ref, cache_ref, *refs):
    fresh_refs, (out_ref, keys, values, bias) = refs[:-4], refs[-4:]
    rows = query_ref.shape[0]
    cached, width = cache_ref.shape[0], cache_ref.shape[1] // 2
    keys[:cached, :] = cache_ref[:, :width]
    values[:cached, :] = cache_ref[:, width:]
    lengths = []
    for block, fresh_ref in enumerate(fresh_refs):
        places = pl.ds(cached + block * rows, rows)
        keys[places, :] = fresh_ref[:rows, :width]
        values[places, :] = fresh_ref[:rows, width:]
        note = fresh_ref[rows : rows + 16, :].astype(jnp.float32)
        lengths.append(note[:1, :1] * 256.0 + note[:1, width : width + 1])
    mine = mine_ref[0]
    offsets = []
    for block in range(len(fresh_refs)):
        offset = jnp.zeros((1, 1), jnp.float32)
        for other in range(len(fresh_refs)):
            before = (mine ^ other) < (mine ^ block)
            offset = offset + lengths[other] * before.astype(jnp.float32)
        offsets.append(offset)
    column = lax.broadcasted_iota(jnp.int32, (1, bias.shape[1]), 1)
    key_place = jnp.zeros((1, bias.shape[1]), jnp.float32)
    for block in range(len(fresh_refs)):
        within = (column - block * rows).astype(jnp.float32)
        place = jnp.where(within < lengths[block], within + offsets[block], 1e9)
        key_place = jnp.where(column >= block * rows, place, key_place)
    row_place = lax.broadcasted_iota(jnp.int32, bias.shape, 0).astype(jnp.float32) + offsets[index]
    bias[...] = jnp.where(key_place <= row_place, 0.0, -1e30)
    scale = math.log2(math.e) / math.sqrt(width)
    for head in range(query_ref.shape[1] // width):
        columns = pl.ds(head * width, width)
        scores = lax.dot_general(
            query_ref[:, columns],
            keys[...],
            (((1,), (1,)), ((), ())),
            preferred_element_type=jnp.float32,
        )
        old, new = scores[:, :cached] * scale, scores[:, cached:] * scale + bias[...]
        row_max = jnp.maximum(
            jnp.max(old, axis=1, keepdims=True), jnp.max(new, axis=1, keepdims=True)
        )
        old, new = jnp.exp2(old - row_max), jnp.exp2(new - row_max)
        totals = jnp.sum(old, axis=1, keepdims=True) + jnp.sum(new, axis=1, keepdims=True)
        result = jnp.dot(
            old.astype(jnp.bfloat16), values[:cached, :], preferred_element_type=jnp.float32
        ) + jnp.dot(
            new.astype(jnp.bfloat16), values[cached:, :], preferred_element_type=jnp.float32
        )
        out_ref[:, columns] = (result / totals).astype(jnp.bfloat16)


def attend_block(index, mine, query, cache_block, fresh):
    rows, columns = query.shape
    cached, width = cache_block.shape[0], cache_block.shape[1] // 2
    new = rows * len(fresh)
    inside = pl.BlockSpec(memory_space=pltpu.VMEM)
    return pl.pallas_call(
        functools.partial(attend_kernel, index),
        out_shape=jax.ShapeDtypeStruct((rows, columns), jnp.bfloat16),
        in_specs=[pl.BlockSpec(memory_space=pltpu.SMEM)] + [inside] * (2 + len(fresh)),
        out_specs=inside,
        scratch_shapes=[
            pltpu.VMEM((cached + new, width), jnp.bfloat16),
            pltpu.VMEM((cached + new, width), jnp.bfloat16),
            pltpu.VMEM((rows, new), jnp.float32),
        ],
        compiler_params=pltpu.CompilerParams(vmem_limit_bytes=12 * 2**20),
        cost_estimate=pl.CostEstimate(
            flops=4 * rows * columns * (cached + new),
            bytes_accessed=4 * (rows * columns + (cached + new) * width),
            transcendentals=rows * columns // width * (cached + new),
        ),
    )(mine, query, cache_block, *fresh)


def norm_kernel(
    length_ref,
    own_ref,
    core_ref,
    far_ref,
    residual_ref,
    gain_ref,
    attended_ref,
    packed_ref,
):
    attn_sum = (
        own_ref[...].astype(jnp.float32)
        + core_ref[...].astype(jnp.float32)
        + far_ref[...].astype(jnp.float32)
    )
    live = lax.broadcasted_iota(jnp.int32, attn_sum.shape, 0) < length_ref[0]
    attended_ref[...] = jnp.where(live, attn_sum, 0.0).astype(jnp.bfloat16)
    mixed = residual_ref[...].astype(jnp.float32) + attn_sum
    scale = lax.rsqrt(jnp.mean(mixed * mixed, axis=1, keepdims=True) + 1e-06)
    normed = (mixed * scale * gain_ref[...]).astype(jnp.bfloat16)
    rows, half = packed_ref.shape[0] // 2, packed_ref.shape[1]
    packed_ref[:rows, :] = normed[:, :half]
    packed_ref[rows:, :] = normed[:, half:]


def normalize(length, own, core, far, residual, gain):
    rows, width = own.shape
    packed = jax.ShapeDtypeStruct((2 * rows, width // 2), jnp.bfloat16)
    inside = pl.BlockSpec(memory_space=pltpu.VMEM)
    return pl.pallas_call(
        norm_kernel,
        out_shape=(jax.ShapeDtypeStruct((rows, width), jnp.bfloat16), packed),
        in_specs=[pl.BlockSpec(memory_space=pltpu.SMEM)] + [inside] * 5,
        out_specs=(inside, inside),
        compiler_params=pltpu.CompilerParams(vmem_limit_bytes=12 * 2**20),
        cost_estimate=pl.CostEstimate(
            flops=10 * rows * width, bytes_accessed=12 * rows * width, transcendentals=rows
        ),
    )(length, own, core, far, residual, gain)


def pick_kernel(capacity, place_ref, *refs):
    blocks, _, rows = place_ref.shape
    own_ref, sibling_ref = refs[-2:]
    half = own_ref.shape[1] // 2
    slot = lax.broadcasted_iota(jnp.int32, (capacity, rows), 0)
    for block in range(blocks):
        pick = jnp.concatenate(
            [(place_ref[block, pl.ds(core, 1), :] == slot) for core in range(2)], axis=0
        )
        pick = jnp.where(pick, 1.0, 0.0).astype(jnp.bfloat16)
        level, spot = block // 4, block % 4
        for side in range(2):
            if spot < 3:
                source = refs[5 * level + spot][pl.ds(side * rows, rows), :]
            else:
                source = refs[5 * level + 3 + side][...]
            chosen = jnp.dot(pick, source, preferred_element_type=jnp.float32)
            chosen = chosen.astype(jnp.bfloat16)
            inner = pl.ds(block * capacity, capacity), pl.ds(side * half, half)
            own_ref[inner] = chosen[:capacity]
            sibling_ref[inner] = chosen[capacity:]


def pick_rows(capacity, place, gathered):
    blocks, _, rows = place.shape
    half = gathered[0].shape[1]
    shape = jax.ShapeDtypeStruct((blocks * capacity, 2 * half), jnp.bfloat16)
    return pl.pallas_call(
        functools.partial(pick_kernel, capacity),
        out_shape=(shape, shape),
        compiler_params=pltpu.CompilerParams(vmem_limit_bytes=20 * 2**20),
        cost_estimate=pl.CostEstimate(
            flops=8 * blocks * capacity * rows * half,
            bytes_accessed=4 * blocks * (rows + 2 * capacity) * half,
            transcendentals=0,
        ),
    )(place, *gathered)


def combine_kernel(place_ref, gate_ref, own_ref, other_ref, *out_refs):
    blocks, _, rows = place_ref.shape
    capacity = own_ref.shape[0] // blocks
    half = own_ref.shape[1] // 2
    slot = lax.broadcasted_iota(jnp.int32, (capacity, rows), 0)
    for block in range(blocks):
        weight = jnp.concatenate(
            [
                jnp.where(
                    place_ref[block, pl.ds(core, 1), :] == slot,
                    gate_ref[block, pl.ds(core, 1), :],
                    0.0,
                )
                for core in range(2)
            ],
            axis=0,
        )
        weight = weight.T.astype(jnp.bfloat16)
        far_x, far_y = block // 2, block % 2
        for side in range(2):
            inner = pl.ds(block * capacity, capacity), pl.ds(side * half, half)
            both = jnp.concatenate([own_ref[inner], other_ref[inner]], axis=0)
            share = jnp.dot(weight, both, preferred_element_type=jnp.float32).astype(jnp.bfloat16)
            sent, place = (far_x, far_y) if side else (far_y, far_x)
            if sent:
                out_refs[3 * side + 2][pl.ds(place * rows, rows), :] = share
            else:
                out_refs[3 * side + place][...] = share


def combine_rows(part, parts, place, gate, own, other):
    blocks, _, rows = place.shape
    half = own.shape[1] // 2
    kept = jax.ShapeDtypeStruct((rows, half), jnp.bfloat16)
    sent = jax.ShapeDtypeStruct((2 * rows, half), jnp.bfloat16)
    count = own.shape[0] // parts
    whole = lambda shape: pl.BlockSpec(shape, lambda j: (0,) * len(shape))
    level = pl.BlockSpec((count, 2 * half), lambda j: (part, 0))
    return pl.pallas_call(
        combine_kernel,
        out_shape=[kept, kept, sent] * 2,
        grid=(1,),
        in_specs=[whole(place.shape), whole(gate.shape), level, level],
        out_specs=[whole(kept.shape), whole(kept.shape), whole(sent.shape)] * 2,
        compiler_params=pltpu.CompilerParams(vmem_limit_bytes=16 * 2**20),
        cost_estimate=pl.CostEstimate(
            flops=8 * count * rows * half,
            bytes_accessed=4 * (blocks * rows + 2 * count) * half,
            transcendentals=0,
        ),
    )(place, gate, own, other)


def routing_start(own_live, expert_ids, gate_values, earlier):
    live_ids = jnp.where(own_live[:, None], expert_ids, -1).astype(jnp.float32)
    routing = after(jnp.concatenate([live_ids, gate_values], axis=1).T, earlier)
    groups = lax.axis_size("grp")
    lines = [routing]
    for hop in range(2, groups, 2):
        lines.append(
            lax.ppermute(routing, "grp", [(g, (g + hop) % groups) for g in range(groups)])
        )
    return jnp.stack(lines)


def routing_pair(routing, swap):
    return jnp.stack([routing, swap(routing)], axis=routing.ndim - 2)


def selections(routing, top_count):
    mine = lax.axis_index(("grp", "sp"))
    depth, rows = routing.shape[0], routing.shape[-1]
    routing = routing.reshape(-1, 2 * top_count, rows)
    ids, gates = routing[:, :top_count].astype(jnp.int32), routing[:, top_count:]
    experts = jnp.stack([mine, mine ^ 1])
    chosen = ids[:, None] == experts[None, :, None, None]
    wanted = jnp.any(chosen, axis=2)
    gate = jnp.sum(jnp.where(chosen, gates[:, None], 0.0), axis=2)
    order = jnp.arange(rows)
    earlier = (order[:, None] < order[None, :]).astype(jnp.bfloat16)
    place = jnp.einsum(
        "bcr,rt->bct", wanted.astype(jnp.bfloat16), earlier, preferred_element_type=jnp.float32
    ).astype(jnp.int32)
    return jnp.where(wanted, place, -1), gate


def expert_kernel(rows_ref, up_gate_ref, down_ref, out_ref, hidden):
    hidden_width, width = down_ref.shape[1], down_ref.shape[2]
    tile = 256
    for start in range(0, hidden_width, tile):
        gate = jnp.dot(
            rows_ref[...],
            up_gate_ref[0, :, start : start + tile],
            preferred_element_type=jnp.float32,
        )
        up = jnp.dot(
            rows_ref[...],
            up_gate_ref[0, :, hidden_width + start : hidden_width + start + tile],
            preferred_element_type=jnp.float32,
        )
        hidden[:, start : start + tile] = (gate / (1.0 + jnp.exp(-gate)) * up).astype(
            jnp.bfloat16
        )
    for start in range(0, width, tile):
        out_ref[:, start : start + tile] = jnp.dot(
            hidden[...], down_ref[0, :, start : start + tile], preferred_element_type=jnp.float32
        ).astype(jnp.bfloat16)


def run_expert(rows, up_gate_weight, down_weight):
    count, width = rows.shape
    hidden_width = down_weight.shape[1]
    return pl.pallas_call(
        expert_kernel,
        out_shape=jax.ShapeDtypeStruct((count, width), jnp.bfloat16),
        scratch_shapes=[pltpu.VMEM((count, hidden_width), jnp.bfloat16)],
        compiler_params=pltpu.CompilerParams(vmem_limit_bytes=20 * 2**20),
        cost_estimate=pl.CostEstimate(
            flops=6 * count * width * hidden_width,
            bytes_accessed=6 * width * hidden_width + 4 * count * width,
            transcendentals=count * hidden_width,
        ),
    )(rows, up_gate_weight, down_weight)


def experts_by_gather(packed, routing, top_count, capacity, up_gate_weight, down_weight):
    depth = lax.axis_size("grp") // 2
    rows = packed.shape[0] // 2
    routing = routing_pair(after(routing, packed), swap_x)
    lines, beside_x, beside_y, diagonal = [packed], [], [], []
    halves = []

    def cross(level, earlier):
        first_x, second_y = halves[level]
        if earlier is not None:
            first_x, second_y = after(first_x, *earlier), after(second_y, *earlier)
        diagonal.append((swap_y(first_x), swap_x(second_y)))

    for level in range(depth):
        line = lines[level]
        if level == 2:
            cross(0, (line, routing))
            cross(1, (line,))
            routing = routing_pair(routing, swap_y)
            line = after(line, *diagonal[0])
        elif level > 2:
            line = after(line, beside_x[level - 1], beside_y[level - 1])
        beside_x.append(swap_x(line))
        beside_y.append(swap_y(line))
        halves.append((beside_x[level][:rows], beside_y[level][rows:]))
        if level + 1 < depth:
            line = lines[level]
            if level:
                line = after(line, beside_x[level - 1], beside_y[level - 1])
            lines.append(shift_z(line))
    for level in range(len(diagonal), depth):
        cross(level, None)
    if depth <= 2:
        routing = routing_pair(routing, swap_y)
    place, gate = selections(routing, top_count)
    per_level = place.shape[0] // depth
    results, kept, sent, back, joined = {}, {}, {}, {}, {}

    def combine(level, *earlier):
        index, count, own_result, other_result = results[level]
        if earlier:
            own_result = after(own_result, *earlier)
        blocks = slice(level * per_level, (level + 1) * per_level)
        parts = combine_rows(index, count, place[blocks], gate[blocks], own_result, other_result)
        first, first_x, first_sent, second, second_y, second_sent = parts
        kept[level] = first, first_x, second, second_y
        sent[level] = first_sent, second_sent

    def send_back(level, *earlier):
        first_sent, second_sent = sent[level]
        if earlier:
            first_sent, second_sent = after(first_sent, *earlier), after(second_sent, *earlier)
        back[level] = swap_y(first_sent), swap_x(second_sent)

    def join(level):
        first, first_x, second, second_y = kept[level]
        first_back, second_back = back[level]
        first, first_x = first + first_back[:rows], first_x + first_back[rows:]
        second, second_y = second + second_back[:rows], second_y + second_back[rows:]
        joined[level] = first, second, swap_x(first_x), swap_y(second_y)

    for start in range(0, depth, 2):
        levels = range(start, min(start + 2, depth))
        gathered = []
        for level in levels:
            gathered += [lines[level], beside_y[level], beside_x[level], *diagonal[level]]
        ahead, last = levels[-1] + 1, levels[-1] + 2
        if start:
            gathered[0] = after(gathered[0], kept[start - 1][0])
        blocks = slice(start * per_level, (start + len(levels)) * per_level)
        own, sibling = pick_rows(capacity, place[blocks], gathered)
        if last < depth:
            sibling = after(sibling, beside_x[ahead], beside_y[ahead], lines[last])
        other = swap_core(sibling)
        other_result = run_expert(other, up_gate_weight, down_weight)
        if last < depth:
            other_result = after(
                other_result, beside_x[last], beside_y[last], *diagonal[ahead]
            )
            own = after(own, other_result)
        if start:
            back[start - 1] = tuple(after(part, other_result) for part in back[start - 1])
            join(start - 1)
            own = after(own, *back[start - 1])
        own_result = run_expert(own, up_gate_weight, down_weight)
        other_result = swap_core(other_result)
        if start:
            own_result = after(own_result, *joined[start - 1])
        for index, level in enumerate(levels):
            results[level] = index, len(levels), own_result, other_result
            if level:
                combine(level)
                send_back(level, *back.get(level - 1, ()))
        for level in levels:
            if level and (ahead >= depth or level < levels[-1]):
                join(level)
    combine(0, *(kept[depth - 1][:1] if depth > 1 else ()))
    send_back(0, *back.get(depth - 1, ()))
    join(0)
    shares = {}
    for level in range(depth):
        first, second, first_far, second_far = joined[level]
        shares[level] = first + first_far, second + second_far
    first, second = shares[0]
    if depth > 1:
        total = jnp.concatenate(shares[1], axis=0)
        for level in range(2, depth):
            total = jnp.concatenate(shares[level], axis=0) + shift_z(total)
        total = shift_z(total)
        first, second = first + total[:rows], second + total[rows:]
    return jnp.concatenate([first, second], axis=1)


def per_device_pairs(
    queries,
    fresh_key_values,
    cache,
    lengths,
    out_weight,
    residual,
    norm_gain,
    expert_ids,
    gate_values,
    up_gate_weight,
    down_weight,
):
    seq_devices = lax.axis_size("sp")
    mine = lax.axis_index("sp")
    slot_rows = queries.shape[0]
    width = cache.shape[-1] // 2
    head_columns = queries.shape[1] // seq_devices
    top_count = expert_ids.shape[1]
    experts = up_gate_weight.shape[0] * lax.axis_size("grp") * seq_devices
    capacity = max(2, 8 * slot_rows * top_count // (5 * experts))
    own_length = lengths[0, 0]
    own_live = jnp.arange(slot_rows, dtype=jnp.int32) < own_length

    def key_values_for(target):
        keys = lax.dynamic_slice(fresh_key_values, (0, target * width), (slot_rows, width))
        values = lax.dynamic_slice(
            fresh_key_values, (0, (seq_devices + target) * width), (slot_rows, width)
        )
        lane = jnp.arange(2 * width, dtype=jnp.int32)[None, :]
        note = jnp.where(lane < width, own_length // 256, own_length % 256)
        note = jnp.broadcast_to(note, (16, 2 * width)).astype(jnp.bfloat16)
        return jnp.concatenate([jnp.concatenate([keys, values], axis=1), note], axis=0)

    def queries_for(target):
        return lax.dynamic_slice(queries, (0, target * head_columns), (slot_rows, head_columns))

    masks = range(1, seq_devices)
    fresh = [key_values_for(mine)] + [xor_group(key_values_for(mine ^ m), m) for m in masks]
    query_blocks = {0: queries_for(mine)}
    query_blocks[3] = xor_group(queries_for(mine ^ 3), 3)
    query_blocks[2] = xor_group(after(queries_for(mine ^ 2), query_blocks[3]), 2)
    query_blocks[1] = xor_group(queries_for(mine ^ 1), 1)
    cache_block = cache[0, 0]

    def share_of(block, query, *earlier):
        heads = attend_block(block, mine[None], query, cache_block, fresh)
        if earlier:
            heads = after(heads, *earlier)
        return jnp.dot(heads, out_weight, preferred_element_type=jnp.float32).astype(jnp.bfloat16)

    own = share_of(0, query_blocks[0])
    far_core = share_of(3, after(query_blocks[3], own), query_blocks[2])
    far = share_of(2, query_blocks[2]) + swap_core(far_core)
    near = share_of(1, after(query_blocks[1], far))
    routing = routing_start(own_live, expert_ids, gate_values, far)
    far = swap_y(far)
    attended, packed = normalize(
        lengths[0], own, swap_core(after(near, far, routing)), far, residual, norm_gain[None, :]
    )
    moe_out = experts_by_gather(
        packed, routing, top_count, capacity, up_gate_weight, down_weight
    )
    return (attended, moe_out)


def per_device(
    queries,
    fresh_key_values,
    cache,
    lengths,
    out_weight,
    residual,
    norm_gain,
    expert_ids,
    gate_values,
    up_gate_weight,
    down_weight,
):
    seq_devices = lax.axis_size("sp")
    slot_rows = queries.shape[0]
    head_width = cache.shape[-1] // 2
    model_width = residual.shape[1]
    kv_heads = fresh_key_values.shape[1] // (2 * head_width)
    repeat = seq_devices // kv_heads
    keys_new = fresh_key_values[:, : kv_heads * head_width].reshape(
        slot_rows, kv_heads, 1, head_width
    )
    values_new = fresh_key_values[:, kv_heads * head_width :].reshape(
        slot_rows, kv_heads, 1, head_width
    )
    paired = jnp.concatenate([keys_new, values_new], axis=3)
    spread = jnp.broadcast_to(paired, (slot_rows, kv_heads, repeat, 2 * head_width)).reshape(
        slot_rows, seq_devices * 2 * head_width
    )
    all_lengths = lax.all_gather(lengths, "sp", axis=1, tiled=True)
    queries_by_head, head_kv = (
        lax.all_to_all(queries, "sp", split_axis=1, concat_axis=0, tiled=True),
        lax.all_to_all(spread, "sp", split_axis=1, concat_axis=0, tiled=True),
    )
    cache_block = cache[0, 0]
    my_index = lax.axis_index("sp")
    for bit_pos in range(repeat.bit_length() - 1):
        partner = partner_2(cache_block, "sp", bit_pos)
        is_upper = my_index // 2**bit_pos % 2 == 1
        cache_block = jnp.where(
            is_upper,
            jnp.concatenate([partner, cache_block], axis=0),
            jnp.concatenate([cache_block, partner], axis=0),
        )
    stretch_lens = all_lengths[0]
    offsets = jnp.cumsum(stretch_lens) - stretch_lens
    rows_of_group = queries_by_head.shape[0]
    slot_ids = jnp.arange(rows_of_group, dtype=jnp.int32)
    source = slot_ids // slot_rows
    within = slot_ids % slot_rows
    from_device = source[:, None] == jnp.arange(seq_devices, dtype=jnp.int32)[None, :]
    is_live = within < jnp.sum(jnp.where(from_device, stretch_lens[None, :], 0), axis=1)
    position = within + jnp.sum(jnp.where(from_device, offsets[None, :], 0), axis=1)
    per_dev = queries_by_head.shape[1] // head_width
    cache_len = cache_block.shape[0]
    key_all = jnp.concatenate([cache_block[:, :head_width], head_kv[:, :head_width]], axis=0)
    value_all = jnp.concatenate([cache_block[:, head_width:], head_kv[:, head_width:]], axis=0)
    block_count = 2 if rows_of_group % 2 == 0 and rows_of_group >= 1024 else 1
    block_rows = rows_of_group // block_count

    def attend(parts):
        query_block, place_block = parts
        scores = jnp.einsum(
            "rhd,kd->hrk", query_block, key_all, preferred_element_type=jnp.float32
        ) / math.sqrt(head_width)
        allowed = jnp.concatenate(
            [
                jnp.ones((block_rows, cache_len), dtype=bool),
                is_live[None, :] & (position[None, :] <= place_block[:, None]),
            ],
            axis=1,
        )
        scores = jnp.where(allowed[None], scores, -jnp.inf)
        row_max = jnp.max(scores, axis=-1, keepdims=True)
        weights = jnp.exp(scores - row_max)
        totals = jnp.sum(weights, axis=-1, keepdims=True)
        result = (
            jnp.einsum(
                "hrk,kd->hrd",
                weights.astype(jnp.bfloat16),
                value_all,
                preferred_element_type=jnp.float32,
            )
            / totals
        )
        return (
            result.astype(jnp.bfloat16).transpose(1, 0, 2).reshape(block_rows, per_dev * head_width)
        )

    attn_heads = lax.map(
        attend,
        (
            queries_by_head.reshape(block_count, block_rows, per_dev, head_width),
            position.reshape(block_count, block_rows),
        ),
    ).reshape(rows_of_group, per_dev * head_width)
    attn_sum = lax.psum_scatter(
        jnp.dot(attn_heads, out_weight, preferred_element_type=jnp.float32).astype(jnp.bfloat16),
        "sp",
        scatter_dimension=0,
        tiled=True,
    ).astype(jnp.float32)
    own_live = jnp.arange(slot_rows, dtype=jnp.int32) < lengths[0, 0]
    attended = jnp.where(own_live[:, None], attn_sum, 0.0).astype(jnp.bfloat16)
    mixed_rows = residual.astype(jnp.float32) + attn_sum
    normed = (
        mixed_rows
        * lax.rsqrt(jnp.mean(mixed_rows * mixed_rows, axis=-1, keepdims=True) + 1e-06)
        * norm_gain
    ).astype(jnp.bfloat16)
    group_count = lax.axis_size("grp")
    experts = up_gate_weight.shape[0] * group_count * seq_devices
    top_count = expert_ids.shape[1]
    capacity = max(2, 8 * slot_rows * top_count // (5 * experts))
    hidden_width = down_weight.shape[1]
    choose = expert_ids[:, :, None] == jnp.arange(experts, dtype=jnp.int32)[None, None, :]
    routed = (jnp.any(choose, axis=1) & own_live[:, None]).astype(jnp.float32)
    earlier = (jnp.arange(slot_rows)[:, None] > jnp.arange(slot_rows)[None, :]).astype(jnp.float32)
    prefix = jnp.dot(earlier, routed, precision=lax.Precision.HIGHEST)
    slot_in = jnp.sum(jnp.where(choose, prefix[:, None, :], 0.0), axis=2).astype(jnp.int32)
    dump_slot = experts * capacity
    target = jnp.where(own_live[:, None], expert_ids * capacity + slot_in, dump_slot)
    source_rows = (
        jnp.full((dump_slot + 1,), slot_rows, jnp.int32)
        .at[target.reshape(-1)]
        .set(jnp.repeat(jnp.arange(slot_rows, dtype=jnp.int32), top_count))[:dump_slot]
    )
    padded = jnp.concatenate([normed, jnp.zeros((1, model_width), jnp.bfloat16)], axis=0)
    outgoing = padded[source_rows].reshape(experts, capacity, model_width)
    received = lax.all_to_all(outgoing, ("grp", "sp"), split_axis=0, concat_axis=0, tiled=True)
    flat_rows = received.reshape(-1, model_width)
    projected = jnp.dot(flat_rows, up_gate_weight[0], preferred_element_type=jnp.float32)
    hidden = (jax.nn.silu(projected[:, :hidden_width]) * projected[:, hidden_width:]).astype(
        jnp.bfloat16
    )
    returned = lax.all_to_all(
        jnp.dot(hidden, down_weight[0], preferred_element_type=jnp.float32)
        .astype(jnp.bfloat16)
        .reshape(received.shape),
        ("grp", "sp"),
        split_axis=0,
        concat_axis=0,
        tiled=True,
    )
    back_rows = jnp.concatenate(
        [returned.reshape(dump_slot, model_width), jnp.zeros((1, model_width), jnp.bfloat16)],
        axis=0,
    )
    picked = back_rows[target]
    combined = jnp.sum(gate_values[:, :, None] * picked.astype(jnp.float32), axis=1)
    moe_out = jnp.where(own_live[:, None], combined, 0.0).astype(jnp.bfloat16)
    return (attended, moe_out)


def solution(mesh):
    in_specs = (
        P(("grp", "sp"), None),
        P(("grp", "sp"), None),
        P("grp", "sp", None, None),
        P("grp", "sp"),
        P("sp", None),
        P(("grp", "sp"), None),
        P(),
        P(("grp", "sp"), None),
        P(("grp", "sp"), None),
        P(("grp", "sp"), None, None),
        P(("grp", "sp"), None, None),
    )
    out_specs = (P(("grp", "sp"), None), P(("grp", "sp"), None))
    groups, seq_devices = mesh.shape["grp"], mesh.shape["sp"]

    def run(*args):
        kv_heads = args[1].shape[1] // args[2].shape[-1]
        experts, top_count = args[9].shape[0], args[7].shape[1]
        pairs = seq_devices == kv_heads == 4 and groups % 2 == 0 and experts <= 4 * top_count
        return mapped(per_device_pairs if pairs else per_device)(*args)

    def mapped(body):
        return jax.shard_map(
            body, mesh=mesh, in_specs=in_specs, out_specs=out_specs, check_vma=False
        )

    return run
```

```python
import functools
import math

import jax
import jax.numpy as jnp
from jax import lax
from jax.experimental import pallas as pl
from jax.experimental.pallas import tpu as pltpu
from jax.sharding import PartitionSpec as P


def partner_2(value, axis, bit):
    mask = 2**bit
    pairs = [(source, source ^ mask) for source in range(lax.axis_size(axis))]
    return lax.ppermute(value, axis, pairs)


def shift_z(value):
    groups = lax.axis_size("grp")
    return lax.ppermute(value, "grp", [(g, (g + 2) % groups) for g in range(groups)])


def swap_x(value):
    return partner_2(value, "grp", 0)


def swap_x_core(value):
    groups, members = lax.axis_size("grp"), lax.axis_size("sp")
    flip = members + 1
    pairs = [(index, index ^ flip) for index in range(groups * members)]
    return lax.ppermute(value, ("grp", "sp"), pairs)


def swap_y(value):
    return partner_2(value, "sp", 1)


def swap_core(value):
    return partner_2(value, "sp", 0)


def after(value, *earlier):
    return lax.optimization_barrier((value, *earlier))[0]


def xor_group(value, mask):
    return lax.ppermute(value, "sp", [(s, s ^ mask) for s in range(lax.axis_size("sp"))])


def attend_kernel(index, mine_ref, query_ref, cache_ref, *refs):
    fresh_refs, (out_ref, keys, values, bias) = refs[:-4], refs[-4:]
    rows = query_ref.shape[0]
    cached, width = cache_ref.shape[0], cache_ref.shape[1] // 2
    keys[:cached, :] = cache_ref[:, :width]
    values[:cached, :] = cache_ref[:, width:]
    lengths = []
    for block, fresh_ref in enumerate(fresh_refs):
        places = pl.ds(cached + block * rows, rows)
        keys[places, :] = fresh_ref[:rows, :width]
        values[places, :] = fresh_ref[:rows, width:]
        note = fresh_ref[rows : rows + 16, :].astype(jnp.float32)
        lengths.append(note[:1, :1] * 256.0 + note[:1, width : width + 1])
    mine = mine_ref[0]
    offsets = []
    for block in range(len(fresh_refs)):
        offset = jnp.zeros((1, 1), jnp.float32)
        for other in range(len(fresh_refs)):
            before = (mine ^ other) < (mine ^ block)
            offset = offset + lengths[other] * before.astype(jnp.float32)
        offsets.append(offset)
    column = lax.broadcasted_iota(jnp.int32, (1, bias.shape[1]), 1)
    key_place = jnp.zeros((1, bias.shape[1]), jnp.float32)
    for block in range(len(fresh_refs)):
        within = (column - block * rows).astype(jnp.float32)
        place = jnp.where(within < lengths[block], within + offsets[block], 1e9)
        key_place = jnp.where(column >= block * rows, place, key_place)
    row_place = lax.broadcasted_iota(jnp.int32, bias.shape, 0).astype(jnp.float32) + offsets[index]
    bias[...] = jnp.where(key_place <= row_place, 0.0, -1e30)
    scale = math.log2(math.e) / math.sqrt(width)
    for head in range(query_ref.shape[1] // width):
        columns = pl.ds(head * width, width)
        scores = lax.dot_general(
            query_ref[:, columns],
            keys[...],
            (((1,), (1,)), ((), ())),
            preferred_element_type=jnp.float32,
        )
        old, new = scores[:, :cached] * scale, scores[:, cached:] * scale + bias[...]
        row_max = jnp.maximum(
            jnp.max(old, axis=1, keepdims=True), jnp.max(new, axis=1, keepdims=True)
        )
        old, new = jnp.exp2(old - row_max), jnp.exp2(new - row_max)
        totals = jnp.sum(old, axis=1, keepdims=True) + jnp.sum(new, axis=1, keepdims=True)
        result = jnp.dot(
            old.astype(jnp.bfloat16), values[:cached, :], preferred_element_type=jnp.float32
        ) + jnp.dot(
            new.astype(jnp.bfloat16), values[cached:, :], preferred_element_type=jnp.float32
        )
        out_ref[:, columns] = (result / totals).astype(jnp.bfloat16)


def attend_block(index, mine, query, cache_block, fresh):
    rows, columns = query.shape
    cached, width = cache_block.shape[0], cache_block.shape[1] // 2
    new = rows * len(fresh)
    inside = pl.BlockSpec(memory_space=pltpu.VMEM)
    return pl.pallas_call(
        functools.partial(attend_kernel, index),
        out_shape=jax.ShapeDtypeStruct((rows, columns), jnp.bfloat16),
        in_specs=[pl.BlockSpec(memory_space=pltpu.SMEM)] + [inside] * (2 + len(fresh)),
        out_specs=inside,
        scratch_shapes=[
            pltpu.VMEM((cached + new, width), jnp.bfloat16),
            pltpu.VMEM((cached + new, width), jnp.bfloat16),
            pltpu.VMEM((rows, new), jnp.float32),
        ],
        compiler_params=pltpu.CompilerParams(vmem_limit_bytes=12 * 2**20),
        cost_estimate=pl.CostEstimate(
            flops=4 * rows * columns * (cached + new),
            bytes_accessed=4 * (rows * columns + (cached + new) * width),
            transcendentals=rows * columns // width * (cached + new),
        ),
    )(mine, query, cache_block, *fresh)


def norm_kernel(
    length_ref,
    own_ref,
    core_ref,
    far_ref,
    residual_ref,
    gain_ref,
    attended_ref,
    packed_ref,
):
    attn_sum = (
        own_ref[...].astype(jnp.float32)
        + core_ref[...].astype(jnp.float32)
        + far_ref[...].astype(jnp.float32)
    )
    live = lax.broadcasted_iota(jnp.int32, attn_sum.shape, 0) < length_ref[0]
    attended_ref[...] = jnp.where(live, attn_sum, 0.0).astype(jnp.bfloat16)
    mixed = residual_ref[...].astype(jnp.float32) + attn_sum
    scale = lax.rsqrt(jnp.mean(mixed * mixed, axis=1, keepdims=True) + 1e-06)
    normed = (mixed * scale * gain_ref[...]).astype(jnp.bfloat16)
    rows, half = packed_ref.shape[0] // 2, packed_ref.shape[1]
    packed_ref[:rows, :] = normed[:, :half]
    packed_ref[rows:, :] = normed[:, half:]


def normalize(length, own, core, far, residual, gain):
    rows, width = own.shape
    packed = jax.ShapeDtypeStruct((2 * rows, width // 2), jnp.bfloat16)
    inside = pl.BlockSpec(memory_space=pltpu.VMEM)
    return pl.pallas_call(
        norm_kernel,
        out_shape=(jax.ShapeDtypeStruct((rows, width), jnp.bfloat16), packed),
        in_specs=[pl.BlockSpec(memory_space=pltpu.SMEM)] + [inside] * 5,
        out_specs=(inside, inside),
        compiler_params=pltpu.CompilerParams(vmem_limit_bytes=12 * 2**20),
        cost_estimate=pl.CostEstimate(
            flops=10 * rows * width, bytes_accessed=12 * rows * width, transcendentals=rows
        ),
    )(length, own, core, far, residual, gain)


def pick_kernel(capacity, place_ref, *refs):
    blocks, _, rows = place_ref.shape
    own_ref, sibling_ref = refs[-2:]
    half = own_ref.shape[1] // 2
    slot = lax.broadcasted_iota(jnp.int32, (capacity, rows), 0)
    for block in range(blocks):
        pick = jnp.concatenate(
            [(place_ref[block, pl.ds(core, 1), :] == slot) for core in range(2)], axis=0
        )
        pick = jnp.where(pick, 1.0, 0.0).astype(jnp.bfloat16)
        level, spot = block // 4, block % 4
        for side in range(2):
            if spot < 3:
                source = refs[5 * level + spot][pl.ds(side * rows, rows), :]
            else:
                source = refs[5 * level + 3 + side][...]
            chosen = jnp.dot(pick, source, preferred_element_type=jnp.float32)
            chosen = chosen.astype(jnp.bfloat16)
            inner = pl.ds(block * capacity, capacity), pl.ds(side * half, half)
            own_ref[inner] = chosen[:capacity]
            sibling_ref[inner] = chosen[capacity:]


def pick_rows(capacity, place, gathered):
    blocks, _, rows = place.shape
    half = gathered[0].shape[1]
    shape = jax.ShapeDtypeStruct((blocks * capacity, 2 * half), jnp.bfloat16)
    return pl.pallas_call(
        functools.partial(pick_kernel, capacity),
        out_shape=(shape, shape),
        compiler_params=pltpu.CompilerParams(vmem_limit_bytes=20 * 2**20),
        cost_estimate=pl.CostEstimate(
            flops=8 * blocks * capacity * rows * half,
            bytes_accessed=4 * blocks * (rows + 2 * capacity) * half,
            transcendentals=0,
        ),
    )(place, *gathered)


def combine_kernel(place_ref, gate_ref, own_ref, core_ref, *refs):
    arrived_refs, out_refs = refs[:4], refs[4:]
    rows = place_ref.shape[2]
    capacity = own_ref.shape[0] // 4
    slot = lax.broadcasted_iota(jnp.int32, (capacity, rows), 0)
    for side in range(2):
        for place in range(2):
            block = place if side else 2 * place
            weight = jnp.concatenate(
                [
                    jnp.where(
                        place_ref[block, pl.ds(expert, 1), :] == slot,
                        gate_ref[block, pl.ds(expert, 1), :],
                        0.0,
                    )
                    for expert in (0, 1, 2 + 2 * side, 3 + 2 * side)
                ],
                axis=0,
            )
            weight = weight.T.astype(jnp.bfloat16)
            kept = pl.ds((2 * side + place) * capacity, capacity)
            arrived = pl.ds(place * capacity, capacity)
            results = jnp.concatenate(
                [
                    own_ref[kept, :],
                    core_ref[kept, :],
                    arrived_refs[2 * side][arrived, :],
                    arrived_refs[2 * side + 1][arrived, :],
                ],
                axis=0,
            )
            out_refs[2 * side + place][...] = jnp.dot(
                weight, results, preferred_element_type=jnp.float32
            ).astype(jnp.bfloat16)


def combine_rows(part, parts, place, gate, own, core, arrived):
    rows = place.shape[2]
    count, half = own.shape[0] // parts, own.shape[1]
    share = jax.ShapeDtypeStruct((rows, half), jnp.bfloat16)
    whole = lambda shape: pl.BlockSpec(shape, lambda j: (0,) * len(shape))
    level = pl.BlockSpec((count, half), lambda j: (part, 0))
    return pl.pallas_call(
        combine_kernel,
        out_shape=[share] * 4,
        grid=(1,),
        in_specs=[whole(place.shape), whole(gate.shape), level, level]
        + [whole(value.shape) for value in arrived],
        out_specs=[whole(share.shape)] * 4,
        compiler_params=pltpu.CompilerParams(vmem_limit_bytes=16 * 2**20),
        cost_estimate=pl.CostEstimate(
            flops=8 * count * rows * half,
            bytes_accessed=8 * (rows + count) * half,
            transcendentals=0,
        ),
    )(place, gate, own, core, *arrived)


def routing_start(own_live, expert_ids, gate_values, earlier):
    live_ids = jnp.where(own_live[:, None], expert_ids, -1).astype(jnp.float32)
    routing = after(jnp.concatenate([live_ids, gate_values], axis=1).T, earlier)
    groups = lax.axis_size("grp")
    lines = [routing]
    for hop in range(2, groups, 2):
        lines.append(
            lax.ppermute(routing, "grp", [(g, (g + hop) % groups) for g in range(groups)])
        )
    return jnp.stack(lines)


def routing_pair(routing, swap):
    return jnp.stack([routing, swap(routing)], axis=routing.ndim - 2)


def selections(routing, top_count):
    mine = lax.axis_index(("grp", "sp"))
    depth, rows = routing.shape[0], routing.shape[-1]
    routing = routing.reshape(-1, 2 * top_count, rows)
    ids, gates = routing[:, :top_count].astype(jnp.int32), routing[:, top_count:]
    beside = lax.axis_size("sp")
    experts = jnp.stack([mine ^ flip for flip in (0, 1, 2, 3, beside, beside + 1)])
    chosen = ids[:, None] == experts[None, :, None, None]
    wanted = jnp.any(chosen, axis=2)
    gate = jnp.sum(jnp.where(chosen, gates[:, None], 0.0), axis=2)
    order = jnp.arange(rows)
    earlier = (order[:, None] < order[None, :]).astype(jnp.bfloat16)
    place = jnp.einsum(
        "bcr,rt->bct", wanted.astype(jnp.bfloat16), earlier, preferred_element_type=jnp.float32
    ).astype(jnp.int32)
    return jnp.where(wanted, place, -1), gate


def expert_kernel(rows_ref, up_gate_ref, down_ref, keep_ref, *refs):
    sent_refs, hidden = refs[:-1], refs[-1]
    hidden_width, width = down_ref.shape[1], down_ref.shape[2]
    half, levels = width // 2, len(sent_refs) // 2
    capacity = rows_ref.shape[0] // (4 * levels)
    tile = 256
    for start in range(0, hidden_width, tile):
        gate = jnp.dot(
            rows_ref[...],
            up_gate_ref[0, :, start : start + tile],
            preferred_element_type=jnp.float32,
        )
        up = jnp.dot(
            rows_ref[...],
            up_gate_ref[0, :, hidden_width + start : hidden_width + start + tile],
            preferred_element_type=jnp.float32,
        )
        hidden[:, start : start + tile] = (gate / (1.0 + jnp.exp(-gate)) * up).astype(
            jnp.bfloat16
        )
    for start in range(0, width, tile):
        result = jnp.dot(
            hidden[...], down_ref[0, :, start : start + tile], preferred_element_type=jnp.float32
        ).astype(jnp.bfloat16)
        side = start // half
        columns = pl.ds(start - side * half, tile)
        for block in range(4 * levels):
            level, far_x, far_y = block // 4, block // 2 % 2, block % 2
            piece = result[block * capacity : (block + 1) * capacity]
            sent, place = (far_x, far_y) if side else (far_y, far_x)
            if sent:
                sent_refs[2 * level + side][pl.ds(place * capacity, capacity), columns] = piece
            else:
                row = (4 * level + 2 * side + place) * capacity
                keep_ref[pl.ds(row, capacity), columns] = piece


def run_expert(rows, levels, up_gate_weight, down_weight):
    count, width = rows.shape
    hidden_width = down_weight.shape[1]
    keep = jax.ShapeDtypeStruct((count, width // 2), jnp.bfloat16)
    sent = jax.ShapeDtypeStruct((count // (2 * levels), width // 2), jnp.bfloat16)
    keep, *sent = pl.pallas_call(
        expert_kernel,
        out_shape=[keep] + [sent] * (2 * levels),
        scratch_shapes=[pltpu.VMEM((count, hidden_width), jnp.bfloat16)],
        compiler_params=pltpu.CompilerParams(vmem_limit_bytes=20 * 2**20),
        cost_estimate=pl.CostEstimate(
            flops=6 * count * width * hidden_width,
            bytes_accessed=6 * width * hidden_width + 4 * count * width,
            transcendentals=count * hidden_width,
        ),
    )(rows, up_gate_weight, down_weight)
    return keep, [sent[2 * level : 2 * level + 2] for level in range(levels)]


def experts_by_gather(packed, routing, top_count, capacity, up_gate_weight, down_weight):
    depth = lax.axis_size("grp") // 2
    rows = packed.shape[0] // 2
    routing = routing_pair(after(routing, packed), swap_x)
    lines, beside_x, beside_y, diagonal = [packed], [], [], []
    halves = []

    def cross(level, earlier):
        first_x, second_y = halves[level]
        if earlier is not None:
            first_x, second_y = after(first_x, *earlier), after(second_y, *earlier)
        diagonal.append((swap_y(first_x), swap_x(second_y)))

    for level in range(depth):
        line = lines[level]
        if level == 1:
            line = after(line, routing)
            routing = routing_pair(after(routing, *halves[0]), swap_y)
        if level == 2:
            cross(0, (line, routing))
            cross(1, (line,))
            line = after(line, *diagonal[0], *diagonal[1])
        elif level > 2:
            line = after(line, beside_x[level - 1], beside_y[level - 1])
        beside_x.append(swap_x(line))
        beside_y.append(swap_y(line))
        halves.append((beside_x[level][:rows], beside_y[level][rows:]))
        if level + 1 < depth:
            line = lines[level]
            if level:
                line = after(line, beside_x[level - 1], beside_y[level - 1])
            lines.append(shift_z(line))
    for level in range(len(diagonal), depth):
        cross(level, None)
    if depth == 1:
        routing = routing_pair(routing, swap_y)
    place, gate = selections(routing, top_count)
    per_level = place.shape[0] // depth
    results, sent, arrived, joined = {}, {}, {}, {}

    def send_back(level, *earlier):
        own_first, own_second, other_first, other_second = (
            after(part, *earlier) if earlier else part for part in sent[level]
        )
        arrived[level] = (
            swap_y(own_first),
            xor_group(other_first, 3),
            swap_x(own_second),
            swap_x_core(other_second),
        )

    def join(level, *earlier):
        index, count, own_keep, core_keep = results[level]
        if earlier:
            own_keep = after(own_keep, *earlier)
        blocks = slice(level * per_level, (level + 1) * per_level)
        first, first_x, second, second_y = combine_rows(
            index, count, place[blocks], gate[blocks], own_keep, core_keep, arrived[level]
        )
        joined[level] = first, second, swap_x(first_x), swap_y(second_y)

    for start in range(0, depth, 2):
        levels = range(start, min(start + 2, depth))
        gathered = []
        for level in levels:
            gathered += [lines[level], beside_y[level], beside_x[level], *diagonal[level]]
        ahead, last = levels[-1] + 1, levels[-1] + 2
        if start:
            gathered[0] = after(gathered[0], results[start - 1][2])
        blocks = slice(start * per_level, (start + len(levels)) * per_level)
        own, sibling = pick_rows(capacity, place[blocks, :2], gathered)
        if last < depth:
            sibling = after(sibling, beside_x[ahead], beside_y[ahead], lines[last])
        other = swap_core(sibling)
        other_keep, other_sent = run_expert(other, len(levels), up_gate_weight, down_weight)
        if last < depth:
            other_keep = after(other_keep, beside_x[last], beside_y[last], *diagonal[ahead])
            own = after(own, other_keep)
        if start:
            join(start - 1, other_keep)
            own = after(own, *arrived[start - 1])
            if 0 not in arrived:
                send_back(0, *arrived[start - 1])
        own_keep, own_sent = run_expert(own, len(levels), up_gate_weight, down_weight)
        core_keep = swap_core(other_keep)
        for index, level in enumerate(levels):
            sent[level] = *own_sent[index], *other_sent[index]
            results[level] = index, len(levels), own_keep, core_keep
            if level:
                send_back(level, *arrived.get(level - 1, ()))
        for level in levels:
            if level and (ahead >= depth or level < levels[-1]):
                join(level, *(joined[start - 1] + arrived[0] if start else ()))
                if level + 1 in levels:
                    far, ready = arrived[level + 1], joined[level]
                    arrived[level + 1] = tuple(after(part, *ready) for part in far)
                    joined[level] = tuple(after(part, *far) for part in ready)
    if 0 not in arrived:
        send_back(0)
    join(0)
    shares = {}
    for level in range(depth):
        first, second, first_far, second_far = joined[level]
        shares[level] = first + first_far, second + second_far
    first, second = shares[0]
    if depth > 1:
        total = jnp.concatenate(shares[1], axis=0)
        for level in range(2, depth):
            total = jnp.concatenate(shares[level], axis=0) + shift_z(total)
        total = shift_z(total)
        first, second = first + total[:rows], second + total[rows:]
    return jnp.concatenate([first, second], axis=1)


def per_device_pairs(
    queries,
    fresh_key_values,
    cache,
    lengths,
    out_weight,
    residual,
    norm_gain,
    expert_ids,
    gate_values,
    up_gate_weight,
    down_weight,
):
    seq_devices = lax.axis_size("sp")
    mine = lax.axis_index("sp")
    slot_rows = queries.shape[0]
    width = cache.shape[-1] // 2
    head_columns = queries.shape[1] // seq_devices
    top_count = expert_ids.shape[1]
    experts = up_gate_weight.shape[0] * lax.axis_size("grp") * seq_devices
    capacity = max(2, 8 * slot_rows * top_count // (5 * experts))
    own_length = lengths[0, 0]
    own_live = jnp.arange(slot_rows, dtype=jnp.int32) < own_length

    def key_values_for(target):
        keys = lax.dynamic_slice(fresh_key_values, (0, target * width), (slot_rows, width))
        values = lax.dynamic_slice(
            fresh_key_values, (0, (seq_devices + target) * width), (slot_rows, width)
        )
        lane = jnp.arange(2 * width, dtype=jnp.int32)[None, :]
        note = jnp.where(lane < width, own_length // 256, own_length % 256)
        note = jnp.broadcast_to(note, (16, 2 * width)).astype(jnp.bfloat16)
        return jnp.concatenate([jnp.concatenate([keys, values], axis=1), note], axis=0)

    def queries_for(target):
        return lax.dynamic_slice(queries, (0, target * head_columns), (slot_rows, head_columns))

    masks = range(1, seq_devices)
    fresh = [key_values_for(mine)] + [xor_group(key_values_for(mine ^ m), m) for m in masks]
    query_blocks = [queries_for(mine)] + [xor_group(queries_for(mine ^ m), m) for m in masks]
    cache_block = cache[0, 0]

    def share_of(block, query):
        heads = attend_block(block, mine[None], query, cache_block, fresh)
        return jnp.dot(heads, out_weight, preferred_element_type=jnp.float32).astype(jnp.bfloat16)

    own = share_of(0, query_blocks[0])
    far_core = share_of(3, after(query_blocks[3], query_blocks[2], own))
    far = share_of(2, query_blocks[2]) + swap_core(far_core)
    near = share_of(1, after(query_blocks[1], far))
    routing = routing_start(own_live, expert_ids, gate_values, far)
    far = swap_y(far)
    attended, packed = normalize(
        lengths[0], own, swap_core(after(near, far, routing)), far, residual, norm_gain[None, :]
    )
    moe_out = experts_by_gather(
        packed, routing, top_count, capacity, up_gate_weight, down_weight
    )
    return (attended, moe_out)


def per_device(
    queries,
    fresh_key_values,
    cache,
    lengths,
    out_weight,
    residual,
    norm_gain,
    expert_ids,
    gate_values,
    up_gate_weight,
    down_weight,
):
    seq_devices = lax.axis_size("sp")
    slot_rows = queries.shape[0]
    head_width = cache.shape[-1] // 2
    model_width = residual.shape[1]
    kv_heads = fresh_key_values.shape[1] // (2 * head_width)
    repeat = seq_devices // kv_heads
    keys_new = fresh_key_values[:, : kv_heads * head_width].reshape(
        slot_rows, kv_heads, 1, head_width
    )
    values_new = fresh_key_values[:, kv_heads * head_width :].reshape(
        slot_rows, kv_heads, 1, head_width
    )
    paired = jnp.concatenate([keys_new, values_new], axis=3)
    spread = jnp.broadcast_to(paired, (slot_rows, kv_heads, repeat, 2 * head_width)).reshape(
        slot_rows, seq_devices * 2 * head_width
    )
    all_lengths = lax.all_gather(lengths, "sp", axis=1, tiled=True)
    queries_by_head, head_kv = (
        lax.all_to_all(queries, "sp", split_axis=1, concat_axis=0, tiled=True),
        lax.all_to_all(spread, "sp", split_axis=1, concat_axis=0, tiled=True),
    )
    cache_block = cache[0, 0]
    my_index = lax.axis_index("sp")
    for bit_pos in range(repeat.bit_length() - 1):
        partner = partner_2(cache_block, "sp", bit_pos)
        is_upper = my_index // 2**bit_pos % 2 == 1
        cache_block = jnp.where(
            is_upper,
            jnp.concatenate([partner, cache_block], axis=0),
            jnp.concatenate([cache_block, partner], axis=0),
        )
    stretch_lens = all_lengths[0]
    offsets = jnp.cumsum(stretch_lens) - stretch_lens
    rows_of_group = queries_by_head.shape[0]
    slot_ids = jnp.arange(rows_of_group, dtype=jnp.int32)
    source = slot_ids // slot_rows
    within = slot_ids % slot_rows
    from_device = source[:, None] == jnp.arange(seq_devices, dtype=jnp.int32)[None, :]
    is_live = within < jnp.sum(jnp.where(from_device, stretch_lens[None, :], 0), axis=1)
    position = within + jnp.sum(jnp.where(from_device, offsets[None, :], 0), axis=1)
    per_dev = queries_by_head.shape[1] // head_width
    cache_len = cache_block.shape[0]
    key_all = jnp.concatenate([cache_block[:, :head_width], head_kv[:, :head_width]], axis=0)
    value_all = jnp.concatenate([cache_block[:, head_width:], head_kv[:, head_width:]], axis=0)
    block_count = 2 if rows_of_group % 2 == 0 and rows_of_group >= 1024 else 1
    block_rows = rows_of_group // block_count

    def attend(parts):
        query_block, place_block = parts
        scores = jnp.einsum(
            "rhd,kd->hrk", query_block, key_all, preferred_element_type=jnp.float32
        ) / math.sqrt(head_width)
        allowed = jnp.concatenate(
            [
                jnp.ones((block_rows, cache_len), dtype=bool),
                is_live[None, :] & (position[None, :] <= place_block[:, None]),
            ],
            axis=1,
        )
        scores = jnp.where(allowed[None], scores, -jnp.inf)
        row_max = jnp.max(scores, axis=-1, keepdims=True)
        weights = jnp.exp(scores - row_max)
        totals = jnp.sum(weights, axis=-1, keepdims=True)
        result = (
            jnp.einsum(
                "hrk,kd->hrd",
                weights.astype(jnp.bfloat16),
                value_all,
                preferred_element_type=jnp.float32,
            )
            / totals
        )
        return (
            result.astype(jnp.bfloat16).transpose(1, 0, 2).reshape(block_rows, per_dev * head_width)
        )

    attn_heads = lax.map(
        attend,
        (
            queries_by_head.reshape(block_count, block_rows, per_dev, head_width),
            position.reshape(block_count, block_rows),
        ),
    ).reshape(rows_of_group, per_dev * head_width)
    attn_sum = lax.psum_scatter(
        jnp.dot(attn_heads, out_weight, preferred_element_type=jnp.float32).astype(jnp.bfloat16),
        "sp",
        scatter_dimension=0,
        tiled=True,
    ).astype(jnp.float32)
    own_live = jnp.arange(slot_rows, dtype=jnp.int32) < lengths[0, 0]
    attended = jnp.where(own_live[:, None], attn_sum, 0.0).astype(jnp.bfloat16)
    mixed_rows = residual.astype(jnp.float32) + attn_sum
    normed = (
        mixed_rows
        * lax.rsqrt(jnp.mean(mixed_rows * mixed_rows, axis=-1, keepdims=True) + 1e-06)
        * norm_gain
    ).astype(jnp.bfloat16)
    group_count = lax.axis_size("grp")
    experts = up_gate_weight.shape[0] * group_count * seq_devices
    top_count = expert_ids.shape[1]
    capacity = max(2, 8 * slot_rows * top_count // (5 * experts))
    hidden_width = down_weight.shape[1]
    choose = expert_ids[:, :, None] == jnp.arange(experts, dtype=jnp.int32)[None, None, :]
    routed = (jnp.any(choose, axis=1) & own_live[:, None]).astype(jnp.float32)
    earlier = (jnp.arange(slot_rows)[:, None] > jnp.arange(slot_rows)[None, :]).astype(jnp.float32)
    prefix = jnp.dot(earlier, routed, precision=lax.Precision.HIGHEST)
    slot_in = jnp.sum(jnp.where(choose, prefix[:, None, :], 0.0), axis=2).astype(jnp.int32)
    dump_slot = experts * capacity
    target = jnp.where(own_live[:, None], expert_ids * capacity + slot_in, dump_slot)
    source_rows = (
        jnp.full((dump_slot + 1,), slot_rows, jnp.int32)
        .at[target.reshape(-1)]
        .set(jnp.repeat(jnp.arange(slot_rows, dtype=jnp.int32), top_count))[:dump_slot]
    )
    padded = jnp.concatenate([normed, jnp.zeros((1, model_width), jnp.bfloat16)], axis=0)
    outgoing = padded[source_rows].reshape(experts, capacity, model_width)
    received = lax.all_to_all(outgoing, ("grp", "sp"), split_axis=0, concat_axis=0, tiled=True)
    flat_rows = received.reshape(-1, model_width)
    projected = jnp.dot(flat_rows, up_gate_weight[0], preferred_element_type=jnp.float32)
    hidden = (jax.nn.silu(projected[:, :hidden_width]) * projected[:, hidden_width:]).astype(
        jnp.bfloat16
    )
    returned = lax.all_to_all(
        jnp.dot(hidden, down_weight[0], preferred_element_type=jnp.float32)
        .astype(jnp.bfloat16)
        .reshape(received.shape),
        ("grp", "sp"),
        split_axis=0,
        concat_axis=0,
        tiled=True,
    )
    back_rows = jnp.concatenate(
        [returned.reshape(dump_slot, model_width), jnp.zeros((1, model_width), jnp.bfloat16)],
        axis=0,
    )
    picked = back_rows[target]
    combined = jnp.sum(gate_values[:, :, None] * picked.astype(jnp.float32), axis=1)
    moe_out = jnp.where(own_live[:, None], combined, 0.0).astype(jnp.bfloat16)
    return (attended, moe_out)


def solution(mesh):
    in_specs = (
        P(("grp", "sp"), None),
        P(("grp", "sp"), None),
        P("grp", "sp", None, None),
        P("grp", "sp"),
        P("sp", None),
        P(("grp", "sp"), None),
        P(),
        P(("grp", "sp"), None),
        P(("grp", "sp"), None),
        P(("grp", "sp"), None, None),
        P(("grp", "sp"), None, None),
    )
    out_specs = (P(("grp", "sp"), None), P(("grp", "sp"), None))
    groups, seq_devices = mesh.shape["grp"], mesh.shape["sp"]

    def run(*args):
        kv_heads = args[1].shape[1] // args[2].shape[-1]
        experts, top_count = args[9].shape[0], args[7].shape[1]
        pairs = seq_devices == kv_heads == 4 and groups % 2 == 0 and experts <= 4 * top_count
        return mapped(per_device_pairs if pairs else per_device)(*args)

    def mapped(body):
        return jax.shard_map(
            body, mesh=mesh, in_specs=in_specs, out_specs=out_specs, check_vma=False
        )

    return run
```

```python
import functools
import math

import jax
import jax.numpy as jnp
from jax import lax
from jax.experimental import pallas as pl
from jax.experimental.pallas import tpu as pltpu
from jax.sharding import PartitionSpec as P


def partner_2(value, axis, bit):
    mask = 2**bit
    pairs = [(source, source ^ mask) for source in range(lax.axis_size(axis))]
    return lax.ppermute(value, axis, pairs)


def shift_z(value):
    groups = lax.axis_size("grp")
    return lax.ppermute(value, "grp", [(g, (g + 2) % groups) for g in range(groups)])


def swap_x(value):
    return partner_2(value, "grp", 0)


def swap_y(value):
    return partner_2(value, "sp", 1)


def swap_core(value):
    return partner_2(value, "sp", 0)


def after(value, *earlier):
    return lax.optimization_barrier((value, *earlier))[0]


def xor_group(value, mask):
    return lax.ppermute(value, "sp", [(s, s ^ mask) for s in range(lax.axis_size("sp"))])


def attend_kernel(index, mine_ref, query_ref, cache_ref, *refs):
    fresh_refs, (out_ref, keys, values, bias) = refs[:-4], refs[-4:]
    rows = query_ref.shape[0]
    cached, width = cache_ref.shape[0], cache_ref.shape[1] // 2
    keys[:cached, :] = cache_ref[:, :width]
    values[:cached, :] = cache_ref[:, width:]
    lengths = []
    for block, fresh_ref in enumerate(fresh_refs):
        places = pl.ds(cached + block * rows, rows)
        keys[places, :] = fresh_ref[:rows, :width]
        values[places, :] = fresh_ref[:rows, width:]
        note = fresh_ref[rows : rows + 16, :].astype(jnp.float32)
        lengths.append(note[:1, :1] * 256.0 + note[:1, width : width + 1])
    mine = mine_ref[0]
    offsets = []
    for block in range(len(fresh_refs)):
        offset = jnp.zeros((1, 1), jnp.float32)
        for other in range(len(fresh_refs)):
            before = (mine ^ other) < (mine ^ block)
            offset = offset + lengths[other] * before.astype(jnp.float32)
        offsets.append(offset)
    column = lax.broadcasted_iota(jnp.int32, (1, bias.shape[1]), 1)
    key_place = jnp.zeros((1, bias.shape[1]), jnp.float32)
    for block in range(len(fresh_refs)):
        within = (column - block * rows).astype(jnp.float32)
        place = jnp.where(within < lengths[block], within + offsets[block], 1e9)
        key_place = jnp.where(column >= block * rows, place, key_place)
    row_place = lax.broadcasted_iota(jnp.int32, bias.shape, 0).astype(jnp.float32) + offsets[index]
    bias[...] = jnp.where(key_place <= row_place, 0.0, -1e30)
    scale = math.log2(math.e) / math.sqrt(width)
    for head in range(query_ref.shape[1] // width):
        columns = pl.ds(head * width, width)
        scores = lax.dot_general(
            query_ref[:, columns],
            keys[...],
            (((1,), (1,)), ((), ())),
            preferred_element_type=jnp.float32,
        )
        old, new = scores[:, :cached] * scale, scores[:, cached:] * scale + bias[...]
        row_max = jnp.maximum(
            jnp.max(old, axis=1, keepdims=True), jnp.max(new, axis=1, keepdims=True)
        )
        old, new = jnp.exp2(old - row_max), jnp.exp2(new - row_max)
        totals = jnp.sum(old, axis=1, keepdims=True) + jnp.sum(new, axis=1, keepdims=True)
        result = jnp.dot(
            old.astype(jnp.bfloat16), values[:cached, :], preferred_element_type=jnp.float32
        ) + jnp.dot(
            new.astype(jnp.bfloat16), values[cached:, :], preferred_element_type=jnp.float32
        )
        out_ref[:, columns] = (result / totals).astype(jnp.bfloat16)


def attend_block(index, mine, query, cache_block, fresh):
    rows, columns = query.shape
    cached, width = cache_block.shape[0], cache_block.shape[1] // 2
    new = rows * len(fresh)
    inside = pl.BlockSpec(memory_space=pltpu.VMEM)
    return pl.pallas_call(
        functools.partial(attend_kernel, index),
        out_shape=jax.ShapeDtypeStruct((rows, columns), jnp.bfloat16),
        in_specs=[pl.BlockSpec(memory_space=pltpu.SMEM)] + [inside] * (2 + len(fresh)),
        out_specs=inside,
        scratch_shapes=[
            pltpu.VMEM((cached + new, width), jnp.bfloat16),
            pltpu.VMEM((cached + new, width), jnp.bfloat16),
            pltpu.VMEM((rows, new), jnp.float32),
        ],
        compiler_params=pltpu.CompilerParams(vmem_limit_bytes=12 * 2**20),
        cost_estimate=pl.CostEstimate(
            flops=4 * rows * columns * (cached + new),
            bytes_accessed=4 * (rows * columns + (cached + new) * width),
            transcendentals=rows * columns // width * (cached + new),
        ),
    )(mine, query, cache_block, *fresh)


def norm_kernel(
    length_ref,
    own_ref,
    core_ref,
    far_ref,
    residual_ref,
    gain_ref,
    attended_ref,
    packed_ref,
):
    attn_sum = (
        own_ref[...].astype(jnp.float32)
        + core_ref[...].astype(jnp.float32)
        + far_ref[...].astype(jnp.float32)
    )
    live = lax.broadcasted_iota(jnp.int32, attn_sum.shape, 0) < length_ref[0]
    attended_ref[...] = jnp.where(live, attn_sum, 0.0).astype(jnp.bfloat16)
    mixed = residual_ref[...].astype(jnp.float32) + attn_sum
    scale = lax.rsqrt(jnp.mean(mixed * mixed, axis=1, keepdims=True) + 1e-06)
    normed = (mixed * scale * gain_ref[...]).astype(jnp.bfloat16)
    rows, half = packed_ref.shape[0] // 2, packed_ref.shape[1]
    packed_ref[:rows, :] = normed[:, :half]
    packed_ref[rows:, :] = normed[:, half:]


def normalize(length, own, core, far, residual, gain):
    rows, width = own.shape
    packed = jax.ShapeDtypeStruct((2 * rows, width // 2), jnp.bfloat16)
    inside = pl.BlockSpec(memory_space=pltpu.VMEM)
    return pl.pallas_call(
        norm_kernel,
        out_shape=(jax.ShapeDtypeStruct((rows, width), jnp.bfloat16), packed),
        in_specs=[pl.BlockSpec(memory_space=pltpu.SMEM)] + [inside] * 5,
        out_specs=(inside, inside),
        compiler_params=pltpu.CompilerParams(vmem_limit_bytes=12 * 2**20),
        cost_estimate=pl.CostEstimate(
            flops=10 * rows * width, bytes_accessed=12 * rows * width, transcendentals=rows
        ),
    )(length, own, core, far, residual, gain)


def pick_kernel(capacity, place_ref, *refs):
    blocks, _, rows = place_ref.shape
    own_ref, sibling_ref = refs[-2:]
    half = own_ref.shape[1] // 2
    slot = lax.broadcasted_iota(jnp.int32, (capacity, rows), 0)
    for block in range(blocks):
        pick = jnp.concatenate(
            [(place_ref[block, pl.ds(core, 1), :] == slot) for core in range(2)], axis=0
        )
        pick = jnp.where(pick, 1.0, 0.0).astype(jnp.bfloat16)
        level, spot = block // 4, block % 4
        for side in range(2):
            if spot < 3:
                source = refs[5 * level + spot][pl.ds(side * rows, rows), :]
            else:
                source = refs[5 * level + 3 + side][...]
            chosen = jnp.dot(pick, source, preferred_element_type=jnp.float32)
            chosen = chosen.astype(jnp.bfloat16)
            inner = pl.ds(block * capacity, capacity), pl.ds(side * half, half)
            own_ref[inner] = chosen[:capacity]
            sibling_ref[inner] = chosen[capacity:]


def pick_rows(capacity, place, gathered):
    blocks, _, rows = place.shape
    half = gathered[0].shape[1]
    shape = jax.ShapeDtypeStruct((blocks * capacity, 2 * half), jnp.bfloat16)
    return pl.pallas_call(
        functools.partial(pick_kernel, capacity),
        out_shape=(shape, shape),
        compiler_params=pltpu.CompilerParams(vmem_limit_bytes=20 * 2**20),
        cost_estimate=pl.CostEstimate(
            flops=8 * blocks * capacity * rows * half,
            bytes_accessed=4 * blocks * (rows + 2 * capacity) * half,
            transcendentals=0,
        ),
    )(place, *gathered)


def combine_kernel(place_ref, gate_ref, own_ref, other_ref, *out_refs):
    blocks, _, rows = place_ref.shape
    capacity = own_ref.shape[0] // blocks
    half = own_ref.shape[1] // 2
    slot = lax.broadcasted_iota(jnp.int32, (capacity, rows), 0)
    for block in range(blocks):
        weight = jnp.concatenate(
            [
                jnp.where(
                    place_ref[block, pl.ds(core, 1), :] == slot,
                    gate_ref[block, pl.ds(core, 1), :],
                    0.0,
                )
                for core in range(2)
            ],
            axis=0,
        )
        weight = weight.T.astype(jnp.bfloat16)
        far_x, far_y = block // 2, block % 2
        for side in range(2):
            inner = pl.ds(block * capacity, capacity), pl.ds(side * half, half)
            both = jnp.concatenate([own_ref[inner], other_ref[inner]], axis=0)
            share = jnp.dot(weight, both, preferred_element_type=jnp.float32).astype(jnp.bfloat16)
            sent, place = (far_x, far_y) if side else (far_y, far_x)
            if sent:
                out_refs[3 * side + 2][pl.ds(place * rows, rows), :] = share
            else:
                out_refs[3 * side + place][...] = share


def combine_rows(part, parts, place, gate, own, other):
    blocks, _, rows = place.shape
    half = own.shape[1] // 2
    kept = jax.ShapeDtypeStruct((rows, half), jnp.bfloat16)
    sent = jax.ShapeDtypeStruct((2 * rows, half), jnp.bfloat16)
    count = own.shape[0] // parts
    whole = lambda shape: pl.BlockSpec(shape, lambda j: (0,) * len(shape))
    level = pl.BlockSpec((count, 2 * half), lambda j: (part, 0))
    return pl.pallas_call(
        combine_kernel,
        out_shape=[kept, kept, sent] * 2,
        grid=(1,),
        in_specs=[whole(place.shape), whole(gate.shape), level, level],
        out_specs=[whole(kept.shape), whole(kept.shape), whole(sent.shape)] * 2,
        compiler_params=pltpu.CompilerParams(vmem_limit_bytes=16 * 2**20),
        cost_estimate=pl.CostEstimate(
            flops=8 * count * rows * half,
            bytes_accessed=4 * (blocks * rows + 2 * count) * half,
            transcendentals=0,
        ),
    )(place, gate, own, other)


def routing_start(own_live, expert_ids, gate_values, earlier):
    live_ids = jnp.where(own_live[:, None], expert_ids, -1).astype(jnp.float32)
    routing = after(jnp.concatenate([live_ids, gate_values], axis=1).T, earlier)
    groups = lax.axis_size("grp")
    lines = [routing]
    for hop in range(2, groups, 2):
        lines.append(
            lax.ppermute(routing, "grp", [(g, (g + hop) % groups) for g in range(groups)])
        )
    return jnp.stack(lines)


def routing_pair(routing, swap):
    return jnp.stack([routing, swap(routing)], axis=routing.ndim - 2)


def selections(routing, top_count):
    mine = lax.axis_index(("grp", "sp"))
    depth, rows = routing.shape[0], routing.shape[-1]
    routing = routing.reshape(-1, 2 * top_count, rows)
    ids, gates = routing[:, :top_count].astype(jnp.int32), routing[:, top_count:]
    experts = jnp.stack([mine, mine ^ 1])
    chosen = ids[:, None] == experts[None, :, None, None]
    wanted = jnp.any(chosen, axis=2)
    gate = jnp.sum(jnp.where(chosen, gates[:, None], 0.0), axis=2)
    order = jnp.arange(rows)
    earlier = (order[:, None] < order[None, :]).astype(jnp.bfloat16)
    place = jnp.einsum(
        "bcr,rt->bct", wanted.astype(jnp.bfloat16), earlier, preferred_element_type=jnp.float32
    ).astype(jnp.int32)
    return jnp.where(wanted, place, -1), gate


def expert_kernel(rows_ref, up_gate_ref, down_ref, out_ref, hidden):
    hidden_width, width = down_ref.shape[1], down_ref.shape[2]
    tile = 256
    for start in range(0, hidden_width, tile):
        gate = jnp.dot(
            rows_ref[...],
            up_gate_ref[0, :, start : start + tile],
            preferred_element_type=jnp.float32,
        )
        up = jnp.dot(
            rows_ref[...],
            up_gate_ref[0, :, hidden_width + start : hidden_width + start + tile],
            preferred_element_type=jnp.float32,
        )
        hidden[:, start : start + tile] = (gate / (1.0 + jnp.exp(-gate)) * up).astype(
            jnp.bfloat16
        )
    for start in range(0, width, tile):
        out_ref[:, start : start + tile] = jnp.dot(
            hidden[...], down_ref[0, :, start : start + tile], preferred_element_type=jnp.float32
        ).astype(jnp.bfloat16)


def run_expert(rows, up_gate_weight, down_weight):
    count, width = rows.shape
    hidden_width = down_weight.shape[1]
    return pl.pallas_call(
        expert_kernel,
        out_shape=jax.ShapeDtypeStruct((count, width), jnp.bfloat16),
        scratch_shapes=[pltpu.VMEM((count, hidden_width), jnp.bfloat16)],
        compiler_params=pltpu.CompilerParams(vmem_limit_bytes=20 * 2**20),
        cost_estimate=pl.CostEstimate(
            flops=6 * count * width * hidden_width,
            bytes_accessed=6 * width * hidden_width + 4 * count * width,
            transcendentals=count * hidden_width,
        ),
    )(rows, up_gate_weight, down_weight)


def experts_by_gather(packed, routing, top_count, capacity, up_gate_weight, down_weight):
    depth = lax.axis_size("grp") // 2
    rows = packed.shape[0] // 2
    routing = routing_pair(after(routing, packed), swap_x)
    lines, beside_x, beside_y, diagonal = [packed], [], [], []
    halves = []

    def cross(level, earlier):
        first_x, second_y = halves[level]
        if earlier is not None:
            first_x, second_y = after(first_x, *earlier), after(second_y, *earlier)
        diagonal.append((swap_y(first_x), swap_x(second_y)))

    for level in range(depth):
        line = lines[level]
        if level == 1:
            routing = routing_pair(after(routing, *halves[0]), swap_y)
        if level == 2:
            cross(0, (line, routing))
            cross(1, (line,))
            line = after(line, *diagonal[0], *diagonal[1])
        elif level > 2:
            line = after(line, beside_x[level - 1], beside_y[level - 1])
        beside_x.append(swap_x(line))
        beside_y.append(swap_y(line))
        halves.append((beside_x[level][:rows], beside_y[level][rows:]))
        if level + 1 < depth:
            line = lines[level]
            if level:
                line = after(line, beside_x[level - 1], beside_y[level - 1])
            lines.append(shift_z(line))
    for level in range(len(diagonal), depth):
        cross(level, None)
    if depth == 1:
        routing = routing_pair(routing, swap_y)
    place, gate = selections(routing, top_count)
    per_level = place.shape[0] // depth
    results, kept, sent, back, joined = {}, {}, {}, {}, {}

    def combine(level, *earlier):
        index, count, own_result, other_result = results[level]
        if earlier:
            own_result = after(own_result, *earlier)
        blocks = slice(level * per_level, (level + 1) * per_level)
        parts = combine_rows(index, count, place[blocks], gate[blocks], own_result, other_result)
        first, first_x, first_sent, second, second_y, second_sent = parts
        kept[level] = first, first_x, second, second_y
        sent[level] = first_sent, second_sent

    def send_back(level, *earlier):
        first_sent, second_sent = sent[level]
        if earlier:
            first_sent, second_sent = after(first_sent, *earlier), after(second_sent, *earlier)
        back[level] = swap_y(first_sent), swap_x(second_sent)

    def join(level):
        first, first_x, second, second_y = kept[level]
        first_back, second_back = back[level]
        first, first_x = first + first_back[:rows], first_x + first_back[rows:]
        second, second_y = second + second_back[:rows], second_y + second_back[rows:]
        joined[level] = first, second, swap_x(first_x), swap_y(second_y)

    for start in range(0, depth, 2):
        levels = range(start, min(start + 2, depth))
        gathered = []
        for level in levels:
            gathered += [lines[level], beside_y[level], beside_x[level], *diagonal[level]]
        ahead, last = levels[-1] + 1, levels[-1] + 2
        if start:
            gathered[0] = after(gathered[0], kept[start - 1][0])
        blocks = slice(start * per_level, (start + len(levels)) * per_level)
        own, sibling = pick_rows(capacity, place[blocks], gathered)
        if last < depth:
            sibling = after(sibling, beside_x[ahead], beside_y[ahead], lines[last])
        other = swap_core(sibling)
        other_result = run_expert(other, up_gate_weight, down_weight)
        if last < depth:
            other_result = after(
                other_result, beside_x[last], beside_y[last], *diagonal[ahead]
            )
            own = after(own, other_result)
        if start:
            back[start - 1] = tuple(after(part, other_result) for part in back[start - 1])
            join(start - 1)
            own = after(own, *back[start - 1])
        own_result = run_expert(own, up_gate_weight, down_weight)
        other_result = swap_core(other_result)
        if start:
            own_result = after(own_result, *joined[start - 1])
        for index, level in enumerate(levels):
            results[level] = index, len(levels), own_result, other_result
            if level:
                combine(level)
                send_back(level, *back.get(level - 1, ()))
        for level in levels:
            if level and (ahead >= depth or level < levels[-1]):
                join(level)
    combine(0, *(kept[depth - 1][:1] if depth > 1 else ()))
    send_back(0, *back.get(depth - 1, ()))
    join(0)
    shares = {}
    for level in range(depth):
        first, second, first_far, second_far = joined[level]
        shares[level] = first + first_far, second + second_far
    first, second = shares[0]
    if depth > 1:
        total = jnp.concatenate(shares[1], axis=0)
        for level in range(2, depth):
            total = jnp.concatenate(shares[level], axis=0) + shift_z(total)
        total = shift_z(total)
        first, second = first + total[:rows], second + total[rows:]
    return jnp.concatenate([first, second], axis=1)


def per_device_pairs(
    queries,
    fresh_key_values,
    cache,
    lengths,
    out_weight,
    residual,
    norm_gain,
    expert_ids,
    gate_values,
    up_gate_weight,
    down_weight,
):
    seq_devices = lax.axis_size("sp")
    mine = lax.axis_index("sp")
    slot_rows = queries.shape[0]
    width = cache.shape[-1] // 2
    head_columns = queries.shape[1] // seq_devices
    top_count = expert_ids.shape[1]
    experts = up_gate_weight.shape[0] * lax.axis_size("grp") * seq_devices
    capacity = max(2, 8 * slot_rows * top_count // (5 * experts))
    own_length = lengths[0, 0]
    own_live = jnp.arange(slot_rows, dtype=jnp.int32) < own_length

    def key_values_for(target):
        keys = lax.dynamic_slice(fresh_key_values, (0, target * width), (slot_rows, width))
        values = lax.dynamic_slice(
            fresh_key_values, (0, (seq_devices + target) * width), (slot_rows, width)
        )
        lane = jnp.arange(2 * width, dtype=jnp.int32)[None, :]
        note = jnp.where(lane < width, own_length // 256, own_length % 256)
        note = jnp.broadcast_to(note, (16, 2 * width)).astype(jnp.bfloat16)
        return jnp.concatenate([jnp.concatenate([keys, values], axis=1), note], axis=0)

    def queries_for(target):
        return lax.dynamic_slice(queries, (0, target * head_columns), (slot_rows, head_columns))

    masks = range(1, seq_devices)
    fresh = [key_values_for(mine)] + [xor_group(key_values_for(mine ^ m), m) for m in masks]
    query_blocks = {m: xor_group(queries_for(mine ^ m), m) for m in (3, 1)}
    cache_block = cache[0, 0]

    def share_of(block, query, *earlier):
        heads = attend_block(block, mine[None], query, cache_block, fresh)
        if earlier:
            heads = after(heads, *earlier)
        return jnp.dot(heads, out_weight, preferred_element_type=jnp.float32).astype(jnp.bfloat16)

    own = share_of(0, queries_for(mine))
    query_blocks[2] = xor_group(after(queries_for(mine ^ 2), own), 2)
    far_core = share_of(3, after(query_blocks[3], own), query_blocks[2])
    far = share_of(2, query_blocks[2]) + swap_core(far_core)
    near = share_of(1, after(query_blocks[1], far))
    routing = routing_start(own_live, expert_ids, gate_values, far)
    far = swap_y(far)
    attended, packed = normalize(
        lengths[0], own, swap_core(after(near, far, routing)), far, residual, norm_gain[None, :]
    )
    moe_out = experts_by_gather(
        packed, routing, top_count, capacity, up_gate_weight, down_weight
    )
    return (attended, moe_out)


def per_device(
    queries,
    fresh_key_values,
    cache,
    lengths,
    out_weight,
    residual,
    norm_gain,
    expert_ids,
    gate_values,
    up_gate_weight,
    down_weight,
):
    seq_devices = lax.axis_size("sp")
    slot_rows = queries.shape[0]
    head_width = cache.shape[-1] // 2
    model_width = residual.shape[1]
    kv_heads = fresh_key_values.shape[1] // (2 * head_width)
    repeat = seq_devices // kv_heads
    keys_new = fresh_key_values[:, : kv_heads * head_width].reshape(
        slot_rows, kv_heads, 1, head_width
    )
    values_new = fresh_key_values[:, kv_heads * head_width :].reshape(
        slot_rows, kv_heads, 1, head_width
    )
    paired = jnp.concatenate([keys_new, values_new], axis=3)
    spread = jnp.broadcast_to(paired, (slot_rows, kv_heads, repeat, 2 * head_width)).reshape(
        slot_rows, seq_devices * 2 * head_width
    )
    all_lengths = lax.all_gather(lengths, "sp", axis=1, tiled=True)
    queries_by_head, head_kv = (
        lax.all_to_all(queries, "sp", split_axis=1, concat_axis=0, tiled=True),
        lax.all_to_all(spread, "sp", split_axis=1, concat_axis=0, tiled=True),
    )
    cache_block = cache[0, 0]
    my_index = lax.axis_index("sp")
    for bit_pos in range(repeat.bit_length() - 1):
        partner = partner_2(cache_block, "sp", bit_pos)
        is_upper = my_index // 2**bit_pos % 2 == 1
        cache_block = jnp.where(
            is_upper,
            jnp.concatenate([partner, cache_block], axis=0),
            jnp.concatenate([cache_block, partner], axis=0),
        )
    stretch_lens = all_lengths[0]
    offsets = jnp.cumsum(stretch_lens) - stretch_lens
    rows_of_group = queries_by_head.shape[0]
    slot_ids = jnp.arange(rows_of_group, dtype=jnp.int32)
    source = slot_ids // slot_rows
    within = slot_ids % slot_rows
    from_device = source[:, None] == jnp.arange(seq_devices, dtype=jnp.int32)[None, :]
    is_live = within < jnp.sum(jnp.where(from_device, stretch_lens[None, :], 0), axis=1)
    position = within + jnp.sum(jnp.where(from_device, offsets[None, :], 0), axis=1)
    per_dev = queries_by_head.shape[1] // head_width
    cache_len = cache_block.shape[0]
    key_all = jnp.concatenate([cache_block[:, :head_width], head_kv[:, :head_width]], axis=0)
    value_all = jnp.concatenate([cache_block[:, head_width:], head_kv[:, head_width:]], axis=0)
    block_count = 2 if rows_of_group % 2 == 0 and rows_of_group >= 1024 else 1
    block_rows = rows_of_group // block_count

    def attend(parts):
        query_block, place_block = parts
        scores = jnp.einsum(
            "rhd,kd->hrk", query_block, key_all, preferred_element_type=jnp.float32
        ) / math.sqrt(head_width)
        allowed = jnp.concatenate(
            [
                jnp.ones((block_rows, cache_len), dtype=bool),
                is_live[None, :] & (position[None, :] <= place_block[:, None]),
            ],
            axis=1,
        )
        scores = jnp.where(allowed[None], scores, -jnp.inf)
        row_max = jnp.max(scores, axis=-1, keepdims=True)
        weights = jnp.exp(scores - row_max)
        totals = jnp.sum(weights, axis=-1, keepdims=True)
        result = (
            jnp.einsum(
                "hrk,kd->hrd",
                weights.astype(jnp.bfloat16),
                value_all,
                preferred_element_type=jnp.float32,
            )
            / totals
        )
        return (
            result.astype(jnp.bfloat16).transpose(1, 0, 2).reshape(block_rows, per_dev * head_width)
        )

    attn_heads = lax.map(
        attend,
        (
            queries_by_head.reshape(block_count, block_rows, per_dev, head_width),
            position.reshape(block_count, block_rows),
        ),
    ).reshape(rows_of_group, per_dev * head_width)
    attn_sum = lax.psum_scatter(
        jnp.dot(attn_heads, out_weight, preferred_element_type=jnp.float32).astype(jnp.bfloat16),
        "sp",
        scatter_dimension=0,
        tiled=True,
    ).astype(jnp.float32)
    own_live = jnp.arange(slot_rows, dtype=jnp.int32) < lengths[0, 0]
    attended = jnp.where(own_live[:, None], attn_sum, 0.0).astype(jnp.bfloat16)
    mixed_rows = residual.astype(jnp.float32) + attn_sum
    normed = (
        mixed_rows
        * lax.rsqrt(jnp.mean(mixed_rows * mixed_rows, axis=-1, keepdims=True) + 1e-06)
        * norm_gain
    ).astype(jnp.bfloat16)
    group_count = lax.axis_size("grp")
    experts = up_gate_weight.shape[0] * group_count * seq_devices
    top_count = expert_ids.shape[1]
    capacity = max(2, 8 * slot_rows * top_count // (5 * experts))
    hidden_width = down_weight.shape[1]
    choose = expert_ids[:, :, None] == jnp.arange(experts, dtype=jnp.int32)[None, None, :]
    routed = (jnp.any(choose, axis=1) & own_live[:, None]).astype(jnp.float32)
    earlier = (jnp.arange(slot_rows)[:, None] > jnp.arange(slot_rows)[None, :]).astype(jnp.float32)
    prefix = jnp.dot(earlier, routed, precision=lax.Precision.HIGHEST)
    slot_in = jnp.sum(jnp.where(choose, prefix[:, None, :], 0.0), axis=2).astype(jnp.int32)
    dump_slot = experts * capacity
    target = jnp.where(own_live[:, None], expert_ids * capacity + slot_in, dump_slot)
    source_rows = (
        jnp.full((dump_slot + 1,), slot_rows, jnp.int32)
        .at[target.reshape(-1)]
        .set(jnp.repeat(jnp.arange(slot_rows, dtype=jnp.int32), top_count))[:dump_slot]
    )
    padded = jnp.concatenate([normed, jnp.zeros((1, model_width), jnp.bfloat16)], axis=0)
    outgoing = padded[source_rows].reshape(experts, capacity, model_width)
    received = lax.all_to_all(outgoing, ("grp", "sp"), split_axis=0, concat_axis=0, tiled=True)
    flat_rows = received.reshape(-1, model_width)
    projected = jnp.dot(flat_rows, up_gate_weight[0], preferred_element_type=jnp.float32)
    hidden = (jax.nn.silu(projected[:, :hidden_width]) * projected[:, hidden_width:]).astype(
        jnp.bfloat16
    )
    returned = lax.all_to_all(
        jnp.dot(hidden, down_weight[0], preferred_element_type=jnp.float32)
        .astype(jnp.bfloat16)
        .reshape(received.shape),
        ("grp", "sp"),
        split_axis=0,
        concat_axis=0,
        tiled=True,
    )
    back_rows = jnp.concatenate(
        [returned.reshape(dump_slot, model_width), jnp.zeros((1, model_width), jnp.bfloat16)],
        axis=0,
    )
    picked = back_rows[target]
    combined = jnp.sum(gate_values[:, :, None] * picked.astype(jnp.float32), axis=1)
    moe_out = jnp.where(own_live[:, None], combined, 0.0).astype(jnp.bfloat16)
    return (attended, moe_out)


def solution(mesh):
    in_specs = (
        P(("grp", "sp"), None),
        P(("grp", "sp"), None),
        P("grp", "sp", None, None),
        P("grp", "sp"),
        P("sp", None),
        P(("grp", "sp"), None),
        P(),
        P(("grp", "sp"), None),
        P(("grp", "sp"), None),
        P(("grp", "sp"), None, None),
        P(("grp", "sp"), None, None),
    )
    out_specs = (P(("grp", "sp"), None), P(("grp", "sp"), None))
    groups, seq_devices = mesh.shape["grp"], mesh.shape["sp"]

    def run(*args):
        kv_heads = args[1].shape[1] // args[2].shape[-1]
        experts, top_count = args[9].shape[0], args[7].shape[1]
        pairs = seq_devices == kv_heads == 4 and groups % 2 == 0 and experts <= 4 * top_count
        return mapped(per_device_pairs if pairs else per_device)(*args)

    def mapped(body):
        return jax.shard_map(
            body, mesh=mesh, in_specs=in_specs, out_specs=out_specs, check_vma=False
        )

    return run
```

```python
import functools
import math

import jax
import jax.numpy as jnp
from jax import lax
from jax.experimental import pallas as pl
from jax.experimental.pallas import tpu as pltpu
from jax.sharding import PartitionSpec as P


def partner_2(value, axis, bit):
    mask = 2**bit
    pairs = [(source, source ^ mask) for source in range(lax.axis_size(axis))]
    return lax.ppermute(value, axis, pairs)


def shift_z(value):
    groups = lax.axis_size("grp")
    return lax.ppermute(value, "grp", [(g, (g + 2) % groups) for g in range(groups)])


def swap_x(value):
    return partner_2(value, "grp", 0)


def swap_y(value):
    return partner_2(value, "sp", 1)


def swap_core(value):
    return partner_2(value, "sp", 0)


def after(value, *earlier):
    return lax.optimization_barrier((value, *earlier))[0]


def xor_group(value, mask):
    return lax.ppermute(value, "sp", [(s, s ^ mask) for s in range(lax.axis_size("sp"))])


def attend_kernel(index, mine_ref, query_ref, cache_ref, *refs):
    fresh_refs, (out_ref, keys, values, bias) = refs[:-4], refs[-4:]
    rows = query_ref.shape[0]
    cached, width = cache_ref.shape[0], cache_ref.shape[1] // 2
    keys[:cached, :] = cache_ref[:, :width]
    values[:cached, :] = cache_ref[:, width:]
    lengths = []
    for block, fresh_ref in enumerate(fresh_refs):
        places = pl.ds(cached + block * rows, rows)
        keys[places, :] = fresh_ref[:rows, :width]
        values[places, :] = fresh_ref[:rows, width:]
        note = fresh_ref[rows : rows + 16, :].astype(jnp.float32)
        lengths.append(note[:1, :1] * 256.0 + note[:1, width : width + 1])
    mine = mine_ref[0]
    offsets = []
    for block in range(len(fresh_refs)):
        offset = jnp.zeros((1, 1), jnp.float32)
        for other in range(len(fresh_refs)):
            before = (mine ^ other) < (mine ^ block)
            offset = offset + lengths[other] * before.astype(jnp.float32)
        offsets.append(offset)
    column = lax.broadcasted_iota(jnp.int32, (1, bias.shape[1]), 1)
    key_place = jnp.zeros((1, bias.shape[1]), jnp.float32)
    for block in range(len(fresh_refs)):
        within = (column - block * rows).astype(jnp.float32)
        place = jnp.where(within < lengths[block], within + offsets[block], 1e9)
        key_place = jnp.where(column >= block * rows, place, key_place)
    row_place = lax.broadcasted_iota(jnp.int32, bias.shape, 0).astype(jnp.float32) + offsets[index]
    bias[...] = jnp.where(key_place <= row_place, 0.0, -1e30)
    scale = math.log2(math.e) / math.sqrt(width)
    for head in range(query_ref.shape[1] // width):
        columns = pl.ds(head * width, width)
        scores = lax.dot_general(
            query_ref[:, columns],
            keys[...],
            (((1,), (1,)), ((), ())),
            preferred_element_type=jnp.float32,
        )
        old, new = scores[:, :cached] * scale, scores[:, cached:] * scale + bias[...]
        row_max = jnp.maximum(
            jnp.max(old, axis=1, keepdims=True), jnp.max(new, axis=1, keepdims=True)
        )
        old, new = jnp.exp2(old - row_max), jnp.exp2(new - row_max)
        totals = jnp.sum(old, axis=1, keepdims=True) + jnp.sum(new, axis=1, keepdims=True)
        result = jnp.dot(
            old.astype(jnp.bfloat16), values[:cached, :], preferred_element_type=jnp.float32
        ) + jnp.dot(
            new.astype(jnp.bfloat16), values[cached:, :], preferred_element_type=jnp.float32
        )
        out_ref[:, columns] = (result / totals).astype(jnp.bfloat16)


def attend_block(index, mine, query, cache_block, fresh):
    rows, columns = query.shape
    cached, width = cache_block.shape[0], cache_block.shape[1] // 2
    new = rows * len(fresh)
    inside = pl.BlockSpec(memory_space=pltpu.VMEM)
    return pl.pallas_call(
        functools.partial(attend_kernel, index),
        out_shape=jax.ShapeDtypeStruct((rows, columns), jnp.bfloat16),
        in_specs=[pl.BlockSpec(memory_space=pltpu.SMEM)] + [inside] * (2 + len(fresh)),
        out_specs=inside,
        scratch_shapes=[
            pltpu.VMEM((cached + new, width), jnp.bfloat16),
            pltpu.VMEM((cached + new, width), jnp.bfloat16),
            pltpu.VMEM((rows, new), jnp.float32),
        ],
        compiler_params=pltpu.CompilerParams(vmem_limit_bytes=12 * 2**20),
        cost_estimate=pl.CostEstimate(
            flops=4 * rows * columns * (cached + new),
            bytes_accessed=4 * (rows * columns + (cached + new) * width),
            transcendentals=rows * columns // width * (cached + new),
        ),
    )(mine, query, cache_block, *fresh)


def norm_kernel(
    length_ref,
    own_ref,
    core_ref,
    far_ref,
    residual_ref,
    gain_ref,
    attended_ref,
    packed_ref,
):
    attn_sum = (
        own_ref[...].astype(jnp.float32)
        + core_ref[...].astype(jnp.float32)
        + far_ref[...].astype(jnp.float32)
    )
    live = lax.broadcasted_iota(jnp.int32, attn_sum.shape, 0) < length_ref[0]
    attended_ref[...] = jnp.where(live, attn_sum, 0.0).astype(jnp.bfloat16)
    mixed = residual_ref[...].astype(jnp.float32) + attn_sum
    scale = lax.rsqrt(jnp.mean(mixed * mixed, axis=1, keepdims=True) + 1e-06)
    normed = (mixed * scale * gain_ref[...]).astype(jnp.bfloat16)
    rows, half = packed_ref.shape[0] // 2, packed_ref.shape[1]
    packed_ref[:rows, :] = normed[:, :half]
    packed_ref[rows:, :] = normed[:, half:]


def normalize(length, own, core, far, residual, gain):
    rows, width = own.shape
    packed = jax.ShapeDtypeStruct((2 * rows, width // 2), jnp.bfloat16)
    inside = pl.BlockSpec(memory_space=pltpu.VMEM)
    return pl.pallas_call(
        norm_kernel,
        out_shape=(jax.ShapeDtypeStruct((rows, width), jnp.bfloat16), packed),
        in_specs=[pl.BlockSpec(memory_space=pltpu.SMEM)] + [inside] * 5,
        out_specs=(inside, inside),
        compiler_params=pltpu.CompilerParams(vmem_limit_bytes=12 * 2**20),
        cost_estimate=pl.CostEstimate(
            flops=10 * rows * width, bytes_accessed=12 * rows * width, transcendentals=rows
        ),
    )(length, own, core, far, residual, gain)


def pick_kernel(capacity, place_ref, *refs):
    blocks, _, rows = place_ref.shape
    own_ref, sibling_ref = refs[-2:]
    half = own_ref.shape[1] // 2
    slot = lax.broadcasted_iota(jnp.int32, (capacity, rows), 0)
    for block in range(blocks):
        pick = jnp.concatenate(
            [(place_ref[block, pl.ds(core, 1), :] == slot) for core in range(2)], axis=0
        )
        pick = jnp.where(pick, 1.0, 0.0).astype(jnp.bfloat16)
        level, spot = block // 4, block % 4
        for side in range(2):
            if spot < 3:
                source = refs[5 * level + spot][pl.ds(side * rows, rows), :]
            else:
                source = refs[5 * level + 3 + side][...]
            chosen = jnp.dot(pick, source, preferred_element_type=jnp.float32)
            chosen = chosen.astype(jnp.bfloat16)
            inner = pl.ds(block * capacity, capacity), pl.ds(side * half, half)
            own_ref[inner] = chosen[:capacity]
            sibling_ref[inner] = chosen[capacity:]


def pick_rows(capacity, place, gathered):
    blocks, _, rows = place.shape
    half = gathered[0].shape[1]
    shape = jax.ShapeDtypeStruct((blocks * capacity, 2 * half), jnp.bfloat16)
    return pl.pallas_call(
        functools.partial(pick_kernel, capacity),
        out_shape=(shape, shape),
        compiler_params=pltpu.CompilerParams(vmem_limit_bytes=20 * 2**20),
        cost_estimate=pl.CostEstimate(
            flops=8 * blocks * capacity * rows * half,
            bytes_accessed=4 * blocks * (rows + 2 * capacity) * half,
            transcendentals=0,
        ),
    )(place, *gathered)


def combine_kernel(place_ref, gate_ref, own_ref, other_ref, *out_refs):
    blocks, _, rows = place_ref.shape
    capacity = own_ref.shape[0] // blocks
    half = own_ref.shape[1] // 2
    slot = lax.broadcasted_iota(jnp.int32, (capacity, rows), 0)
    for block in range(blocks):
        weight = jnp.concatenate(
            [
                jnp.where(
                    place_ref[block, pl.ds(core, 1), :] == slot,
                    gate_ref[block, pl.ds(core, 1), :],
                    0.0,
                )
                for core in range(2)
            ],
            axis=0,
        )
        weight = weight.T.astype(jnp.bfloat16)
        far_x, far_y = block // 2, block % 2
        for side in range(2):
            inner = pl.ds(block * capacity, capacity), pl.ds(side * half, half)
            both = jnp.concatenate([own_ref[inner], other_ref[inner]], axis=0)
            share = jnp.dot(weight, both, preferred_element_type=jnp.float32).astype(jnp.bfloat16)
            sent, place = (far_x, far_y) if side else (far_y, far_x)
            if sent:
                out_refs[3 * side + 2][pl.ds(place * rows, rows), :] = share
            else:
                out_refs[3 * side + place][...] = share


def combine_rows(part, parts, place, gate, own, other):
    blocks, _, rows = place.shape
    half = own.shape[1] // 2
    kept = jax.ShapeDtypeStruct((rows, half), jnp.bfloat16)
    sent = jax.ShapeDtypeStruct((2 * rows, half), jnp.bfloat16)
    count = own.shape[0] // parts
    whole = lambda shape: pl.BlockSpec(shape, lambda j: (0,) * len(shape))
    level = pl.BlockSpec((count, 2 * half), lambda j: (part, 0))
    return pl.pallas_call(
        combine_kernel,
        out_shape=[kept, kept, sent] * 2,
        grid=(1,),
        in_specs=[whole(place.shape), whole(gate.shape), level, level],
        out_specs=[whole(kept.shape), whole(kept.shape), whole(sent.shape)] * 2,
        compiler_params=pltpu.CompilerParams(vmem_limit_bytes=16 * 2**20),
        cost_estimate=pl.CostEstimate(
            flops=8 * count * rows * half,
            bytes_accessed=4 * (blocks * rows + 2 * count) * half,
            transcendentals=0,
        ),
    )(place, gate, own, other)


def routing_start(own_live, expert_ids, gate_values, earlier):
    live_ids = jnp.where(own_live[:, None], expert_ids, -1).astype(jnp.float32)
    routing = after(jnp.concatenate([live_ids, gate_values], axis=1).T, earlier)
    groups = lax.axis_size("grp")
    lines = [routing]
    for hop in range(2, groups, 2):
        lines.append(
            lax.ppermute(routing, "grp", [(g, (g + hop) % groups) for g in range(groups)])
        )
    return jnp.stack(lines)


def routing_pair(routing, swap):
    return jnp.stack([routing, swap(routing)], axis=routing.ndim - 2)


def selections(routing, top_count):
    mine = lax.axis_index(("grp", "sp"))
    depth, rows = routing.shape[0], routing.shape[-1]
    routing = routing.reshape(-1, 2 * top_count, rows)
    ids, gates = routing[:, :top_count].astype(jnp.int32), routing[:, top_count:]
    experts = jnp.stack([mine, mine ^ 1])
    chosen = ids[:, None] == experts[None, :, None, None]
    wanted = jnp.any(chosen, axis=2)
    gate = jnp.sum(jnp.where(chosen, gates[:, None], 0.0), axis=2)
    order = jnp.arange(rows)
    earlier = (order[:, None] < order[None, :]).astype(jnp.bfloat16)
    place = jnp.einsum(
        "bcr,rt->bct", wanted.astype(jnp.bfloat16), earlier, preferred_element_type=jnp.float32
    ).astype(jnp.int32)
    return jnp.where(wanted, place, -1), gate


def expert_kernel(rows_ref, up_gate_ref, down_ref, out_ref, hidden):
    hidden_width, width = down_ref.shape[1], down_ref.shape[2]
    tile = 256
    for start in range(0, hidden_width, tile):
        gate = jnp.dot(
            rows_ref[...],
            up_gate_ref[0, :, start : start + tile],
            preferred_element_type=jnp.float32,
        )
        up = jnp.dot(
            rows_ref[...],
            up_gate_ref[0, :, hidden_width + start : hidden_width + start + tile],
            preferred_element_type=jnp.float32,
        )
        hidden[:, start : start + tile] = (gate / (1.0 + jnp.exp(-gate)) * up).astype(
            jnp.bfloat16
        )
    for start in range(0, width, tile):
        out_ref[:, start : start + tile] = jnp.dot(
            hidden[...], down_ref[0, :, start : start + tile], preferred_element_type=jnp.float32
        ).astype(jnp.bfloat16)


def run_expert(rows, up_gate_weight, down_weight):
    count, width = rows.shape
    hidden_width = down_weight.shape[1]
    return pl.pallas_call(
        expert_kernel,
        out_shape=jax.ShapeDtypeStruct((count, width), jnp.bfloat16),
        scratch_shapes=[pltpu.VMEM((count, hidden_width), jnp.bfloat16)],
        compiler_params=pltpu.CompilerParams(vmem_limit_bytes=20 * 2**20),
        cost_estimate=pl.CostEstimate(
            flops=6 * count * width * hidden_width,
            bytes_accessed=6 * width * hidden_width + 4 * count * width,
            transcendentals=count * hidden_width,
        ),
    )(rows, up_gate_weight, down_weight)


def experts_by_gather(packed, routing, top_count, capacity, up_gate_weight, down_weight):
    depth = lax.axis_size("grp") // 2
    rows = packed.shape[0] // 2
    routing = routing_pair(after(routing, packed), swap_x)
    lines, beside_x, beside_y, diagonal = [packed], [], [], []
    halves = []

    def cross(level, earlier):
        first_x, second_y = halves[level]
        if earlier is not None:
            first_x, second_y = after(first_x, *earlier), after(second_y, *earlier)
        diagonal.append((swap_y(first_x), swap_x(second_y)))

    for level in range(depth):
        line = lines[level]
        if level == 1:
            line = after(line, routing)
            routing = routing_pair(after(routing, *halves[0]), swap_y)
        if level == 2:
            cross(0, (line, routing))
            cross(1, (line,))
            line = after(line, *diagonal[0], *diagonal[1])
        elif level > 2:
            line = after(line, beside_x[level - 1], beside_y[level - 1])
        beside_x.append(swap_x(line))
        beside_y.append(swap_y(line))
        halves.append((beside_x[level][:rows], beside_y[level][rows:]))
        if level + 1 < depth:
            line = lines[level]
            if level:
                line = after(line, beside_x[level - 1], beside_y[level - 1])
            lines.append(shift_z(line))
    for level in range(len(diagonal), depth):
        cross(level, None)
    if depth == 1:
        routing = routing_pair(routing, swap_y)
    place, gate = selections(routing, top_count)
    per_level = place.shape[0] // depth
    results, kept, sent, back, joined = {}, {}, {}, {}, {}

    def combine(level, *earlier):
        index, count, own_result, other_result = results[level]
        if earlier:
            own_result = after(own_result, *earlier)
        blocks = slice(level * per_level, (level + 1) * per_level)
        parts = combine_rows(index, count, place[blocks], gate[blocks], own_result, other_result)
        first, first_x, first_sent, second, second_y, second_sent = parts
        kept[level] = first, first_x, second, second_y
        sent[level] = first_sent, second_sent

    def send_back(level, *earlier):
        first_sent, second_sent = sent[level]
        if earlier:
            first_sent, second_sent = after(first_sent, *earlier), after(second_sent, *earlier)
        back[level] = swap_y(first_sent), swap_x(second_sent)

    def join(level):
        first, first_x, second, second_y = kept[level]
        first_back, second_back = back[level]
        first, first_x = first + first_back[:rows], first_x + first_back[rows:]
        second, second_y = second + second_back[:rows], second_y + second_back[rows:]
        joined[level] = first, second, swap_x(first_x), swap_y(second_y)

    for start in range(0, depth, 2):
        levels = range(start, min(start + 2, depth))
        gathered = []
        for level in levels:
            gathered += [lines[level], beside_y[level], beside_x[level], *diagonal[level]]
        ahead, last = levels[-1] + 1, levels[-1] + 2
        if start:
            gathered[0] = after(gathered[0], kept[start - 1][0])
        blocks = slice(start * per_level, (start + len(levels)) * per_level)
        own, sibling = pick_rows(capacity, place[blocks], gathered)
        if last < depth:
            sibling = after(sibling, beside_x[ahead], beside_y[ahead], lines[last])
        other = swap_core(sibling)
        other_result = run_expert(other, up_gate_weight, down_weight)
        if last < depth:
            other_result = after(
                other_result, beside_x[last], beside_y[last], *diagonal[ahead]
            )
            own = after(own, other_result)
        if start:
            back[start - 1] = tuple(after(part, other_result) for part in back[start - 1])
            join(start - 1)
            own = after(own, *back[start - 1])
        own_result = run_expert(own, up_gate_weight, down_weight)
        other_result = swap_core(other_result)
        if start:
            own_result = after(own_result, *joined[start - 1])
        for index, level in enumerate(levels):
            results[level] = index, len(levels), own_result, other_result
            if level:
                combine(level)
                send_back(level, *back.get(level - 1, ()))
        for level in levels:
            if level and (ahead >= depth or level < levels[-1]):
                join(level)
    combine(0, *(kept[depth - 1][:1] if depth > 1 else ()))
    send_back(0, *back.get(depth - 1, ()))
    join(0)
    shares = {}
    for level in range(depth):
        first, second, first_far, second_far = joined[level]
        shares[level] = first + first_far, second + second_far
    first, second = shares[0]
    if depth > 1:
        total = jnp.concatenate(shares[1], axis=0)
        for level in range(2, depth):
            total = jnp.concatenate(shares[level], axis=0) + shift_z(total)
        total = shift_z(total)
        first, second = first + total[:rows], second + total[rows:]
    return jnp.concatenate([first, second], axis=1)


def per_device_pairs(
    queries,
    fresh_key_values,
    cache,
    lengths,
    out_weight,
    residual,
    norm_gain,
    expert_ids,
    gate_values,
    up_gate_weight,
    down_weight,
):
    seq_devices = lax.axis_size("sp")
    mine = lax.axis_index("sp")
    slot_rows = queries.shape[0]
    width = cache.shape[-1] // 2
    head_columns = queries.shape[1] // seq_devices
    top_count = expert_ids.shape[1]
    experts = up_gate_weight.shape[0] * lax.axis_size("grp") * seq_devices
    capacity = max(2, 8 * slot_rows * top_count // (5 * experts))
    own_length = lengths[0, 0]
    own_live = jnp.arange(slot_rows, dtype=jnp.int32) < own_length

    def key_values_for(target):
        keys = lax.dynamic_slice(fresh_key_values, (0, target * width), (slot_rows, width))
        values = lax.dynamic_slice(
            fresh_key_values, (0, (seq_devices + target) * width), (slot_rows, width)
        )
        lane = jnp.arange(2 * width, dtype=jnp.int32)[None, :]
        note = jnp.where(lane < width, own_length // 256, own_length % 256)
        note = jnp.broadcast_to(note, (16, 2 * width)).astype(jnp.bfloat16)
        return jnp.concatenate([jnp.concatenate([keys, values], axis=1), note], axis=0)

    def queries_for(target):
        return lax.dynamic_slice(queries, (0, target * head_columns), (slot_rows, head_columns))

    masks = range(1, seq_devices)
    fresh = [key_values_for(mine)] + [xor_group(key_values_for(mine ^ m), m) for m in masks]
    query_blocks = {m: xor_group(queries_for(mine ^ m), m) for m in (3, 1)}
    cache_block = cache[0, 0]

    def share_of(block, query, *earlier):
        heads = attend_block(block, mine[None], query, cache_block, fresh)
        if earlier:
            heads = after(heads, *earlier)
        return jnp.dot(heads, out_weight, preferred_element_type=jnp.float32).astype(jnp.bfloat16)

    own = share_of(0, queries_for(mine))
    query_blocks[2] = xor_group(after(queries_for(mine ^ 2), own), 2)
    far_core = share_of(3, after(query_blocks[3], own), query_blocks[2])
    far = share_of(2, query_blocks[2]) + swap_core(far_core)
    near = share_of(1, after(query_blocks[1], far))
    routing = routing_start(own_live, expert_ids, gate_values, far)
    far = swap_y(far)
    attended, packed = normalize(
        lengths[0], own, swap_core(after(near, far, routing)), far, residual, norm_gain[None, :]
    )
    moe_out = experts_by_gather(
        packed, routing, top_count, capacity, up_gate_weight, down_weight
    )
    return (attended, moe_out)


def per_device(
    queries,
    fresh_key_values,
    cache,
    lengths,
    out_weight,
    residual,
    norm_gain,
    expert_ids,
    gate_values,
    up_gate_weight,
    down_weight,
):
    seq_devices = lax.axis_size("sp")
    slot_rows = queries.shape[0]
    head_width = cache.shape[-1] // 2
    model_width = residual.shape[1]
    kv_heads = fresh_key_values.shape[1] // (2 * head_width)
    repeat = seq_devices // kv_heads
    keys_new = fresh_key_values[:, : kv_heads * head_width].reshape(
        slot_rows, kv_heads, 1, head_width
    )
    values_new = fresh_key_values[:, kv_heads * head_width :].reshape(
        slot_rows, kv_heads, 1, head_width
    )
    paired = jnp.concatenate([keys_new, values_new], axis=3)
    spread = jnp.broadcast_to(paired, (slot_rows, kv_heads, repeat, 2 * head_width)).reshape(
        slot_rows, seq_devices * 2 * head_width
    )
    all_lengths = lax.all_gather(lengths, "sp", axis=1, tiled=True)
    queries_by_head, head_kv = (
        lax.all_to_all(queries, "sp", split_axis=1, concat_axis=0, tiled=True),
        lax.all_to_all(spread, "sp", split_axis=1, concat_axis=0, tiled=True),
    )
    cache_block = cache[0, 0]
    my_index = lax.axis_index("sp")
    for bit_pos in range(repeat.bit_length() - 1):
        partner = partner_2(cache_block, "sp", bit_pos)
        is_upper = my_index // 2**bit_pos % 2 == 1
        cache_block = jnp.where(
            is_upper,
            jnp.concatenate([partner, cache_block], axis=0),
            jnp.concatenate([cache_block, partner], axis=0),
        )
    stretch_lens = all_lengths[0]
    offsets = jnp.cumsum(stretch_lens) - stretch_lens
    rows_of_group = queries_by_head.shape[0]
    slot_ids = jnp.arange(rows_of_group, dtype=jnp.int32)
    source = slot_ids // slot_rows
    within = slot_ids % slot_rows
    from_device = source[:, None] == jnp.arange(seq_devices, dtype=jnp.int32)[None, :]
    is_live = within < jnp.sum(jnp.where(from_device, stretch_lens[None, :], 0), axis=1)
    position = within + jnp.sum(jnp.where(from_device, offsets[None, :], 0), axis=1)
    per_dev = queries_by_head.shape[1] // head_width
    cache_len = cache_block.shape[0]
    key_all = jnp.concatenate([cache_block[:, :head_width], head_kv[:, :head_width]], axis=0)
    value_all = jnp.concatenate([cache_block[:, head_width:], head_kv[:, head_width:]], axis=0)
    block_count = 2 if rows_of_group % 2 == 0 and rows_of_group >= 1024 else 1
    block_rows = rows_of_group // block_count

    def attend(parts):
        query_block, place_block = parts
        scores = jnp.einsum(
            "rhd,kd->hrk", query_block, key_all, preferred_element_type=jnp.float32
        ) / math.sqrt(head_width)
        allowed = jnp.concatenate(
            [
                jnp.ones((block_rows, cache_len), dtype=bool),
                is_live[None, :] & (position[None, :] <= place_block[:, None]),
            ],
            axis=1,
        )
        scores = jnp.where(allowed[None], scores, -jnp.inf)
        row_max = jnp.max(scores, axis=-1, keepdims=True)
        weights = jnp.exp(scores - row_max)
        totals = jnp.sum(weights, axis=-1, keepdims=True)
        result = (
            jnp.einsum(
                "hrk,kd->hrd",
                weights.astype(jnp.bfloat16),
                value_all,
                preferred_element_type=jnp.float32,
            )
            / totals
        )
        return (
            result.astype(jnp.bfloat16).transpose(1, 0, 2).reshape(block_rows, per_dev * head_width)
        )

    attn_heads = lax.map(
        attend,
        (
            queries_by_head.reshape(block_count, block_rows, per_dev, head_width),
            position.reshape(block_count, block_rows),
        ),
    ).reshape(rows_of_group, per_dev * head_width)
    attn_sum = lax.psum_scatter(
        jnp.dot(attn_heads, out_weight, preferred_element_type=jnp.float32).astype(jnp.bfloat16),
        "sp",
        scatter_dimension=0,
        tiled=True,
    ).astype(jnp.float32)
    own_live = jnp.arange(slot_rows, dtype=jnp.int32) < lengths[0, 0]
    attended = jnp.where(own_live[:, None], attn_sum, 0.0).astype(jnp.bfloat16)
    mixed_rows = residual.astype(jnp.float32) + attn_sum
    normed = (
        mixed_rows
        * lax.rsqrt(jnp.mean(mixed_rows * mixed_rows, axis=-1, keepdims=True) + 1e-06)
        * norm_gain
    ).astype(jnp.bfloat16)
    group_count = lax.axis_size("grp")
    experts = up_gate_weight.shape[0] * group_count * seq_devices
    top_count = expert_ids.shape[1]
    capacity = max(2, 8 * slot_rows * top_count // (5 * experts))
    hidden_width = down_weight.shape[1]
    choose = expert_ids[:, :, None] == jnp.arange(experts, dtype=jnp.int32)[None, None, :]
    routed = (jnp.any(choose, axis=1) & own_live[:, None]).astype(jnp.float32)
    earlier = (jnp.arange(slot_rows)[:, None] > jnp.arange(slot_rows)[None, :]).astype(jnp.float32)
    prefix = jnp.dot(earlier, routed, precision=lax.Precision.HIGHEST)
    slot_in = jnp.sum(jnp.where(choose, prefix[:, None, :], 0.0), axis=2).astype(jnp.int32)
    dump_slot = experts * capacity
    target = jnp.where(own_live[:, None], expert_ids * capacity + slot_in, dump_slot)
    source_rows = (
        jnp.full((dump_slot + 1,), slot_rows, jnp.int32)
        .at[target.reshape(-1)]
        .set(jnp.repeat(jnp.arange(slot_rows, dtype=jnp.int32), top_count))[:dump_slot]
    )
    padded = jnp.concatenate([normed, jnp.zeros((1, model_width), jnp.bfloat16)], axis=0)
    outgoing = padded[source_rows].reshape(experts, capacity, model_width)
    received = lax.all_to_all(outgoing, ("grp", "sp"), split_axis=0, concat_axis=0, tiled=True)
    flat_rows = received.reshape(-1, model_width)
    projected = jnp.dot(flat_rows, up_gate_weight[0], preferred_element_type=jnp.float32)
    hidden = (jax.nn.silu(projected[:, :hidden_width]) * projected[:, hidden_width:]).astype(
        jnp.bfloat16
    )
    returned = lax.all_to_all(
        jnp.dot(hidden, down_weight[0], preferred_element_type=jnp.float32)
        .astype(jnp.bfloat16)
        .reshape(received.shape),
        ("grp", "sp"),
        split_axis=0,
        concat_axis=0,
        tiled=True,
    )
    back_rows = jnp.concatenate(
        [returned.reshape(dump_slot, model_width), jnp.zeros((1, model_width), jnp.bfloat16)],
        axis=0,
    )
    picked = back_rows[target]
    combined = jnp.sum(gate_values[:, :, None] * picked.astype(jnp.float32), axis=1)
    moe_out = jnp.where(own_live[:, None], combined, 0.0).astype(jnp.bfloat16)
    return (attended, moe_out)


def solution(mesh):
    in_specs = (
        P(("grp", "sp"), None),
        P(("grp", "sp"), None),
        P("grp", "sp", None, None),
        P("grp", "sp"),
        P("sp", None),
        P(("grp", "sp"), None),
        P(),
        P(("grp", "sp"), None),
        P(("grp", "sp"), None),
        P(("grp", "sp"), None, None),
        P(("grp", "sp"), None, None),
    )
    out_specs = (P(("grp", "sp"), None), P(("grp", "sp"), None))
    groups, seq_devices = mesh.shape["grp"], mesh.shape["sp"]

    def run(*args):
        kv_heads = args[1].shape[1] // args[2].shape[-1]
        experts, top_count = args[9].shape[0], args[7].shape[1]
        pairs = seq_devices == kv_heads == 4 and groups % 2 == 0 and experts <= 4 * top_count
        return mapped(per_device_pairs if pairs else per_device)(*args)

    def mapped(body):
        return jax.shard_map(
            body, mesh=mesh, in_specs=in_specs, out_specs=out_specs, check_vma=False
        )

    return run
```

```python
import functools
import math

import jax
import jax.numpy as jnp
from jax import lax
from jax.experimental import pallas as pl
from jax.experimental.pallas import tpu as pltpu
from jax.sharding import PartitionSpec as P


def partner_2(value, axis, bit):
    mask = 2**bit
    pairs = [(source, source ^ mask) for source in range(lax.axis_size(axis))]
    return lax.ppermute(value, axis, pairs)


def shift_z(value):
    groups = lax.axis_size("grp")
    return lax.ppermute(value, "grp", [(g, (g + 2) % groups) for g in range(groups)])


def swap_x(value):
    return partner_2(value, "grp", 0)


def swap_y(value):
    return partner_2(value, "sp", 1)


def swap_core(value):
    return partner_2(value, "sp", 0)


def after(value, *earlier):
    return lax.optimization_barrier((value, *earlier))[0]


def xor_group(value, mask):
    return lax.ppermute(value, "sp", [(s, s ^ mask) for s in range(lax.axis_size("sp"))])


def attend_kernel(index, mine_ref, query_ref, cache_ref, *refs):
    fresh_refs, (out_ref, keys, values, bias) = refs[:-4], refs[-4:]
    rows = query_ref.shape[0]
    cached, width = cache_ref.shape[0], cache_ref.shape[1] // 2
    keys[:cached, :] = cache_ref[:, :width]
    values[:cached, :] = cache_ref[:, width:]
    lengths = []
    for block, fresh_ref in enumerate(fresh_refs):
        places = pl.ds(cached + block * rows, rows)
        keys[places, :] = fresh_ref[:rows, :width]
        values[places, :] = fresh_ref[:rows, width:]
        note = fresh_ref[rows : rows + 16, :].astype(jnp.float32)
        lengths.append(note[:1, :1] * 256.0 + note[:1, width : width + 1])
    mine = mine_ref[0]
    offsets = []
    for block in range(len(fresh_refs)):
        offset = jnp.zeros((1, 1), jnp.float32)
        for other in range(len(fresh_refs)):
            before = (mine ^ other) < (mine ^ block)
            offset = offset + lengths[other] * before.astype(jnp.float32)
        offsets.append(offset)
    column = lax.broadcasted_iota(jnp.int32, (1, bias.shape[1]), 1)
    key_place = jnp.zeros((1, bias.shape[1]), jnp.float32)
    for block in range(len(fresh_refs)):
        within = (column - block * rows).astype(jnp.float32)
        place = jnp.where(within < lengths[block], within + offsets[block], 1e9)
        key_place = jnp.where(column >= block * rows, place, key_place)
    row_place = lax.broadcasted_iota(jnp.int32, bias.shape, 0).astype(jnp.float32) + offsets[index]
    bias[...] = jnp.where(key_place <= row_place, 0.0, -1e30)
    scale = math.log2(math.e) / math.sqrt(width)
    for head in range(query_ref.shape[1] // width):
        columns = pl.ds(head * width, width)
        scores = lax.dot_general(
            query_ref[:, columns],
            keys[...],
            (((1,), (1,)), ((), ())),
            preferred_element_type=jnp.float32,
        )
        old, new = scores[:, :cached] * scale, scores[:, cached:] * scale + bias[...]
        row_max = jnp.maximum(
            jnp.max(old, axis=1, keepdims=True), jnp.max(new, axis=1, keepdims=True)
        )
        old, new = jnp.exp2(old - row_max), jnp.exp2(new - row_max)
        totals = jnp.sum(old, axis=1, keepdims=True) + jnp.sum(new, axis=1, keepdims=True)
        result = jnp.dot(
            old.astype(jnp.bfloat16), values[:cached, :], preferred_element_type=jnp.float32
        ) + jnp.dot(
            new.astype(jnp.bfloat16), values[cached:, :], preferred_element_type=jnp.float32
        )
        out_ref[:, columns] = (result / totals).astype(jnp.bfloat16)


def attend_block(index, mine, query, cache_block, fresh):
    rows, columns = query.shape
    cached, width = cache_block.shape[0], cache_block.shape[1] // 2
    new = rows * len(fresh)
    inside = pl.BlockSpec(memory_space=pltpu.VMEM)
    return pl.pallas_call(
        functools.partial(attend_kernel, index),
        out_shape=jax.ShapeDtypeStruct((rows, columns), jnp.bfloat16),
        in_specs=[pl.BlockSpec(memory_space=pltpu.SMEM)] + [inside] * (2 + len(fresh)),
        out_specs=inside,
        scratch_shapes=[
            pltpu.VMEM((cached + new, width), jnp.bfloat16),
            pltpu.VMEM((cached + new, width), jnp.bfloat16),
            pltpu.VMEM((rows, new), jnp.float32),
        ],
        compiler_params=pltpu.CompilerParams(vmem_limit_bytes=12 * 2**20),
        cost_estimate=pl.CostEstimate(
            flops=4 * rows * columns * (cached + new),
            bytes_accessed=4 * (rows * columns + (cached + new) * width),
            transcendentals=rows * columns // width * (cached + new),
        ),
    )(mine, query, cache_block, *fresh)


def norm_kernel(
    length_ref,
    own_ref,
    core_ref,
    far_ref,
    residual_ref,
    gain_ref,
    attended_ref,
    packed_ref,
):
    attn_sum = (
        own_ref[...].astype(jnp.float32)
        + core_ref[...].astype(jnp.float32)
        + far_ref[...].astype(jnp.float32)
    )
    live = lax.broadcasted_iota(jnp.int32, attn_sum.shape, 0) < length_ref[0]
    attended_ref[...] = jnp.where(live, attn_sum, 0.0).astype(jnp.bfloat16)
    mixed = residual_ref[...].astype(jnp.float32) + attn_sum
    scale = lax.rsqrt(jnp.mean(mixed * mixed, axis=1, keepdims=True) + 1e-06)
    normed = (mixed * scale * gain_ref[...]).astype(jnp.bfloat16)
    rows, half = packed_ref.shape[0] // 2, packed_ref.shape[1]
    packed_ref[:rows, :] = normed[:, :half]
    packed_ref[rows:, :] = normed[:, half:]


def normalize(length, own, core, far, residual, gain):
    rows, width = own.shape
    packed = jax.ShapeDtypeStruct((2 * rows, width // 2), jnp.bfloat16)
    inside = pl.BlockSpec(memory_space=pltpu.VMEM)
    return pl.pallas_call(
        norm_kernel,
        out_shape=(jax.ShapeDtypeStruct((rows, width), jnp.bfloat16), packed),
        in_specs=[pl.BlockSpec(memory_space=pltpu.SMEM)] + [inside] * 5,
        out_specs=(inside, inside),
        compiler_params=pltpu.CompilerParams(vmem_limit_bytes=12 * 2**20),
        cost_estimate=pl.CostEstimate(
            flops=10 * rows * width, bytes_accessed=12 * rows * width, transcendentals=rows
        ),
    )(length, own, core, far, residual, gain)


def pick_kernel(capacity, place_ref, *refs):
    blocks, _, rows = place_ref.shape
    own_ref, sibling_ref = refs[-2:]
    half = own_ref.shape[1] // 2
    slot = lax.broadcasted_iota(jnp.int32, (capacity, rows), 0)
    for block in range(blocks):
        pick = jnp.concatenate(
            [(place_ref[block, pl.ds(core, 1), :] == slot) for core in range(2)], axis=0
        )
        pick = jnp.where(pick, 1.0, 0.0).astype(jnp.bfloat16)
        level, spot = block // 4, block % 4
        for side in range(2):
            if spot < 3:
                source = refs[5 * level + spot][pl.ds(side * rows, rows), :]
            else:
                source = refs[5 * level + 3 + side][...]
            chosen = jnp.dot(pick, source, preferred_element_type=jnp.float32)
            chosen = chosen.astype(jnp.bfloat16)
            inner = pl.ds(block * capacity, capacity), pl.ds(side * half, half)
            own_ref[inner] = chosen[:capacity]
            sibling_ref[inner] = chosen[capacity:]


def pick_rows(capacity, place, gathered):
    blocks, _, rows = place.shape
    half = gathered[0].shape[1]
    shape = jax.ShapeDtypeStruct((blocks * capacity, 2 * half), jnp.bfloat16)
    return pl.pallas_call(
        functools.partial(pick_kernel, capacity),
        out_shape=(shape, shape),
        compiler_params=pltpu.CompilerParams(vmem_limit_bytes=20 * 2**20),
        cost_estimate=pl.CostEstimate(
            flops=8 * blocks * capacity * rows * half,
            bytes_accessed=4 * blocks * (rows + 2 * capacity) * half,
            transcendentals=0,
        ),
    )(place, *gathered)


def combine_kernel(place_ref, gate_ref, own_ref, other_ref, *out_refs):
    blocks, _, rows = place_ref.shape
    capacity = own_ref.shape[0] // blocks
    half = own_ref.shape[1] // 2
    slot = lax.broadcasted_iota(jnp.int32, (capacity, rows), 0)
    for block in range(blocks):
        weight = jnp.concatenate(
            [
                jnp.where(
                    place_ref[block, pl.ds(core, 1), :] == slot,
                    gate_ref[block, pl.ds(core, 1), :],
                    0.0,
                )
                for core in range(2)
            ],
            axis=0,
        )
        weight = weight.T.astype(jnp.bfloat16)
        far_x, far_y = block // 2, block % 2
        for side in range(2):
            inner = pl.ds(block * capacity, capacity), pl.ds(side * half, half)
            both = jnp.concatenate([own_ref[inner], other_ref[inner]], axis=0)
            share = jnp.dot(weight, both, preferred_element_type=jnp.float32).astype(jnp.bfloat16)
            sent, place = (far_x, far_y) if side else (far_y, far_x)
            if sent:
                out_refs[3 * side + 2][pl.ds(place * rows, rows), :] = share
            else:
                out_refs[3 * side + place][...] = share


def combine_rows(part, parts, place, gate, own, other):
    blocks, _, rows = place.shape
    half = own.shape[1] // 2
    kept = jax.ShapeDtypeStruct((rows, half), jnp.bfloat16)
    sent = jax.ShapeDtypeStruct((2 * rows, half), jnp.bfloat16)
    count = own.shape[0] // parts
    whole = lambda shape: pl.BlockSpec(shape, lambda j: (0,) * len(shape))
    level = pl.BlockSpec((count, 2 * half), lambda j: (part, 0))
    return pl.pallas_call(
        combine_kernel,
        out_shape=[kept, kept, sent] * 2,
        grid=(1,),
        in_specs=[whole(place.shape), whole(gate.shape), level, level],
        out_specs=[whole(kept.shape), whole(kept.shape), whole(sent.shape)] * 2,
        compiler_params=pltpu.CompilerParams(vmem_limit_bytes=16 * 2**20),
        cost_estimate=pl.CostEstimate(
            flops=8 * count * rows * half,
            bytes_accessed=4 * (blocks * rows + 2 * count) * half,
            transcendentals=0,
        ),
    )(place, gate, own, other)


def routing_start(own_live, expert_ids, gate_values, earlier):
    live_ids = jnp.where(own_live[:, None], expert_ids, -1).astype(jnp.float32)
    routing = after(jnp.concatenate([live_ids, gate_values], axis=1).T, earlier)
    groups = lax.axis_size("grp")
    lines = [routing]
    for hop in range(2, groups, 2):
        lines.append(
            lax.ppermute(routing, "grp", [(g, (g + hop) % groups) for g in range(groups)])
        )
    return jnp.stack(lines)


def routing_pair(routing, swap):
    return jnp.stack([routing, swap(routing)], axis=routing.ndim - 2)


def selections(routing, top_count):
    mine = lax.axis_index(("grp", "sp"))
    depth, rows = routing.shape[0], routing.shape[-1]
    routing = routing.reshape(-1, 2 * top_count, rows)
    ids, gates = routing[:, :top_count].astype(jnp.int32), routing[:, top_count:]
    experts = jnp.stack([mine, mine ^ 1])
    chosen = ids[:, None] == experts[None, :, None, None]
    wanted = jnp.any(chosen, axis=2)
    gate = jnp.sum(jnp.where(chosen, gates[:, None], 0.0), axis=2)
    order = jnp.arange(rows)
    earlier = (order[:, None] < order[None, :]).astype(jnp.bfloat16)
    place = jnp.einsum(
        "bcr,rt->bct", wanted.astype(jnp.bfloat16), earlier, preferred_element_type=jnp.float32
    ).astype(jnp.int32)
    return jnp.where(wanted, place, -1), gate


def expert_kernel(rows_ref, up_gate_ref, down_ref, out_ref, hidden):
    hidden_width, width = down_ref.shape[1], down_ref.shape[2]
    tile = 256
    for start in range(0, hidden_width, tile):
        gate = jnp.dot(
            rows_ref[...],
            up_gate_ref[0, :, start : start + tile],
            preferred_element_type=jnp.float32,
        )
        up = jnp.dot(
            rows_ref[...],
            up_gate_ref[0, :, hidden_width + start : hidden_width + start + tile],
            preferred_element_type=jnp.float32,
        )
        hidden[:, start : start + tile] = (gate / (1.0 + jnp.exp(-gate)) * up).astype(
            jnp.bfloat16
        )
    for start in range(0, width, tile):
        out_ref[:, start : start + tile] = jnp.dot(
            hidden[...], down_ref[0, :, start : start + tile], preferred_element_type=jnp.float32
        ).astype(jnp.bfloat16)


def run_expert(rows, up_gate_weight, down_weight):
    count, width = rows.shape
    hidden_width = down_weight.shape[1]
    return pl.pallas_call(
        expert_kernel,
        out_shape=jax.ShapeDtypeStruct((count, width), jnp.bfloat16),
        scratch_shapes=[pltpu.VMEM((count, hidden_width), jnp.bfloat16)],
        compiler_params=pltpu.CompilerParams(vmem_limit_bytes=20 * 2**20),
        cost_estimate=pl.CostEstimate(
            flops=6 * count * width * hidden_width,
            bytes_accessed=6 * width * hidden_width + 4 * count * width,
            transcendentals=count * hidden_width,
        ),
    )(rows, up_gate_weight, down_weight)


def experts_by_gather(packed, routing, top_count, capacity, up_gate_weight, down_weight):
    depth = lax.axis_size("grp") // 2
    rows = packed.shape[0] // 2
    routing = routing_pair(after(routing, packed), swap_x)
    lines, beside_x, beside_y, diagonal = [packed], [], [], []
    halves = []

    def cross(level, earlier):
        first_x, second_y = halves[level]
        if earlier is not None:
            first_x, second_y = after(first_x, *earlier), after(second_y, *earlier)
        diagonal.append((swap_y(first_x), swap_x(second_y)))

    for level in range(depth):
        line = lines[level]
        if level == 1:
            line = after(line, routing)
            routing = routing_pair(after(routing, *halves[0]), swap_y)
        if level == 2:
            cross(0, (line, routing))
            cross(1, (line,))
            line = after(line, *diagonal[0], *diagonal[1])
        elif level > 2:
            line = after(line, beside_x[level - 1], beside_y[level - 1])
        beside_x.append(swap_x(line))
        beside_y.append(swap_y(line))
        halves.append((beside_x[level][:rows], beside_y[level][rows:]))
        if level + 1 < depth:
            line = lines[level]
            if level:
                line = after(line, beside_x[level - 1], beside_y[level - 1])
            lines.append(shift_z(line))
    for level in range(len(diagonal), depth):
        cross(level, None)
    if depth == 1:
        routing = routing_pair(routing, swap_y)
    place, gate = selections(routing, top_count)
    per_level = place.shape[0] // depth
    results, kept, sent, back, joined = {}, {}, {}, {}, {}

    def combine(level, *earlier):
        index, count, own_result, other_result = results[level]
        if earlier:
            own_result = after(own_result, *earlier)
        blocks = slice(level * per_level, (level + 1) * per_level)
        parts = combine_rows(index, count, place[blocks], gate[blocks], own_result, other_result)
        first, first_x, first_sent, second, second_y, second_sent = parts
        kept[level] = first, first_x, second, second_y
        sent[level] = first_sent, second_sent

    def send_back(level, *earlier):
        first_sent, second_sent = sent[level]
        if earlier:
            first_sent, second_sent = after(first_sent, *earlier), after(second_sent, *earlier)
        back[level] = swap_y(first_sent), swap_x(second_sent)

    def join(level):
        first, first_x, second, second_y = kept[level]
        first_back, second_back = back[level]
        first, first_x = first + first_back[:rows], first_x + first_back[rows:]
        second, second_y = second + second_back[:rows], second_y + second_back[rows:]
        joined[level] = first, second, swap_x(first_x), swap_y(second_y)

    for start in range(0, depth, 2):
        levels = range(start, min(start + 2, depth))
        gathered = []
        for level in levels:
            gathered += [lines[level], beside_y[level], beside_x[level], *diagonal[level]]
        ahead, last = levels[-1] + 1, levels[-1] + 2
        if start:
            gathered[0] = after(gathered[0], kept[start - 1][0])
        blocks = slice(start * per_level, (start + len(levels)) * per_level)
        own, sibling = pick_rows(capacity, place[blocks], gathered)
        if last < depth:
            sibling = after(sibling, beside_x[ahead], beside_y[ahead], lines[last])
        other = swap_core(sibling)
        other_result = run_expert(other, up_gate_weight, down_weight)
        if last < depth:
            other_result = after(
                other_result, beside_x[last], beside_y[last], *diagonal[ahead]
            )
            own = after(own, other_result)
        if start:
            back[start - 1] = tuple(after(part, other_result) for part in back[start - 1])
            join(start - 1)
        own_result = run_expert(own, up_gate_weight, down_weight)
        if start:
            other_result = after(other_result, own_result, *back[start - 1])
        other_result = swap_core(other_result)
        if start:
            own_result = after(own_result, *back[start - 1])
        for index, level in enumerate(levels):
            results[level] = index, len(levels), own_result, other_result
            if level:
                combine(level)
                send_back(level, *back.get(level - 1, ()))
        for level in levels:
            if level and (ahead >= depth or level < levels[-1]):
                join(level)
    combine(0, *(kept[depth - 1][:1] if depth > 1 else ()))
    send_back(0, *back.get(depth - 1, ()))
    join(0)
    shares = {}
    for level in range(depth):
        first, second, first_far, second_far = joined[level]
        shares[level] = first + first_far, second + second_far
    first, second = shares[0]
    if depth > 1:
        total = jnp.concatenate(shares[1], axis=0)
        for level in range(2, depth):
            total = jnp.concatenate(shares[level], axis=0) + shift_z(total)
        total = shift_z(total)
        first, second = first + total[:rows], second + total[rows:]
    return jnp.concatenate([first, second], axis=1)


def per_device_pairs(
    queries,
    fresh_key_values,
    cache,
    lengths,
    out_weight,
    residual,
    norm_gain,
    expert_ids,
    gate_values,
    up_gate_weight,
    down_weight,
):
    seq_devices = lax.axis_size("sp")
    mine = lax.axis_index("sp")
    slot_rows = queries.shape[0]
    width = cache.shape[-1] // 2
    head_columns = queries.shape[1] // seq_devices
    top_count = expert_ids.shape[1]
    experts = up_gate_weight.shape[0] * lax.axis_size("grp") * seq_devices
    capacity = max(2, 8 * slot_rows * top_count // (5 * experts))
    own_length = lengths[0, 0]
    own_live = jnp.arange(slot_rows, dtype=jnp.int32) < own_length

    def key_values_for(target):
        keys = lax.dynamic_slice(fresh_key_values, (0, target * width), (slot_rows, width))
        values = lax.dynamic_slice(
            fresh_key_values, (0, (seq_devices + target) * width), (slot_rows, width)
        )
        lane = jnp.arange(2 * width, dtype=jnp.int32)[None, :]
        note = jnp.where(lane < width, own_length // 256, own_length % 256)
        note = jnp.broadcast_to(note, (16, 2 * width)).astype(jnp.bfloat16)
        return jnp.concatenate([jnp.concatenate([keys, values], axis=1), note], axis=0)

    def queries_for(target):
        return lax.dynamic_slice(queries, (0, target * head_columns), (slot_rows, head_columns))

    masks = range(1, seq_devices)
    fresh = [key_values_for(mine)] + [xor_group(key_values_for(mine ^ m), m) for m in masks]
    query_blocks = {m: xor_group(queries_for(mine ^ m), m) for m in (3, 1)}
    cache_block = cache[0, 0]

    def share_of(block, query, *earlier):
        heads = attend_block(block, mine[None], query, cache_block, fresh)
        if earlier:
            heads = after(heads, *earlier)
        return jnp.dot(heads, out_weight, preferred_element_type=jnp.float32).astype(jnp.bfloat16)

    own = share_of(0, queries_for(mine))
    query_blocks[2] = xor_group(after(queries_for(mine ^ 2), own), 2)
    far_core = share_of(3, after(query_blocks[3], own), query_blocks[2])
    far = share_of(2, query_blocks[2]) + swap_core(far_core)
    near = share_of(1, after(query_blocks[1], far))
    routing = routing_start(own_live, expert_ids, gate_values, far)
    far = swap_y(far)
    attended, packed = normalize(
        lengths[0], own, swap_core(after(near, far, routing)), far, residual, norm_gain[None, :]
    )
    moe_out = experts_by_gather(
        packed, routing, top_count, capacity, up_gate_weight, down_weight
    )
    return (attended, moe_out)


def per_device(
    queries,
    fresh_key_values,
    cache,
    lengths,
    out_weight,
    residual,
    norm_gain,
    expert_ids,
    gate_values,
    up_gate_weight,
    down_weight,
):
    seq_devices = lax.axis_size("sp")
    slot_rows = queries.shape[0]
    head_width = cache.shape[-1] // 2
    model_width = residual.shape[1]
    kv_heads = fresh_key_values.shape[1] // (2 * head_width)
    repeat = seq_devices // kv_heads
    keys_new = fresh_key_values[:, : kv_heads * head_width].reshape(
        slot_rows, kv_heads, 1, head_width
    )
    values_new = fresh_key_values[:, kv_heads * head_width :].reshape(
        slot_rows, kv_heads, 1, head_width
    )
    paired = jnp.concatenate([keys_new, values_new], axis=3)
    spread = jnp.broadcast_to(paired, (slot_rows, kv_heads, repeat, 2 * head_width)).reshape(
        slot_rows, seq_devices * 2 * head_width
    )
    all_lengths = lax.all_gather(lengths, "sp", axis=1, tiled=True)
    queries_by_head, head_kv = (
        lax.all_to_all(queries, "sp", split_axis=1, concat_axis=0, tiled=True),
        lax.all_to_all(spread, "sp", split_axis=1, concat_axis=0, tiled=True),
    )
    cache_block = cache[0, 0]
    my_index = lax.axis_index("sp")
    for bit_pos in range(repeat.bit_length() - 1):
        partner = partner_2(cache_block, "sp", bit_pos)
        is_upper = my_index // 2**bit_pos % 2 == 1
        cache_block = jnp.where(
            is_upper,
            jnp.concatenate([partner, cache_block], axis=0),
            jnp.concatenate([cache_block, partner], axis=0),
        )
    stretch_lens = all_lengths[0]
    offsets = jnp.cumsum(stretch_lens) - stretch_lens
    rows_of_group = queries_by_head.shape[0]
    slot_ids = jnp.arange(rows_of_group, dtype=jnp.int32)
    source = slot_ids // slot_rows
    within = slot_ids % slot_rows
    from_device = source[:, None] == jnp.arange(seq_devices, dtype=jnp.int32)[None, :]
    is_live = within < jnp.sum(jnp.where(from_device, stretch_lens[None, :], 0), axis=1)
    position = within + jnp.sum(jnp.where(from_device, offsets[None, :], 0), axis=1)
    per_dev = queries_by_head.shape[1] // head_width
    cache_len = cache_block.shape[0]
    key_all = jnp.concatenate([cache_block[:, :head_width], head_kv[:, :head_width]], axis=0)
    value_all = jnp.concatenate([cache_block[:, head_width:], head_kv[:, head_width:]], axis=0)
    block_count = 2 if rows_of_group % 2 == 0 and rows_of_group >= 1024 else 1
    block_rows = rows_of_group // block_count

    def attend(parts):
        query_block, place_block = parts
        scores = jnp.einsum(
            "rhd,kd->hrk", query_block, key_all, preferred_element_type=jnp.float32
        ) / math.sqrt(head_width)
        allowed = jnp.concatenate(
            [
                jnp.ones((block_rows, cache_len), dtype=bool),
                is_live[None, :] & (position[None, :] <= place_block[:, None]),
            ],
            axis=1,
        )
        scores = jnp.where(allowed[None], scores, -jnp.inf)
        row_max = jnp.max(scores, axis=-1, keepdims=True)
        weights = jnp.exp(scores - row_max)
        totals = jnp.sum(weights, axis=-1, keepdims=True)
        result = (
            jnp.einsum(
                "hrk,kd->hrd",
                weights.astype(jnp.bfloat16),
                value_all,
                preferred_element_type=jnp.float32,
            )
            / totals
        )
        return (
            result.astype(jnp.bfloat16).transpose(1, 0, 2).reshape(block_rows, per_dev * head_width)
        )

    attn_heads = lax.map(
        attend,
        (
            queries_by_head.reshape(block_count, block_rows, per_dev, head_width),
            position.reshape(block_count, block_rows),
        ),
    ).reshape(rows_of_group, per_dev * head_width)
    attn_sum = lax.psum_scatter(
        jnp.dot(attn_heads, out_weight, preferred_element_type=jnp.float32).astype(jnp.bfloat16),
        "sp",
        scatter_dimension=0,
        tiled=True,
    ).astype(jnp.float32)
    own_live = jnp.arange(slot_rows, dtype=jnp.int32) < lengths[0, 0]
    attended = jnp.where(own_live[:, None], attn_sum, 0.0).astype(jnp.bfloat16)
    mixed_rows = residual.astype(jnp.float32) + attn_sum
    normed = (
        mixed_rows
        * lax.rsqrt(jnp.mean(mixed_rows * mixed_rows, axis=-1, keepdims=True) + 1e-06)
        * norm_gain
    ).astype(jnp.bfloat16)
    group_count = lax.axis_size("grp")
    experts = up_gate_weight.shape[0] * group_count * seq_devices
    top_count = expert_ids.shape[1]
    capacity = max(2, 8 * slot_rows * top_count // (5 * experts))
    hidden_width = down_weight.shape[1]
    choose = expert_ids[:, :, None] == jnp.arange(experts, dtype=jnp.int32)[None, None, :]
    routed = (jnp.any(choose, axis=1) & own_live[:, None]).astype(jnp.float32)
    earlier = (jnp.arange(slot_rows)[:, None] > jnp.arange(slot_rows)[None, :]).astype(jnp.float32)
    prefix = jnp.dot(earlier, routed, precision=lax.Precision.HIGHEST)
    slot_in = jnp.sum(jnp.where(choose, prefix[:, None, :], 0.0), axis=2).astype(jnp.int32)
    dump_slot = experts * capacity
    target = jnp.where(own_live[:, None], expert_ids * capacity + slot_in, dump_slot)
    source_rows = (
        jnp.full((dump_slot + 1,), slot_rows, jnp.int32)
        .at[target.reshape(-1)]
        .set(jnp.repeat(jnp.arange(slot_rows, dtype=jnp.int32), top_count))[:dump_slot]
    )
    padded = jnp.concatenate([normed, jnp.zeros((1, model_width), jnp.bfloat16)], axis=0)
    outgoing = padded[source_rows].reshape(experts, capacity, model_width)
    received = lax.all_to_all(outgoing, ("grp", "sp"), split_axis=0, concat_axis=0, tiled=True)
    flat_rows = received.reshape(-1, model_width)
    projected = jnp.dot(flat_rows, up_gate_weight[0], preferred_element_type=jnp.float32)
    hidden = (jax.nn.silu(projected[:, :hidden_width]) * projected[:, hidden_width:]).astype(
        jnp.bfloat16
    )
    returned = lax.all_to_all(
        jnp.dot(hidden, down_weight[0], preferred_element_type=jnp.float32)
        .astype(jnp.bfloat16)
        .reshape(received.shape),
        ("grp", "sp"),
        split_axis=0,
        concat_axis=0,
        tiled=True,
    )
    back_rows = jnp.concatenate(
        [returned.reshape(dump_slot, model_width), jnp.zeros((1, model_width), jnp.bfloat16)],
        axis=0,
    )
    picked = back_rows[target]
    combined = jnp.sum(gate_values[:, :, None] * picked.astype(jnp.float32), axis=1)
    moe_out = jnp.where(own_live[:, None], combined, 0.0).astype(jnp.bfloat16)
    return (attended, moe_out)


def solution(mesh):
    in_specs = (
        P(("grp", "sp"), None),
        P(("grp", "sp"), None),
        P("grp", "sp", None, None),
        P("grp", "sp"),
        P("sp", None),
        P(("grp", "sp"), None),
        P(),
        P(("grp", "sp"), None),
        P(("grp", "sp"), None),
        P(("grp", "sp"), None, None),
        P(("grp", "sp"), None, None),
    )
    out_specs = (P(("grp", "sp"), None), P(("grp", "sp"), None))
    groups, seq_devices = mesh.shape["grp"], mesh.shape["sp"]

    def run(*args):
        kv_heads = args[1].shape[1] // args[2].shape[-1]
        experts, top_count = args[9].shape[0], args[7].shape[1]
        pairs = seq_devices == kv_heads == 4 and groups % 2 == 0 and experts <= 4 * top_count
        return mapped(per_device_pairs if pairs else per_device)(*args)

    def mapped(body):
        return jax.shard_map(
            body, mesh=mesh, in_specs=in_specs, out_specs=out_specs, check_vma=False
        )

    return run
```

```python
import functools
import math

import jax
import jax.numpy as jnp
from jax import lax
from jax.experimental import pallas as pl
from jax.experimental.pallas import tpu as pltpu
from jax.sharding import PartitionSpec as P


def partner_2(value, axis, bit):
    mask = 2**bit
    pairs = [(source, source ^ mask) for source in range(lax.axis_size(axis))]
    return lax.ppermute(value, axis, pairs)


def shift_z(value):
    groups = lax.axis_size("grp")
    return lax.ppermute(value, "grp", [(g, (g + 2) % groups) for g in range(groups)])


def swap_x(value):
    return partner_2(value, "grp", 0)


def swap_y(value):
    return partner_2(value, "sp", 1)


def swap_core(value):
    return partner_2(value, "sp", 0)


def after(value, *earlier):
    return lax.optimization_barrier((value, *earlier))[0]


def xor_group(value, mask):
    return lax.ppermute(value, "sp", [(s, s ^ mask) for s in range(lax.axis_size("sp"))])


def attend_kernel(index, mine_ref, query_ref, cache_ref, *refs):
    fresh_refs, (out_ref, keys, values, bias) = refs[:-4], refs[-4:]
    rows = query_ref.shape[0]
    cached, width = cache_ref.shape[0], cache_ref.shape[1] // 2
    keys[:cached, :] = cache_ref[:, :width]
    values[:cached, :] = cache_ref[:, width:]
    lengths = []
    for block, fresh_ref in enumerate(fresh_refs):
        places = pl.ds(cached + block * rows, rows)
        keys[places, :] = fresh_ref[:rows, :width]
        values[places, :] = fresh_ref[:rows, width:]
        note = fresh_ref[rows : rows + 16, :].astype(jnp.float32)
        lengths.append(note[:1, :1] * 256.0 + note[:1, width : width + 1])
    mine = mine_ref[0]
    offsets = []
    for block in range(len(fresh_refs)):
        offset = jnp.zeros((1, 1), jnp.float32)
        for other in range(len(fresh_refs)):
            before = (mine ^ other) < (mine ^ block)
            offset = offset + lengths[other] * before.astype(jnp.float32)
        offsets.append(offset)
    column = lax.broadcasted_iota(jnp.int32, (1, bias.shape[1]), 1)
    key_place = jnp.zeros((1, bias.shape[1]), jnp.float32)
    for block in range(len(fresh_refs)):
        within = (column - block * rows).astype(jnp.float32)
        place = jnp.where(within < lengths[block], within + offsets[block], 1e9)
        key_place = jnp.where(column >= block * rows, place, key_place)
    row_place = lax.broadcasted_iota(jnp.int32, bias.shape, 0).astype(jnp.float32) + offsets[index]
    bias[...] = jnp.where(key_place <= row_place, 0.0, -1e30)
    scale = math.log2(math.e) / math.sqrt(width)
    for head in range(query_ref.shape[1] // width):
        columns = pl.ds(head * width, width)
        scores = lax.dot_general(
            query_ref[:, columns],
            keys[...],
            (((1,), (1,)), ((), ())),
            preferred_element_type=jnp.float32,
        )
        old, new = scores[:, :cached] * scale, scores[:, cached:] * scale + bias[...]
        row_max = jnp.maximum(
            jnp.max(old, axis=1, keepdims=True), jnp.max(new, axis=1, keepdims=True)
        )
        old, new = jnp.exp2(old - row_max), jnp.exp2(new - row_max)
        totals = jnp.sum(old, axis=1, keepdims=True) + jnp.sum(new, axis=1, keepdims=True)
        result = jnp.dot(
            old.astype(jnp.bfloat16), values[:cached, :], preferred_element_type=jnp.float32
        ) + jnp.dot(
            new.astype(jnp.bfloat16), values[cached:, :], preferred_element_type=jnp.float32
        )
        out_ref[:, columns] = (result / totals).astype(jnp.bfloat16)


def attend_block(index, mine, query, cache_block, fresh):
    rows, columns = query.shape
    cached, width = cache_block.shape[0], cache_block.shape[1] // 2
    new = rows * len(fresh)
    inside = pl.BlockSpec(memory_space=pltpu.VMEM)
    return pl.pallas_call(
        functools.partial(attend_kernel, index),
        out_shape=jax.ShapeDtypeStruct((rows, columns), jnp.bfloat16),
        in_specs=[pl.BlockSpec(memory_space=pltpu.SMEM)] + [inside] * (2 + len(fresh)),
        out_specs=inside,
        scratch_shapes=[
            pltpu.VMEM((cached + new, width), jnp.bfloat16),
            pltpu.VMEM((cached + new, width), jnp.bfloat16),
            pltpu.VMEM((rows, new), jnp.float32),
        ],
        compiler_params=pltpu.CompilerParams(vmem_limit_bytes=12 * 2**20),
        cost_estimate=pl.CostEstimate(
            flops=4 * rows * columns * (cached + new),
            bytes_accessed=4 * (rows * columns + (cached + new) * width),
            transcendentals=rows * columns // width * (cached + new),
        ),
    )(mine, query, cache_block, *fresh)


def norm_kernel(
    length_ref,
    own_ref,
    core_ref,
    far_ref,
    residual_ref,
    gain_ref,
    attended_ref,
    packed_ref,
):
    attn_sum = (
        own_ref[...].astype(jnp.float32)
        + core_ref[...].astype(jnp.float32)
        + far_ref[...].astype(jnp.float32)
    )
    live = lax.broadcasted_iota(jnp.int32, attn_sum.shape, 0) < length_ref[0]
    attended_ref[...] = jnp.where(live, attn_sum, 0.0).astype(jnp.bfloat16)
    mixed = residual_ref[...].astype(jnp.float32) + attn_sum
    scale = lax.rsqrt(jnp.mean(mixed * mixed, axis=1, keepdims=True) + 1e-06)
    normed = (mixed * scale * gain_ref[...]).astype(jnp.bfloat16)
    rows, half = packed_ref.shape[0] // 2, packed_ref.shape[1]
    packed_ref[:rows, :] = normed[:, :half]
    packed_ref[rows:, :] = normed[:, half:]


def normalize(length, own, core, far, residual, gain):
    rows, width = own.shape
    packed = jax.ShapeDtypeStruct((2 * rows, width // 2), jnp.bfloat16)
    inside = pl.BlockSpec(memory_space=pltpu.VMEM)
    return pl.pallas_call(
        norm_kernel,
        out_shape=(jax.ShapeDtypeStruct((rows, width), jnp.bfloat16), packed),
        in_specs=[pl.BlockSpec(memory_space=pltpu.SMEM)] + [inside] * 5,
        out_specs=(inside, inside),
        compiler_params=pltpu.CompilerParams(vmem_limit_bytes=12 * 2**20),
        cost_estimate=pl.CostEstimate(
            flops=10 * rows * width, bytes_accessed=12 * rows * width, transcendentals=rows
        ),
    )(length, own, core, far, residual, gain)


def pick_kernel(capacity, place_ref, *refs):
    blocks, _, rows = place_ref.shape
    own_ref, sibling_ref = refs[-2:]
    half = own_ref.shape[1] // 2
    slot = lax.broadcasted_iota(jnp.int32, (capacity, rows), 0)
    for block in range(blocks):
        pick = jnp.concatenate(
            [(place_ref[block, pl.ds(core, 1), :] == slot) for core in range(2)], axis=0
        )
        pick = jnp.where(pick, 1.0, 0.0).astype(jnp.bfloat16)
        level, spot = block // 4, block % 4
        for side in range(2):
            if spot < 3:
                source = refs[5 * level + spot][pl.ds(side * rows, rows), :]
            else:
                source = refs[5 * level + 3 + side][...]
            chosen = jnp.dot(pick, source, preferred_element_type=jnp.float32)
            chosen = chosen.astype(jnp.bfloat16)
            inner = pl.ds(block * capacity, capacity), pl.ds(side * half, half)
            own_ref[inner] = chosen[:capacity]
            sibling_ref[inner] = chosen[capacity:]


def pick_rows(capacity, place, gathered):
    blocks, _, rows = place.shape
    half = gathered[0].shape[1]
    shape = jax.ShapeDtypeStruct((blocks * capacity, 2 * half), jnp.bfloat16)
    return pl.pallas_call(
        functools.partial(pick_kernel, capacity),
        out_shape=(shape, shape),
        compiler_params=pltpu.CompilerParams(vmem_limit_bytes=10 * 2**20),
        cost_estimate=pl.CostEstimate(
            flops=8 * blocks * capacity * rows * half,
            bytes_accessed=4 * blocks * (rows + 2 * capacity) * half,
            transcendentals=0,
        ),
    )(place, *gathered)


def combine_kernel(place_ref, gate_ref, own_ref, other_ref, *out_refs):
    blocks, _, rows = place_ref.shape
    capacity = own_ref.shape[0] // blocks
    half = own_ref.shape[1] // 2
    slot = lax.broadcasted_iota(jnp.int32, (capacity, rows), 0)
    for block in range(blocks):
        weight = jnp.concatenate(
            [
                jnp.where(
                    place_ref[block, pl.ds(core, 1), :] == slot,
                    gate_ref[block, pl.ds(core, 1), :],
                    0.0,
                )
                for core in range(2)
            ],
            axis=0,
        )
        weight = weight.T.astype(jnp.bfloat16)
        far_x, far_y = block // 2, block % 2
        for side in range(2):
            inner = pl.ds(block * capacity, capacity), pl.ds(side * half, half)
            both = jnp.concatenate([own_ref[inner], other_ref[inner]], axis=0)
            share = jnp.dot(weight, both, preferred_element_type=jnp.float32).astype(jnp.bfloat16)
            sent, place = (far_x, far_y) if side else (far_y, far_x)
            if sent:
                out_refs[3 * side + 2][pl.ds(place * rows, rows), :] = share
            else:
                out_refs[3 * side + place][...] = share


def combine_rows(part, parts, place, gate, own, other):
    blocks, _, rows = place.shape
    half = own.shape[1] // 2
    kept = jax.ShapeDtypeStruct((rows, half), jnp.bfloat16)
    sent = jax.ShapeDtypeStruct((2 * rows, half), jnp.bfloat16)
    count = own.shape[0] // parts
    whole = lambda shape: pl.BlockSpec(shape, lambda j: (0,) * len(shape))
    level = pl.BlockSpec((count, 2 * half), lambda j: (part, 0))
    return pl.pallas_call(
        combine_kernel,
        out_shape=[kept, kept, sent] * 2,
        grid=(1,),
        in_specs=[whole(place.shape), whole(gate.shape), level, level],
        out_specs=[whole(kept.shape), whole(kept.shape), whole(sent.shape)] * 2,
        compiler_params=pltpu.CompilerParams(vmem_limit_bytes=8 * 2**20),
        cost_estimate=pl.CostEstimate(
            flops=8 * count * rows * half,
            bytes_accessed=4 * (blocks * rows + 2 * count) * half,
            transcendentals=0,
        ),
    )(place, gate, own, other)


def routing_start(own_live, expert_ids, gate_values, earlier):
    live_ids = jnp.where(own_live[:, None], expert_ids, -1).astype(jnp.float32)
    routing = after(jnp.concatenate([live_ids, gate_values], axis=1).T, earlier)
    groups = lax.axis_size("grp")
    lines = [routing]
    for hop in range(2, groups, 2):
        lines.append(
            lax.ppermute(routing, "grp", [(g, (g + hop) % groups) for g in range(groups)])
        )
    return jnp.stack(lines)


def routing_pair(routing, swap):
    return jnp.stack([routing, swap(routing)], axis=routing.ndim - 2)


def selections(routing, top_count):
    mine = lax.axis_index(("grp", "sp"))
    depth, rows = routing.shape[0], routing.shape[-1]
    routing = routing.reshape(-1, 2 * top_count, rows)
    ids, gates = routing[:, :top_count].astype(jnp.int32), routing[:, top_count:]
    experts = jnp.stack([mine, mine ^ 1])
    chosen = ids[:, None] == experts[None, :, None, None]
    wanted = jnp.any(chosen, axis=2)
    gate = jnp.sum(jnp.where(chosen, gates[:, None], 0.0), axis=2)
    order = jnp.arange(rows)
    earlier = (order[:, None] < order[None, :]).astype(jnp.bfloat16)
    place = jnp.einsum(
        "bcr,rt->bct", wanted.astype(jnp.bfloat16), earlier, preferred_element_type=jnp.float32
    ).astype(jnp.int32)
    return jnp.where(wanted, place, -1), gate


def expert_kernel(rows_ref, up_gate_ref, down_ref, out_ref, hidden):
    hidden_width, width = down_ref.shape[1], down_ref.shape[2]
    tile = 256
    for start in range(0, hidden_width, tile):
        gate = jnp.dot(
            rows_ref[...],
            up_gate_ref[0, :, start : start + tile],
            preferred_element_type=jnp.float32,
        )
        up = jnp.dot(
            rows_ref[...],
            up_gate_ref[0, :, hidden_width + start : hidden_width + start + tile],
            preferred_element_type=jnp.float32,
        )
        hidden[:, start : start + tile] = (gate / (1.0 + jnp.exp(-gate)) * up).astype(
            jnp.bfloat16
        )
    for start in range(0, width, tile):
        out_ref[:, start : start + tile] = jnp.dot(
            hidden[...], down_ref[0, :, start : start + tile], preferred_element_type=jnp.float32
        ).astype(jnp.bfloat16)


def run_expert(rows, up_gate_weight, down_weight):
    count, width = rows.shape
    hidden_width = down_weight.shape[1]
    return pl.pallas_call(
        expert_kernel,
        out_shape=jax.ShapeDtypeStruct((count, width), jnp.bfloat16),
        scratch_shapes=[pltpu.VMEM((count, hidden_width), jnp.bfloat16)],
        compiler_params=pltpu.CompilerParams(vmem_limit_bytes=10 * 2**20),
        cost_estimate=pl.CostEstimate(
            flops=6 * count * width * hidden_width,
            bytes_accessed=6 * width * hidden_width + 4 * count * width,
            transcendentals=count * hidden_width,
        ),
    )(rows, up_gate_weight, down_weight)


def experts_by_gather(packed, routing, top_count, capacity, up_gate_weight, down_weight):
    depth = lax.axis_size("grp") // 2
    rows = packed.shape[0] // 2
    routing = routing_pair(after(routing, packed), swap_x)
    lines, beside_x, beside_y, diagonal = [packed], [], [], []
    halves = []

    def cross(level, earlier):
        first_x, second_y = halves[level]
        if earlier is not None:
            first_x, second_y = after(first_x, *earlier), after(second_y, *earlier)
        diagonal.append((swap_y(first_x), swap_x(second_y)))

    for level in range(depth):
        line = lines[level]
        if level == 1:
            line = after(line, routing)
            routing = routing_pair(after(routing, *halves[0]), swap_y)
        if level == 2:
            cross(0, (line, routing))
            cross(1, (line,))
            line = after(line, *diagonal[0], *diagonal[1])
        elif level > 2:
            line = after(line, beside_x[level - 1], beside_y[level - 1])
        beside_x.append(swap_x(line))
        beside_y.append(swap_y(line))
        halves.append((beside_x[level][:rows], beside_y[level][rows:]))
        if level + 1 < depth:
            line = lines[level]
            if level:
                line = after(line, beside_x[level - 1], beside_y[level - 1])
            lines.append(shift_z(line))
    for level in range(len(diagonal), depth):
        cross(level, None)
    if depth == 1:
        routing = routing_pair(routing, swap_y)
    place, gate = selections(routing, top_count)
    per_level = place.shape[0] // depth
    results, kept, sent, back, joined = {}, {}, {}, {}, {}

    def combine(level, *earlier):
        index, count, own_result, other_result = results[level]
        if earlier:
            own_result = after(own_result, *earlier)
        blocks = slice(level * per_level, (level + 1) * per_level)
        parts = combine_rows(index, count, place[blocks], gate[blocks], own_result, other_result)
        first, first_x, first_sent, second, second_y, second_sent = parts
        kept[level] = first, first_x, second, second_y
        sent[level] = first_sent, second_sent

    def send_back(level, *earlier):
        first_sent, second_sent = sent[level]
        if earlier:
            first_sent, second_sent = after(first_sent, *earlier), after(second_sent, *earlier)
        back[level] = swap_y(first_sent), swap_x(second_sent)

    def join(level):
        first, first_x, second, second_y = kept[level]
        first_back, second_back = back[level]
        first, first_x = first + first_back[:rows], first_x + first_back[rows:]
        second, second_y = second + second_back[:rows], second_y + second_back[rows:]
        joined[level] = first, second, swap_x(first_x), swap_y(second_y)

    for start in range(0, depth, 2):
        levels = range(start, min(start + 2, depth))
        gathered = []
        for level in levels:
            gathered += [lines[level], beside_y[level], beside_x[level], *diagonal[level]]
        ahead, last = levels[-1] + 1, levels[-1] + 2
        if start:
            gathered[0] = after(gathered[0], kept[start - 1][0])
        blocks = slice(start * per_level, (start + len(levels)) * per_level)
        own, sibling = pick_rows(capacity, place[blocks], gathered)
        if last < depth:
            sibling = after(sibling, beside_x[ahead], beside_y[ahead], lines[last])
        other = swap_core(sibling)
        other_result = run_expert(other, up_gate_weight, down_weight)
        if last < depth:
            other_result = after(
                other_result, beside_x[last], beside_y[last], *diagonal[ahead]
            )
            own = after(own, other_result)
        if start:
            back[start - 1] = tuple(after(part, other_result) for part in back[start - 1])
            join(start - 1)
            own = after(own, *back[start - 1])
        own_result = run_expert(own, up_gate_weight, down_weight)
        other_result = swap_core(other_result)
        if start:
            own_result = after(own_result, *joined[start - 1])
        for index, level in enumerate(levels):
            results[level] = index, len(levels), own_result, other_result
            if level:
                combine(level)
                send_back(level, *back.get(level - 1, ()))
        for level in levels:
            if level and (ahead >= depth or level < levels[-1]):
                join(level)
    combine(0, *(kept[depth - 1][:1] if depth > 1 else ()))
    send_back(0, *back.get(depth - 1, ()))
    join(0)
    shares = {}
    for level in range(depth):
        first, second, first_far, second_far = joined[level]
        shares[level] = first + first_far, second + second_far
    first, second = shares[0]
    if depth > 1:
        total = jnp.concatenate(shares[1], axis=0)
        for level in range(2, depth):
            total = jnp.concatenate(shares[level], axis=0) + shift_z(total)
        total = shift_z(total)
        first, second = first + total[:rows], second + total[rows:]
    return jnp.concatenate([first, second], axis=1)


def per_device_pairs(
    queries,
    fresh_key_values,
    cache,
    lengths,
    out_weight,
    residual,
    norm_gain,
    expert_ids,
    gate_values,
    up_gate_weight,
    down_weight,
):
    seq_devices = lax.axis_size("sp")
    mine = lax.axis_index("sp")
    slot_rows = queries.shape[0]
    width = cache.shape[-1] // 2
    head_columns = queries.shape[1] // seq_devices
    top_count = expert_ids.shape[1]
    experts = up_gate_weight.shape[0] * lax.axis_size("grp") * seq_devices
    capacity = max(2, 8 * slot_rows * top_count // (5 * experts))
    own_length = lengths[0, 0]
    own_live = jnp.arange(slot_rows, dtype=jnp.int32) < own_length

    def key_values_for(target):
        keys = lax.dynamic_slice(fresh_key_values, (0, target * width), (slot_rows, width))
        values = lax.dynamic_slice(
            fresh_key_values, (0, (seq_devices + target) * width), (slot_rows, width)
        )
        lane = jnp.arange(2 * width, dtype=jnp.int32)[None, :]
        note = jnp.where(lane < width, own_length // 256, own_length % 256)
        note = jnp.broadcast_to(note, (16, 2 * width)).astype(jnp.bfloat16)
        return jnp.concatenate([jnp.concatenate([keys, values], axis=1), note], axis=0)

    def queries_for(target):
        return lax.dynamic_slice(queries, (0, target * head_columns), (slot_rows, head_columns))

    masks = range(1, seq_devices)
    fresh = [key_values_for(mine)] + [xor_group(key_values_for(mine ^ m), m) for m in masks]
    query_blocks = {m: xor_group(queries_for(mine ^ m), m) for m in (3, 1)}
    cache_block = cache[0, 0]

    def share_of(block, query, *earlier):
        heads = attend_block(block, mine[None], query, cache_block, fresh)
        if earlier:
            heads = after(heads, *earlier)
        return jnp.dot(heads, out_weight, preferred_element_type=jnp.float32).astype(jnp.bfloat16)

    own = share_of(0, queries_for(mine))
    query_blocks[2] = xor_group(after(queries_for(mine ^ 2), own), 2)
    far_core = share_of(3, after(query_blocks[3], own), query_blocks[2])
    far = share_of(2, query_blocks[2]) + swap_core(far_core)
    near = share_of(1, after(query_blocks[1], far))
    routing = routing_start(own_live, expert_ids, gate_values, far)
    far = swap_y(far)
    attended, packed = normalize(
        lengths[0], own, swap_core(after(near, far, routing)), far, residual, norm_gain[None, :]
    )
    moe_out = experts_by_gather(
        packed, routing, top_count, capacity, up_gate_weight, down_weight
    )
    return (attended, moe_out)


def per_device(
    queries,
    fresh_key_values,
    cache,
    lengths,
    out_weight,
    residual,
    norm_gain,
    expert_ids,
    gate_values,
    up_gate_weight,
    down_weight,
):
    seq_devices = lax.axis_size("sp")
    slot_rows = queries.shape[0]
    head_width = cache.shape[-1] // 2
    model_width = residual.shape[1]
    kv_heads = fresh_key_values.shape[1] // (2 * head_width)
    repeat = seq_devices // kv_heads
    keys_new = fresh_key_values[:, : kv_heads * head_width].reshape(
        slot_rows, kv_heads, 1, head_width
    )
    values_new = fresh_key_values[:, kv_heads * head_width :].reshape(
        slot_rows, kv_heads, 1, head_width
    )
    paired = jnp.concatenate([keys_new, values_new], axis=3)
    spread = jnp.broadcast_to(paired, (slot_rows, kv_heads, repeat, 2 * head_width)).reshape(
        slot_rows, seq_devices * 2 * head_width
    )
    all_lengths = lax.all_gather(lengths, "sp", axis=1, tiled=True)
    queries_by_head, head_kv = (
        lax.all_to_all(queries, "sp", split_axis=1, concat_axis=0, tiled=True),
        lax.all_to_all(spread, "sp", split_axis=1, concat_axis=0, tiled=True),
    )
    cache_block = cache[0, 0]
    my_index = lax.axis_index("sp")
    for bit_pos in range(repeat.bit_length() - 1):
        partner = partner_2(cache_block, "sp", bit_pos)
        is_upper = my_index // 2**bit_pos % 2 == 1
        cache_block = jnp.where(
            is_upper,
            jnp.concatenate([partner, cache_block], axis=0),
            jnp.concatenate([cache_block, partner], axis=0),
        )
    stretch_lens = all_lengths[0]
    offsets = jnp.cumsum(stretch_lens) - stretch_lens
    rows_of_group = queries_by_head.shape[0]
    slot_ids = jnp.arange(rows_of_group, dtype=jnp.int32)
    source = slot_ids // slot_rows
    within = slot_ids % slot_rows
    from_device = source[:, None] == jnp.arange(seq_devices, dtype=jnp.int32)[None, :]
    is_live = within < jnp.sum(jnp.where(from_device, stretch_lens[None, :], 0), axis=1)
    position = within + jnp.sum(jnp.where(from_device, offsets[None, :], 0), axis=1)
    per_dev = queries_by_head.shape[1] // head_width
    cache_len = cache_block.shape[0]
    key_all = jnp.concatenate([cache_block[:, :head_width], head_kv[:, :head_width]], axis=0)
    value_all = jnp.concatenate([cache_block[:, head_width:], head_kv[:, head_width:]], axis=0)
    block_count = 2 if rows_of_group % 2 == 0 and rows_of_group >= 1024 else 1
    block_rows = rows_of_group // block_count

    def attend(parts):
        query_block, place_block = parts
        scores = jnp.einsum(
            "rhd,kd->hrk", query_block, key_all, preferred_element_type=jnp.float32
        ) / math.sqrt(head_width)
        allowed = jnp.concatenate(
            [
                jnp.ones((block_rows, cache_len), dtype=bool),
                is_live[None, :] & (position[None, :] <= place_block[:, None]),
            ],
            axis=1,
        )
        scores = jnp.where(allowed[None], scores, -jnp.inf)
        row_max = jnp.max(scores, axis=-1, keepdims=True)
        weights = jnp.exp(scores - row_max)
        totals = jnp.sum(weights, axis=-1, keepdims=True)
        result = (
            jnp.einsum(
                "hrk,kd->hrd",
                weights.astype(jnp.bfloat16),
                value_all,
                preferred_element_type=jnp.float32,
            )
            / totals
        )
        return (
            result.astype(jnp.bfloat16).transpose(1, 0, 2).reshape(block_rows, per_dev * head_width)
        )

    attn_heads = lax.map(
        attend,
        (
            queries_by_head.reshape(block_count, block_rows, per_dev, head_width),
            position.reshape(block_count, block_rows),
        ),
    ).reshape(rows_of_group, per_dev * head_width)
    attn_sum = lax.psum_scatter(
        jnp.dot(attn_heads, out_weight, preferred_element_type=jnp.float32).astype(jnp.bfloat16),
        "sp",
        scatter_dimension=0,
        tiled=True,
    ).astype(jnp.float32)
    own_live = jnp.arange(slot_rows, dtype=jnp.int32) < lengths[0, 0]
    attended = jnp.where(own_live[:, None], attn_sum, 0.0).astype(jnp.bfloat16)
    mixed_rows = residual.astype(jnp.float32) + attn_sum
    normed = (
        mixed_rows
        * lax.rsqrt(jnp.mean(mixed_rows * mixed_rows, axis=-1, keepdims=True) + 1e-06)
        * norm_gain
    ).astype(jnp.bfloat16)
    group_count = lax.axis_size("grp")
    experts = up_gate_weight.shape[0] * group_count * seq_devices
    top_count = expert_ids.shape[1]
    capacity = max(2, 8 * slot_rows * top_count // (5 * experts))
    hidden_width = down_weight.shape[1]
    choose = expert_ids[:, :, None] == jnp.arange(experts, dtype=jnp.int32)[None, None, :]
    routed = (jnp.any(choose, axis=1) & own_live[:, None]).astype(jnp.float32)
    earlier = (jnp.arange(slot_rows)[:, None] > jnp.arange(slot_rows)[None, :]).astype(jnp.float32)
    prefix = jnp.dot(earlier, routed, precision=lax.Precision.HIGHEST)
    slot_in = jnp.sum(jnp.where(choose, prefix[:, None, :], 0.0), axis=2).astype(jnp.int32)
    dump_slot = experts * capacity
    target = jnp.where(own_live[:, None], expert_ids * capacity + slot_in, dump_slot)
    source_rows = (
        jnp.full((dump_slot + 1,), slot_rows, jnp.int32)
        .at[target.reshape(-1)]
        .set(jnp.repeat(jnp.arange(slot_rows, dtype=jnp.int32), top_count))[:dump_slot]
    )
    padded = jnp.concatenate([normed, jnp.zeros((1, model_width), jnp.bfloat16)], axis=0)
    outgoing = padded[source_rows].reshape(experts, capacity, model_width)
    received = lax.all_to_all(outgoing, ("grp", "sp"), split_axis=0, concat_axis=0, tiled=True)
    flat_rows = received.reshape(-1, model_width)
    projected = jnp.dot(flat_rows, up_gate_weight[0], preferred_element_type=jnp.float32)
    hidden = (jax.nn.silu(projected[:, :hidden_width]) * projected[:, hidden_width:]).astype(
        jnp.bfloat16
    )
    returned = lax.all_to_all(
        jnp.dot(hidden, down_weight[0], preferred_element_type=jnp.float32)
        .astype(jnp.bfloat16)
        .reshape(received.shape),
        ("grp", "sp"),
        split_axis=0,
        concat_axis=0,
        tiled=True,
    )
    back_rows = jnp.concatenate(
        [returned.reshape(dump_slot, model_width), jnp.zeros((1, model_width), jnp.bfloat16)],
        axis=0,
    )
    picked = back_rows[target]
    combined = jnp.sum(gate_values[:, :, None] * picked.astype(jnp.float32), axis=1)
    moe_out = jnp.where(own_live[:, None], combined, 0.0).astype(jnp.bfloat16)
    return (attended, moe_out)


def solution(mesh):
    in_specs = (
        P(("grp", "sp"), None),
        P(("grp", "sp"), None),
        P("grp", "sp", None, None),
        P("grp", "sp"),
        P("sp", None),
        P(("grp", "sp"), None),
        P(),
        P(("grp", "sp"), None),
        P(("grp", "sp"), None),
        P(("grp", "sp"), None, None),
        P(("grp", "sp"), None, None),
    )
    out_specs = (P(("grp", "sp"), None), P(("grp", "sp"), None))
    groups, seq_devices = mesh.shape["grp"], mesh.shape["sp"]

    def run(*args):
        kv_heads = args[1].shape[1] // args[2].shape[-1]
        experts, top_count = args[9].shape[0], args[7].shape[1]
        pairs = seq_devices == kv_heads == 4 and groups % 2 == 0 and experts <= 4 * top_count
        return mapped(per_device_pairs if pairs else per_device)(*args)

    def mapped(body):
        return jax.shard_map(
            body, mesh=mesh, in_specs=in_specs, out_specs=out_specs, check_vma=False
        )

    return run
```
